32 devices in a mesh: dp: 16 (over z, y, x), tensor: 2 (over core).
Axes of the slice: x: 2, y: 2, z: 4, core: 2. Of those that a mesh axis runs over, the one named last changes fastest.
Arguments:
- tokens: bfloat16 [4096, 768], P('dp'), may hold values from -6 to 6
- cotangent: bfloat16 [4096, 768], P('dp'), may hold values from -6 to 6
- attn_gain: float32 [768], P('dp'), may hold values from 0.5 to 1.5
- w_query: float32 [768, 768], P('dp', 'tensor'), may hold values from -0.21875 to 0.21875
- w_key: float32 [768, 768], P('dp', 'tensor'), may hold values from -0.21875 to 0.21875
- w_value: float32 [768, 768], P('dp', 'tensor'), may hold values from -0.21875 to 0.21875
- w_out: float32 [768, 768], P('tensor', 'dp'), may hold values from -0.875 to 0.875
- ffn_gain: float32 [768], P('dp'), may hold values from 0.5 to 1.5
- w_router: float32 [768, 16], P('dp'), may hold values from -0.15625 to 0.15625
- w_sgate: float32 [768, 2048], P('dp', 'tensor'), may hold values from -0.21875 to 0.21875
- w_sup: float32 [768, 2048], P('dp', 'tensor'), may hold values from -0.21875 to 0.21875
- w_sdown: float32 [2048, 768], P('tensor', 'dp'), may hold values from -0.125 to 0.125
- e_gate: float32 [768, 32768], P(None, ('dp', 'tensor')), may hold values from -0.21875 to 0.21875
- e_up: float32 [768, 32768], P(None, ('dp', 'tensor')), may hold values from -0.21875 to 0.21875
- e_down: float32 [32768, 768], P(('dp', 'tensor')), may hold values from -2 to 2
- routes: int32 [4096, 2], P('dp'), may hold values from 0 to 15, all different within a row; in each aligned block of 256 rows (0 to 255, 256 to 511, ...) at most 64 rows name the same one
- segments: int32 [4096], replicated, may hold values from 0 to 15, never falling along the last dimension, each value on 1 to 2048 neighbouring positions
Outputs:
- output: bfloat16 [4096, 768], P('dp')
- token_input_gradient: float32 [4096, 768], P('dp')
- grad_attn_gain: float32 [768], P('dp')
- grad_w_query: float32 [768, 768], P('dp', 'tensor')
- grad_w_key: float32 [768, 768], P('dp', 'tensor')
- grad_w_value: float32 [768, 768], P('dp', 'tensor')
- grad_w_out: float32 [768, 768], P('tensor', 'dp')
- grad_ffn_gain: float32 [768], P('dp')
- grad_w_router: float32 [768, 16], P('dp')
- grad_w_sgate: float32 [768, 2048], P('dp', 'tensor')
- grad_w_sup: float32 [768, 2048], P('dp', 'tensor')
- grad_w_sdown: float32 [2048, 768], P('tensor', 'dp')
- grad_e_gate: float32 [768, 32768], P(None, ('dp', 'tensor'))
- grad_e_up: float32 [768, 32768], P(None, ('dp', 'tensor'))
- grad_e_down: float32 [32768, 768], P(('dp', 'tensor'))
The draws below stay inside these ranges and needn't reach their ends.
Inputs may be any that keep to these rules, and one draw needn't show every extreme that they name: `routes`: the 2 experts of a token differ. Among the 256 rows of one index of dp, no expert is named by more than 64 rows, and in every draw some expert is named by exactly 64 rows of some index. `segments`: document numbers never fall along the tokens; each document holds 1 to 2048 tokens, and one holds exactly 2048.
All inputs are finite; a program needn't handle non-finite values.
Results may differ from the reference program's by a relative error of at most 0.024.
Values may be sent and summed in bfloat16 or wider, within the bound.
A program may use at most 256 MiB of HBM per device.

```python
import math
import jax
import jax.numpy as jnp
import numpy as np
from jax import lax

D = 768
HEADS = 12
HEAD = 64
FF = 2048
EXPERTS = 16
TOP = 2
SH = 2048
WINDOW = 1024
TOK_DEV = 256
TOKENS = 4096
SEQ = 4096
CAP = 64
HID = 1024
QW = 768
DOCS = 16
N_DP = 16


def steps_of(rng, extent, shards, low, top_value):
    def one(dim, blocks):
        steps = jax.random.uniform(jax.random.fold_in(jax.random.fold_in(rng, 6), dim), (blocks,), jnp.float32, low / len(shards), top_value / len(shards))
        return jnp.repeat(jnp.exp(steps), extent[dim] // blocks).reshape((-1,) + (1,) * (len(extent) - dim - 1))

    loudness = one(*shards[0])
    for cut in shards[1:]:
        loudness = loudness * one(*cut)
    return loudness


def split_up(count, total, most, lean):
    portions = [(1 << 20) // math.isqrt(grade ** lean) + 1 for grade in range(2, count + 1)]
    rest, holding = total - most - (count - 1), [1] * (count - 1)
    while rest > 0:
        movable = [i for i in range(count - 1) if holding[i] < most]
        pool, remaining = sum([portions[i] for i in movable]), rest
        for i in movable:
            extra = min(most - holding[i], max(1, remaining * portions[i] // pool), rest)
            holding[i] = holding[i] + extra
            rest = rest - extra
    return np.array([most] + holding)


def ragged_sizes(own_key, count, total, limit, skew):
    if count == 2:
        one = jax.random.randint(own_key, (), max(1, total - limit), min(limit, total - 1) + 1)
        return jnp.stack([one, total - one])
    tallies = jnp.asarray(split_up(count, total, limit, skew), jnp.int32)
    twos = (count - 1) // 2
    donor, taker = tallies[1:1 + 2 * twos:2], tallies[2:2 + 2 * twos:2]
    margin = jnp.minimum(donor - 1, limit - taker)
    moved = jax.random.randint(jax.random.fold_in(own_key, 1), (twos,), 0, 1 << 20) % (margin + 1)
    tallies = tallies.at[1:1 + 2 * twos:2].set(donor - moved).at[2:2 + 2 * twos:2].set(taker + moved)
    return tallies[jax.random.permutation(jax.random.fold_in(own_key, 2), count)]


def deal_out(stream_key, own, number, rows, amount, top, limit, skew):
    sequence = jax.random.permutation(stream_key, amount)
    crowded, ordinary = load_shares(amount, rows * top, limit, skew, True), load_shares(amount, rows * top, limit, skew, False)
    places = jnp.arange(amount)

    def named(tallies, rotation):
        used = int((tallies > 0).sum())
        fixed = max(1, used // 4)
        shifted = fixed + (places - fixed + rotation * (used - fixed)) % max(1, amount - fixed)
        return jnp.zeros((amount,), jnp.int32).at[sequence[jnp.where(places < fixed, places, shifted)]].set(jnp.asarray(tallies, jnp.int32))

    tallies = jnp.where(number % 4 == 0, named(crowded, number // 4), named(ordinary, number - number // 4 - 1))
    mixed = jax.random.permutation(jax.random.fold_in(own, 3), amount)
    donor, receiver = mixed[0:amount // 2 * 2:2], mixed[1:amount // 2 * 2:2]
    slack = jnp.minimum(tallies[donor] - 1, limit - tallies[receiver]) // 2
    slack = jnp.where((donor == sequence[0]) | (receiver == sequence[0]) | (tallies[receiver] == 0), 0, jnp.maximum(slack, 0))
    shifted = jax.random.randint(jax.random.fold_in(own, 4), (amount // 2,), 0, 1 << 20) % (slack + 1)
    tallies = tallies.at[donor].add(-shifted).at[receiver].add(shifted)
    items = jnp.searchsorted(jnp.cumsum(tallies), jnp.arange(rows * top), side="right").astype(jnp.int32)
    grid = items.reshape(top, rows).T
    grid = grid[jax.random.permutation(jax.random.fold_in(own, 1), rows)]
    rotation = jax.random.randint(jax.random.fold_in(own, 2), (rows, 1), 0, top)
    return jnp.take_along_axis(grid, (jnp.arange(top)[None, :] + rotation) % top, axis=1)


def load_shares(count, total, reach, skew, full):
    loads = [(1 << 20) // math.isqrt(grade ** skew) + 1 for grade in range(1, count + 1)]
    largest = reach if full else min(reach, max(-(-total // count), total * loads[0] // sum(loads)))
    least = 1 if total - largest >= count - 1 else 0
    holding, spare = [largest] + [least] * (count - 1), total - largest - least * (count - 1)
    while spare > 0:
        candidates = [i for i in range(1, count) if holding[i] < largest] or [i for i in range(1, count) if holding[i] < reach]
        whole, remaining = sum([loads[i] for i in candidates]), spare
        for i in candidates:
            addition = min(reach - holding[i], max(1, remaining * loads[i] // whole), spare)
            holding[i] = holding[i] + addition
            spare = spare - addition
    return np.array(holding)


def noise(key, extent, scale, bound, shards=(), held_as=jnp.bfloat16):
    result = jax.random.normal(key, extent, jnp.float32) * scale
    if len(shards) > 0:
        result = steps_of(key, extent, shards, -0.22, 0.18) * result
    return jnp.clip(result, min=-bound, max=bound).astype(held_as)


def setup_inputs(seed: int = 0) -> dict:
    arg_keys = jax.random.split(jax.random.key(seed), 18)
    tokens = noise(arg_keys[0], (TOKENS, D), 1.0, 6.0, ((0, 16),))
    cotangent = noise(arg_keys[1], (TOKENS, D), 1.0, 6.0, ((0, 16),))
    attn_gain = jnp.clip(1.0 + 0.1 * jax.random.normal(arg_keys[2], (D,), jnp.float32), 0.5, 1.5)
    w_query = noise(arg_keys[3], (D, QW), D ** -0.5, 0.21875, ((0, 16), (1, 2)), jnp.float32)
    w_key = noise(arg_keys[4], (D, QW), D ** -0.5, 0.21875, ((0, 16), (1, 2)), jnp.float32)
    w_value = noise(arg_keys[5], (D, QW), D ** -0.5, 0.21875, ((0, 16), (1, 2)), jnp.float32)
    w_out = noise(arg_keys[6], (QW, D), (QW // 16) ** -0.5, 0.875, ((0, 2), (1, 16)), jnp.float32)
    ffn_gain = jnp.clip(1.0 + 0.1 * jax.random.normal(arg_keys[7], (D,), jnp.float32), 0.5, 1.5)
    w_router = noise(arg_keys[8], (D, EXPERTS), (2 * D) ** -0.5, 0.15625, ((0, 16),), jnp.float32)
    w_sgate = noise(arg_keys[9], (D, SH), D ** -0.5, 0.21875, ((0, 16), (1, 2)), jnp.float32)
    w_sup = noise(arg_keys[10], (D, SH), D ** -0.5, 0.21875, ((0, 16), (1, 2)), jnp.float32)
    w_sdown = noise(arg_keys[11], (SH, D), SH ** -0.5, 0.125, ((0, 2), (1, 16)), jnp.float32)
    e_gate = noise(arg_keys[12], (D, EXPERTS * FF), D ** -0.5, 0.21875, ((1, 32),), jnp.float32)
    e_up = noise(arg_keys[13], (D, EXPERTS * FF), D ** -0.5, 0.21875, ((1, 32),), jnp.float32)
    e_down = noise(arg_keys[14], (EXPERTS * FF, D), (max(FF // 256, 1)) ** -0.5, 2.0, ((0, 32),), jnp.float32)
    routes_keys = jax.random.split(jax.random.fold_in(arg_keys[15], 1), TOKENS // TOK_DEV)
    routes_turns = jax.random.permutation(jax.random.fold_in(arg_keys[15], 3), TOKENS // TOK_DEV)
    routes = jax.vmap(lambda own, number: deal_out(jax.random.fold_in(arg_keys[15], 2), own, number, TOK_DEV, EXPERTS, TOP, CAP, 1))(routes_keys, routes_turns).reshape((TOKENS, TOP))
    segments = jnp.searchsorted(jnp.cumsum(ragged_sizes(arg_keys[16], DOCS, TOKENS, 8 * TOK_DEV, 2)), jnp.arange(TOKENS), side="right").astype(jnp.int32)
    return {"tokens": tokens, "cotangent": cotangent, "attn_gain": attn_gain, "w_query": w_query, "w_key": w_key, "w_value": w_value, "w_out": w_out, "ffn_gain": ffn_gain, "w_router": w_router, "w_sgate": w_sgate, "w_sup": w_sup, "w_sdown": w_sdown, "e_gate": e_gate, "e_up": e_up, "e_down": e_down, "routes": routes, "segments": segments}


@jax.custom_vjp
def low(v):
    return lax.optimization_barrier(v.astype(jnp.bfloat16)).astype(jnp.float32)

@jax.custom_vjp
def low_back(v):
    return v

def low_keep(v):
    return (low(v), None)

def low_pass(kept, grad):
    return (grad,)

def back_keep(v):
    return (v, None)

def back_low(kept, grad):
    return (low(grad),)
low.defvjp(low_keep, low_pass)
low_back.defvjp(back_keep, back_low)
highest = lax.Precision.HIGHEST
eps = 1e-06
masked = -1e+30

def product(left, right):
    return jnp.dot(left, right, precision=highest)

def rms_norm(values, gain):
    return values * lax.rsqrt(lax.optimization_barrier(jnp.mean(values * values, axis=-1, keepdims=True)) + eps) * gain

def rotary(token_rows):
    freqs = 10000.0 ** (-jnp.arange(HEAD // 2, dtype=jnp.float32) * (2.0 / HEAD))
    phase = (token_rows % SEQ).astype(jnp.float32)[:, None] * freqs[None, :]
    return (jnp.cos(phase)[:, None, :], jnp.sin(phase)[:, None, :])

def rotate(values, cosines, sines):
    half = HEAD // 2
    first = values[..., :half]
    second = values[..., half:]
    return jnp.concatenate([first * cosines - second * sines, second * cosines + first * sines], axis=-1)

def softmax_rows(scores):
    peak = lax.optimization_barrier(jnp.max(scores, axis=-1, keepdims=True))
    expo = jnp.exp(scores - peak)
    return expo / lax.optimization_barrier(jnp.sum(expo, axis=-1, keepdims=True))

def attend(queries, keys, values, segments):
    total = queries.shape[0]
    block = TOK_DEV
    span = WINDOW + block
    pad_keys = jnp.concatenate([jnp.zeros((WINDOW,) + keys.shape[1:], jnp.float32), keys], axis=0)
    pad_values = jnp.concatenate([jnp.zeros((WINDOW,) + values.shape[1:], jnp.float32), values], axis=0)
    pad_segments = jnp.concatenate([jnp.full((WINDOW,), -1, jnp.int32), segments], axis=0)

    def one_block(start):
        query_block = lax.dynamic_slice_in_dim(queries, start, block, 0)
        key_block = lax.dynamic_slice_in_dim(pad_keys, start, span, 0)
        value_block = lax.dynamic_slice_in_dim(pad_values, start, span, 0)
        seg_query = lax.dynamic_slice_in_dim(segments, start, block, 0)
        seg_key = lax.dynamic_slice_in_dim(pad_segments, start, span, 0)
        later = (start + jnp.arange(block, dtype=jnp.int32))[:, None]
        earlier = (start - WINDOW + jnp.arange(span, dtype=jnp.int32))[None, :]
        valid = (earlier >= 0) & (earlier <= later) & (later - earlier < WINDOW)
        valid = valid & (earlier // SEQ == later // SEQ) & (seg_key[None, :] == seg_query[:, None])
        scores = low_back(jnp.einsum('qhe,khe->hqk', query_block, key_block, precision=highest))
        scores = jnp.where(valid[None, :, :], scores, masked)
        weights = softmax_rows(scores)
        return jnp.einsum('hqk,khe->qhe', low(weights), value_block, precision=highest)
    starts = jnp.arange(total // block, dtype=jnp.int32) * block
    blocks_out = lax.map(jax.checkpoint(one_block), starts)
    return blocks_out.reshape(total, HEADS * HEAD)

def experts(branch_in, routes, e_gate, e_up, e_down):
    total = branch_in.shape[0]
    pair_expert = routes.reshape(-1)
    pair_token = jnp.arange(total * TOP, dtype=jnp.int32) // TOP
    order = jnp.argsort(pair_expert, stable=True).astype(jnp.int32)
    counts = lax.optimization_barrier(jnp.sum((pair_expert[:, None] == jnp.arange(EXPERTS, dtype=jnp.int32)[None, :]).astype(jnp.int32), axis=0))
    firsts = jnp.cumsum(counts) - counts
    room = N_DP * CAP
    padded = jnp.concatenate([order, jnp.zeros((room,), jnp.int32)])
    picks = padded[firsts[:, None] + jnp.arange(room, dtype=jnp.int32)[None, :]]
    alive = (jnp.arange(room, dtype=jnp.int32)[None, :] < counts[:, None]).astype(jnp.float32)
    blocks = FF // HID
    gate_all = low(e_gate).reshape(D, EXPERTS, blocks, HID)
    up_all = low(e_up).reshape(D, EXPERTS, blocks, HID)
    down_all = low(e_down).reshape(EXPERTS, blocks, HID, D)

    def one_expert(operands):
        expert, pick_row, alive_row = operands
        rows_in = branch_in[pair_token[pick_row]]
        spread = low_back(jnp.broadcast_to(rows_in[:, None, :], (room, blocks, D)))
        gate_hidden = low_back(jnp.einsum('rbd,dbh->rbh', spread, gate_all[:, expert], precision=highest))
        up_hidden = low_back(jnp.einsum('rbd,dbh->rbh', spread, up_all[:, expert], precision=highest))
        hidden = low(jax.nn.silu(gate_hidden) * up_hidden)
        parts = low(jnp.einsum('rbh,bhd->rbd', hidden, down_all[expert], precision=highest))
        return low_back(lax.optimization_barrier(jnp.sum(parts, axis=1))) * alive_row[:, None]
    results = lax.map(jax.checkpoint(one_expert), (jnp.arange(EXPERTS, dtype=jnp.int32), picks, alive))
    pair_out = jnp.zeros((total * TOP, D), jnp.float32).at[picks.reshape(-1)].add(results.reshape(-1, D))
    return pair_out.reshape(total, TOP, D)

def layer(tokens, attn_gain, w_query, w_key, w_value, w_out, ffn_gain, w_router, w_sgate, w_sup, w_sdown, e_gate, e_up, e_down, routes, segments):
    total = tokens.shape[0]
    cosines, sines = rotary(jnp.arange(total, dtype=jnp.int32))
    head_shape = (total, HEADS, HEAD)
    attn_in = low(rms_norm(tokens, low(attn_gain)))
    queries = low(rotate(low_back(product(attn_in, low(w_query))).reshape(head_shape), cosines, sines) * HEAD ** (-0.5))
    keys = low(rotate(low_back(product(attn_in, low(w_key))).reshape(head_shape), cosines, sines))
    values = low(low_back(product(attn_in, low(w_value))).reshape(head_shape))
    heads_out = low(low_back(attend(queries, keys, values, segments)))
    middle = tokens + low_back(product(heads_out, low(w_out)))
    branch_in = low(rms_norm(middle, low(ffn_gain)))
    logits = low_back(product(branch_in, low(w_router)))
    probs_router = softmax_rows(logits)
    picked = (routes[:, :, None] == jnp.arange(EXPERTS, dtype=jnp.int32)[None, None, :]).astype(jnp.float32)
    gates = lax.optimization_barrier(jnp.sum(probs_router[:, None, :] * picked, axis=-1))
    shared_gate = low_back(product(branch_in, low(w_sgate)))
    shared_up = low_back(product(branch_in, low(w_sup)))
    shared_hidden = low(jax.nn.silu(shared_gate) * shared_up)
    shared_out = low_back(product(shared_hidden, low(w_sdown)))
    expert_out = experts(branch_in, routes, e_gate, e_up, e_down)
    return middle + shared_out + lax.optimization_barrier(jnp.sum(gates[:, :, None] * expert_out, axis=1))

def reference(tokens, cotangent, attn_gain, w_query, w_key, w_value, w_out, ffn_gain, w_router, w_sgate, w_sup, w_sdown, e_gate, e_up, e_down, routes, segments):
    primals = (tokens.astype(jnp.float32), attn_gain, w_query, w_key, w_value, w_out, ffn_gain, w_router, w_sgate, w_sup, w_sdown, e_gate, e_up, e_down)

    def forward(*inputs):
        return layer(*inputs, routes, segments)
    after, pullback = jax.vjp(forward, *primals)
    grads = pullback(cotangent.astype(jnp.float32))
    return (after.astype(jnp.bfloat16), grads[0], grads[1], grads[2], grads[3], grads[4], grads[5], grads[6], grads[7], grads[8], grads[9], grads[10], grads[11], grads[12], grads[13])
```

```python
import functools

import jax
import jax.numpy as jnp
from jax import lax
from jax.experimental import pallas as pl
from jax.experimental.pallas import tpu as pltpu
from jax.sharding import PartitionSpec as P

HEAD = 64
WINDOW = 1024
LANES = 128
PLANE = 4

MESH = pl.DeviceIdType.MESH
f32 = jnp.float32
bf16 = jnp.bfloat16

eps = 1e-06
masked = -1e30


def matmul(left, right):
    return jnp.dot(left, right, preferred_element_type=f32)


def weight_grad(left, right):
    return lax.dot_general(
        left, right, (((0,), (0,)), ((), ())), preferred_element_type=f32
    )


def input_grad(left, right):
    return lax.dot_general(
        left, right, (((1,), (1,)), ((), ())), preferred_element_type=f32
    )


def rms_parts(values):
    factor = lax.rsqrt(jnp.mean(values * values, axis=-1, keepdims=True) + eps)
    return (values * factor, factor)


def rotary_tables(positions):
    freqs = 10000.0 ** (-jnp.arange(HEAD // 2, dtype=f32) * (2.0 / HEAD))
    phase = positions.astype(f32)[:, None] * freqs[None, :]
    return (jnp.cos(phase)[:, None, :], jnp.sin(phase)[:, None, :])


def rotate(values, cosines, sines):
    half = values.shape[-1] // 2
    first = values[..., :half]
    second = values[..., half:]
    return jnp.concatenate(
        [first * cosines - second * sines, second * cosines + first * sines], axis=-1
    )


def unrotate(grads, cosines, sines):
    half = grads.shape[-1] // 2
    first = grads[..., :half]
    second = grads[..., half:]
    return jnp.concatenate(
        [first * cosines + second * sines, second * cosines - first * sines], axis=-1
    )


def silu_grad(values):
    sigma = jax.nn.sigmoid(values)
    return sigma * (1.0 + values * (1.0 - sigma))


def masked_scores(queries, keys, valid):
    scores = jnp.einsum("qhe,khe->hqk", queries, keys, preferred_element_type=f32)
    return jnp.where(valid[None, :, :], scores, masked)


def digits(me):
    return lax.div(me, PLANE), lax.rem(lax.div(me, 2), 2), lax.rem(me, 2)


def index_of(z, y, x):
    return z * PLANE + y * 2 + x


def push(src, dst, send, recv, device):
    copy = pltpu.make_async_remote_copy(
        src_ref=src,
        dst_ref=dst,
        send_sem=send,
        recv_sem=recv,
        device_id=device,
        device_id_type=MESH,
    )
    copy.start()
    return copy


def greet(devices):
    barrier = pltpu.get_barrier_semaphore()
    for device in devices:
        pl.semaphore_signal(barrier, inc=1, device_id=device, device_id_type=MESH)
    pl.semaphore_wait(barrier, len(devices))


def comm_params(collective_id, limit=48 << 20):
    return pltpu.CompilerParams(
        collective_id=collective_id, has_side_effects=True, vmem_limit_bytes=limit
    )


def dma(*shape):
    return pltpu.SemaphoreType.DMA(shape)


IN_HBM = pl.BlockSpec(memory_space=pl.ANY)
IN_VMEM = pl.BlockSpec(memory_space=pltpu.VMEM)


def grid_peers(depth, z, y, x):
    peers = [{"dp": index_of(lax.rem(z + k, depth), y, x)} for k in range(1, depth)]
    return peers, {"dp": index_of(z, 1 - y, x)}, {"dp": index_of(z, y, 1 - x)}


def gather_kernel(
    depth, reach, cuts, shard, tok, full, window,
    z_send, z_recv, p_send, p_recv, t_send, t_recv, f_send, f_recv, own,
):
    n = depth * PLANE
    me, core = lax.axis_index("dp"), lax.axis_index("tensor")
    z, y, x = digits(me)
    z_peers, y_peer, x_peer = grid_peers(depth, z, y, x)
    sibling = {"tensor": 1 - core}
    ahead = [{"dp": lax.rem(me + k, n)} for k in range(1, reach + 1)]
    behind = [{"dp": lax.rem(me + n - k, n)} for k in range(1, reach + 1)]
    greet(z_peers + [y_peer, x_peer, sibling] + ahead + behind)
    own_shard = pltpu.make_async_copy(shard, full.at[z, y, x], own.at[0])
    own_shard.start()
    own_tok = pltpu.make_async_copy(tok, window.at[reach], own.at[1])
    own_tok.start()
    half = tok.shape[0] // 2
    rows = pl.ds(pl.multiple_of(core * half, half), half)
    z_copies = []
    t_copies = []
    for c, (start, middle, stop) in enumerate(cuts):
        cols = pl.ds(start, stop - start)
        z_copies.append(
            [
                push(
                    shard.at[:, cols],
                    full.at[z, y, x, :, cols],
                    z_send.at[c, k],
                    z_recv.at[c, k],
                    z_peers[k],
                )
                for k in range(depth - 1)
            ]
        )
        if c == 0:
            for k in range(reach):
                t_copies.append(
                    push(
                        tok.at[rows],
                        window.at[reach - 1 - k, rows],
                        t_send.at[k],
                        t_recv.at[k],
                        ahead[k],
                    )
                )
    own_shard.wait()
    second, third, forwards = [], [], []
    for c in range(len(cuts) + 2):
        if c < len(cuts):
            start, middle, stop = cuts[c]
            left, right = pl.ds(start, middle - start), pl.ds(middle, stop - middle)
            for copy in z_copies[c]:
                copy.wait_recv()
            second.append(
                [
                    push(
                        full.at[:, y, x, :, left],
                        full.at[:, y, x, :, left],
                        p_send.at[c, 0],
                        p_recv.at[c, 0],
                        y_peer,
                    ),
                    push(
                        full.at[:, y, x, :, right],
                        full.at[:, y, x, :, right],
                        p_send.at[c, 1],
                        p_recv.at[c, 1],
                        x_peer,
                    ),
                ]
            )
        if c == 0:
            for k, copy in enumerate(t_copies):
                copy.wait_recv()
                forwards.append(
                    push(
                        window.at[reach - 1 - k, rows],
                        window.at[reach - 1 - k, rows],
                        f_send.at[k],
                        f_recv.at[k],
                        sibling,
                    )
                )
        if 1 <= c <= len(cuts):
            start, middle, stop = cuts[c - 1]
            left, right = pl.ds(start, middle - start), pl.ds(middle, stop - middle)
            for copy in second[c - 1]:
                copy.wait_recv()
            third.append(
                [
                    push(
                        full.at[:, :, x, :, left],
                        full.at[:, :, x, :, left],
                        p_send.at[c - 1, 2],
                        p_recv.at[c - 1, 2],
                        x_peer,
                    ),
                    push(
                        full.at[:, y, :, :, right],
                        full.at[:, y, :, :, right],
                        p_send.at[c - 1, 3],
                        p_recv.at[c - 1, 3],
                        y_peer,
                    ),
                ]
            )
    for copies in third:
        for copy in copies:
            copy.wait_recv()
    for copy in forwards:
        copy.wait_recv()
    own_tok.wait()
    for copies in z_copies + second + third + [t_copies, forwards]:
        for copy in copies:
            copy.wait_send()


def gather_all(shard, tokens, depth, reach, cuts):
    parts = len(cuts)
    full, window = pl.pallas_call(
        functools.partial(gather_kernel, depth, reach, cuts),
        out_shape=(
            jax.ShapeDtypeStruct((depth, 2, 2) + shard.shape, shard.dtype),
            jax.ShapeDtypeStruct((reach + 1,) + tokens.shape, tokens.dtype),
        ),
        in_specs=[IN_HBM] * 2,
        out_specs=(IN_HBM, IN_HBM),
        scratch_shapes=[
            dma(parts, depth - 1), dma(parts, depth - 1), dma(parts, 4), dma(parts, 4),
            dma(reach), dma(reach), dma(reach), dma(reach), dma(2),
        ],
        compiler_params=comm_params(1),
        name="gather_weights",
    )(shard, tokens)
    return full.reshape(-1, shard.shape[1]), window.reshape(-1, tokens.shape[1])


def swap_kernel(count, *refs):
    sources, targets, (send, recv) = refs[:count], refs[count : 2 * count], refs[2 * count :]
    sibling = {"tensor": 1 - lax.axis_index("tensor")}
    greet([sibling])
    copies = [
        push(a, b, send.at[i], recv.at[i], sibling)
        for i, (a, b) in enumerate(zip(sources, targets))
    ]
    for copy in copies:
        copy.wait()


def swap(arrays, collective_id):
    count = len(arrays)
    return pl.pallas_call(
        functools.partial(swap_kernel, count),
        out_shape=tuple(jax.ShapeDtypeStruct(a.shape, a.dtype) for a in arrays),
        in_specs=[IN_VMEM] * count,
        out_specs=(IN_VMEM,) * count,
        scratch_shapes=[dma(count), dma(count)],
        compiler_params=comm_params(collective_id),
        name="swap_cores",
    )(*arrays)


def dispatch_kernel(n, owners, first, second, got_first, got_second, send, recv, f_send, f_recv, own):
    me, core = lax.axis_index("dp"), lax.axis_index("tensor")
    sibling = {"tensor": 1 - core}
    greet([{"dp": lax.rem(me + k, n)} for k in range(1, n)] + [sibling])
    half = first.shape[-1] // 2
    cols = pl.ds(pl.multiple_of(core * half, half), half)
    pairs = ((first, got_first), (second, got_second))
    mine = lax.div(me, owners)
    copies = []
    for k in range(1, n):
        to = lax.rem(me + k, n)
        for i, (source, target) in enumerate(pairs):
            copies.append(
                push(
                    source.at[lax.div(to, owners), :, cols],
                    target.at[me, :, cols],
                    send.at[i, k],
                    recv.at[i, k],
                    {"dp": to},
                )
            )
    local = [
        pltpu.make_async_copy(source.at[mine], target.at[me], own.at[i])
        for i, (source, target) in enumerate(pairs)
    ]
    for copy in local:
        copy.start()
    forwards = []
    for k in range(1, n):
        source_of = lax.rem(me + n - k, n)
        for i, (source, target) in enumerate(pairs):
            copies[2 * (k - 1) + i].wait_recv()
            block = target.at[source_of, :, cols]
            forwards.append(push(block, block, f_send.at[i, k], f_recv.at[i, k], sibling))
    for copy in forwards:
        copy.wait_recv()
    for copy in local:
        copy.wait()
    for copy in copies + forwards:
        copy.wait_send()


def dispatch(first, second, n, owners):
    shape = jax.ShapeDtypeStruct((n,) + first.shape[1:], first.dtype)
    return pl.pallas_call(
        functools.partial(dispatch_kernel, n, owners),
        out_shape=(shape, shape),
        in_specs=[IN_HBM] * 2,
        out_specs=(IN_HBM, IN_HBM),
        scratch_shapes=[dma(2, n), dma(2, n), dma(2, n), dma(2, n), dma(2)],
        compiler_params=comm_params(2),
        name="dispatch_rows",
    )(first, second)


def return_kernel(n, groups, first, second, got_first, got_second, part, total, send, recv, f_send, f_recv, own):
    me, core = lax.axis_index("dp"), lax.axis_index("tensor")
    sibling = {"tensor": 1 - core}
    greet([{"dp": lax.rem(me + k, n)} for k in range(1, n)] + [sibling])
    half = first.shape[-1] // 2
    mine = pl.ds(pl.multiple_of(core * half, half), half)
    theirs = pl.ds(pl.multiple_of((1 - core) * half, half), half)
    pairs = ((first, got_first), (second, got_second))
    each = n // groups
    swaps = []
    for g in range(groups):
        block = pl.ds(g * each, each)
        for i, (source, target) in enumerate(pairs):
            swaps.append(
                push(
                    source.at[block, :, theirs],
                    part.at[i, block],
                    f_send.at[i, g],
                    f_recv.at[i, g],
                    sibling,
                )
            )
    for g in range(groups):
        block = pl.ds(g * each, each)
        for i, (source, target) in enumerate(pairs):
            swaps[2 * g + i].wait_recv()
            total[i, block] = (
                source[block, :, mine].astype(f32) + part[i, block].astype(f32)
            ).astype(bf16)
        for slot in range(g * each, (g + 1) * each):
            for i, (source, target) in enumerate(pairs):
                @pl.when(slot != me)
                def _():
                    push(
                        total.at[i, slot],
                        target.at[me],
                        send.at[i, slot],
                        recv.at[i, me],
                        {"dp": slot},
                    )
    local = [
        pltpu.make_async_copy(total.at[i, me], pairs[i][1].at[me], own.at[i]) for i in range(2)
    ]
    for copy in local:
        copy.start()
    for k in range(1, n):
        to, source_of = lax.rem(me + k, n), lax.rem(me + n - k, n)
        for i, (source, target) in enumerate(pairs):
            pltpu.make_async_remote_copy(
                total.at[i, to], target.at[source_of], send.at[i, to], recv.at[i, source_of],
                device_id={"dp": to}, device_id_type=MESH,
            ).wait()
    for copy in local:
        copy.wait()
    for copy in swaps:
        copy.wait_send()


def give_back(first, second, groups=4):
    n, capacity, width = first.shape
    half = jax.ShapeDtypeStruct((n, capacity, width // 2), first.dtype)
    buffer = pltpu.VMEM((2, n, capacity, width // 2), first.dtype)
    return pl.pallas_call(
        functools.partial(return_kernel, n, groups),
        out_shape=(half, half),
        in_specs=[IN_VMEM] * 2,
        out_specs=(IN_HBM, IN_HBM),
        scratch_shapes=[buffer, buffer, dma(2, n), dma(2, n), dma(2, groups), dma(2, groups), dma(2)],
        compiler_params=comm_params(3),
        name="return_rows",
    )(first, second)


def scatter_kernel(
    depth, reach, cuts, per_core, grads, d_part, total, d_full,
    first_l, first_r, second_l, second_r, last, d_swap, d_sum, d_got, gain_got,
    p_send, p_recv, z_send, z_recv, t_send, t_recv, f_send, f_recv,
):
    n = depth * PLANE
    me, core = lax.axis_index("dp"), lax.axis_index("tensor")
    z, y, x = digits(me)
    z_peers, y_peer, x_peer = grid_peers(depth, z, y, x)
    sibling = {"tensor": 1 - core}
    ahead = [{"dp": lax.rem(me + k, n)} for k in range(1, reach + 1)]
    behind = [{"dp": lax.rem(me + n - k, n)} for k in range(1, reach + 1)]
    greet(z_peers + [y_peer, x_peer, sibling] + ahead + behind)
    width = d_part.shape[-1] // 2
    mine = pl.ds(pl.multiple_of(core * width, width), width)
    theirs = pl.ds(pl.multiple_of((1 - core) * width, width), width)
    swapped = push(d_part.at[:, :, theirs], d_swap, f_send.at[0], f_recv.at[0], sibling)
    ones = []
    for c, (start, middle, stop) in enumerate(cuts):
        left, right = pl.ds(start, middle - start), pl.ds(middle, stop - middle)
        ones.append(
            [
                push(
                    grads.at[:, :, 1 - x, :, left],
                    first_l.at[:, :, :, pl.ds(start // 2, middle - start)],
                    p_send.at[c, 0], p_recv.at[c, 0], x_peer,
                ),
                push(
                    grads.at[:, 1 - y, :, :, right],
                    first_r.at[:, :, :, pl.ds(start // 2, stop - middle)],
                    p_send.at[c, 1], p_recv.at[c, 1], y_peer,
                ),
            ]
        )
    swapped.wait_recv()
    d_sum[...] = (d_part[:, :, mine].astype(f32) + d_swap[...].astype(f32)).astype(bf16)
    back = [
        push(d_sum.at[reach - 1 - k], d_got.at[k], t_send.at[k], t_recv.at[k], behind[k])
        for k in range(reach)
    ]
    twos, threes = [], []
    for c in range(len(cuts) + 2):
        if c < len(cuts):
            start, middle, stop = cuts[c]
            span = middle - start
            left, right = pl.ds(start, span), pl.ds(middle, span)
            here = pl.ds(start // 2, span)
            for copy in ones[c]:
                copy.wait_recv()

            def add_first(i, carry):
                for j in range(2):
                    first_l[i, j, :, here] = (
                        first_l[i, j, :, here].astype(f32) + grads[i, j, x, :, left].astype(f32)
                    ).astype(bf16)
                    first_r[i, j, :, here] = (
                        first_r[i, j, :, here].astype(f32) + grads[i, y, j, :, right].astype(f32)
                    ).astype(bf16)
                return carry

            lax.fori_loop(0, depth, add_first, 0)
            twos.append(
                [
                    push(
                        first_l.at[:, 1 - y, :, here], second_l.at[:, :, here],
                        p_send.at[c, 2], p_recv.at[c, 2], y_peer,
                    ),
                    push(
                        first_r.at[:, 1 - x, :, here], second_r.at[:, :, here],
                        p_send.at[c, 3], p_recv.at[c, 3], x_peer,
                    ),
                ]
            )
        if 1 <= c <= len(cuts):
            start, middle, stop = cuts[c - 1]
            span = middle - start
            here = pl.ds(start // 2, span)
            for copy in twos[c - 1]:
                copy.wait_recv()

            def add_second(i, carry):
                second_l[i, :, here] = (
                    second_l[i, :, here].astype(f32) + first_l[i, y, :, here].astype(f32)
                ).astype(bf16)
                second_r[i, :, here] = (
                    second_r[i, :, here].astype(f32) + first_r[i, x, :, here].astype(f32)
                ).astype(bf16)
                return carry

            lax.fori_loop(0, depth, add_second, 0)
            threes.append(
                [
                    push(
                        source.at[lax.rem(z + k + 1, depth), :, here],
                        last.at[k, side, :, here],
                        z_send.at[c - 1, side, k], z_recv.at[c - 1, side, k], z_peers[k],
                    )
                    for side, source in ((0, second_l), (1, second_r))
                    for k in range(depth - 1)
                ]
            )
        if c >= 2:
            start, middle, stop = cuts[c - 2]
            span = middle - start
            here = pl.ds(start // 2, span)
            for copy in threes[c - 2]:
                copy.wait_recv()
            for side, source, at in ((0, second_l, start), (1, second_r, middle)):
                value = source[z, :, here].astype(f32)
                for k in range(depth - 1):
                    value = value + last[k, side, :, here].astype(f32)
                total[:, pl.ds(at, span)] = value
    d_mine = d_sum[reach].astype(f32)
    for k, copy in enumerate(back):
        copy.wait_recv()
        d_mine = d_mine + d_got[k].astype(f32)
    d_full[:, mine] = d_mine.astype(bf16)
    both = push(d_full.at[:, mine], d_full.at[:, mine], f_send.at[1], f_recv.at[1], sibling)
    split = pl.ds(per_core, LANES)
    gain = push(total.at[:, split], gain_got, f_send.at[2], f_recv.at[2], sibling)
    both.wait_recv()
    gain.wait()
    total[:, split] = total[:, split] + gain_got[...]
    for copies in ones + twos + threes + [back, [swapped, both]]:
        for copy in copies:
            copy.wait_send()


def scatter_all(grads, d_part, per_core, depth, reach, cuts):
    rows, columns = grads.shape[0] // (depth * PLANE), grads.shape[1]
    grads = grads.reshape(depth, 2, 2, rows, columns)
    count, width = d_part.shape[0] // (reach + 1), d_part.shape[1]
    d_part = d_part.reshape(reach + 1, count, width)
    parts, half = len(cuts), columns // 2
    first = pltpu.VMEM((depth, 2, rows, half), bf16)
    second = pltpu.VMEM((depth, rows, half), bf16)
    return pl.pallas_call(
        functools.partial(scatter_kernel, depth, reach, cuts, per_core),
        out_shape=(
            jax.ShapeDtypeStruct((rows, columns), f32),
            jax.ShapeDtypeStruct((count, width), bf16),
        ),
        in_specs=[IN_VMEM] * 2,
        out_specs=(IN_VMEM, IN_VMEM),
        scratch_shapes=[
            first, first, second, second,
            pltpu.VMEM((depth - 1, 2, rows, half), bf16),
            pltpu.VMEM((reach + 1, count, width // 2), bf16),
            pltpu.VMEM((reach + 1, count, width // 2), bf16),
            pltpu.VMEM((reach, count, width // 2), bf16),
            pltpu.VMEM((rows, LANES), f32),
            dma(parts, 4), dma(parts, 4),
            dma(parts, 2, depth - 1), dma(parts, 2, depth - 1),
            dma(reach), dma(reach), dma(3), dma(3),
        ],
        compiler_params=comm_params(4),
        name="scatter_grads",
    )(grads, d_part)


def local(
    tokens, cotangent, attn_gain, w_query, w_key, w_value, w_out, ffn_gain, w_router,
    w_sgate, w_sup, w_sdown, e_gate, e_up, e_down, routes, segments,
):
    tok_count, width = tokens.shape
    n = lax.axis_size("dp")
    depth = n // PLANE
    me = lax.axis_index("dp")
    core = lax.axis_index("tensor")
    experts = w_router.shape[1]
    owners = n // experts
    capacity = tok_count // 4
    reach = (WINDOW + tok_count - 1) // tok_count
    score_scale = HEAD ** (-0.5)
    shard_rows = w_query.shape[0]
    heads_width = w_query.shape[1]
    local_heads = heads_width // HEAD
    hidden = w_sgate.shape[1]
    half = width // 2

    small = 2 * LANES
    packed = jnp.concatenate(
        [
            w_query, w_key, w_value, w_out.T,
            jnp.pad(
                jnp.concatenate([w_router, attn_gain[:, None], ffn_gain[:, None]], axis=1),
                ((0, 0), (0, small - experts - 2)),
            ),
            w_sgate, w_sup, w_sdown.T,
        ],
        axis=1,
    ).astype(bf16)
    at_small = 4 * heads_width
    at_shared = at_small + small
    columns = at_shared + 3 * hidden
    edges = [0, at_small, at_shared + hidden, at_shared + 2 * hidden, columns]
    cuts = tuple((a, (a + b) // 2, b) for a, b in zip(edges[:-1], edges[1:]))
    full, window = gather_all(packed, tokens, depth, reach, cuts)
    query_w = full[:, :heads_width]
    key_w = full[:, heads_width : 2 * heads_width]
    value_w = full[:, 2 * heads_width : 3 * heads_width]
    out_t = full[:, 3 * heads_width : at_small]
    router_w = full[:, at_small : at_small + experts]
    gain_first = full[:, at_small + experts].astype(f32)
    gain_second = full[:, at_small + experts + 1].astype(f32)
    sgate_w = full[:, at_shared : at_shared + hidden]
    sup_w = full[:, at_shared + hidden : at_shared + 2 * hidden]
    sdown_t = full[:, at_shared + 2 * hidden :]
    expert_gate = e_gate.astype(bf16)
    expert_up = e_up.astype(bf16)
    expert_down = e_down.astype(bf16)

    span = (reach + 1) * tok_count
    token_rows = me * tok_count + jnp.arange(tok_count, dtype=jnp.int32)
    key_rows = (me - reach) * tok_count + jnp.arange(span, dtype=jnp.int32)
    cos_all, sin_all = rotary_tables(key_rows)
    cosines, sines = cos_all[reach * tok_count :], sin_all[reach * tok_count :]
    padded = jnp.pad(segments, (reach * tok_count, 0), constant_values=-1)
    seg_key = lax.dynamic_slice_in_dim(padded, me * tok_count, span)
    seg_query = seg_key[reach * tok_count :]
    later, earlier = token_rows[:, None], key_rows[None, :]
    valid = (earlier >= 0) & (earlier <= later) & (later - earlier < WINDOW)
    valid = valid & (seg_key[None, :] == seg_query[:, None])
    head_shape = (tok_count, local_heads, HEAD)
    span_shape = (span, local_heads, HEAD)
    x_all = window.astype(f32)
    normed_all, scale_all = rms_parts(x_all)
    attn_in_all = (normed_all * gain_first).astype(bf16)
    attn_in = attn_in_all[reach * tok_count :]
    x_float = tokens.astype(f32)
    normed_one, scale_one = rms_parts(x_float)
    queries = (
        rotate(matmul(attn_in, query_w).reshape(head_shape), cosines, sines) * score_scale
    ).astype(bf16)
    all_keys = rotate(matmul(attn_in_all, key_w).reshape(span_shape), cos_all, sin_all).astype(bf16)
    all_values = matmul(attn_in_all, value_w).astype(bf16).reshape(span_shape)
    scores = masked_scores(queries, all_keys, valid)
    peak = jnp.max(scores, axis=-1, keepdims=True)
    lse = peak + jnp.log(jnp.sum(jnp.exp(scores - peak), axis=-1, keepdims=True))
    weights = jnp.exp(scores - lse)
    heads_out = (
        jnp.einsum("hqk,khe->qhe", weights.astype(bf16), all_values, preferred_element_type=f32)
        .astype(bf16)
        .reshape(tok_count, -1)
    )
    out_part = input_grad(heads_out, out_t).astype(bf16)
    (out_other,) = swap([out_part], 5)
    middle = x_float + (out_part.astype(f32) + out_other.astype(f32))

    normed_two, scale_two = rms_parts(middle)
    branch_in = (normed_two * gain_second).astype(bf16)
    logits = matmul(branch_in, router_w)
    expo = jnp.exp(logits - jnp.max(logits, axis=-1, keepdims=True))
    probs = expo / jnp.sum(expo, axis=-1, keepdims=True)
    picked = (routes[:, :, None] == jnp.arange(experts, dtype=jnp.int32)[None, None, :]).astype(f32)
    gates = jnp.sum(probs[:, None, :] * picked, axis=2)
    chosen = jnp.sum(picked, axis=1)
    places = jnp.arange(tok_count, dtype=jnp.int32)
    below = (places[:, None] > places[None, :]).astype(bf16)
    before = matmul(below, chosen.astype(bf16))
    slots = jnp.arange(capacity, dtype=f32)
    taken = (before.T[:, None, :] == slots[None, :, None]) & (chosen.T[:, None, :] > 0.5)
    gate_slot = jnp.sum(jnp.where(taken, probs.T[:, None, :], 0.0), axis=2)
    chooser = taken.astype(bf16).reshape(experts * capacity, tok_count)
    pair_slot = routes * capacity + jnp.sum(picked * before[:, None, :], axis=2).astype(jnp.int32)
    all_slots = jnp.arange(experts * capacity, dtype=jnp.int32)
    pick = [(pair_slot[:, k : k + 1] == all_slots[None, :]).astype(bf16) for k in range(routes.shape[1])]
    rows_out = matmul(chooser, branch_in).astype(bf16).reshape(experts, capacity, width)
    d_after = cotangent.astype(f32)
    d_rows_out = (
        gate_slot.reshape(-1, 1) * matmul(chooser, cotangent)
    ).astype(bf16).reshape(experts, capacity, width)
    rows_in, d_rows_in = dispatch(rows_out, d_rows_out, n, owners)

    rows_in = rows_in.reshape(n * capacity, width)
    d_rows_in = d_rows_in.reshape(n * capacity, width)
    gate_hidden = matmul(rows_in, expert_gate)
    up_hidden = matmul(rows_in, expert_up)
    gate_act = jax.nn.silu(gate_hidden)
    expert_hidden = (gate_act * up_hidden).astype(bf16)
    part_rows = matmul(expert_hidden, expert_down).astype(bf16)
    d_hidden = input_grad(d_rows_in, expert_down)
    d_gate_hidden = (d_hidden * up_hidden * silu_grad(gate_hidden)).astype(bf16)
    d_up_hidden = (d_hidden * gate_act).astype(bf16)
    d_part_rows = (
        input_grad(d_gate_hidden, expert_gate) + input_grad(d_up_hidden, expert_up)
    ).astype(bf16)
    returned, d_returned = give_back(
        part_rows.reshape(n, capacity, width), d_part_rows.reshape(n, capacity, width)
    )
    grad_e_down = weight_grad(expert_hidden, d_rows_in)
    grad_e_gate = weight_grad(rows_in, d_gate_hidden)
    grad_e_up = weight_grad(rows_in, d_up_hidden)

    shared_gate = matmul(branch_in, sgate_w)
    shared_up = matmul(branch_in, sup_w)
    shared_act = jax.nn.silu(shared_gate)
    shared_hidden = (shared_act * shared_up).astype(bf16)
    shared_part = input_grad(shared_hidden, sdown_t)
    d_shared = matmul(cotangent, sdown_t)
    grad_sdown_t = weight_grad(cotangent, shared_hidden)
    d_sgate = (d_shared * shared_up * silu_grad(shared_gate)).astype(bf16)
    d_sup = (d_shared * shared_act).astype(bf16)
    grad_sgate = weight_grad(branch_in, d_sgate)
    grad_sup = weight_grad(branch_in, d_sup)
    d_shared_in = input_grad(d_sgate, sgate_w) + input_grad(d_sup, sup_w)

    def incoming(rows):
        rows = rows.reshape(experts, owners, capacity, half)
        if owners > 1:
            rows = jnp.sum(rows.astype(f32), axis=1).astype(bf16)
        return rows.reshape(experts * capacity, half)

    def placed(values):
        own = jnp.concatenate([values, jnp.zeros_like(values)], axis=1)
        other = jnp.concatenate([jnp.zeros_like(values), values], axis=1)
        return jnp.where(core == 0, own, other)

    result_rows, d_result_rows = incoming(returned), incoming(d_returned)
    pair_out = [matmul(p, result_rows) for p in pick]
    d_pairs = matmul(sum(pick), d_result_rows)
    moe_half = sum(gates[:, k : k + 1] * pair_out[k] for k in range(len(pick)))
    d_half = lax.dynamic_slice_in_dim(cotangent, core * half, half, axis=1).astype(f32)
    d_gates_part = jnp.concatenate(
        [jnp.sum(d_half * p, axis=1, keepdims=True) for p in pair_out], axis=1
    )
    after_part = (placed(moe_half) + shared_part).astype(bf16)
    d_branch_part = (d_shared_in + placed(d_pairs)).astype(bf16)
    d_gates_part = jnp.pad(d_gates_part, ((0, 0), (0, LANES - len(pick))))
    after_other, d_branch_other, d_gates_other = swap(
        [after_part, d_branch_part, d_gates_part], 6
    )
    output = (middle + (after_part.astype(f32) + after_other.astype(f32))).astype(bf16)
    d_branch_sum = d_branch_part.astype(f32) + d_branch_other.astype(f32)
    d_gates = (d_gates_part + d_gates_other)[:, : len(pick)]
    d_probs = jnp.sum(d_gates[:, :, None] * picked, axis=1)
    d_logits = (probs * (d_probs - jnp.sum(probs * d_probs, axis=-1, keepdims=True))).astype(bf16)
    grad_router = weight_grad(branch_in, d_logits)
    d_branch_in = d_branch_sum + input_grad(d_logits, router_w)
    grad_gain_two = jnp.sum(d_branch_in * normed_two, axis=0)
    d_norm_two = d_branch_in * gain_second
    d_middle = d_after + scale_two * (
        d_norm_two - normed_two * jnp.mean(d_norm_two * normed_two, axis=-1, keepdims=True)
    )

    d_attn = d_middle.astype(bf16)
    grad_out_t = weight_grad(d_attn, heads_out)
    d_heads = matmul(d_attn, out_t).astype(bf16).reshape(head_shape)
    again = jnp.exp(masked_scores(queries, all_keys, valid) - lse)
    d_weights = jnp.einsum("qhe,khe->hqk", d_heads, all_values, preferred_element_type=f32)
    d_scores = (again * (d_weights - jnp.sum(again * d_weights, axis=-1, keepdims=True))).astype(bf16)
    d_queries = (
        jnp.einsum("hqk,khe->qhe", d_scores, all_keys, preferred_element_type=f32) * score_scale
    )
    d_keys = jnp.einsum("hqk,qhe->khe", d_scores, queries, preferred_element_type=f32)
    d_values = jnp.einsum("hqk,qhe->khe", again.astype(bf16), d_heads, preferred_element_type=f32)
    d_query_pre = unrotate(d_queries, cosines, sines).astype(bf16).reshape(tok_count, -1)
    d_key_pre = unrotate(d_keys, cos_all, sin_all).astype(bf16).reshape(span, -1)
    d_value_pre = d_values.astype(bf16).reshape(span, -1)
    grad_query = weight_grad(attn_in, d_query_pre)
    grad_key = weight_grad(attn_in_all, d_key_pre)
    grad_value = weight_grad(attn_in_all, d_value_pre)
    d_attn_part = input_grad(d_key_pre, key_w) + input_grad(d_value_pre, value_w)
    d_attn_part = jnp.concatenate(
        [
            d_attn_part[: reach * tok_count],
            d_attn_part[reach * tok_count :] + input_grad(d_query_pre, query_w),
        ],
        axis=0,
    )
    grad_gain_one = jnp.sum(d_attn_part * normed_all, axis=0)
    grad_small = jnp.concatenate(
        [
            grad_router,
            grad_gain_two[:, None],
            jnp.zeros((width, LANES - experts - 1), f32),
            grad_gain_one[:, None],
            jnp.zeros((width, small - LANES - 1), f32),
        ],
        axis=1,
    )
    grads = jnp.concatenate(
        [grad_query, grad_key, grad_value, grad_out_t, grad_small, grad_sgate, grad_sup, grad_sdown_t],
        axis=1,
    ).astype(bf16)
    total, d_attn_in = scatter_all(grads, d_attn_part.astype(bf16), at_small + LANES, depth, reach, cuts)
    d_attn_in = d_attn_in.astype(f32)
    d_norm_one = d_attn_in * gain_first
    token_input_gradient = d_middle + scale_one * (
        d_norm_one - normed_one * jnp.mean(d_norm_one * normed_one, axis=-1, keepdims=True)
    )
    return (
        output,
        token_input_gradient,
        total[:, at_small + LANES],
        total[:, :heads_width],
        total[:, heads_width : 2 * heads_width],
        total[:, 2 * heads_width : 3 * heads_width],
        total[:, 3 * heads_width : at_small].T,
        total[:, at_small + experts],
        total[:, at_small : at_small + experts],
        total[:, at_shared : at_shared + hidden],
        total[:, at_shared + hidden : at_shared + 2 * hidden],
        total[:, at_shared + 2 * hidden :].T,
        grad_e_gate,
        grad_e_up,
        grad_e_down,
    )


def solution(mesh):
    by_dp, both, turned = P("dp", None), P("dp", "tensor"), P("tensor", "dp")
    wide, tall = P(None, ("dp", "tensor")), P(("dp", "tensor"), None)
    weights = (P("dp"), both, both, both, turned, P("dp"), by_dp, both, both, turned, wide, wide, tall)
    return jax.shard_map(
        local,
        mesh=mesh,
        in_specs=(by_dp, by_dp) + weights + (by_dp, P()),
        out_specs=(by_dp, by_dp) + weights,
        check_vma=False,
    )
```

```python
import functools

import jax
import jax.numpy as jnp
from jax import lax
from jax.experimental import pallas as pl
from jax.experimental.pallas import tpu as pltpu
from jax.sharding import PartitionSpec as P

HEAD = 64
WINDOW = 1024
LANES = 128
PLANE = 4

MESH = pl.DeviceIdType.MESH
f32 = jnp.float32
bf16 = jnp.bfloat16

eps = 1e-06
masked = -1e30


def matmul(left, right):
    return jnp.dot(left, right, preferred_element_type=f32)


def weight_grad(left, right):
    return lax.dot_general(
        left, right, (((0,), (0,)), ((), ())), preferred_element_type=f32
    )


def input_grad(left, right):
    return lax.dot_general(
        left, right, (((1,), (1,)), ((), ())), preferred_element_type=f32
    )


def rms_parts(values):
    factor = lax.rsqrt(jnp.mean(values * values, axis=-1, keepdims=True) + eps)
    return (values * factor, factor)


def rotary_tables(positions):
    freqs = 10000.0 ** (-jnp.arange(HEAD // 2, dtype=f32) * (2.0 / HEAD))
    phase = positions.astype(f32)[:, None] * freqs[None, :]
    return (jnp.cos(phase)[:, None, :], jnp.sin(phase)[:, None, :])


def rotate(values, cosines, sines):
    half = values.shape[-1] // 2
    first = values[..., :half]
    second = values[..., half:]
    return jnp.concatenate(
        [first * cosines - second * sines, second * cosines + first * sines], axis=-1
    )


def unrotate(grads, cosines, sines):
    half = grads.shape[-1] // 2
    first = grads[..., :half]
    second = grads[..., half:]
    return jnp.concatenate(
        [first * cosines + second * sines, second * cosines - first * sines], axis=-1
    )


def silu_grad(values):
    sigma = jax.nn.sigmoid(values)
    return sigma * (1.0 + values * (1.0 - sigma))


def masked_scores(queries, keys, valid):
    scores = jnp.einsum("qhe,khe->hqk", queries, keys, preferred_element_type=f32)
    return jnp.where(valid[None, :, :], scores, masked)


def digits(me):
    return lax.div(me, PLANE), lax.rem(lax.div(me, 2), 2), lax.rem(me, 2)


def index_of(z, y, x):
    return z * PLANE + y * 2 + x


def push(src, dst, send, recv, device):
    copy = pltpu.make_async_remote_copy(
        src_ref=src,
        dst_ref=dst,
        send_sem=send,
        recv_sem=recv,
        device_id=device,
        device_id_type=MESH,
    )
    copy.start()
    return copy


def greet(devices):
    barrier = pltpu.get_barrier_semaphore()
    for device in devices:
        pl.semaphore_signal(barrier, inc=1, device_id=device, device_id_type=MESH)
    pl.semaphore_wait(barrier, len(devices))


def comm_params(collective_id, limit=48 << 20):
    return pltpu.CompilerParams(
        collective_id=collective_id, has_side_effects=True, vmem_limit_bytes=limit
    )


def dma(*shape):
    return pltpu.SemaphoreType.DMA(shape)


IN_HBM = pl.BlockSpec(memory_space=pl.ANY)
IN_VMEM = pl.BlockSpec(memory_space=pltpu.VMEM)


def grid_peers(depth, z, y, x):
    peers = [{"dp": index_of(lax.rem(z + k, depth), y, x)} for k in range(1, depth)]
    return peers, {"dp": index_of(z, 1 - y, x)}, {"dp": index_of(z, y, 1 - x)}


def gather_kernel(
    depth, reach, cuts, shard, tok, full, window,
    z_send, z_recv, p_send, p_recv, t_send, t_recv, f_send, f_recv, own,
):
    n = depth * PLANE
    me, core = lax.axis_index("dp"), lax.axis_index("tensor")
    z, y, x = digits(me)
    z_peers, y_peer, x_peer = grid_peers(depth, z, y, x)
    sibling = {"tensor": 1 - core}
    ahead = [{"dp": lax.rem(me + k, n)} for k in range(1, reach + 1)]
    behind = [{"dp": lax.rem(me + n - k, n)} for k in range(1, reach + 1)]
    greet(z_peers + [y_peer, x_peer, sibling] + ahead + behind)
    own_shard = pltpu.make_async_copy(shard, full.at[z, y, x], own.at[0])
    own_shard.start()
    own_tok = pltpu.make_async_copy(tok, window.at[reach], own.at[1])
    own_tok.start()
    half = tok.shape[0] // 2
    rows = pl.ds(pl.multiple_of(core * half, half), half)
    z_copies = []

    def start_first(c):
        cols = pl.ds(cuts[c][0], cuts[c][2] - cuts[c][0])
        z_copies.append(
            [
                push(
                    shard.at[:, cols],
                    full.at[z, y, x, :, cols],
                    z_send.at[c, k],
                    z_recv.at[c, k],
                    z_peers[k],
                )
                for k in range(depth - 1)
            ]
        )

    start_first(0)
    start_first(1)
    t_copies = [
        push(
            tok.at[rows],
            window.at[reach - 1 - k, rows],
            t_send.at[k],
            t_recv.at[k],
            ahead[k],
        )
        for k in range(reach)
    ]
    own_shard.wait()
    second, third, forwards = [], [], []
    for c in range(len(cuts) + 2):
        if c < len(cuts):
            start, middle, stop = cuts[c]
            left, right = pl.ds(start, middle - start), pl.ds(middle, stop - middle)
            for copy in z_copies[c]:
                copy.wait_recv()
            second.append(
                [
                    push(
                        full.at[:, y, x, :, left],
                        full.at[:, y, x, :, left],
                        p_send.at[c, 0],
                        p_recv.at[c, 0],
                        y_peer,
                    ),
                    push(
                        full.at[:, y, x, :, right],
                        full.at[:, y, x, :, right],
                        p_send.at[c, 1],
                        p_recv.at[c, 1],
                        x_peer,
                    ),
                ]
            )
            if c + 2 < len(cuts):
                start_first(c + 2)
        if c == 1:
            for k, copy in enumerate(t_copies):
                copy.wait_recv()
                forwards.append(
                    push(
                        window.at[reach - 1 - k, rows],
                        window.at[reach - 1 - k, rows],
                        f_send.at[k],
                        f_recv.at[k],
                        sibling,
                    )
                )
        if 1 <= c <= len(cuts):
            start, middle, stop = cuts[c - 1]
            left, right = pl.ds(start, middle - start), pl.ds(middle, stop - middle)
            for copy in second[c - 1]:
                copy.wait_recv()
            third.append(
                [
                    push(
                        full.at[:, :, x, :, left],
                        full.at[:, :, x, :, left],
                        p_send.at[c - 1, 2],
                        p_recv.at[c - 1, 2],
                        x_peer,
                    ),
                    push(
                        full.at[:, y, :, :, right],
                        full.at[:, y, :, :, right],
                        p_send.at[c - 1, 3],
                        p_recv.at[c - 1, 3],
                        y_peer,
                    ),
                ]
            )
        if c >= 2:
            for copy in third[c - 2]:
                copy.wait_recv()
    for copy in forwards:
        copy.wait_recv()
    own_tok.wait()
    for copies in z_copies + second + third + [t_copies, forwards]:
        for copy in copies:
            copy.wait_send()


def cut_columns(columns, parts):
    step = 2 * LANES
    edges = [step * (columns // step * i // parts) for i in range(parts + 1)]
    return tuple((a, (a + b) // 2, b) for a, b in zip(edges[:-1], edges[1:]))


def gather_all(shard, tokens, depth, reach, cuts):
    parts = len(cuts)
    full, window = pl.pallas_call(
        functools.partial(gather_kernel, depth, reach, cuts),
        out_shape=(
            jax.ShapeDtypeStruct((depth, 2, 2) + shard.shape, shard.dtype),
            jax.ShapeDtypeStruct((reach + 1,) + tokens.shape, tokens.dtype),
        ),
        in_specs=[IN_HBM] * 2,
        out_specs=(IN_HBM, IN_HBM),
        scratch_shapes=[
            dma(parts, depth - 1), dma(parts, depth - 1), dma(parts, 4), dma(parts, 4),
            dma(reach), dma(reach), dma(reach), dma(reach), dma(2),
        ],
        compiler_params=comm_params(1),
        name="gather_weights",
    )(shard, tokens)
    return full.reshape(-1, shard.shape[1]), window.reshape(-1, tokens.shape[1])


def swap_kernel(count, *refs):
    sources, targets, (send, recv) = refs[:count], refs[count : 2 * count], refs[2 * count :]
    sibling = {"tensor": 1 - lax.axis_index("tensor")}
    greet([sibling])
    copies = [
        push(a, b, send.at[i], recv.at[i], sibling)
        for i, (a, b) in enumerate(zip(sources, targets))
    ]
    for copy in copies:
        copy.wait()


def swap(arrays, collective_id):
    count = len(arrays)
    return pl.pallas_call(
        functools.partial(swap_kernel, count),
        out_shape=tuple(jax.ShapeDtypeStruct(a.shape, a.dtype) for a in arrays),
        in_specs=[IN_VMEM] * count,
        out_specs=(IN_VMEM,) * count,
        scratch_shapes=[dma(count), dma(count)],
        compiler_params=comm_params(collective_id),
        name="swap_cores",
    )(*arrays)


def dispatch_kernel(n, owners, first, second, got_first, got_second, send, recv, f_send, f_recv, own):
    me, core = lax.axis_index("dp"), lax.axis_index("tensor")
    sibling = {"tensor": 1 - core}
    greet([{"dp": lax.rem(me + k, n)} for k in range(1, n)] + [sibling])
    half = first.shape[-1] // 2
    cols = pl.ds(pl.multiple_of(core * half, half), half)
    pairs = ((first, got_first), (second, got_second))
    mine = lax.div(me, owners)
    copies = []
    for k in range(1, n):
        to = lax.rem(me + k, n)
        for i, (source, target) in enumerate(pairs):
            copies.append(
                push(
                    source.at[lax.div(to, owners), :, cols],
                    target.at[me, :, cols],
                    send.at[i, k],
                    recv.at[i, k],
                    {"dp": to},
                )
            )
    local = [
        pltpu.make_async_copy(source.at[mine], target.at[me], own.at[i])
        for i, (source, target) in enumerate(pairs)
    ]
    for copy in local:
        copy.start()
    forwards = []
    for k in range(1, n):
        source_of = lax.rem(me + n - k, n)
        for i, (source, target) in enumerate(pairs):
            copies[2 * (k - 1) + i].wait_recv()
            block = target.at[source_of, :, cols]
            forwards.append(push(block, block, f_send.at[i, k], f_recv.at[i, k], sibling))
    for copy in forwards:
        copy.wait_recv()
    for copy in local:
        copy.wait()
    for copy in copies + forwards:
        copy.wait_send()


def dispatch(first, second, n, owners):
    shape = jax.ShapeDtypeStruct((n,) + first.shape[1:], first.dtype)
    return pl.pallas_call(
        functools.partial(dispatch_kernel, n, owners),
        out_shape=(shape, shape),
        in_specs=[IN_HBM] * 2,
        out_specs=(IN_HBM, IN_HBM),
        scratch_shapes=[dma(2, n), dma(2, n), dma(2, n), dma(2, n), dma(2)],
        compiler_params=comm_params(2),
        name="dispatch_rows",
    )(first, second)


def return_kernel(n, groups, first, second, got_first, got_second, part, total, send, recv, f_send, f_recv, own):
    me, core = lax.axis_index("dp"), lax.axis_index("tensor")
    sibling = {"tensor": 1 - core}
    greet([{"dp": lax.rem(me + k, n)} for k in range(1, n)] + [sibling])
    half = first.shape[-1] // 2
    mine = pl.ds(pl.multiple_of(core * half, half), half)
    theirs = pl.ds(pl.multiple_of((1 - core) * half, half), half)
    pairs = ((first, got_first), (second, got_second))
    each = n // groups
    swaps = []
    for g in range(groups):
        block = pl.ds(g * each, each)
        for i, (source, target) in enumerate(pairs):
            swaps.append(
                push(
                    source.at[block, :, theirs],
                    part.at[i, block],
                    f_send.at[i, g],
                    f_recv.at[i, g],
                    sibling,
                )
            )
    for g in range(groups):
        block = pl.ds(g * each, each)
        for i, (source, target) in enumerate(pairs):
            swaps[2 * g + i].wait_recv()
            total[i, block] = (
                source[block, :, mine].astype(f32) + part[i, block].astype(f32)
            ).astype(bf16)
        for slot in range(g * each, (g + 1) * each):
            for i, (source, target) in enumerate(pairs):
                @pl.when(slot != me)
                def _():
                    push(
                        total.at[i, slot],
                        target.at[me],
                        send.at[i, slot],
                        recv.at[i, me],
                        {"dp": slot},
                    )
    local = [
        pltpu.make_async_copy(total.at[i, me], pairs[i][1].at[me], own.at[i]) for i in range(2)
    ]
    for copy in local:
        copy.start()
    for k in range(1, n):
        to, source_of = lax.rem(me + k, n), lax.rem(me + n - k, n)
        for i, (source, target) in enumerate(pairs):
            pltpu.make_async_remote_copy(
                total.at[i, to], target.at[source_of], send.at[i, to], recv.at[i, source_of],
                device_id={"dp": to}, device_id_type=MESH,
            ).wait()
    for copy in local:
        copy.wait()
    for copy in swaps:
        copy.wait_send()


def give_back(first, second, groups=4):
    n, capacity, width = first.shape
    half = jax.ShapeDtypeStruct((n, capacity, width // 2), first.dtype)
    buffer = pltpu.VMEM((2, n, capacity, width // 2), first.dtype)
    return pl.pallas_call(
        functools.partial(return_kernel, n, groups),
        out_shape=(half, half),
        in_specs=[IN_VMEM] * 2,
        out_specs=(IN_HBM, IN_HBM),
        scratch_shapes=[buffer, buffer, dma(2, n), dma(2, n), dma(2, groups), dma(2, groups), dma(2)],
        compiler_params=comm_params(3),
        name="return_rows",
    )(first, second)


class Scatter:
    def __init__(self, depth, chunks, total, buffers, semaphores):
        self.depth, self.chunks, self.total = depth, chunks, total
        self.first_l, self.first_r, self.second_l, self.second_r, self.last = buffers
        self.p_send, self.p_recv, self.z_send, self.z_recv = semaphores
        self.z, self.y, self.x = digits(lax.axis_index("dp"))
        self.z_peers, self.y_peer, self.x_peer = grid_peers(depth, self.z, self.y, self.x)
        self.at_l, self.at_r, l, r = [], [], 0, 0
        for left, lc, lw, right, rc, rw, out in chunks:
            self.at_l.append(pl.ds(l, lw))
            self.at_r.append(pl.ds(r, rw))
            l, r = l + lw, r + rw
        self.ones, self.twos, self.threes = {}, {}, {}

    def start(self, c):
        left, lc, lw, right, rc, rw, out = self.chunks[c]
        self.ones[c] = [
            push(
                left.at[:, :, 1 - self.x, :, pl.ds(lc, lw)],
                self.first_l.at[:, :, :, self.at_l[c]],
                self.p_send.at[c, 0], self.p_recv.at[c, 0], self.x_peer,
            ),
            push(
                right.at[:, 1 - self.y, :, :, pl.ds(rc, rw)],
                self.first_r.at[:, :, :, self.at_r[c]],
                self.p_send.at[c, 1], self.p_recv.at[c, 1], self.y_peer,
            ),
        ]

    def second(self, c):
        left, lc, lw, right, rc, rw, out = self.chunks[c]
        in_l, in_r, first_l, first_r = self.at_l[c], self.at_r[c], self.first_l, self.first_r
        for copy in self.ones[c]:
            copy.wait_recv()

        def add(i, carry):
            for j in range(2):
                first_l[i, j, :, in_l] = (
                    first_l[i, j, :, in_l].astype(f32) + left[i, j, self.x, :, pl.ds(lc, lw)].astype(f32)
                ).astype(bf16)
                first_r[i, j, :, in_r] = (
                    first_r[i, j, :, in_r].astype(f32) + right[i, self.y, j, :, pl.ds(rc, rw)].astype(f32)
                ).astype(bf16)
            return carry

        lax.fori_loop(0, self.depth, add, 0)
        self.twos[c] = [
            push(
                first_l.at[:, 1 - self.y, :, in_l], self.second_l.at[:, :, in_l],
                self.p_send.at[c, 2], self.p_recv.at[c, 2], self.y_peer,
            ),
            push(
                first_r.at[:, 1 - self.x, :, in_r], self.second_r.at[:, :, in_r],
                self.p_send.at[c, 3], self.p_recv.at[c, 3], self.x_peer,
            ),
        ]

    def third(self, c):
        for copy in self.twos[c]:
            copy.wait_recv()
        sides = (
            (self.second_l, self.first_l, self.y, self.at_l[c]),
            (self.second_r, self.first_r, self.x, self.at_r[c]),
        )

        def add(i, carry):
            for source, before, place, here in sides:
                source[i, :, here] = (
                    source[i, :, here].astype(f32) + before[i, place, :, here].astype(f32)
                ).astype(bf16)
            return carry

        lax.fori_loop(0, self.depth, add, 0)
        self.threes[c] = [
            push(
                source.at[lax.rem(self.z + k + 1, self.depth), :, here],
                self.last.at[k, side, :, here],
                self.z_send.at[c, side, k], self.z_recv.at[c, side, k], self.z_peers[k],
            )
            for side, (source, before, place, here) in enumerate(sides)
            for k in range(self.depth - 1)
        ]

    def finish(self, c):
        left, lc, lw, right, rc, rw, out = self.chunks[c]
        for copy in self.threes[c]:
            copy.wait_recv()
        for side, source, here, at, span in (
            (0, self.second_l, self.at_l[c], out, lw),
            (1, self.second_r, self.at_r[c], out + lw, rw),
        ):
            value = source[self.z, :, here].astype(f32)
            for k in range(self.depth - 1):
                value = value + self.last[k, side, :, here].astype(f32)
            self.total[:, pl.ds(at, span)] = value

    def drain(self):
        for copies in list(self.ones.values()) + list(self.twos.values()) + list(self.threes.values()):
            for copy in copies:
                copy.wait_send()


def lanes_of(part):
    lane = lax.broadcasted_iota(jnp.int32, (1, LANES), 1)
    return (lax.div(lane, HEAD) == part).astype(f32).astype(bf16)


def swap_halves(values):
    lane = lax.broadcasted_iota(jnp.int32, (1, LANES), 1)
    low = lax.rem(lane, HEAD) < HEAD // 2
    return jnp.where(
        low, pltpu.roll(values, LANES - HEAD // 2, 1), pltpu.roll(values, HEAD // 2, 1)
    )


def put_rows(target, values, columns):
    rows = target.shape[3]
    for b in range(values.shape[0] // rows):
        target[b // PLANE, (b // 2) % 2, b % 2, :, columns] = values[b * rows : (b + 1) * rows]


def backward_kernel(
    depth, reach, per_core, g_gate, g_up, g_down, g_small, window, q, k, v, lse, heads_out, d_attn,
    query_w, key_w, value_w, out_t, gain, cosines, sines, bias, total, d_full,
    grads, attn_t, d_heads, dq_all, dk_all, dv_all, d_part, d_swap, d_sum, d_got, gain_got,
    first_l, first_r, second_l, second_r, last,
    p_send, p_recv, z_send, z_recv, t_send, t_recv, s_send, s_recv, f_send, f_recv,
):
    n = depth * PLANE
    me, core = lax.axis_index("dp"), lax.axis_index("tensor")
    sibling = {"tensor": 1 - core}
    ahead = [{"dp": lax.rem(me + i, n)} for i in range(1, reach + 1)]
    behind = [{"dp": lax.rem(me + n - i, n)} for i in range(1, reach + 1)]
    heads_width = q.shape[1]
    count = q.shape[0]
    pairs = heads_width // LANES
    hidden = g_gate.shape[4]
    chunks = []
    out = 0
    step = 2 * LANES
    for source in (g_gate, g_up, g_down):
        for at in range(0, hidden, 2 * step):
            chunks.append((source, at, step, source, at + step, step, out))
            out += 2 * step
    early = len(chunks)
    widths = [(step, step)] + [(step, LANES), (LANES, step)] * pairs
    widths = widths[:pairs] + [(step, step)]
    at = 0
    for left, right in widths:
        chunks.append((grads, at, left, grads, at + left, right, out + at))
        at += left + right
    scatter = Scatter(
        depth, chunks, total, (first_l, first_r, second_l, second_r, last),
        (p_send, p_recv, z_send, z_recv),
    )
    greet(scatter.z_peers + [scatter.y_peer, scatter.x_peer, sibling] + ahead + behind)
    for c in range(3):
        scatter.start(c)

    d_heads[...] = matmul(d_attn[...], out_t[...]).astype(bf16)
    put_rows(grads, weight_grad(d_attn[...], heads_out[...]).astype(bf16), pl.ds(0, heads_width))
    grads[:, :, :, :, pl.ds(heads_width, LANES)] = g_small[...]

    def normed(block):
        values = window[block].astype(f32)
        return values * lax.rsqrt(jnp.mean(values * values, axis=-1, keepdims=True) + eps)

    def turned(block, carry):
        rows = pl.ds(pl.multiple_of(block * count, count), count)
        attn_t[:, rows] = (normed(block) * gain[...]).T.astype(bf16)
        return carry

    for block in range(reach + 1):
        turned(block, 0)
    scatter.start(early)
    own = pl.ds(reach * count, count)
    done = 0
    for pair in range(pairs):
        columns = pl.ds(pair * LANES, LANES)
        k_pair, v_pair, q_pair, d_pair = k[:, columns], v[:, columns], q[:, columns], d_heads[:, columns]
        dq = dk = dv = None
        for part in range(2):
            head = 2 * pair + part
            lanes = lanes_of(part)
            q_head, d_head, k_head = q_pair * lanes, d_pair * lanes, k_pair * lanes
            probs = jnp.exp(input_grad(k_pair, q_head) + bias[...] - lse[head : head + 1, :])
            d_probs = input_grad(v_pair, d_head)
            inner = jnp.sum(probs * d_probs, axis=0, keepdims=True)
            d_scores = (probs * (d_probs - inner)).astype(bf16)
            parts = (
                weight_grad(d_scores, k_head),
                matmul(d_scores, q_head),
                matmul(probs.astype(bf16), d_head),
            )
            dq, dk, dv = parts if part == 0 else (dq + parts[0], dk + parts[1], dv + parts[2])
            if done < early + 1:
                scatter.second(done)
                if done + 3 < early:
                    scatter.start(done + 3)
            if 1 <= done:
                scatter.third(done - 1)
            if 2 <= done:
                scatter.finish(done - 2)
            done += 1
        dq = dq * (HEAD ** (-0.5))
        cos_own, sin_own = cosines[own, :], sines[own, :]
        dq_low = (dq * cos_own - swap_halves(dq) * sin_own).astype(bf16)
        dk_low = (dk * cosines[...] - swap_halves(dk) * sines[...]).astype(bf16)
        dv_low = dv.astype(bf16)
        dq_all[:, columns] = dq_low
        dk_all[:, columns] = dk_low
        dv_all[:, columns] = dv_low
        at = heads_width + LANES + pair * 3 * LANES
        put_rows(grads, matmul(attn_t[:, own], dq_low).astype(bf16), pl.ds(at, LANES))
        put_rows(grads, matmul(attn_t[...], dk_low).astype(bf16), pl.ds(at + LANES, LANES))
        put_rows(grads, matmul(attn_t[...], dv_low).astype(bf16), pl.ds(at + 2 * LANES, LANES))
        if pair < pairs - 1:
            scatter.start(early + 1 + pair)

    width = d_part.shape[-1] // 2
    mine = pl.ds(pl.multiple_of(core * width, width), width)
    theirs = pl.ds(pl.multiple_of((1 - core) * width, width), width)
    swaps = []
    gain_row = jnp.zeros((1, 2 * width), f32)
    for block in range(reach + 1):
        rows = pl.ds(block * count, count)
        value = input_grad(dk_all[rows, :], key_w[...]) + input_grad(dv_all[rows, :], value_w[...])
        if block == reach:
            value = value + input_grad(dq_all[...], query_w[...])
        gain_row = gain_row + jnp.sum(value * normed(block), axis=0, keepdims=True)
        d_part[block] = value.astype(bf16)
        swaps.append(
            push(
                d_part.at[block, :, theirs], d_swap.at[block],
                s_send.at[block], s_recv.at[block], sibling,
            )
        )
    put_rows(
        grads,
        jnp.broadcast_to(gain_row, (LANES, 2 * width)).T.astype(bf16),
        pl.ds(heads_width + LANES + pairs * 3 * LANES, LANES),
    )
    final = len(chunks) - 1
    scatter.start(final)
    back = []
    for block in range(reach + 1):
        swaps[block].wait_recv()
        d_sum[block] = (
            d_part[block, :, mine].astype(f32) + d_swap[block].astype(f32)
        ).astype(bf16)
        if block < reach:
            i = reach - 1 - block
            back.append(
                push(d_sum.at[block], d_got.at[i], t_send.at[i], t_recv.at[i], behind[i])
            )
    seconds = [c for c in range(len(chunks)) if c not in scatter.twos]
    for c in range(done - 1, len(chunks) + 2):
        if c < len(chunks) and c not in scatter.twos:
            scatter.second(c)
        if c - 1 < len(chunks) and c - 1 not in scatter.threes:
            scatter.third(c - 1)
        if c >= 2 and c - 2 >= done - 2:
            scatter.finish(c - 2)
    d_mine = d_sum[reach].astype(f32)
    for copy in back:
        copy.wait_recv()
    for i in range(reach):
        d_mine = d_mine + d_got[i].astype(f32)
    d_full[:, mine] = d_mine.astype(bf16)
    both = push(d_full.at[:, mine], d_full.at[:, mine], f_send.at[0], f_recv.at[0], sibling)
    split = pl.ds(per_core, LANES)
    gain_copy = push(total.at[:, split], gain_got, f_send.at[1], f_recv.at[1], sibling)
    both.wait()
    gain_copy.wait()
    total[:, split] = total[:, split] + gain_got[...]
    scatter.drain()
    for copy in back + swaps:
        copy.wait_send()


def backward(arrays, rows, columns, shared, count, heads_width, width, depth, reach):
    span = (reach + 1) * count
    half = columns // 2
    parts = shared // (4 * LANES) + 2 + heads_width // LANES
    first = pltpu.VMEM((depth, 2, rows, half), bf16)
    second = pltpu.VMEM((depth, rows, half), bf16)
    own = columns - shared
    return pl.pallas_call(
        functools.partial(backward_kernel, depth, reach, columns - LANES),
        out_shape=(
            jax.ShapeDtypeStruct((rows, columns), f32),
            jax.ShapeDtypeStruct((count, width), bf16),
        ),
        in_specs=[IN_VMEM] * len(arrays),
        out_specs=(IN_VMEM, IN_VMEM),
        scratch_shapes=[
            pltpu.VMEM((depth, 2, 2, rows, own), bf16),
            pltpu.VMEM((width, span), bf16),
            pltpu.VMEM((count, heads_width), bf16),
            pltpu.VMEM((count, heads_width), bf16),
            pltpu.VMEM((span, heads_width), bf16),
            pltpu.VMEM((span, heads_width), bf16),
            pltpu.VMEM((reach + 1, count, width), bf16),
            pltpu.VMEM((reach + 1, count, width // 2), bf16),
            pltpu.VMEM((reach + 1, count, width // 2), bf16),
            pltpu.VMEM((reach, count, width // 2), bf16),
            pltpu.VMEM((rows, LANES), f32),
            first, first, second, second,
            pltpu.VMEM((depth - 1, 2, rows, half), bf16),
            dma(parts, 4), dma(parts, 4),
            dma(parts, 2, depth - 1), dma(parts, 2, depth - 1),
            dma(reach), dma(reach), dma(reach + 1), dma(reach + 1), dma(2), dma(2),
        ],
        compiler_params=comm_params(4, 58 << 20),
        name="attention_backward",
    )(*arrays)


def local(
    tokens, cotangent, attn_gain, w_query, w_key, w_value, w_out, ffn_gain, w_router,
    w_sgate, w_sup, w_sdown, e_gate, e_up, e_down, routes, segments,
):
    tok_count, width = tokens.shape
    n = lax.axis_size("dp")
    depth = n // PLANE
    me = lax.axis_index("dp")
    core = lax.axis_index("tensor")
    experts = w_router.shape[1]
    owners = n // experts
    capacity = tok_count // 4
    reach = (WINDOW + tok_count - 1) // tok_count
    score_scale = HEAD ** (-0.5)
    shard_rows = w_query.shape[0]
    heads_width = w_query.shape[1]
    local_heads = heads_width // HEAD
    hidden = w_sgate.shape[1]
    half = width // 2

    small = 2 * LANES
    packed = jnp.concatenate(
        [
            w_query, w_key, w_value, w_out.T,
            jnp.pad(
                jnp.concatenate([w_router, attn_gain[:, None], ffn_gain[:, None]], axis=1),
                ((0, 0), (0, small - experts - 2)),
            ),
            w_sgate, w_sup, w_sdown.T,
        ],
        axis=1,
    ).astype(bf16)
    at_small = 4 * heads_width
    at_shared = at_small + small
    columns = at_shared + 3 * hidden
    cuts = cut_columns(columns, 7)
    full, window = gather_all(packed, tokens, depth, reach, cuts)
    query_w = full[:, :heads_width]
    key_w = full[:, heads_width : 2 * heads_width]
    value_w = full[:, 2 * heads_width : 3 * heads_width]
    out_t = full[:, 3 * heads_width : at_small]
    router_w = full[:, at_small : at_small + experts]
    gain_first = full[:, at_small + experts].astype(f32)
    gain_second = full[:, at_small + experts + 1].astype(f32)
    sgate_w = full[:, at_shared : at_shared + hidden]
    sup_w = full[:, at_shared + hidden : at_shared + 2 * hidden]
    sdown_t = full[:, at_shared + 2 * hidden :]
    expert_gate = e_gate.astype(bf16)
    expert_up = e_up.astype(bf16)
    expert_down = e_down.astype(bf16)

    span = (reach + 1) * tok_count
    token_rows = me * tok_count + jnp.arange(tok_count, dtype=jnp.int32)
    key_rows = (me - reach) * tok_count + jnp.arange(span, dtype=jnp.int32)
    cos_all, sin_all = rotary_tables(key_rows)
    cosines, sines = cos_all[reach * tok_count :], sin_all[reach * tok_count :]
    padded = jnp.pad(segments, (reach * tok_count, 0), constant_values=-1)
    seg_key = lax.dynamic_slice_in_dim(padded, me * tok_count, span)
    seg_query = seg_key[reach * tok_count :]
    later, earlier = token_rows[:, None], key_rows[None, :]
    valid = (earlier >= 0) & (earlier <= later) & (later - earlier < WINDOW)
    valid = valid & (seg_key[None, :] == seg_query[:, None])
    head_shape = (tok_count, local_heads, HEAD)
    span_shape = (span, local_heads, HEAD)
    x_all = window.astype(f32)
    normed_all, scale_all = rms_parts(x_all)
    attn_in_all = (normed_all * gain_first).astype(bf16)
    attn_in = attn_in_all[reach * tok_count :]
    x_float = tokens.astype(f32)
    normed_one, scale_one = rms_parts(x_float)
    queries = (
        rotate(matmul(attn_in, query_w).reshape(head_shape), cosines, sines) * score_scale
    ).astype(bf16)
    all_keys = rotate(matmul(attn_in_all, key_w).reshape(span_shape), cos_all, sin_all).astype(bf16)
    all_values = matmul(attn_in_all, value_w).astype(bf16).reshape(span_shape)
    scores = masked_scores(queries, all_keys, valid)
    peak = jnp.max(scores, axis=-1, keepdims=True)
    lse = peak + jnp.log(jnp.sum(jnp.exp(scores - peak), axis=-1, keepdims=True))
    weights = jnp.exp(scores - lse)
    heads_out = (
        jnp.einsum("hqk,khe->qhe", weights.astype(bf16), all_values, preferred_element_type=f32)
        .astype(bf16)
        .reshape(tok_count, -1)
    )
    out_part = input_grad(heads_out, out_t).astype(bf16)
    (out_other,) = swap([out_part], 5)
    middle = x_float + (out_part.astype(f32) + out_other.astype(f32))

    normed_two, scale_two = rms_parts(middle)
    branch_in = (normed_two * gain_second).astype(bf16)
    logits = matmul(branch_in, router_w)
    expo = jnp.exp(logits - jnp.max(logits, axis=-1, keepdims=True))
    probs = expo / jnp.sum(expo, axis=-1, keepdims=True)
    picked = (routes[:, :, None] == jnp.arange(experts, dtype=jnp.int32)[None, None, :]).astype(f32)
    gates = jnp.sum(probs[:, None, :] * picked, axis=2)
    chosen = jnp.sum(picked, axis=1)
    places = jnp.arange(tok_count, dtype=jnp.int32)
    below = (places[:, None] > places[None, :]).astype(bf16)
    before = matmul(below, chosen.astype(bf16))
    slots = jnp.arange(capacity, dtype=f32)
    taken = (before.T[:, None, :] == slots[None, :, None]) & (chosen.T[:, None, :] > 0.5)
    gate_slot = jnp.sum(jnp.where(taken, probs.T[:, None, :], 0.0), axis=2)
    chooser = taken.astype(bf16).reshape(experts * capacity, tok_count)
    pair_slot = routes * capacity + jnp.sum(picked * before[:, None, :], axis=2).astype(jnp.int32)
    all_slots = jnp.arange(experts * capacity, dtype=jnp.int32)
    pick = [(pair_slot[:, k : k + 1] == all_slots[None, :]).astype(bf16) for k in range(routes.shape[1])]
    rows_out = matmul(chooser, branch_in).astype(bf16).reshape(experts, capacity, width)
    d_after = cotangent.astype(f32)
    d_rows_out = (
        gate_slot.reshape(-1, 1) * matmul(chooser, cotangent)
    ).astype(bf16).reshape(experts, capacity, width)
    rows_in, d_rows_in = dispatch(rows_out, d_rows_out, n, owners)

    rows_in = rows_in.reshape(n * capacity, width)
    d_rows_in = d_rows_in.reshape(n * capacity, width)
    gate_hidden = matmul(rows_in, expert_gate)
    up_hidden = matmul(rows_in, expert_up)
    gate_act = jax.nn.silu(gate_hidden)
    expert_hidden = (gate_act * up_hidden).astype(bf16)
    part_rows = matmul(expert_hidden, expert_down).astype(bf16)
    d_hidden = input_grad(d_rows_in, expert_down)
    d_gate_hidden = (d_hidden * up_hidden * silu_grad(gate_hidden)).astype(bf16)
    d_up_hidden = (d_hidden * gate_act).astype(bf16)
    d_part_rows = (
        input_grad(d_gate_hidden, expert_gate) + input_grad(d_up_hidden, expert_up)
    ).astype(bf16)
    returned, d_returned = give_back(
        part_rows.reshape(n, capacity, width), d_part_rows.reshape(n, capacity, width)
    )
    grad_e_down = weight_grad(expert_hidden, d_rows_in)
    grad_e_gate = weight_grad(rows_in, d_gate_hidden)
    grad_e_up = weight_grad(rows_in, d_up_hidden)

    shared_gate = matmul(branch_in, sgate_w)
    shared_up = matmul(branch_in, sup_w)
    shared_act = jax.nn.silu(shared_gate)
    shared_hidden = (shared_act * shared_up).astype(bf16)
    shared_part = input_grad(shared_hidden, sdown_t)
    d_shared = matmul(cotangent, sdown_t)
    grad_sdown_t = weight_grad(cotangent, shared_hidden)
    d_sgate = (d_shared * shared_up * silu_grad(shared_gate)).astype(bf16)
    d_sup = (d_shared * shared_act).astype(bf16)
    grad_sgate = weight_grad(branch_in, d_sgate)
    grad_sup = weight_grad(branch_in, d_sup)
    d_shared_in = input_grad(d_sgate, sgate_w) + input_grad(d_sup, sup_w)

    def incoming(rows):
        rows = rows.reshape(experts, owners, capacity, half)
        if owners > 1:
            rows = jnp.sum(rows.astype(f32), axis=1).astype(bf16)
        return rows.reshape(experts * capacity, half)

    def placed(values):
        own = jnp.concatenate([values, jnp.zeros_like(values)], axis=1)
        other = jnp.concatenate([jnp.zeros_like(values), values], axis=1)
        return jnp.where(core == 0, own, other)

    result_rows, d_result_rows = incoming(returned), incoming(d_returned)
    pair_out = [matmul(p, result_rows) for p in pick]
    d_pairs = matmul(sum(pick), d_result_rows)
    moe_half = sum(gates[:, k : k + 1] * pair_out[k] for k in range(len(pick)))
    d_half = lax.dynamic_slice_in_dim(cotangent, core * half, half, axis=1).astype(f32)
    d_gates_part = jnp.concatenate(
        [jnp.sum(d_half * p, axis=1, keepdims=True) for p in pair_out], axis=1
    )
    after_part = (placed(moe_half) + shared_part).astype(bf16)
    d_branch_part = (d_shared_in + placed(d_pairs)).astype(bf16)
    d_gates_part = jnp.pad(d_gates_part, ((0, 0), (0, LANES - len(pick))))
    after_other, d_branch_other, d_gates_other = swap(
        [after_part, d_branch_part, d_gates_part], 6
    )
    output = (middle + (after_part.astype(f32) + after_other.astype(f32))).astype(bf16)
    d_branch_sum = d_branch_part.astype(f32) + d_branch_other.astype(f32)
    d_gates = (d_gates_part + d_gates_other)[:, : len(pick)]
    d_probs = jnp.sum(d_gates[:, :, None] * picked, axis=1)
    d_logits = (probs * (d_probs - jnp.sum(probs * d_probs, axis=-1, keepdims=True))).astype(bf16)
    grad_router = weight_grad(branch_in, d_logits)
    d_branch_in = d_branch_sum + input_grad(d_logits, router_w)
    grad_gain_two = jnp.sum(d_branch_in * normed_two, axis=0)
    d_norm_two = d_branch_in * gain_second
    d_middle = d_after + scale_two * (
        d_norm_two - normed_two * jnp.mean(d_norm_two * normed_two, axis=-1, keepdims=True)
    )

    cos_wide = jnp.tile(cos_all[:, 0, :], (1, 4))
    sin_wide = jnp.tile(sin_all[:, 0, :], (1, 4)) * jnp.where(
        jnp.arange(LANES) % HEAD < HEAD // 2, -1.0, 1.0
    )
    bias = jnp.where(valid.T, 0.0, masked).astype(f32)
    lse_rows = jnp.pad(lse[:, :, 0], ((0, -local_heads % 8), (0, 0)))
    blocks = (depth, 2, 2, shard_rows)
    grad_small = jnp.concatenate(
        [grad_router, grad_gain_two[:, None], jnp.zeros((width, LANES - experts - 1), f32)], axis=1
    ).astype(bf16)
    total, d_attn_in = backward(
        [
            grad_sgate.astype(bf16).reshape(blocks + (hidden,)),
            grad_sup.astype(bf16).reshape(blocks + (hidden,)),
            grad_sdown_t.astype(bf16).reshape(blocks + (hidden,)),
            grad_small.reshape(blocks + (LANES,)),
            window.reshape(reach + 1, tok_count, width),
            queries.reshape(tok_count, -1),
            all_keys.reshape(span, -1),
            all_values.reshape(span, -1),
            lse_rows,
            heads_out,
            d_middle.astype(bf16),
            query_w, key_w, value_w, out_t,
            gain_first[None, :],
            cos_wide, sin_wide, bias,
        ],
        shard_rows, columns, 3 * hidden, tok_count, heads_width, width, depth, reach,
    )
    def columns_of(at, count):
        return total[:, at : at + count]

    at_out = 3 * hidden
    at_pairs = at_out + heads_width + LANES
    grad_parts = [
        jnp.concatenate(
            [
                columns_of(at_pairs + (3 * pair + i) * LANES, LANES)
                for pair in range(heads_width // LANES)
            ],
            axis=1,
        )
        for i in range(3)
    ]
    d_attn_in = d_attn_in.astype(f32)
    d_norm_one = d_attn_in * gain_first
    token_input_gradient = d_middle + scale_one * (
        d_norm_one - normed_one * jnp.mean(d_norm_one * normed_one, axis=-1, keepdims=True)
    )
    return (
        output,
        token_input_gradient,
        total[:, columns - LANES],
        grad_parts[0],
        grad_parts[1],
        grad_parts[2],
        columns_of(at_out, heads_width).T,
        total[:, at_out + heads_width + experts],
        columns_of(at_out + heads_width, experts),
        columns_of(0, hidden),
        columns_of(hidden, hidden),
        columns_of(2 * hidden, hidden).T,
        grad_e_gate,
        grad_e_up,
        grad_e_down,
    )


def solution(mesh):
    by_dp, both, turned = P("dp", None), P("dp", "tensor"), P("tensor", "dp")
    wide, tall = P(None, ("dp", "tensor")), P(("dp", "tensor"), None)
    weights = (P("dp"), both, both, both, turned, P("dp"), by_dp, both, both, turned, wide, wide, tall)
    return jax.shard_map(
        local,
        mesh=mesh,
        in_specs=(by_dp, by_dp) + weights + (by_dp, P()),
        out_specs=(by_dp, by_dp) + weights,
        check_vma=False,
    )
```

```python
import functools

import jax
import jax.numpy as jnp
import numpy as np
from jax import lax
from jax.experimental import pallas as pl
from jax.experimental.pallas import tpu as pltpu
from jax.sharding import PartitionSpec as P

HEAD = 64
WINDOW = 1024
LANES = 128
PLANE = 4

MESH = pl.DeviceIdType.MESH
f32 = jnp.float32
bf16 = jnp.bfloat16

eps = 1e-06
masked = -1e30


def matmul(left, right):
    return jnp.dot(left, right, preferred_element_type=f32)


def weight_grad(left, right):
    return lax.dot_general(
        left, right, (((0,), (0,)), ((), ())), preferred_element_type=f32
    )


def input_grad(left, right):
    return lax.dot_general(
        left, right, (((1,), (1,)), ((), ())), preferred_element_type=f32
    )


def rms_parts(values):
    factor = lax.rsqrt(jnp.mean(values * values, axis=-1, keepdims=True) + eps)
    return (values * factor, factor)


def silu_grad(values):
    sigma = jax.nn.sigmoid(values)
    return sigma * (1.0 + values * (1.0 - sigma))


def digits(me):
    return lax.div(me, PLANE), lax.rem(lax.div(me, 2), 2), lax.rem(me, 2)


def index_of(z, y, x):
    return z * PLANE + y * 2 + x


def push(src, dst, send, recv, device):
    copy = pltpu.make_async_remote_copy(
        src_ref=src,
        dst_ref=dst,
        send_sem=send,
        recv_sem=recv,
        device_id=device,
        device_id_type=MESH,
    )
    copy.start()
    return copy


def greet(devices):
    barrier = pltpu.get_barrier_semaphore()
    for device in devices:
        pl.semaphore_signal(barrier, inc=1, device_id=device, device_id_type=MESH)
    pl.semaphore_wait(barrier, len(devices))


def comm_params(collective_id, limit=48 << 20):
    return pltpu.CompilerParams(
        collective_id=collective_id, has_side_effects=True, vmem_limit_bytes=limit
    )


def dma(*shape):
    return pltpu.SemaphoreType.DMA(shape)


IN_HBM = pl.BlockSpec(memory_space=pl.ANY)
IN_VMEM = pl.BlockSpec(memory_space=pltpu.VMEM)


def grid_peers(depth, z, y, x):
    peers = [{"dp": index_of(lax.rem(z + k, depth), y, x)} for k in range(1, depth)]
    return peers, {"dp": index_of(z, 1 - y, x)}, {"dp": index_of(z, y, 1 - x)}


def swap_kernel(count, *refs):
    sources, targets, (send, recv) = refs[:count], refs[count : 2 * count], refs[2 * count :]
    sibling = {"tensor": 1 - lax.axis_index("tensor")}
    greet([sibling])
    copies = [
        push(a, b, send.at[i], recv.at[i], sibling)
        for i, (a, b) in enumerate(zip(sources, targets))
    ]
    for copy in copies:
        copy.wait()


def swap(arrays, collective_id):
    count = len(arrays)
    return pl.pallas_call(
        functools.partial(swap_kernel, count),
        out_shape=tuple(jax.ShapeDtypeStruct(a.shape, a.dtype) for a in arrays),
        in_specs=[IN_VMEM] * count,
        out_specs=(IN_VMEM,) * count,
        scratch_shapes=[dma(count), dma(count)],
        compiler_params=comm_params(collective_id),
        name="swap_cores",
    )(*arrays)


def dispatch_kernel(n, owners, first, second, got_first, got_second, send, recv, f_send, f_recv, own):
    me, core = lax.axis_index("dp"), lax.axis_index("tensor")
    sibling = {"tensor": 1 - core}
    greet([{"dp": lax.rem(me + k, n)} for k in range(1, n)] + [sibling])
    half = first.shape[-1] // 2
    cols = pl.ds(pl.multiple_of(core * half, half), half)
    pairs = ((first, got_first), (second, got_second))
    mine = lax.div(me, owners)
    copies = []
    for k in range(1, n):
        to = lax.rem(me + k, n)
        for i, (source, target) in enumerate(pairs):
            copies.append(
                push(
                    source.at[lax.div(to, owners), :, cols],
                    target.at[me, :, cols],
                    send.at[i, k],
                    recv.at[i, k],
                    {"dp": to},
                )
            )
    local = [
        pltpu.make_async_copy(source.at[mine], target.at[me], own.at[i])
        for i, (source, target) in enumerate(pairs)
    ]
    for copy in local:
        copy.start()
    forwards = []
    for k in range(1, n):
        source_of = lax.rem(me + n - k, n)
        for i, (source, target) in enumerate(pairs):
            copies[2 * (k - 1) + i].wait_recv()
            block = target.at[source_of, :, cols]
            forwards.append(push(block, block, f_send.at[i, k], f_recv.at[i, k], sibling))
    for copy in forwards:
        copy.wait_recv()
    for copy in local:
        copy.wait()
    for copy in copies + forwards:
        copy.wait_send()


def dispatch(first, second, n, owners):
    shape = jax.ShapeDtypeStruct((n,) + first.shape[1:], first.dtype)
    return pl.pallas_call(
        functools.partial(dispatch_kernel, n, owners),
        out_shape=(shape, shape),
        in_specs=[IN_HBM] * 2,
        out_specs=(IN_HBM, IN_HBM),
        scratch_shapes=[dma(2, n), dma(2, n), dma(2, n), dma(2, n), dma(2)],
        compiler_params=comm_params(2),
        name="dispatch_rows",
    )(first, second)


def return_kernel(n, groups, first, second, got_first, got_second, part, total, send, recv, f_send, f_recv, own):
    me, core = lax.axis_index("dp"), lax.axis_index("tensor")
    sibling = {"tensor": 1 - core}
    greet([{"dp": lax.rem(me + k, n)} for k in range(1, n)] + [sibling])
    half = first.shape[-1] // 2
    mine = pl.ds(pl.multiple_of(core * half, half), half)
    theirs = pl.ds(pl.multiple_of((1 - core) * half, half), half)
    pairs = ((first, got_first), (second, got_second))
    each = n // groups
    swaps = []
    for g in range(groups):
        block = pl.ds(g * each, each)
        for i, (source, target) in enumerate(pairs):
            swaps.append(
                push(
                    source.at[block, :, theirs],
                    part.at[i, block],
                    f_send.at[i, g],
                    f_recv.at[i, g],
                    sibling,
                )
            )
    for g in range(groups):
        block = pl.ds(g * each, each)
        for i, (source, target) in enumerate(pairs):
            swaps[2 * g + i].wait_recv()
            total[i, block] = (
                source[block, :, mine].astype(f32) + part[i, block].astype(f32)
            ).astype(bf16)
        for slot in range(g * each, (g + 1) * each):
            for i, (source, target) in enumerate(pairs):
                @pl.when(slot != me)
                def _():
                    push(
                        total.at[i, slot],
                        target.at[me],
                        send.at[i, slot],
                        recv.at[i, me],
                        {"dp": slot},
                    )
    local = [
        pltpu.make_async_copy(total.at[i, me], pairs[i][1].at[me], own.at[i]) for i in range(2)
    ]
    for copy in local:
        copy.start()
    for k in range(1, n):
        to, source_of = lax.rem(me + k, n), lax.rem(me + n - k, n)
        for i, (source, target) in enumerate(pairs):
            pltpu.make_async_remote_copy(
                total.at[i, to], target.at[source_of], send.at[i, to], recv.at[i, source_of],
                device_id={"dp": to}, device_id_type=MESH,
            ).wait()
    for copy in local:
        copy.wait()
    for copy in swaps:
        copy.wait_send()


def give_back(first, second, groups=4):
    n, capacity, width = first.shape
    half = jax.ShapeDtypeStruct((n, capacity, width // 2), first.dtype)
    buffer = pltpu.VMEM((2, n, capacity, width // 2), first.dtype)
    return pl.pallas_call(
        functools.partial(return_kernel, n, groups),
        out_shape=(half, half),
        in_specs=[IN_VMEM] * 2,
        out_specs=(IN_HBM, IN_HBM),
        scratch_shapes=[buffer, buffer, dma(2, n), dma(2, n), dma(2, groups), dma(2, groups), dma(2)],
        compiler_params=comm_params(3),
        name="return_rows",
    )(first, second)


class Scatter:
    def __init__(self, depth, chunks, total, buffers, semaphores):
        self.depth, self.chunks, self.total = depth, chunks, total
        self.first_l, self.first_r, self.second_l, self.second_r, self.last = buffers
        self.p_send, self.p_recv, self.z_send, self.z_recv = semaphores
        self.z, self.y, self.x = digits(lax.axis_index("dp"))
        self.z_peers, self.y_peer, self.x_peer = grid_peers(depth, self.z, self.y, self.x)
        self.at_l, self.at_r, l, r = [], [], 0, 0
        for left, lc, lw, right, rc, rw, out in chunks:
            self.at_l.append(pl.ds(l, lw))
            self.at_r.append(pl.ds(r, rw))
            l, r = l + lw, r + rw
        self.ones, self.twos, self.threes = {}, {}, {}

    def start(self, c):
        left, lc, lw, right, rc, rw, out = self.chunks[c]
        self.ones[c] = [
            push(
                left.at[:, :, 1 - self.x, :, pl.ds(lc, lw)],
                self.first_l.at[:, :, :, self.at_l[c]],
                self.p_send.at[c, 0], self.p_recv.at[c, 0], self.x_peer,
            ),
            push(
                right.at[:, 1 - self.y, :, :, pl.ds(rc, rw)],
                self.first_r.at[:, :, :, self.at_r[c]],
                self.p_send.at[c, 1], self.p_recv.at[c, 1], self.y_peer,
            ),
        ]

    def second(self, c):
        left, lc, lw, right, rc, rw, out = self.chunks[c]
        in_l, in_r, first_l, first_r = self.at_l[c], self.at_r[c], self.first_l, self.first_r
        for copy in self.ones[c]:
            copy.wait_recv()

        def add(i, carry):
            for j in range(2):
                first_l[i, j, :, in_l] = (
                    first_l[i, j, :, in_l].astype(f32) + left[i, j, self.x, :, pl.ds(lc, lw)].astype(f32)
                ).astype(bf16)
                first_r[i, j, :, in_r] = (
                    first_r[i, j, :, in_r].astype(f32) + right[i, self.y, j, :, pl.ds(rc, rw)].astype(f32)
                ).astype(bf16)
            return carry

        lax.fori_loop(0, self.depth, add, 0)
        self.twos[c] = [
            push(
                first_l.at[:, 1 - self.y, :, in_l], self.second_l.at[:, :, in_l],
                self.p_send.at[c, 2], self.p_recv.at[c, 2], self.y_peer,
            ),
            push(
                first_r.at[:, 1 - self.x, :, in_r], self.second_r.at[:, :, in_r],
                self.p_send.at[c, 3], self.p_recv.at[c, 3], self.x_peer,
            ),
        ]

    def third(self, c):
        for copy in self.twos[c]:
            copy.wait_recv()
        sides = (
            (self.second_l, self.first_l, self.y, self.at_l[c]),
            (self.second_r, self.first_r, self.x, self.at_r[c]),
        )

        def add(i, carry):
            for source, before, place, here in sides:
                source[i, :, here] = (
                    source[i, :, here].astype(f32) + before[i, place, :, here].astype(f32)
                ).astype(bf16)
            return carry

        lax.fori_loop(0, self.depth, add, 0)
        self.threes[c] = [
            push(
                source.at[lax.rem(self.z + k + 1, self.depth), :, here],
                self.last.at[k, side, :, here],
                self.z_send.at[c, side, k], self.z_recv.at[c, side, k], self.z_peers[k],
            )
            for side, (source, before, place, here) in enumerate(sides)
            for k in range(self.depth - 1)
        ]

    def finish(self, c):
        left, lc, lw, right, rc, rw, out = self.chunks[c]
        for copy in self.threes[c]:
            copy.wait_recv()
        for side, source, here, at, span in (
            (0, self.second_l, self.at_l[c], out, lw),
            (1, self.second_r, self.at_r[c], out + lw, rw),
        ):
            value = source[self.z, :, here].astype(f32)
            for k in range(self.depth - 1):
                value = value + self.last[k, side, :, here].astype(f32)
            self.total[:, pl.ds(at, span)] = value

    def drain(self):
        for copies in list(self.ones.values()) + list(self.twos.values()) + list(self.threes.values()):
            for copy in copies:
                copy.wait_send()


def lanes_of(part):
    lane = lax.broadcasted_iota(jnp.int32, (1, LANES), 1)
    return (lax.div(lane, HEAD) == part).astype(f32).astype(bf16)


def swap_halves(values):
    lane = lax.broadcasted_iota(jnp.int32, (1, LANES), 1)
    low = lax.rem(lane, HEAD) < HEAD // 2
    return jnp.where(
        low, pltpu.roll(values, LANES - HEAD // 2, 1), pltpu.roll(values, HEAD // 2, 1)
    )


def put_rows(target, values, columns):
    rows = target.shape[3]
    for b in range(values.shape[0] // rows):
        target[b // PLANE, (b // 2) % 2, b % 2, :, columns] = values[b * rows : (b + 1) * rows]


def backward_kernel(
    depth, reach, per_core, g_gate, g_up, g_down, g_small, window, q, k, v, lse, heads_out, d_attn,
    near, gains, cosines, sines, bias, total, d_full,
    grads, attn_t, d_heads, dq_all, dk_all, dv_all, d_part, d_swap, d_sum, d_got, gain_got,
    first_l, first_r, second_l, second_r, last,
    p_send, p_recv, z_send, z_recv, t_send, t_recv, s_send, s_recv, f_send, f_recv,
):
    n = depth * PLANE
    me, core = lax.axis_index("dp"), lax.axis_index("tensor")
    sibling = {"tensor": 1 - core}
    ahead = [{"dp": lax.rem(me + i, n)} for i in range(1, reach + 1)]
    behind = [{"dp": lax.rem(me + n - i, n)} for i in range(1, reach + 1)]
    heads_width = q.shape[1]
    count = q.shape[0]
    pairs = heads_width // LANES
    hidden = g_gate.shape[4]
    chunks = []
    out = 0
    step = 2 * LANES
    for source in (g_gate, g_up, g_down):
        for at in range(0, hidden, 2 * step):
            chunks.append((source, at, step, source, at + step, step, out))
            out += 2 * step
    early = len(chunks)
    widths = [(step, step)] + [(step, LANES), (LANES, step)] * pairs
    widths = widths[:pairs] + [(step, step)]
    at = 0
    for left, right in widths:
        chunks.append((grads, at, left, grads, at + left, right, out + at))
        at += left + right
    scatter = Scatter(
        depth, chunks, total, (first_l, first_r, second_l, second_r, last),
        (p_send, p_recv, z_send, z_recv),
    )
    greet(scatter.z_peers + [scatter.y_peer, scatter.x_peer, sibling] + ahead + behind)
    for c in range(3):
        scatter.start(c)

    query_w, key_w, value_w, out_w = (
        pl.ds(LANES + i * heads_width, heads_width) for i in range(4)
    )
    gain = gains[0:1, :]
    d_heads[...] = matmul(d_attn[...], stacked(near, out_w)).astype(bf16)
    put_rows(grads, weight_grad(d_attn[...], heads_out[...]).astype(bf16), pl.ds(0, heads_width))
    grads[:, :, :, :, pl.ds(heads_width, LANES)] = g_small[...]

    def normed(block):
        values = window[block].astype(f32)
        return values * lax.rsqrt(jnp.mean(values * values, axis=-1, keepdims=True) + eps)

    def turned(block, carry):
        rows = pl.ds(pl.multiple_of(block * count, count), count)
        attn_t[:, rows] = (normed(block) * gain).T.astype(bf16)
        return carry

    for block in range(reach + 1):
        turned(block, 0)
    scatter.start(early)
    own = pl.ds(reach * count, count)
    done = 0
    for pair in range(pairs):
        columns = pl.ds(pair * LANES, LANES)
        k_pair, v_pair, q_pair, d_pair = k[:, columns], v[:, columns], q[:, columns], d_heads[:, columns]
        k_turned = k_pair.T
        dq, dk, dv = [], None, None
        for part in range(2):
            head = 2 * pair + part
            lanes = lanes_of(part)
            q_head, d_head = q_pair * lanes, d_pair * lanes
            probs = jnp.exp(input_grad(k_pair, q_head) + bias[...] - lse[head : head + 1, :])
            d_probs = input_grad(v_pair, d_head)
            inner = jnp.sum(probs * d_probs, axis=0, keepdims=True)
            d_scores = (probs * (d_probs - inner)).astype(bf16)
            dq.append(matmul(k_turned, d_scores)[part * HEAD : (part + 1) * HEAD, :])
            parts = matmul(d_scores, q_head), matmul(probs.astype(bf16), d_head)
            dk, dv = parts if part == 0 else (dk + parts[0], dv + parts[1])
            if done < early + 1:
                scatter.second(done)
                if done + 3 < early:
                    scatter.start(done + 3)
            if 1 <= done:
                scatter.third(done - 1)
            if 2 <= done:
                scatter.finish(done - 2)
            done += 1
        dq = jnp.concatenate(dq, axis=0).T * (HEAD ** (-0.5))
        cos_own, sin_own = cosines[own, :], sines[own, :]
        dq_low = turn(dq, cos_own, -sin_own).astype(bf16)
        dk_low = turn(dk, cosines[...], -sines[...]).astype(bf16)
        dv_low = dv.astype(bf16)
        dq_all[:, columns] = dq_low
        dk_all[:, columns] = dk_low
        dv_all[:, columns] = dv_low
        at = heads_width + LANES + pair * 3 * LANES
        put_rows(grads, matmul(attn_t[:, own], dq_low).astype(bf16), pl.ds(at, LANES))
        put_rows(grads, matmul(attn_t[...], dk_low).astype(bf16), pl.ds(at + LANES, LANES))
        put_rows(grads, matmul(attn_t[...], dv_low).astype(bf16), pl.ds(at + 2 * LANES, LANES))
        if pair < pairs - 1:
            scatter.start(early + 1 + pair)

    width = d_part.shape[-1] // 2
    mine = pl.ds(pl.multiple_of(core * width, width), width)
    theirs = pl.ds(pl.multiple_of((1 - core) * width, width), width)
    swaps = []
    query_v, key_v, value_v = (stacked(near, at) for at in (query_w, key_w, value_w))
    gain_row = jnp.zeros((1, 2 * width), f32)
    for block in range(reach + 1):
        rows = pl.ds(block * count, count)
        value = input_grad(dk_all[rows, :], key_v) + input_grad(dv_all[rows, :], value_v)
        if block == reach:
            value = value + input_grad(dq_all[...], query_v)
        gain_row = gain_row + jnp.sum(value * normed(block), axis=0, keepdims=True)
        d_part[block] = value.astype(bf16)
        swaps.append(
            push(
                d_part.at[block, :, theirs], d_swap.at[block],
                s_send.at[block], s_recv.at[block], sibling,
            )
        )
    put_rows(
        grads,
        jnp.broadcast_to(gain_row, (LANES, 2 * width)).T.astype(bf16),
        pl.ds(heads_width + LANES + pairs * 3 * LANES, LANES),
    )
    final = len(chunks) - 1
    scatter.start(final)
    back = []
    for block in range(reach + 1):
        swaps[block].wait_recv()
        d_sum[block] = (
            d_part[block, :, mine].astype(f32) + d_swap[block].astype(f32)
        ).astype(bf16)
        if block < reach:
            i = reach - 1 - block
            back.append(
                push(d_sum.at[block], d_got.at[i], t_send.at[i], t_recv.at[i], behind[i])
            )
    seconds = [c for c in range(len(chunks)) if c not in scatter.twos]
    for c in range(done - 1, len(chunks) + 2):
        if c < len(chunks) and c not in scatter.twos:
            scatter.second(c)
        if c - 1 < len(chunks) and c - 1 not in scatter.threes:
            scatter.third(c - 1)
        if c >= 2 and c - 2 >= done - 2:
            scatter.finish(c - 2)
    d_mine = d_sum[reach].astype(f32)
    for copy in back:
        copy.wait_recv()
    for i in range(reach):
        d_mine = d_mine + d_got[i].astype(f32)
    d_full[:, mine] = d_mine.astype(bf16)
    both = push(d_full.at[:, mine], d_full.at[:, mine], f_send.at[0], f_recv.at[0], sibling)
    split = pl.ds(per_core, LANES)
    gain_copy = push(total.at[:, split], gain_got, f_send.at[1], f_recv.at[1], sibling)
    both.wait()
    gain_copy.wait()
    total[:, split] = total[:, split] + gain_got[...]
    scatter.drain()
    for copy in back + swaps:
        copy.wait_send()


def backward(arrays, rows, columns, shared, count, heads_width, width, depth, reach):
    span = (reach + 1) * count
    half = columns // 2
    parts = shared // (4 * LANES) + 2 + heads_width // LANES
    first = pltpu.VMEM((depth, 2, rows, half), bf16)
    second = pltpu.VMEM((depth, rows, half), bf16)
    own = columns - shared
    return pl.pallas_call(
        functools.partial(backward_kernel, depth, reach, columns - LANES),
        out_shape=(
            jax.ShapeDtypeStruct((rows, columns), f32),
            jax.ShapeDtypeStruct((count, width), bf16),
        ),
        in_specs=[IN_VMEM] * len(arrays),
        out_specs=(IN_VMEM, IN_VMEM),
        scratch_shapes=[
            pltpu.VMEM((depth, 2, 2, rows, own), bf16),
            pltpu.VMEM((width, span), bf16),
            pltpu.VMEM((count, heads_width), bf16),
            pltpu.VMEM((count, heads_width), bf16),
            pltpu.VMEM((span, heads_width), bf16),
            pltpu.VMEM((span, heads_width), bf16),
            pltpu.VMEM((reach + 1, count, width), bf16),
            pltpu.VMEM((reach + 1, count, width // 2), bf16),
            pltpu.VMEM((reach + 1, count, width // 2), bf16),
            pltpu.VMEM((reach, count, width // 2), bf16),
            pltpu.VMEM((rows, LANES), f32),
            first, first, second, second,
            pltpu.VMEM((depth - 1, 2, rows, half), bf16),
            dma(parts, 4), dma(parts, 4),
            dma(parts, 2, depth - 1), dma(parts, 2, depth - 1),
            dma(reach), dma(reach), dma(reach + 1), dma(reach + 1), dma(2), dma(2),
        ],
        compiler_params=comm_params(4, 58 << 20),
        name="attention_backward",
    )(*arrays)


class Gather:
    def __init__(self, depth, chunks, shard, full, semaphores):
        self.depth, self.chunks, self.shard, self.full = depth, chunks, shard, full
        self.z_send, self.z_recv, self.p_send, self.p_recv = semaphores
        self.z, self.y, self.x = digits(lax.axis_index("dp"))
        self.z_peers, self.y_peer, self.x_peer = grid_peers(depth, self.z, self.y, self.x)
        self.ones, self.twos, self.threes = {}, {}, {}

    def _sides(self, c):
        at, left, right = self.chunks[c]
        return pl.ds(at, left), pl.ds(at + left, right)

    def first(self, c):
        at, left, right = self.chunks[c]
        columns = pl.ds(at, left + right)
        self.ones[c] = [
            push(
                self.shard.at[:, columns],
                self.full.at[self.z, self.y, self.x, :, columns],
                self.z_send.at[c, k], self.z_recv.at[c, k], self.z_peers[k],
            )
            for k in range(self.depth - 1)
        ]

    def second(self, c):
        left, right = self._sides(c)
        for copy in self.ones[c]:
            copy.wait_recv()
        a = self.full.at[:, self.y, self.x, :, left]
        b = self.full.at[:, self.y, self.x, :, right]
        self.twos[c] = [
            push(a, a, self.p_send.at[c, 0], self.p_recv.at[c, 0], self.y_peer),
            push(b, b, self.p_send.at[c, 1], self.p_recv.at[c, 1], self.x_peer),
        ]

    def third(self, c):
        left, right = self._sides(c)
        for copy in self.twos[c]:
            copy.wait_recv()
        a = self.full.at[:, :, self.x, :, left]
        b = self.full.at[:, self.y, :, :, right]
        self.threes[c] = [
            push(a, a, self.p_send.at[c, 2], self.p_recv.at[c, 2], self.x_peer),
            push(b, b, self.p_send.at[c, 3], self.p_recv.at[c, 3], self.y_peer),
        ]

    def finish(self, c):
        for copy in self.threes[c]:
            copy.wait_recv()

    def plan(self, lead):
        count = len(self.chunks)
        steps = []
        for s in range(count + 2):
            if s < count:
                steps.append((self.second, s))
                if s + lead < count:
                    steps.append((self.first, s + lead))
            if 1 <= s <= count:
                steps.append((self.third, s - 1))
            if s >= 2:
                steps.append((self.finish, s - 2))
        return steps

    def drain(self):
        for copies in list(self.ones.values()) + list(self.twos.values()) + list(self.threes.values()):
            for copy in copies:
                copy.wait_send()


def stacked(ref, columns):
    rows = ref.shape[3]
    if rows % 16 == 0:
        return ref[:, :, :, :, columns].reshape(-1, columns.size)
    blocks = [
        ref[b // PLANE, (b // 2) % 2, b % 2, :, columns].astype(f32)
        for b in range(ref.shape[0] * PLANE)
    ]
    return jnp.concatenate(blocks, axis=0).astype(bf16)


def turn(values, cos, sin):
    return values * cos + swap_halves(values) * sin


def forward_kernel(
    depth, reach, experts, chunks, near_edges, small, w_query, w_key, w_value, out_shard, w_sgate, w_sup, down_shard,
    tokens, cotangent, routes, segments, row_cos, row_sin, block_cos, block_sin,
    full, near, window, q, k, v, lse, heads_out, cosines, sines, bias, gains, middle, branch_in, probs, gates, pick,
    rows_out, d_rows_out,
    shard, part, other,
    z_send, z_recv, p_send, p_recv, t_send, t_recv, f_send, f_recv, s_send, s_recv, own,
):
    n = depth * PLANE
    me, core = lax.axis_index("dp"), lax.axis_index("tensor")
    sibling = {"tensor": 1 - core}
    ahead = [{"dp": lax.rem(me + i, n)} for i in range(1, reach + 1)]
    behind = [{"dp": lax.rem(me + n - i, n)} for i in range(1, reach + 1)]
    gather = Gather(depth, chunks, shard, full, (z_send, z_recv, p_send, p_recv))
    at = 0
    for piece in (small, w_query, w_key, w_value, out_shard, w_sgate, w_sup, down_shard):
        shard[:, pl.ds(at, piece.shape[1])] = piece[...].astype(bf16)
        at += piece.shape[1]
    greet(gather.z_peers + [gather.y_peer, gather.x_peer, sibling] + ahead + behind)
    gather.first(0)
    gather.first(1)
    own_shard = pltpu.make_async_copy(shard, full.at[gather.z, gather.y, gather.x], own.at[0])
    own_shard.start()
    count, width = tokens.shape
    half = count // 2
    rows = pl.ds(pl.multiple_of(core * half, half), half)
    t_copies = [
        push(
            tokens.at[rows], window.at[reach - 1 - i, rows],
            t_send.at[i], t_recv.at[i], ahead[i],
        )
        for i in range(reach)
    ]
    window[reach] = tokens[...]

    lane = lax.broadcasted_iota(jnp.int32, (1, LANES), 1)
    sign = jnp.where(lax.rem(lane, HEAD) < HEAD // 2, -1.0, 1.0)
    seg_query = segments[pl.ds(me, 1), :].astype(f32)
    key_place = lax.broadcasted_iota(jnp.int32, (count, count), 0)
    query_place = lax.broadcasted_iota(jnp.int32, (count, count), 1)
    for b in range(reach + 1):
        at = pl.ds(b * count, count)
        c_b, s_b = block_cos[pl.ds(me + b, 1), :], block_sin[pl.ds(me + b, 1), :]
        cosines[at, :] = c_b * row_cos[...] - s_b * row_sin[...]
        sines[at, :] = (s_b * row_cos[...] + c_b * row_sin[...]) * sign
        block = me - reach + b
        seg_key = segments[pl.ds(lax.max(block, 0), 1), :].astype(f32)
        seg_key = jnp.broadcast_to(seg_key, (LANES, count)).T[:, :1]
        distance = (reach - b) * count + query_place - key_place
        limit = lax.select(block >= 0, WINDOW, 0)
        seen = (distance >= 0) & (distance < limit) & (seg_key == seg_query)
        bias[at, :] = jnp.where(seen, 0.0, masked)

    def normed(b):
        values = window[b].astype(f32)
        return values * lax.rsqrt(jnp.mean(values * values, axis=-1, keepdims=True) + eps)

    own_shard.wait()
    steps = gather.plan(2)
    done = [0]

    def advance(until=None, most=None):
        begun = done[0]
        while done[0] < len(steps) and (most is None or done[0] < begun + most):
            action, c = steps[done[0]]
            done[0] += 1
            action(c)
            if (action, c) == until:
                break

    advance((gather.second, 1))
    forwards = []
    for i, copy in enumerate(t_copies):
        copy.wait_recv()
        block = window.at[reach - 1 - i, rows]
        forwards.append(push(block, block, f_send.at[i], f_recv.at[i], sibling))
    landed = 0
    copies = []
    for i, (edge, c) in enumerate(near_edges):
        copies.append((c, pl.ds(landed, edge - landed), own.at[1 + i]))
        landed = edge

    def land(i):
        c, columns, semaphore = copies[i]
        advance((gather.finish, c))
        copy = pltpu.make_async_copy(
            full.at[:, :, :, :, columns], near.at[:, :, :, :, columns], semaphore
        )
        copy.start()
        copy.wait()

    land(0)
    for copy in forwards:
        copy.wait_recv()
    heads_width = q.shape[1]
    pairs = heads_width // LANES
    small_all = stacked(near, pl.ds(0, LANES))
    small_turned = small_all.astype(f32).T
    gain_first, gain_second = small_turned[experts : experts + 1, :], small_turned[experts + 1 : experts + 2, :]
    gains[...] = small_turned[experts : experts + 8, :]
    query_w = stacked(near, pl.ds(LANES, heads_width))
    key_w = stacked(near, pl.ds(LANES + heads_width, heads_width))
    value_w = stacked(near, pl.ds(LANES + 2 * heads_width, heads_width))
    for b in range(reach + 1):
        at = pl.ds(b * count, count)
        rows_in = (normed(b) * gain_first).astype(bf16)
        keys = matmul(rows_in, key_w)
        v[at, :] = matmul(rows_in, value_w).astype(bf16)
        for pair in range(pairs):
            columns = slice(pair * LANES, (pair + 1) * LANES)
            k[at, columns] = turn(keys[:, columns], cosines[at, :], sines[at, :]).astype(bf16)
        if b == reach:
            queries = matmul(rows_in, query_w)
            for pair in range(pairs):
                columns = slice(pair * LANES, (pair + 1) * LANES)
                q[:, columns] = (
                    turn(queries[:, columns], cosines[at, :], sines[at, :]) * (HEAD ** (-0.5))
                ).astype(bf16)
    lse[...] = jnp.zeros_like(lse)
    for pair in range(pairs):
        columns = pl.ds(pair * LANES, LANES)
        k_pair, v_pair, q_pair = k[:, columns], v[:, columns], q[:, columns]
        v_turned = v_pair.T
        outs = []
        for part_of in range(2):
            head = 2 * pair + part_of
            scores = input_grad(k_pair, q_pair * lanes_of(part_of)) + bias[...]
            peak = jnp.max(scores, axis=0, keepdims=True)
            expo = jnp.exp(scores - peak)
            total = jnp.sum(expo, axis=0, keepdims=True)
            lse[head : head + 1, :] = peak + jnp.log(total)
            weights = (expo * (1.0 / total)).astype(bf16)
            outs.append(matmul(v_turned, weights)[part_of * HEAD : (part_of + 1) * HEAD, :])
            advance(most=3)
        heads_out[:, columns] = jnp.concatenate(outs, axis=0).T.astype(bf16)
    land(1)
    out_w = stacked(near, pl.ds(LANES + 3 * heads_width, heads_width))
    part[...] = input_grad(heads_out[...], out_w).astype(bf16)
    swapped = push(part, other, s_send.at[0], s_recv.at[0], sibling)
    swapped.wait()
    middle_all = tokens[...].astype(f32) + (part[...].astype(f32) + other[...].astype(f32))
    middle[...] = middle_all
    factor = lax.rsqrt(jnp.mean(middle_all * middle_all, axis=-1, keepdims=True) + eps)
    branch = (middle_all * factor * gain_second).astype(bf16)
    branch_in[...] = branch

    logits = jnp.where(lane < experts, matmul(branch, small_all), masked)
    expo = jnp.exp(logits - jnp.max(logits, axis=-1, keepdims=True))
    chance = expo / jnp.sum(expo, axis=-1, keepdims=True)
    probs[...] = chance
    named = [(routes[:, i : i + 1] == lane).astype(f32) for i in range(routes.shape[1])]
    chosen = sum(named)
    below = (key_place > query_place).astype(f32).astype(bf16)
    before = matmul(below, chosen.astype(bf16))
    capacity = rows_out.shape[1]
    slot_of = lax.broadcasted_iota(jnp.int32, (count, experts * capacity), 1)
    d_gathered = jnp.zeros((experts * capacity, width), f32)
    gate_lanes = jnp.zeros((count, LANES), f32)
    for i, name in enumerate(named):
        place = jnp.sum(name * before, axis=-1, keepdims=True).astype(jnp.int32)
        place = place + routes[:, i : i + 1] * capacity
        choice = (slot_of == place).astype(f32).astype(bf16)
        pick[i] = choice
        gate = jnp.sum(chance * name, axis=-1, keepdims=True)
        gate_lanes = gate_lanes + jnp.where(lane == i, gate, 0.0)
        d_rows = (gate * cotangent[...].astype(f32)).astype(bf16)
        d_gathered = d_gathered + weight_grad(choice, d_rows)
    gates[...] = gate_lanes
    gathered = weight_grad(pick[0] + pick[1], branch)
    rows_out[...] = gathered.astype(bf16).reshape(rows_out.shape)
    d_rows_out[...] = d_gathered.astype(bf16).reshape(rows_out.shape)
    advance()
    gather.drain()
    for copy in t_copies + forwards:
        copy.wait_send()


def angle_tables(tok_count, blocks, reach):
    freqs = (10000.0 ** (-np.arange(HEAD // 2, dtype=np.float32) * np.float32(2.0 / HEAD))).astype(np.float64)
    freqs = np.tile(freqs, LANES // (HEAD // 2))[None, :]
    inner = np.arange(tok_count)[:, None] * freqs
    starts = np.maximum(np.arange(-reach, blocks), 0) * tok_count
    starts = np.pad(starts, (0, -len(starts) % 8))[:, None] * freqs
    return [jnp.asarray(f(a), f32) for a in (inner, starts) for f in (np.cos, np.sin)]


def forward(arrays, tokens, cotangent, routes, segments, depth, reach, experts, heads_width, hidden):
    count, width = tokens.shape
    n = depth * PLANE
    rows = arrays[0].shape[0]
    span = (reach + 1) * count
    near_width = LANES + 4 * heads_width
    columns = near_width + 3 * hidden
    capacity = count // 4
    qkv = LANES + 3 * heads_width
    step = 4 * LANES
    widths = [qkv // 2, qkv // 2, heads_width] + [step] * ((columns - near_width) // step)
    chunks, at = [], 0
    for w in widths:
        left = (w // LANES + (len(chunks) + 1) % 2) // 2 * LANES
        chunks.append((at, left, w - left))
        at += w
    near_edges = ((qkv, 1), (near_width, 2))
    parts = len(chunks)
    tables = angle_tables(count, n, reach)
    segment_rows = segments.reshape(-1, count)

    def shape(*dims, dtype=bf16):
        return jax.ShapeDtypeStruct(dims, dtype)

    outs = (
        shape(depth, 2, 2, rows, columns),
        shape(depth, 2, 2, rows, near_width),
        shape(reach + 1, count, width),
        shape(count, heads_width), shape(span, heads_width), shape(span, heads_width),
        shape(-(-heads_width // HEAD // 8) * 8, count, dtype=f32),
        shape(count, heads_width),
        shape(span, LANES, dtype=f32), shape(span, LANES, dtype=f32), shape(span, count, dtype=f32),
        shape(8, width, dtype=f32),
        shape(count, width, dtype=f32), shape(count, width),
        shape(count, LANES, dtype=f32), shape(count, LANES, dtype=f32),
        shape(routes.shape[1], count, experts * capacity),
        shape(experts, capacity, width), shape(experts, capacity, width),
    )
    inputs = list(arrays) + [tokens, cotangent, routes, segment_rows, tables[0], tables[1], tables[2], tables[3]]
    return pl.pallas_call(
        functools.partial(forward_kernel, depth, reach, experts, tuple(chunks), near_edges),
        out_shape=outs,
        in_specs=[IN_VMEM] * len(inputs),
        out_specs=(IN_HBM,) + (IN_VMEM,) * (len(outs) - 1),
        scratch_shapes=[
            pltpu.VMEM((rows, columns), bf16),
            pltpu.VMEM((count, width), bf16),
            pltpu.VMEM((count, width), bf16),
            dma(parts, depth - 1), dma(parts, depth - 1), dma(parts, 4), dma(parts, 4),
            dma(reach), dma(reach), dma(reach), dma(reach), dma(1), dma(1), dma(3),
        ],
        compiler_params=comm_params(1, 58 << 20),
        name="gather_and_attend",
    )(*inputs)


def local(
    tokens, cotangent, attn_gain, w_query, w_key, w_value, w_out, ffn_gain, w_router,
    w_sgate, w_sup, w_sdown, e_gate, e_up, e_down, routes, segments,
):
    tok_count, width = tokens.shape
    n = lax.axis_size("dp")
    depth = n // PLANE
    me = lax.axis_index("dp")
    core = lax.axis_index("tensor")
    experts = w_router.shape[1]
    owners = n // experts
    capacity = tok_count // 4
    reach = (WINDOW + tok_count - 1) // tok_count
    shard_rows = w_query.shape[0]
    heads_width = w_query.shape[1]
    hidden = w_sgate.shape[1]
    half = width // 2

    small = jnp.pad(
        jnp.concatenate([w_router, attn_gain[:, None], ffn_gain[:, None]], axis=1),
        ((0, 0), (0, LANES - experts - 2)),
    )
    near_width = LANES + 4 * heads_width
    columns = near_width + 3 * hidden + LANES
    (
        full, near, window, queries, all_keys, all_values, lse, heads_out, cosines, sines, bias, gains,
        middle, branch_in, probs, gates, pick, rows_out, d_rows_out,
    ) = forward(
        (small, w_query, w_key, w_value, w_out.T, w_sgate, w_sup, w_sdown.T),
        tokens, cotangent, routes, segments, depth, reach, experts, heads_width, hidden,
    )
    sgate_w, sup_w, sdown_t = (
        full[:, :, :, :, near_width + i * hidden : near_width + (i + 1) * hidden].reshape(width, hidden)
        for i in range(3)
    )
    router_w = near[:, :, :, :, :experts].reshape(width, experts)
    gain_first, gain_second = gains[0], gains[1]
    expert_gate = e_gate.astype(bf16)
    expert_up = e_up.astype(bf16)
    expert_down = e_down.astype(bf16)
    x_float = tokens.astype(f32)
    normed_one, scale_one = rms_parts(x_float)
    normed_two, scale_two = rms_parts(middle)
    probs = probs[:, :experts]
    picked = (routes[:, :, None] == jnp.arange(experts, dtype=jnp.int32)[None, None, :]).astype(f32)
    d_after = cotangent.astype(f32)
    rows_in, d_rows_in = dispatch(rows_out, d_rows_out, n, owners)

    rows_in = rows_in.reshape(n * capacity, width)
    d_rows_in = d_rows_in.reshape(n * capacity, width)
    gate_hidden = matmul(rows_in, expert_gate)
    up_hidden = matmul(rows_in, expert_up)
    gate_act = jax.nn.silu(gate_hidden)
    expert_hidden = (gate_act * up_hidden).astype(bf16)
    part_rows = matmul(expert_hidden, expert_down).astype(bf16)
    d_hidden = input_grad(d_rows_in, expert_down)
    d_gate_hidden = (d_hidden * up_hidden * silu_grad(gate_hidden)).astype(bf16)
    d_up_hidden = (d_hidden * gate_act).astype(bf16)
    d_part_rows = (
        input_grad(d_gate_hidden, expert_gate) + input_grad(d_up_hidden, expert_up)
    ).astype(bf16)
    returned, d_returned = give_back(
        part_rows.reshape(n, capacity, width), d_part_rows.reshape(n, capacity, width)
    )
    grad_e_down = weight_grad(expert_hidden, d_rows_in)
    grad_e_gate = weight_grad(rows_in, d_gate_hidden)
    grad_e_up = weight_grad(rows_in, d_up_hidden)

    shared_gate = matmul(branch_in, sgate_w)
    shared_up = matmul(branch_in, sup_w)
    shared_act = jax.nn.silu(shared_gate)
    shared_hidden = (shared_act * shared_up).astype(bf16)
    shared_part = input_grad(shared_hidden, sdown_t)
    d_shared = matmul(cotangent, sdown_t)
    grad_sdown_t = weight_grad(cotangent, shared_hidden)
    d_sgate = (d_shared * shared_up * silu_grad(shared_gate)).astype(bf16)
    d_sup = (d_shared * shared_act).astype(bf16)
    grad_sgate = weight_grad(branch_in, d_sgate)
    grad_sup = weight_grad(branch_in, d_sup)
    d_shared_in = input_grad(d_sgate, sgate_w) + input_grad(d_sup, sup_w)

    def incoming(rows):
        rows = rows.reshape(experts, owners, capacity, half)
        if owners > 1:
            rows = jnp.sum(rows.astype(f32), axis=1).astype(bf16)
        return rows.reshape(experts * capacity, half)

    def placed(values):
        own = jnp.concatenate([values, jnp.zeros_like(values)], axis=1)
        other = jnp.concatenate([jnp.zeros_like(values), values], axis=1)
        return jnp.where(core == 0, own, other)

    result_rows, d_result_rows = incoming(returned), incoming(d_returned)
    pair_out = [matmul(pick[k], result_rows) for k in range(pick.shape[0])]
    d_pairs = matmul(pick[0] + pick[1], d_result_rows)
    moe_half = sum(gates[:, k : k + 1] * pair_out[k] for k in range(pick.shape[0]))
    d_half = lax.dynamic_slice_in_dim(cotangent, core * half, half, axis=1).astype(f32)
    d_gates_part = jnp.concatenate(
        [jnp.sum(d_half * p, axis=1, keepdims=True) for p in pair_out], axis=1
    )
    after_part = (placed(moe_half) + shared_part).astype(bf16)
    d_branch_part = (d_shared_in + placed(d_pairs)).astype(bf16)
    d_gates_part = jnp.pad(d_gates_part, ((0, 0), (0, LANES - pick.shape[0])))
    after_other, d_branch_other, d_gates_other = swap(
        [after_part, d_branch_part, d_gates_part], 6
    )
    output = (middle + (after_part.astype(f32) + after_other.astype(f32))).astype(bf16)
    d_branch_sum = d_branch_part.astype(f32) + d_branch_other.astype(f32)
    d_gates = (d_gates_part + d_gates_other)[:, : pick.shape[0]]
    d_probs = jnp.sum(d_gates[:, :, None] * picked, axis=1)
    d_logits = (probs * (d_probs - jnp.sum(probs * d_probs, axis=-1, keepdims=True))).astype(bf16)
    grad_router = weight_grad(branch_in, d_logits)
    d_branch_in = d_branch_sum + input_grad(d_logits, router_w)
    grad_gain_two = jnp.sum(d_branch_in * normed_two, axis=0)
    d_norm_two = d_branch_in * gain_second
    d_middle = d_after + scale_two * (
        d_norm_two - normed_two * jnp.mean(d_norm_two * normed_two, axis=-1, keepdims=True)
    )

    blocks = (depth, 2, 2, shard_rows)
    grad_small = jnp.concatenate(
        [grad_router, grad_gain_two[:, None], jnp.zeros((width, LANES - experts - 1), f32)], axis=1
    ).astype(bf16)
    total, d_attn_in = backward(
        [
            grad_sgate.astype(bf16).reshape(blocks + (hidden,)),
            grad_sup.astype(bf16).reshape(blocks + (hidden,)),
            grad_sdown_t.astype(bf16).reshape(blocks + (hidden,)),
            grad_small.reshape(blocks + (LANES,)),
            window, queries, all_keys, all_values, lse, heads_out,
            d_middle.astype(bf16), near, gains, cosines, sines, bias,
        ],
        shard_rows, columns, 3 * hidden, tok_count, heads_width, width, depth, reach,
    )
    def columns_of(at, count):
        return total[:, at : at + count]

    at_out = 3 * hidden
    at_pairs = at_out + heads_width + LANES
    grad_parts = [
        jnp.concatenate(
            [
                columns_of(at_pairs + (3 * pair + i) * LANES, LANES)
                for pair in range(heads_width // LANES)
            ],
            axis=1,
        )
        for i in range(3)
    ]
    d_attn_in = d_attn_in.astype(f32)
    d_norm_one = d_attn_in * gain_first
    token_input_gradient = d_middle + scale_one * (
        d_norm_one - normed_one * jnp.mean(d_norm_one * normed_one, axis=-1, keepdims=True)
    )
    return (
        output,
        token_input_gradient,
        total[:, columns - LANES],
        grad_parts[0],
        grad_parts[1],
        grad_parts[2],
        columns_of(at_out, heads_width).T,
        total[:, at_out + heads_width + experts],
        columns_of(at_out + heads_width, experts),
        columns_of(0, hidden),
        columns_of(hidden, hidden),
        columns_of(2 * hidden, hidden).T,
        grad_e_gate,
        grad_e_up,
        grad_e_down,
    )


def solution(mesh):
    by_dp, both, turned = P("dp", None), P("dp", "tensor"), P("tensor", "dp")
    wide, tall = P(None, ("dp", "tensor")), P(("dp", "tensor"), None)
    weights = (P("dp"), both, both, both, turned, P("dp"), by_dp, both, both, turned, wide, wide, tall)
    return jax.shard_map(
        local,
        mesh=mesh,
        in_specs=(by_dp, by_dp) + weights + (by_dp, P()),
        out_specs=(by_dp, by_dp) + weights,
        check_vma=False,
    )
```

```python
import functools

import jax
import jax.numpy as jnp
import numpy as np
from jax import lax
from jax.experimental import pallas as pl
from jax.experimental.pallas import tpu as pltpu
from jax.sharding import PartitionSpec as P

HEAD = 64
WINDOW = 1024
LANES = 128
PLANE = 4

MESH = pl.DeviceIdType.MESH
f32 = jnp.float32
bf16 = jnp.bfloat16

eps = 1e-06
masked = -1e30


def matmul(left, right):
    return jnp.dot(left, right, preferred_element_type=f32)


def weight_grad(left, right):
    return lax.dot_general(
        left, right, (((0,), (0,)), ((), ())), preferred_element_type=f32
    )


def input_grad(left, right):
    return lax.dot_general(
        left, right, (((1,), (1,)), ((), ())), preferred_element_type=f32
    )


def rms_parts(values):
    factor = lax.rsqrt(jnp.mean(values * values, axis=-1, keepdims=True) + eps)
    return (values * factor, factor)


def silu_grad(values):
    sigma = jax.nn.sigmoid(values)
    return sigma * (1.0 + values * (1.0 - sigma))


def digits(me):
    return lax.div(me, PLANE), lax.rem(lax.div(me, 2), 2), lax.rem(me, 2)


def index_of(z, y, x):
    return z * PLANE + y * 2 + x


def push(src, dst, send, recv, device):
    copy = pltpu.make_async_remote_copy(
        src_ref=src,
        dst_ref=dst,
        send_sem=send,
        recv_sem=recv,
        device_id=device,
        device_id_type=MESH,
    )
    copy.start()
    return copy


def greet(devices):
    barrier = pltpu.get_barrier_semaphore()
    for device in devices:
        pl.semaphore_signal(barrier, inc=1, device_id=device, device_id_type=MESH)
    pl.semaphore_wait(barrier, len(devices))


def comm_params(collective_id, limit=48 << 20):
    return pltpu.CompilerParams(
        collective_id=collective_id, has_side_effects=True, vmem_limit_bytes=limit
    )


def dma(*shape):
    return pltpu.SemaphoreType.DMA(shape)


IN_HBM = pl.BlockSpec(memory_space=pl.ANY)
IN_VMEM = pl.BlockSpec(memory_space=pltpu.VMEM)


def grid_peers(depth, z, y, x):
    peers = [{"dp": index_of(lax.rem(z + k, depth), y, x)} for k in range(1, depth)]
    return peers, {"dp": index_of(z, 1 - y, x)}, {"dp": index_of(z, y, 1 - x)}


def swap_kernel(count, *refs):
    sources, targets, (send, recv) = refs[:count], refs[count : 2 * count], refs[2 * count :]
    sibling = {"tensor": 1 - lax.axis_index("tensor")}
    greet([sibling])
    copies = [
        push(a, b, send.at[i], recv.at[i], sibling)
        for i, (a, b) in enumerate(zip(sources, targets))
    ]
    for copy in copies:
        copy.wait()


def swap(arrays, collective_id):
    count = len(arrays)
    return pl.pallas_call(
        functools.partial(swap_kernel, count),
        out_shape=tuple(jax.ShapeDtypeStruct(a.shape, a.dtype) for a in arrays),
        in_specs=[IN_VMEM] * count,
        out_specs=(IN_VMEM,) * count,
        scratch_shapes=[dma(count), dma(count)],
        compiler_params=comm_params(collective_id),
        name="swap_cores",
    )(*arrays)


def dispatch_kernel(n, owners, first, second, got_first, got_second, send, recv, f_send, f_recv, own):
    me, core = lax.axis_index("dp"), lax.axis_index("tensor")
    sibling = {"tensor": 1 - core}
    greet([{"dp": lax.rem(me + k, n)} for k in range(1, n)] + [sibling])
    half = first.shape[-1] // 2
    cols = pl.ds(pl.multiple_of(core * half, half), half)
    pairs = ((first, got_first), (second, got_second))
    mine = lax.div(me, owners)
    copies = []
    for k in range(1, n):
        to = lax.rem(me + k, n)
        for i, (source, target) in enumerate(pairs):
            copies.append(
                push(
                    source.at[lax.div(to, owners), :, cols],
                    target.at[me, :, cols],
                    send.at[i, k],
                    recv.at[i, k],
                    {"dp": to},
                )
            )
    local = [
        pltpu.make_async_copy(source.at[mine], target.at[me], own.at[i])
        for i, (source, target) in enumerate(pairs)
    ]
    for copy in local:
        copy.start()
    forwards = []
    for k in range(1, n):
        source_of = lax.rem(me + n - k, n)
        for i, (source, target) in enumerate(pairs):
            copies[2 * (k - 1) + i].wait_recv()
            block = target.at[source_of, :, cols]
            forwards.append(push(block, block, f_send.at[i, k], f_recv.at[i, k], sibling))
    for copy in forwards:
        copy.wait_recv()
    for copy in local:
        copy.wait()
    for copy in copies + forwards:
        copy.wait_send()


def dispatch(first, second, n, owners):
    shape = jax.ShapeDtypeStruct((n,) + first.shape[1:], first.dtype)
    return pl.pallas_call(
        functools.partial(dispatch_kernel, n, owners),
        out_shape=(shape, shape),
        in_specs=[IN_HBM] * 2,
        out_specs=(IN_HBM, IN_HBM),
        scratch_shapes=[dma(2, n), dma(2, n), dma(2, n), dma(2, n), dma(2)],
        compiler_params=comm_params(2),
        name="dispatch_rows",
    )(first, second)


def return_kernel(n, groups, first, second, got_first, got_second, part, total, send, recv, f_send, f_recv, own):
    me, core = lax.axis_index("dp"), lax.axis_index("tensor")
    sibling = {"tensor": 1 - core}
    greet([{"dp": lax.rem(me + k, n)} for k in range(1, n)] + [sibling])
    half = first.shape[-1] // 2
    mine = pl.ds(pl.multiple_of(core * half, half), half)
    theirs = pl.ds(pl.multiple_of((1 - core) * half, half), half)
    pairs = ((first, got_first), (second, got_second))
    each = n // groups
    swaps = []
    for g in range(groups):
        block = pl.ds(g * each, each)
        for i, (source, target) in enumerate(pairs):
            swaps.append(
                push(
                    source.at[block, :, theirs],
                    part.at[i, block],
                    f_send.at[i, g],
                    f_recv.at[i, g],
                    sibling,
                )
            )
    for g in range(groups):
        block = pl.ds(g * each, each)
        for i, (source, target) in enumerate(pairs):
            swaps[2 * g + i].wait_recv()
            total[i, block] = (
                source[block, :, mine].astype(f32) + part[i, block].astype(f32)
            ).astype(bf16)
        for slot in range(g * each, (g + 1) * each):
            for i, (source, target) in enumerate(pairs):
                @pl.when(slot != me)
                def _():
                    push(
                        total.at[i, slot],
                        target.at[me],
                        send.at[i, slot],
                        recv.at[i, me],
                        {"dp": slot},
                    )
    local = [
        pltpu.make_async_copy(total.at[i, me], pairs[i][1].at[me], own.at[i]) for i in range(2)
    ]
    for copy in local:
        copy.start()
    for k in range(1, n):
        to, source_of = lax.rem(me + k, n), lax.rem(me + n - k, n)
        for i, (source, target) in enumerate(pairs):
            pltpu.make_async_remote_copy(
                total.at[i, to], target.at[source_of], send.at[i, to], recv.at[i, source_of],
                device_id={"dp": to}, device_id_type=MESH,
            ).wait()
    for copy in local:
        copy.wait()
    for copy in swaps:
        copy.wait_send()


def give_back(first, second, groups=4):
    n, capacity, width = first.shape
    half = jax.ShapeDtypeStruct((n, capacity, width // 2), first.dtype)
    buffer = pltpu.VMEM((2, n, capacity, width // 2), first.dtype)
    return pl.pallas_call(
        functools.partial(return_kernel, n, groups),
        out_shape=(half, half),
        in_specs=[IN_VMEM] * 2,
        out_specs=(IN_HBM, IN_HBM),
        scratch_shapes=[buffer, buffer, dma(2, n), dma(2, n), dma(2, groups), dma(2, groups), dma(2)],
        compiler_params=comm_params(3),
        name="return_rows",
    )(first, second)


def experts_kernel(
    n, groups, rows_out, d_rows_out, e_gate, e_up, e_down, full, branch_in, cotangent, middle, probs, gates, pick,
    routes, gains, small,
    output, d_middle, g_gate, g_up, g_down, g_small, ge_gate, ge_up, ge_down,
    got, gate_w, up_w, down_w, staged, shared_w, hid, d_gate, d_up, part, swapped, total, returned,
    shared_part, shared_in, tiles, wide, ends, ends_other, d_gates, d_gates_other,
    send, recv, f_send, f_recv, s_send, s_recv, r_send, r_recv, e_send, e_recv, own, load, store,
):
    me, core = lax.axis_index("dp"), lax.axis_index("tensor")
    sibling = {"tensor": 1 - core}
    greet([{"dp": lax.rem(me + i, n)} for i in range(1, n)] + [sibling])
    capacity, width = rows_out.shape[1:]
    count = branch_in.shape[0]
    half = width // 2
    mine = pl.ds(pl.multiple_of(core * half, half), half)
    theirs = pl.ds(pl.multiple_of((1 - core) * half, half), half)
    sources = (rows_out, d_rows_out)

    sent = {}
    for i in range(1, n):
        to = lax.rem(me + i, n)
        for a in range(2):
            sent[a, i] = push(
                sources[a].at[to, :, mine], got.at[a, i, :, mine],
                send.at[a, i], recv.at[a, i], {"dp": to},
            )
    local = [pltpu.make_async_copy(sources[a].at[me], got.at[a, 0], own.at[a]) for a in range(2)]
    hidden = shared_w.shape[4] // 3
    loads = [
        pltpu.make_async_copy(
            full.at[:, :, :, :, pl.ds(full.shape[4] - 3 * hidden, 3 * hidden)], shared_w, load.at[2]
        )
    ]
    for copy in local + loads:
        copy.start()

    pieces = []
    for source, target in ((e_gate, gate_w), (e_up, up_w), (e_down, down_w)):
        step = source.shape[0] // 4
        pieces += [(source, target, pl.ds(j * step, step)) for j in range(4)]

    def fetch(j):
        source, target, rows = pieces[j]
        return pltpu.make_async_copy(
            source.at[rows],
            staged.at[j % 2, pl.ds(0, rows.size), pl.ds(0, source.shape[1])],
            load.at[j % 2],
        )

    fetch(0).start()
    fetch(1).start()

    def take(j):
        source, target, rows = pieces[j]
        fetch(j).wait()
        target[rows, :] = staged[j % 2, : rows.size, : source.shape[1]].astype(bf16)
        if j + 2 < len(pieces):
            fetch(j + 2).start()

    forwards = {}

    def arrive(group):
        for i in range(group * n // groups, (group + 1) * n // groups):
            if i == 0:
                for copy in local:
                    copy.wait()
                continue
            for a in range(2):
                sent[a, i].wait_recv()
                block = got.at[a, i, :, mine]
                forwards[a, i] = push(block, block, f_send.at[a, i], f_recv.at[a, i], sibling)

    swaps = {}

    def work(group):
        first, each = group * n // groups, n // groups
        for i in range(max(first, 1), first + each):
            for a in range(2):
                forwards[a, i].wait_recv()
        slots = pl.ds(first, each)
        rows = pl.ds(first * capacity, each * capacity)
        rows_in = got[0, slots].reshape(each * capacity, width)
        d_rows = got[1, slots].reshape(each * capacity, width)
        gate, up = matmul(rows_in, gate_w[...]), matmul(rows_in, up_w[...])
        sigma = 1.0 / (1.0 + jnp.exp(-gate))
        act = gate * sigma
        hid_low = (act * up).astype(bf16)
        hid[rows, :] = hid_low
        part[0, slots] = matmul(hid_low, down_w[...]).astype(bf16).reshape(each, capacity, width)
        d_hid = input_grad(d_rows, down_w[...])
        d_gate_low = (d_hid * up * (sigma * (1.0 + gate * (1.0 - sigma)))).astype(bf16)
        d_up_low = (d_hid * act).astype(bf16)
        d_gate[rows, :] = d_gate_low
        d_up[rows, :] = d_up_low
        part[1, slots] = (
            (input_grad(d_gate_low, gate_w[...]) + input_grad(d_up_low, up_w[...]))
            .astype(bf16)
            .reshape(each, capacity, width)
        )
        for a in (1, 0):
            swaps[a, group] = push(
                part.at[a, slots, :, theirs], swapped.at[a, slots],
                s_send.at[a, group], s_recv.at[a, group], sibling,
            )

    back = {}

    def give(group):
        first, each = group * n // groups, n // groups
        slots = pl.ds(first, each)
        for a in (1, 0):
            swaps[a, group].wait_recv()
            total[a, slots] = (
                part[a, slots, :, mine].astype(f32) + swapped[a, slots].astype(f32)
            ).astype(bf16)
            for i in range(max(first, 1), first + each):
                back[a, i] = push(
                    total.at[a, i], returned.at[a, me],
                    r_send.at[a, i], r_recv.at[a, i], {"dp": lax.rem(me + n - i, n)},
                )

    loads[0].wait()
    branch, cot = branch_in[...], cotangent[...]
    sgate_w, sup_w, sdown_w = (stacked(shared_w, pl.ds(i * hidden, hidden)) for i in range(3))
    gate, up = matmul(branch, sgate_w), matmul(branch, sup_w)
    sigma = 1.0 / (1.0 + jnp.exp(-gate))
    act = gate * sigma
    shared_hid = (act * up).astype(bf16)
    shared_part[...] = input_grad(shared_hid, sdown_w)
    d_shared = matmul(cot, sdown_w)
    d_sgate = (d_shared * up * (sigma * (1.0 + gate * (1.0 - sigma)))).astype(bf16)
    d_sup = (d_shared * act).astype(bf16)
    shared_in[...] = input_grad(d_sgate, sgate_w) + input_grad(d_sup, sup_w)
    for j in range(6):
        take(j)
    arrive(0)
    for j in range(6, 12):
        take(j)
    arrive(1)
    work(0)
    put_rows(g_gate, weight_grad(branch, d_sgate).astype(bf16), pl.ds(0, hidden))
    arrive(2)
    work(1)
    give(0)
    put_rows(g_up, weight_grad(branch, d_sup).astype(bf16), pl.ds(0, hidden))
    arrive(3)
    work(2)
    give(1)
    work(3)
    give(2)
    put_rows(g_down, weight_grad(cot, shared_hid).astype(bf16), pl.ds(0, hidden))
    give(3)
    keep = [
        pltpu.make_async_copy(total.at[a, 0], returned.at[a, me], own.at[2 + a]) for a in range(2)
    ]
    for copy in keep:
        copy.start()

    stores = []

    def emit(value, tile, target):
        slot = len(stores) % 2
        if len(stores) >= 2:
            stores[-2].wait()
        tile[slot] = value
        stores.append(pltpu.make_async_copy(tile.at[slot], target, store.at[slot]))
        stores[-1].start()

    rows_all = got[0].reshape(n * capacity, width)
    units = hid.shape[1]
    span = min(units, 256)
    for source, target in ((d_gate, ge_gate), (d_up, ge_up)):
        for at in range(0, units, span):
            columns = pl.ds(at, span)
            emit(weight_grad(rows_all, source[:, columns]), tiles, target.at[:, columns])
    d_rows_all = got[1].reshape(n * capacity, width)
    for at in range(0, units, span):
        columns = pl.ds(at, span)
        emit(weight_grad(hid[:, columns], d_rows_all), wide, ge_down.at[columns, :])

    for copy in keep:
        copy.wait()
    for a in range(2):
        for i in range(1, n):
            back[a, i].wait_recv()
    lane = lax.broadcasted_iota(jnp.int32, (1, LANES), 1)
    rows_back = returned[0].reshape(n * capacity, half)
    d_rows_back = returned[1].reshape(n * capacity, half)
    cot_half = cotangent[:, mine].astype(f32)
    d_pairs = matmul(pick[0] + pick[1], d_rows_back)
    d_gate_lanes = jnp.zeros((count, LANES), f32)
    moe = jnp.zeros((count, half), f32)
    for i in range(2):
        pair = matmul(pick[i], rows_back)
        moe = moe + gates[:, i : i + 1] * pair
        inner = jnp.sum(cot_half * pair, axis=-1, keepdims=True)
        d_gate_lanes = d_gate_lanes + jnp.where(lane == i, inner, 0.0)
    d_gates[...] = d_gate_lanes
    shared_part[:, mine] = shared_part[:, mine] + moe
    shared_in[:, mine] = shared_in[:, mine] + d_pairs
    ends[0] = shared_part[...].astype(bf16)
    ends[1] = shared_in[...].astype(bf16)
    last = [
        push(ends, ends_other, e_send.at[0], e_recv.at[0], sibling),
        push(d_gates, d_gates_other, e_send.at[1], e_recv.at[1], sibling),
    ]
    for copy in last:
        copy.wait()

    middle_all = middle[...]
    output[...] = (
        middle_all + (ends[0].astype(f32) + ends_other[0].astype(f32))
    ).astype(bf16)
    d_gates_all = d_gates[...] + d_gates_other[...]
    d_probs = jnp.zeros((count, LANES), f32)
    for i in range(2):
        d_probs = d_probs + jnp.where(routes[:, i : i + 1] == lane, d_gates_all[:, i : i + 1], 0.0)
    chance = probs[...]
    d_logits = (
        chance * (d_probs - jnp.sum(chance * d_probs, axis=-1, keepdims=True))
    ).astype(bf16)
    small_all = stacked(small, pl.ds(0, LANES))
    d_branch = (
        ends[1].astype(f32) + ends_other[1].astype(f32) + input_grad(d_logits, small_all)
    )
    factor = lax.rsqrt(jnp.mean(middle_all * middle_all, axis=-1, keepdims=True) + eps)
    normed = middle_all * factor
    gain_row = jnp.sum(d_branch * normed, axis=0, keepdims=True)
    d_norm = d_branch * gains[1:2, :]
    d_middle[...] = cotangent[...].astype(f32) + factor * (
        d_norm - normed * jnp.mean(d_norm * normed, axis=-1, keepdims=True)
    )
    put_rows(
        g_small,
        jnp.where(
            lane == n, jnp.broadcast_to(gain_row, (LANES, width)).T, weight_grad(branch, d_logits)
        ).astype(bf16),
        pl.ds(0, LANES),
    )
    for copy in stores[-2:]:
        copy.wait()
    for copies in (sent, forwards, swaps, back):
        for copy in copies.values():
            copy.wait_send()


def experts_fused(
    rows_out, d_rows_out, weights, full, branch_in, cotangent, middle, probs, gates, pick, routes, gains, near,
    depth, hidden, groups=4,
):
    n, capacity, width = rows_out.shape
    count = branch_in.shape[0]
    units = weights[0].shape[1]
    rows = near.shape[3]
    span = min(units, 256)
    half = width // 2

    def shape(*dims, dtype=bf16):
        return jax.ShapeDtypeStruct(dims, dtype)

    shared = shape(depth, 2, 2, rows, hidden)
    slots = pltpu.VMEM((2, n, capacity, half), bf16)
    return pl.pallas_call(
        functools.partial(experts_kernel, n, groups),
        out_shape=(
            shape(count, width), shape(count, width, dtype=f32), shared, shared, shared,
            shape(depth, 2, 2, rows, LANES),
            shape(width, units, dtype=f32), shape(width, units, dtype=f32), shape(units, width, dtype=f32),
        ),
        in_specs=[IN_HBM] * 6 + [IN_VMEM] * 9,
        out_specs=(IN_VMEM,) * 6 + (IN_HBM,) * 3,
        scratch_shapes=[
            pltpu.VMEM((2, n, capacity, width), bf16),
            pltpu.VMEM((width, units), bf16), pltpu.VMEM((width, units), bf16), pltpu.VMEM((units, width), bf16),
            pltpu.VMEM((2, max(width, units) // 4, max(width, units)), f32),
            pltpu.VMEM((depth, 2, 2, rows, 3 * hidden), bf16),
            pltpu.VMEM((n * capacity, units), bf16),
            pltpu.VMEM((n * capacity, units), bf16),
            pltpu.VMEM((n * capacity, units), bf16),
            pltpu.VMEM((2, n, capacity, width), bf16),
            slots, slots, slots,
            pltpu.VMEM((count, width), f32), pltpu.VMEM((count, width), f32),
            pltpu.VMEM((2, width, span), f32), pltpu.VMEM((2, span, width), f32),
            pltpu.VMEM((2, count, width), bf16), pltpu.VMEM((2, count, width), bf16),
            pltpu.VMEM((count, LANES), f32), pltpu.VMEM((count, LANES), f32),
            dma(2, n), dma(2, n), dma(2, n), dma(2, n), dma(2, groups), dma(2, groups),
            dma(2, n), dma(2, n), dma(2), dma(2), dma(4), dma(3), dma(2),
        ],
        compiler_params=comm_params(7, 62 << 20),
        name="experts_and_shared",
    )(
        rows_out, d_rows_out, *weights, full, branch_in, cotangent, middle, probs, gates, pick, routes, gains,
        near[:, :, :, :, :LANES],
    )


class Scatter:
    def __init__(self, depth, chunks, total, buffers, semaphores):
        self.depth, self.chunks, self.total = depth, chunks, total
        self.first_l, self.first_r, self.second_l, self.second_r, self.last = buffers
        self.p_send, self.p_recv, self.z_send, self.z_recv = semaphores
        self.z, self.y, self.x = digits(lax.axis_index("dp"))
        self.z_peers, self.y_peer, self.x_peer = grid_peers(depth, self.z, self.y, self.x)
        self.at_l, self.at_r, l, r = [], [], 0, 0
        for left, lc, lw, right, rc, rw, out in chunks:
            self.at_l.append(pl.ds(l, lw))
            self.at_r.append(pl.ds(r, rw))
            l, r = l + lw, r + rw
        self.ones, self.twos, self.threes = {}, {}, {}

    def start(self, c):
        left, lc, lw, right, rc, rw, out = self.chunks[c]
        self.ones[c] = [
            push(
                left.at[:, :, 1 - self.x, :, pl.ds(lc, lw)],
                self.first_l.at[:, :, :, self.at_l[c]],
                self.p_send.at[c, 0], self.p_recv.at[c, 0], self.x_peer,
            ),
            push(
                right.at[:, 1 - self.y, :, :, pl.ds(rc, rw)],
                self.first_r.at[:, :, :, self.at_r[c]],
                self.p_send.at[c, 1], self.p_recv.at[c, 1], self.y_peer,
            ),
        ]

    def second(self, c):
        left, lc, lw, right, rc, rw, out = self.chunks[c]
        in_l, in_r, first_l, first_r = self.at_l[c], self.at_r[c], self.first_l, self.first_r
        for copy in self.ones[c]:
            copy.wait_recv()

        def add(i, carry):
            for j in range(2):
                first_l[i, j, :, in_l] = (
                    first_l[i, j, :, in_l].astype(f32) + left[i, j, self.x, :, pl.ds(lc, lw)].astype(f32)
                ).astype(bf16)
                first_r[i, j, :, in_r] = (
                    first_r[i, j, :, in_r].astype(f32) + right[i, self.y, j, :, pl.ds(rc, rw)].astype(f32)
                ).astype(bf16)
            return carry

        lax.fori_loop(0, self.depth, add, 0)
        self.twos[c] = [
            push(
                first_l.at[:, 1 - self.y, :, in_l], self.second_l.at[:, :, in_l],
                self.p_send.at[c, 2], self.p_recv.at[c, 2], self.y_peer,
            ),
            push(
                first_r.at[:, 1 - self.x, :, in_r], self.second_r.at[:, :, in_r],
                self.p_send.at[c, 3], self.p_recv.at[c, 3], self.x_peer,
            ),
        ]

    def third(self, c):
        for copy in self.twos[c]:
            copy.wait_recv()
        sides = (
            (self.second_l, self.first_l, self.y, self.at_l[c]),
            (self.second_r, self.first_r, self.x, self.at_r[c]),
        )

        def add(i, carry):
            for source, before, place, here in sides:
                source[i, :, here] = (
                    source[i, :, here].astype(f32) + before[i, place, :, here].astype(f32)
                ).astype(bf16)
            return carry

        lax.fori_loop(0, self.depth, add, 0)
        self.threes[c] = [
            push(
                source.at[lax.rem(self.z + k + 1, self.depth), :, here],
                self.last.at[k, side, :, here],
                self.z_send.at[c, side, k], self.z_recv.at[c, side, k], self.z_peers[k],
            )
            for side, (source, before, place, here) in enumerate(sides)
            for k in range(self.depth - 1)
        ]

    def finish(self, c):
        left, lc, lw, right, rc, rw, out = self.chunks[c]
        for copy in self.threes[c]:
            copy.wait_recv()
        for side, source, here, at, span in (
            (0, self.second_l, self.at_l[c], out, lw),
            (1, self.second_r, self.at_r[c], out + lw, rw),
        ):
            value = source[self.z, :, here].astype(f32)
            for k in range(self.depth - 1):
                value = value + self.last[k, side, :, here].astype(f32)
            self.total[:, pl.ds(at, span)] = value

    def drain(self):
        for copies in list(self.ones.values()) + list(self.twos.values()) + list(self.threes.values()):
            for copy in copies:
                copy.wait_send()


def lanes_of(part):
    lane = lax.broadcasted_iota(jnp.int32, (1, LANES), 1)
    return (lax.div(lane, HEAD) == part).astype(f32).astype(bf16)


def swap_halves(values):
    lane = lax.broadcasted_iota(jnp.int32, (1, LANES), 1)
    low = lax.rem(lane, HEAD) < HEAD // 2
    return jnp.where(
        low, pltpu.roll(values, LANES - HEAD // 2, 1), pltpu.roll(values, HEAD // 2, 1)
    )


def put_rows(target, values, columns):
    rows = target.shape[3]
    for b in range(values.shape[0] // rows):
        target[b // PLANE, (b // 2) % 2, b % 2, :, columns] = values[b * rows : (b + 1) * rows]


def backward_kernel(
    depth, reach, per_core, g_gate, g_up, g_down, g_small, window, q, k, v, lse, heads_out, d_attn,
    near, gains, cosines, sines, bias, total, d_full,
    grads, attn_t, d_heads, dq_all, dk_all, dv_all, d_part, d_swap, d_sum, d_got, gain_got,
    first_l, first_r, second_l, second_r, last,
    p_send, p_recv, z_send, z_recv, t_send, t_recv, s_send, s_recv, f_send, f_recv,
):
    n = depth * PLANE
    me, core = lax.axis_index("dp"), lax.axis_index("tensor")
    sibling = {"tensor": 1 - core}
    plane, z_next, z_before = Plane(me), *z_neighbours(me, n)
    heads_width = q.shape[1]
    count = q.shape[0]
    pairs = heads_width // LANES
    hidden = g_gate.shape[4]
    chunks = []
    out = 0
    step = 2 * LANES
    for source in (g_gate, g_up, g_down):
        for at in range(0, hidden, 2 * step):
            chunks.append((source, at, step, source, at + step, step, out))
            out += 2 * step
    early = len(chunks)
    widths = [(step, step)] + [(step, LANES), (LANES, step)] * pairs
    widths = widths[:pairs] + [(step, step)]
    at = 0
    for left, right in widths:
        chunks.append((grads, at, left, grads, at + left, right, out + at))
        at += left + right
    scatter = Scatter(
        depth, chunks, total, (first_l, first_r, second_l, second_r, last),
        (p_send, p_recv, z_send, z_recv),
    )
    greet(scatter.z_peers + plane.peers + [sibling, z_next, z_before])
    lead = 4
    for c in range(lead):
        scatter.start(c)
    steps = []
    for c in range(len(chunks) + 2):
        if c < len(chunks):
            steps.append((scatter.second, c))
        if 1 <= c <= len(chunks):
            steps.append((scatter.third, c - 1))
        if c >= 2:
            steps.append((scatter.finish, c - 2))
    done = [0]

    def advance(count=1):
        for action, c in steps[done[0] : done[0] + count]:
            if action == scatter.second and c not in scatter.ones:
                break
            done[0] += 1
            action(c)
            if action == scatter.second and c + lead < early:
                scatter.start(c + lead)

    query_w, key_w, value_w, out_w = (
        pl.ds(LANES + i * heads_width, heads_width) for i in range(4)
    )
    gain = gains[0:1, :]
    d_heads[...] = matmul(d_attn[...], stacked(near, out_w)).astype(bf16)
    put_rows(grads, weight_grad(d_attn[...], heads_out[...]).astype(bf16), pl.ds(0, heads_width))
    grads[:, :, :, :, pl.ds(heads_width, LANES)] = g_small[...]

    def normed(block):
        values = window[block].astype(f32)
        return values * lax.rsqrt(jnp.mean(values * values, axis=-1, keepdims=True) + eps)

    def turned(block, carry):
        rows = pl.ds(pl.multiple_of(block * count, count), count)
        attn_t[:, rows] = (normed(block) * gain).T.astype(bf16)
        return carry

    for block in range(reach + 1):
        turned(block, 0)
    scatter.start(early)
    own = pl.ds(reach * count, count)
    for pair in range(pairs):
        columns = pl.ds(pair * LANES, LANES)
        k_pair, v_pair, q_pair, d_pair = k[:, columns], v[:, columns], q[:, columns], d_heads[:, columns]
        k_turned = k_pair.T
        dq, dk, dv = [], None, None
        for part in range(2):
            head = 2 * pair + part
            lanes = lanes_of(part)
            q_head, d_head = q_pair * lanes, d_pair * lanes
            probs = jnp.exp(input_grad(k_pair, q_head) + bias[...] - lse[head : head + 1, :])
            d_probs = input_grad(v_pair, d_head)
            inner = jnp.sum(probs * d_probs, axis=0, keepdims=True)
            d_scores = (probs * (d_probs - inner)).astype(bf16)
            advance()
            dq.append(matmul(k_turned, d_scores)[part * HEAD : (part + 1) * HEAD, :])
            parts = matmul(d_scores, q_head), matmul(probs.astype(bf16), d_head)
            dk, dv = parts if part == 0 else (dk + parts[0], dv + parts[1])
            advance()
        dq = jnp.concatenate(dq, axis=0).T * (HEAD ** (-0.5))
        cos_own, sin_own = cosines[own, :], sines[own, :]
        dq_low = turn(dq, cos_own, -sin_own).astype(bf16)
        dk_low = turn(dk, cosines[...], -sines[...]).astype(bf16)
        dv_low = dv.astype(bf16)
        dq_all[:, columns] = dq_low
        dk_all[:, columns] = dk_low
        dv_all[:, columns] = dv_low
        at = heads_width + LANES + pair * 3 * LANES
        put_rows(grads, matmul(attn_t[:, own], dq_low).astype(bf16), pl.ds(at, LANES))
        put_rows(grads, matmul(attn_t[...], dk_low).astype(bf16), pl.ds(at + LANES, LANES))
        put_rows(grads, matmul(attn_t[...], dv_low).astype(bf16), pl.ds(at + 2 * LANES, LANES))
        if pair < pairs - 1:
            scatter.start(early + 1 + pair)
        advance(2)

    width = d_part.shape[-1] // 2
    mine = pl.ds(pl.multiple_of(core * width, width), width)
    theirs = pl.ds(pl.multiple_of((1 - core) * width, width), width)
    swaps = []
    query_v, key_v, value_v = (stacked(near, at) for at in (query_w, key_w, value_w))
    gain_row = jnp.zeros((1, 2 * width), f32)
    for block in range(reach + 1):
        rows = pl.ds(block * count, count)
        value = input_grad(dk_all[rows, :], key_v) + input_grad(dv_all[rows, :], value_v)
        if block == reach:
            value = value + input_grad(dq_all[...], query_v)
        gain_row = gain_row + jnp.sum(value * normed(block), axis=0, keepdims=True)
        d_part[block] = value.astype(bf16)
        swaps.append(
            push(
                d_part.at[block, :, theirs], d_swap.at[block],
                s_send.at[block], s_recv.at[block], sibling,
            )
        )
        advance()
    put_rows(
        grads,
        jnp.broadcast_to(gain_row, (LANES, 2 * width)).T.astype(bf16),
        pl.ds(heads_width + LANES + pairs * 3 * LANES, LANES),
    )
    final = len(chunks) - 1
    scatter.start(final)
    for block in range(reach + 1):
        swaps[block].wait_recv()
        d_sum[block] = (
            d_part[block, :, mine].astype(f32) + d_swap[block].astype(f32)
        ).astype(bf16)
    back = [
        push(
            d_sum.at[lax.rem(plane.places[j] - plane.place + PLANE, PLANE)],
            d_got.at[j], t_send.at[j], t_recv.at[j], plane.peers[j - 1],
        )
        for j in range(1, PLANE)
    ]
    advance(5)
    d_mine, d_before = d_sum[reach].astype(f32), d_sum[0].astype(f32)
    for j in range(1, PLANE):
        back[j - 1].wait_recv()
        ours = lax.select(plane.places[j] > plane.place, 1.0, 0.0)
        value = d_got[j].astype(f32)
        d_mine, d_before = d_mine + value * ours, d_before + value * (1.0 - ours)
    d_sum[reach] = d_before.astype(bf16)
    back.append(push(d_sum.at[reach], d_got.at[0], t_send.at[0], t_recv.at[0], z_before))
    advance(len(steps))
    back[-1].wait_recv()
    d_mine = d_mine + d_got[0].astype(f32)
    d_full[:, mine] = d_mine.astype(bf16)
    both = push(d_full.at[:, mine], d_full.at[:, mine], f_send.at[0], f_recv.at[0], sibling)
    split = pl.ds(per_core, LANES)
    gain_copy = push(total.at[:, split], gain_got, f_send.at[1], f_recv.at[1], sibling)
    both.wait()
    gain_copy.wait()
    total[:, split] = total[:, split] + gain_got[...]
    scatter.drain()
    for copy in back + swaps:
        copy.wait_send()


def backward(arrays, rows, columns, shared, count, heads_width, width, depth, reach):
    span = (reach + 1) * count
    half = columns // 2
    parts = shared // (4 * LANES) + 2 + heads_width // LANES
    first = pltpu.VMEM((depth, 2, rows, half), bf16)
    second = pltpu.VMEM((depth, rows, half), bf16)
    own = columns - shared
    return pl.pallas_call(
        functools.partial(backward_kernel, depth, reach, columns - LANES),
        out_shape=(
            jax.ShapeDtypeStruct((rows, columns), f32),
            jax.ShapeDtypeStruct((count, width), bf16),
        ),
        in_specs=[IN_VMEM] * len(arrays),
        out_specs=(IN_VMEM, IN_VMEM),
        scratch_shapes=[
            pltpu.VMEM((depth, 2, 2, rows, own), bf16),
            pltpu.VMEM((width, span), bf16),
            pltpu.VMEM((count, heads_width), bf16),
            pltpu.VMEM((count, heads_width), bf16),
            pltpu.VMEM((span, heads_width), bf16),
            pltpu.VMEM((span, heads_width), bf16),
            pltpu.VMEM((reach + 1, count, width), bf16),
            pltpu.VMEM((reach + 1, count, width // 2), bf16),
            pltpu.VMEM((reach + 1, count, width // 2), bf16),
            pltpu.VMEM((reach, count, width // 2), bf16),
            pltpu.VMEM((rows, LANES), f32),
            first, first, second, second,
            pltpu.VMEM((depth - 1, 2, rows, half), bf16),
            dma(parts, 4), dma(parts, 4),
            dma(parts, 2, depth - 1), dma(parts, 2, depth - 1),
            dma(reach), dma(reach), dma(reach + 1), dma(reach + 1), dma(2), dma(2),
        ],
        compiler_params=comm_params(4, 58 << 20),
        name="attention_backward",
    )(*arrays)


class Plane:
    def __init__(self, me):
        z, y, x = digits(me)
        self.place = y * 2 + x
        self.places, self.peers = [self.place], []
        for j in range(1, PLANE):
            y_j, x_j = (1 - y if j & 2 else y), (1 - x if j & 1 else x)
            self.places.append(y_j * 2 + x_j)
            self.peers.append({"dp": index_of(z, y_j, x_j)})


def z_neighbours(me, n):
    return {"dp": lax.rem(me + PLANE, n)}, {"dp": lax.rem(me + n - PLANE, n)}


class Gather:
    def __init__(self, depth, chunks, shard, full, semaphores):
        self.depth, self.chunks, self.shard, self.full = depth, chunks, shard, full
        self.z_send, self.z_recv, self.p_send, self.p_recv = semaphores
        self.z, self.y, self.x = digits(lax.axis_index("dp"))
        self.z_peers, self.y_peer, self.x_peer = grid_peers(depth, self.z, self.y, self.x)
        self.ones, self.twos, self.threes = {}, {}, {}

    def _sides(self, c):
        at, left, right = self.chunks[c]
        return pl.ds(at, left), pl.ds(at + left, right)

    def first(self, c):
        at, left, right = self.chunks[c]
        columns = pl.ds(at, left + right)
        self.ones[c] = [
            push(
                self.shard.at[:, columns],
                self.full.at[self.z, self.y, self.x, :, columns],
                self.z_send.at[c, k], self.z_recv.at[c, k], self.z_peers[k],
            )
            for k in range(self.depth - 1)
        ]

    def second(self, c):
        left, right = self._sides(c)
        for copy in self.ones[c]:
            copy.wait_recv()
        a = self.full.at[:, self.y, self.x, :, left]
        b = self.full.at[:, self.y, self.x, :, right]
        self.twos[c] = [
            push(a, a, self.p_send.at[c, 0], self.p_recv.at[c, 0], self.y_peer),
            push(b, b, self.p_send.at[c, 1], self.p_recv.at[c, 1], self.x_peer),
        ]

    def third(self, c):
        left, right = self._sides(c)
        for copy in self.twos[c]:
            copy.wait_recv()
        a = self.full.at[:, :, self.x, :, left]
        b = self.full.at[:, self.y, :, :, right]
        self.threes[c] = [
            push(a, a, self.p_send.at[c, 2], self.p_recv.at[c, 2], self.x_peer),
            push(b, b, self.p_send.at[c, 3], self.p_recv.at[c, 3], self.y_peer),
        ]

    def finish(self, c):
        for copy in self.threes[c]:
            copy.wait_recv()

    def plan(self, lead):
        count = len(self.chunks)
        steps = []
        for s in range(count + 2):
            if s < count:
                steps.append((self.second, s))
                if s + lead < count:
                    steps.append((self.first, s + lead))
            if 1 <= s <= count:
                steps.append((self.third, s - 1))
            if s >= 2:
                steps.append((self.finish, s - 2))
        return steps

    def drain(self):
        for copies in list(self.ones.values()) + list(self.twos.values()) + list(self.threes.values()):
            for copy in copies:
                copy.wait_send()


def stacked(ref, columns):
    rows = ref.shape[3]
    if rows % 16 == 0:
        return ref[:, :, :, :, columns].reshape(-1, columns.size)
    blocks = [
        ref[b // PLANE, (b // 2) % 2, b % 2, :, columns].astype(f32)
        for b in range(ref.shape[0] * PLANE)
    ]
    return jnp.concatenate(blocks, axis=0).astype(bf16)


def turn(values, cos, sin):
    return values * cos + swap_halves(values) * sin


def forward_kernel(
    depth, reach, experts, chunks, near_edges, small, w_query, w_key, w_value, out_shard, w_sgate, w_sup, down_shard,
    tokens, cotangent, routes, segments, row_cos, row_sin, block_cos, block_sin,
    full, near, window, q, k, v, lse, heads_out, cosines, sines, bias, gains, middle, branch_in, probs, gates, pick,
    rows_out, d_rows_out,
    shard, part, other,
    z_send, z_recv, p_send, p_recv, t_send, t_recv, f_send, f_recv, s_send, s_recv, own,
):
    n = depth * PLANE
    me, core = lax.axis_index("dp"), lax.axis_index("tensor")
    sibling = {"tensor": 1 - core}
    gather = Gather(depth, chunks, shard, full, (z_send, z_recv, p_send, p_recv))
    at = 0
    for piece in (small, w_query, w_key, w_value, out_shard, w_sgate, w_sup, down_shard):
        shard[:, pl.ds(at, piece.shape[1])] = piece[...].astype(bf16)
        at += piece.shape[1]
    plane, z_next, z_before = Plane(me), *z_neighbours(me, n)
    greet(gather.z_peers + plane.peers + [sibling, z_next, z_before])
    count, width = tokens.shape
    half = count // 2
    rows = pl.ds(pl.multiple_of(core * half, half), half)
    from_before = push(tokens.at[rows], window.at[0, rows], t_send.at[0], t_recv.at[0], z_next)
    lead = 3
    for c in range(lead):
        gather.first(c)
    own_shard = pltpu.make_async_copy(shard, full.at[gather.z, gather.y, gather.x], own.at[0])
    own_shard.start()
    window[reach] = tokens[...]

    lane = lax.broadcasted_iota(jnp.int32, (1, LANES), 1)
    sign = jnp.where(lax.rem(lane, HEAD) < HEAD // 2, -1.0, 1.0)
    seg_query = segments[pl.ds(me, 1), :].astype(f32)
    key_place = lax.broadcasted_iota(jnp.int32, (count, count), 0)
    query_place = lax.broadcasted_iota(jnp.int32, (count, count), 1)
    for b in range(reach + 1):
        at = pl.ds(b * count, count)
        c_b, s_b = block_cos[pl.ds(me + b, 1), :], block_sin[pl.ds(me + b, 1), :]
        cosines[at, :] = c_b * row_cos[...] - s_b * row_sin[...]
        sines[at, :] = (s_b * row_cos[...] + c_b * row_sin[...]) * sign
        block = me - reach + b
        seg_key = segments[pl.ds(lax.max(block, 0), 1), :].astype(f32)
        seg_key = jnp.broadcast_to(seg_key, (LANES, count)).T[:, :1]
        distance = (reach - b) * count + query_place - key_place
        limit = lax.select(block >= 0, WINDOW, 0)
        seen = (distance >= 0) & (distance < limit) & (seg_key == seg_query)
        bias[at, :] = jnp.where(seen, 0.0, masked)

    def normed(b):
        values = window[b].astype(f32)
        return values * lax.rsqrt(jnp.mean(values * values, axis=-1, keepdims=True) + eps)

    own_shard.wait()
    steps = gather.plan(lead)
    done = [0]

    def advance(until=None, waits=None):
        while done[0] < len(steps) and waits != 0:
            action, c = steps[done[0]]
            done[0] += 1
            action(c)
            if waits is not None and action != gather.first:
                waits -= 1
            if (action, c) == until:
                break

    from_before.wait_recv()
    t_copies = [from_before]
    for j in range(1, PLANE):
        source = window.at[lax.select(plane.places[j] < plane.place, 0, reach), rows]
        target = window.at[lax.rem(plane.place - plane.places[j] + PLANE, PLANE), rows]
        t_copies.append(push(source, target, t_send.at[j], t_recv.at[j], plane.peers[j - 1]))
    advance((gather.second, 1))
    forwards = []
    for j, copy in enumerate(t_copies):
        if j:
            copy.wait_recv()
        block = window.at[lax.rem(plane.places[j] - plane.place + PLANE, PLANE), rows]
        forwards.append(push(block, block, f_send.at[j], f_recv.at[j], sibling))
    landed = 0
    copies = []
    for i, (edge, c) in enumerate(near_edges):
        copies.append((c, pl.ds(landed, edge - landed), own.at[1 + i]))
        landed = edge

    def land(i):
        c, columns, semaphore = copies[i]
        advance((gather.finish, c))
        copy = pltpu.make_async_copy(
            full.at[:, :, :, :, columns], near.at[:, :, :, :, columns], semaphore
        )
        copy.start()
        copy.wait()

    land(0)
    for copy in forwards:
        copy.wait_recv()
    heads_width = q.shape[1]
    pairs = heads_width // LANES
    small_all = stacked(near, pl.ds(0, LANES))
    small_turned = small_all.astype(f32).T
    gain_first, gain_second = small_turned[experts : experts + 1, :], small_turned[experts + 1 : experts + 2, :]
    gains[...] = small_turned[experts : experts + 8, :]
    query_w = stacked(near, pl.ds(LANES, heads_width))
    key_w = stacked(near, pl.ds(LANES + heads_width, heads_width))
    value_w = stacked(near, pl.ds(LANES + 2 * heads_width, heads_width))
    for b in range(reach + 1):
        at = pl.ds(b * count, count)
        rows_in = (normed(b) * gain_first).astype(bf16)
        keys = matmul(rows_in, key_w)
        v[at, :] = matmul(rows_in, value_w).astype(bf16)
        for pair in range(pairs):
            columns = slice(pair * LANES, (pair + 1) * LANES)
            k[at, columns] = turn(keys[:, columns], cosines[at, :], sines[at, :]).astype(bf16)
        if b % 2:
            advance(waits=1)
        if b == reach:
            queries = matmul(rows_in, query_w)
            for pair in range(pairs):
                columns = slice(pair * LANES, (pair + 1) * LANES)
                q[:, columns] = (
                    turn(queries[:, columns], cosines[at, :], sines[at, :]) * (HEAD ** (-0.5))
                ).astype(bf16)
    lse[...] = jnp.zeros_like(lse)
    for pair in range(pairs):
        columns = pl.ds(pair * LANES, LANES)
        k_pair, v_pair, q_pair = k[:, columns], v[:, columns], q[:, columns]
        v_turned = v_pair.T
        outs = []
        for part_of in range(2):
            head = 2 * pair + part_of
            scores = input_grad(k_pair, q_pair * lanes_of(part_of)) + bias[...]
            peak = jnp.max(scores, axis=0, keepdims=True)
            expo = jnp.exp(scores - peak)
            total = jnp.sum(expo, axis=0, keepdims=True)
            lse[head : head + 1, :] = peak + jnp.log(total)
            weights = (expo * (1.0 / total)).astype(bf16)
            outs.append(matmul(v_turned, weights)[part_of * HEAD : (part_of + 1) * HEAD, :])
            advance(waits=1)
        heads_out[:, columns] = jnp.concatenate(outs, axis=0).T.astype(bf16)
    land(1)
    out_w = stacked(near, pl.ds(LANES + 3 * heads_width, heads_width))
    part[...] = input_grad(heads_out[...], out_w).astype(bf16)
    swapped = push(part, other, s_send.at[0], s_recv.at[0], sibling)
    swapped.wait()
    middle_all = tokens[...].astype(f32) + (part[...].astype(f32) + other[...].astype(f32))
    middle[...] = middle_all
    factor = lax.rsqrt(jnp.mean(middle_all * middle_all, axis=-1, keepdims=True) + eps)
    branch = (middle_all * factor * gain_second).astype(bf16)
    branch_in[...] = branch

    logits = jnp.where(lane < experts, matmul(branch, small_all), masked)
    expo = jnp.exp(logits - jnp.max(logits, axis=-1, keepdims=True))
    chance = expo / jnp.sum(expo, axis=-1, keepdims=True)
    probs[...] = chance
    named = [(routes[:, i : i + 1] == lane).astype(f32) for i in range(routes.shape[1])]
    chosen = sum(named)
    below = (key_place > query_place).astype(f32).astype(bf16)
    before = matmul(below, chosen.astype(bf16))
    capacity = rows_out.shape[1]
    slot_of = lax.broadcasted_iota(jnp.int32, (count, experts * capacity), 1)
    d_gathered = jnp.zeros((experts * capacity, width), f32)
    gate_lanes = jnp.zeros((count, LANES), f32)
    for i, name in enumerate(named):
        place = jnp.sum(name * before, axis=-1, keepdims=True).astype(jnp.int32)
        place = place + routes[:, i : i + 1] * capacity
        choice = (slot_of == place).astype(f32).astype(bf16)
        pick[i] = choice
        gate = jnp.sum(chance * name, axis=-1, keepdims=True)
        gate_lanes = gate_lanes + jnp.where(lane == i, gate, 0.0)
        d_rows = (gate * cotangent[...].astype(f32)).astype(bf16)
        d_gathered = d_gathered + weight_grad(choice, d_rows)
    gates[...] = gate_lanes
    gathered = weight_grad(pick[0] + pick[1], branch)
    rows_out[...] = gathered.astype(bf16).reshape(rows_out.shape)
    d_rows_out[...] = d_gathered.astype(bf16).reshape(rows_out.shape)
    advance()
    gather.drain()
    for copy in t_copies + forwards:
        copy.wait_send()


def angle_tables(tok_count, blocks, reach):
    freqs = (10000.0 ** (-np.arange(HEAD // 2, dtype=np.float32) * np.float32(2.0 / HEAD))).astype(np.float64)
    freqs = np.tile(freqs, LANES // (HEAD // 2))[None, :]
    inner = np.arange(tok_count)[:, None] * freqs
    starts = np.maximum(np.arange(-reach, blocks), 0) * tok_count
    starts = np.pad(starts, (0, -len(starts) % 8))[:, None] * freqs
    return [jnp.asarray(f(a), f32) for a in (inner, starts) for f in (np.cos, np.sin)]


def forward(arrays, tokens, cotangent, routes, segments, depth, reach, experts, heads_width, hidden):
    count, width = tokens.shape
    n = depth * PLANE
    rows = arrays[0].shape[0]
    span = (reach + 1) * count
    near_width = LANES + 4 * heads_width
    columns = near_width + 3 * hidden
    capacity = count // 4
    qkv = LANES + 3 * heads_width
    step = 4 * LANES
    widths = [qkv // 2, qkv // 2, heads_width] + [step] * ((columns - near_width) // step)
    chunks, at = [], 0
    for w in widths:
        left = (w // LANES + (len(chunks) + 1) % 2) // 2 * LANES
        chunks.append((at, left, w - left))
        at += w
    near_edges = ((qkv, 1), (near_width, 2))
    parts = len(chunks)
    tables = angle_tables(count, n, reach)
    segment_rows = segments.reshape(-1, count)

    def shape(*dims, dtype=bf16):
        return jax.ShapeDtypeStruct(dims, dtype)

    outs = (
        shape(depth, 2, 2, rows, columns),
        shape(depth, 2, 2, rows, near_width),
        shape(reach + 1, count, width),
        shape(count, heads_width), shape(span, heads_width), shape(span, heads_width),
        shape(-(-heads_width // HEAD // 8) * 8, count, dtype=f32),
        shape(count, heads_width),
        shape(span, LANES, dtype=f32), shape(span, LANES, dtype=f32), shape(span, count, dtype=f32),
        shape(8, width, dtype=f32),
        shape(count, width, dtype=f32), shape(count, width),
        shape(count, LANES, dtype=f32), shape(count, LANES, dtype=f32),
        shape(routes.shape[1], count, experts * capacity),
        shape(experts, capacity, width), shape(experts, capacity, width),
    )
    inputs = list(arrays) + [tokens, cotangent, routes, segment_rows, tables[0], tables[1], tables[2], tables[3]]
    return pl.pallas_call(
        functools.partial(forward_kernel, depth, reach, experts, tuple(chunks), near_edges),
        out_shape=outs,
        in_specs=[IN_VMEM] * len(inputs),
        out_specs=(IN_HBM,) + (IN_VMEM,) * (len(outs) - 1),
        scratch_shapes=[
            pltpu.VMEM((rows, columns), bf16),
            pltpu.VMEM((count, width), bf16),
            pltpu.VMEM((count, width), bf16),
            dma(parts, depth - 1), dma(parts, depth - 1), dma(parts, 4), dma(parts, 4),
            dma(reach), dma(reach), dma(reach), dma(reach), dma(1), dma(1), dma(3),
        ],
        compiler_params=comm_params(1, 58 << 20),
        name="gather_and_attend",
    )(*inputs)


def unpack_experts(results):
    return results[0], results[1], results[2:5], results[5], results[6:]


def local(
    tokens, cotangent, attn_gain, w_query, w_key, w_value, w_out, ffn_gain, w_router,
    w_sgate, w_sup, w_sdown, e_gate, e_up, e_down, routes, segments,
):
    tok_count, width = tokens.shape
    n = lax.axis_size("dp")
    depth = n // PLANE
    me = lax.axis_index("dp")
    core = lax.axis_index("tensor")
    experts = w_router.shape[1]
    owners = n // experts
    capacity = tok_count // 4
    reach = (WINDOW + tok_count - 1) // tok_count
    shard_rows = w_query.shape[0]
    heads_width = w_query.shape[1]
    hidden = w_sgate.shape[1]
    half = width // 2

    small = jnp.pad(
        jnp.concatenate([w_router, attn_gain[:, None], ffn_gain[:, None]], axis=1),
        ((0, 0), (0, LANES - experts - 2)),
    )
    near_width = LANES + 4 * heads_width
    columns = near_width + 3 * hidden + LANES
    (
        full, near, window, queries, all_keys, all_values, lse, heads_out, cosines, sines, bias, gains,
        middle, branch_in, probs, gates, pick, rows_out, d_rows_out,
    ) = forward(
        (small, w_query, w_key, w_value, w_out.T, w_sgate, w_sup, w_sdown.T),
        tokens, cotangent, routes, segments, depth, reach, experts, heads_width, hidden,
    )
    x_float = tokens.astype(f32)
    normed_one, scale_one = rms_parts(x_float)
    gain_first, gain_second = gains[0], gains[1]
    blocks = (depth, 2, 2, shard_rows)
    if owners == 1:
        (
            output, d_middle, shared_grads, small_grads, expert_grads
        ) = unpack_experts(
            experts_fused(
                rows_out, d_rows_out, (e_gate, e_up, e_down), full, branch_in, cotangent, middle, probs, gates,
                pick, routes, gains, near, depth, hidden,
            )
        )
    else:
        sgate_w, sup_w, sdown_t = (
            full[:, :, :, :, near_width + i * hidden : near_width + (i + 1) * hidden].reshape(width, hidden)
            for i in range(3)
        )
        router_w = near[:, :, :, :, :experts].reshape(width, experts)
        expert_gate = e_gate.astype(bf16)
        expert_up = e_up.astype(bf16)
        expert_down = e_down.astype(bf16)
        normed_two, scale_two = rms_parts(middle)
        probs = probs[:, :experts]
        picked = (routes[:, :, None] == jnp.arange(experts, dtype=jnp.int32)[None, None, :]).astype(f32)
        d_after = cotangent.astype(f32)
        rows_in, d_rows_in = dispatch(rows_out, d_rows_out, n, owners)

        rows_in = rows_in.reshape(n * capacity, width)
        d_rows_in = d_rows_in.reshape(n * capacity, width)
        gate_hidden = matmul(rows_in, expert_gate)
        up_hidden = matmul(rows_in, expert_up)
        gate_act = jax.nn.silu(gate_hidden)
        expert_hidden = (gate_act * up_hidden).astype(bf16)
        part_rows = matmul(expert_hidden, expert_down).astype(bf16)
        d_hidden = input_grad(d_rows_in, expert_down)
        d_gate_hidden = (d_hidden * up_hidden * silu_grad(gate_hidden)).astype(bf16)
        d_up_hidden = (d_hidden * gate_act).astype(bf16)
        d_part_rows = (
            input_grad(d_gate_hidden, expert_gate) + input_grad(d_up_hidden, expert_up)
        ).astype(bf16)
        returned, d_returned = give_back(
            part_rows.reshape(n, capacity, width), d_part_rows.reshape(n, capacity, width)
        )
        grad_e_down = weight_grad(expert_hidden, d_rows_in)
        grad_e_gate = weight_grad(rows_in, d_gate_hidden)
        grad_e_up = weight_grad(rows_in, d_up_hidden)

        shared_gate = matmul(branch_in, sgate_w)
        shared_up = matmul(branch_in, sup_w)
        shared_act = jax.nn.silu(shared_gate)
        shared_hidden = (shared_act * shared_up).astype(bf16)
        shared_part = input_grad(shared_hidden, sdown_t)
        d_shared = matmul(cotangent, sdown_t)
        grad_sdown_t = weight_grad(cotangent, shared_hidden)
        d_sgate = (d_shared * shared_up * silu_grad(shared_gate)).astype(bf16)
        d_sup = (d_shared * shared_act).astype(bf16)
        grad_sgate = weight_grad(branch_in, d_sgate)
        grad_sup = weight_grad(branch_in, d_sup)
        d_shared_in = input_grad(d_sgate, sgate_w) + input_grad(d_sup, sup_w)

        def incoming(rows):
            rows = rows.reshape(experts, owners, capacity, half)
            if owners > 1:
                rows = jnp.sum(rows.astype(f32), axis=1).astype(bf16)
            return rows.reshape(experts * capacity, half)

        def placed(values):
            own = jnp.concatenate([values, jnp.zeros_like(values)], axis=1)
            other = jnp.concatenate([jnp.zeros_like(values), values], axis=1)
            return jnp.where(core == 0, own, other)

        result_rows, d_result_rows = incoming(returned), incoming(d_returned)
        pair_out = [matmul(pick[k], result_rows) for k in range(pick.shape[0])]
        d_pairs = matmul(pick[0] + pick[1], d_result_rows)
        moe_half = sum(gates[:, k : k + 1] * pair_out[k] for k in range(pick.shape[0]))
        d_half = lax.dynamic_slice_in_dim(cotangent, core * half, half, axis=1).astype(f32)
        d_gates_part = jnp.concatenate(
            [jnp.sum(d_half * p, axis=1, keepdims=True) for p in pair_out], axis=1
        )
        after_part = (placed(moe_half) + shared_part).astype(bf16)
        d_branch_part = (d_shared_in + placed(d_pairs)).astype(bf16)
        d_gates_part = jnp.pad(d_gates_part, ((0, 0), (0, LANES - pick.shape[0])))
        after_other, d_branch_other, d_gates_other = swap(
            [after_part, d_branch_part, d_gates_part], 6
        )
        output = (middle + (after_part.astype(f32) + after_other.astype(f32))).astype(bf16)
        d_branch_sum = d_branch_part.astype(f32) + d_branch_other.astype(f32)
        d_gates = (d_gates_part + d_gates_other)[:, : pick.shape[0]]
        d_probs = jnp.sum(d_gates[:, :, None] * picked, axis=1)
        d_logits = (probs * (d_probs - jnp.sum(probs * d_probs, axis=-1, keepdims=True))).astype(bf16)
        grad_router = weight_grad(branch_in, d_logits)
        d_branch_in = d_branch_sum + input_grad(d_logits, router_w)
        grad_gain_two = jnp.sum(d_branch_in * normed_two, axis=0)
        d_norm_two = d_branch_in * gain_second
        d_middle = d_after + scale_two * (
            d_norm_two - normed_two * jnp.mean(d_norm_two * normed_two, axis=-1, keepdims=True)
        )

        shared_grads = [
            value.astype(bf16).reshape(blocks + (hidden,)) for value in (grad_sgate, grad_sup, grad_sdown_t)
        ]
        small_grads = jnp.concatenate(
            [grad_router, grad_gain_two[:, None], jnp.zeros((width, LANES - experts - 1), f32)], axis=1
        ).astype(bf16).reshape(blocks + (LANES,))
        expert_grads = [grad_e_gate, grad_e_up, grad_e_down]
    total, d_attn_in = backward(
        list(shared_grads) + [
            small_grads,
            window, queries, all_keys, all_values, lse, heads_out,
            d_middle.astype(bf16), near, gains, cosines, sines, bias,
        ],
        shard_rows, columns, 3 * hidden, tok_count, heads_width, width, depth, reach,
    )
    def columns_of(at, count):
        return total[:, at : at + count]

    at_out = 3 * hidden
    at_pairs = at_out + heads_width + LANES
    grad_parts = [
        jnp.concatenate(
            [
                columns_of(at_pairs + (3 * pair + i) * LANES, LANES)
                for pair in range(heads_width // LANES)
            ],
            axis=1,
        )
        for i in range(3)
    ]
    d_attn_in = d_attn_in.astype(f32)
    d_norm_one = d_attn_in * gain_first
    token_input_gradient = d_middle + scale_one * (
        d_norm_one - normed_one * jnp.mean(d_norm_one * normed_one, axis=-1, keepdims=True)
    )
    return (
        output,
        token_input_gradient,
        total[:, columns - LANES],
        grad_parts[0],
        grad_parts[1],
        grad_parts[2],
        columns_of(at_out, heads_width).T,
        total[:, at_out + heads_width + experts],
        columns_of(at_out + heads_width, experts),
        columns_of(0, hidden),
        columns_of(hidden, hidden),
        columns_of(2 * hidden, hidden).T,
    ) + tuple(expert_grads)


def solution(mesh):
    by_dp, both, turned = P("dp", None), P("dp", "tensor"), P("tensor", "dp")
    wide, tall = P(None, ("dp", "tensor")), P(("dp", "tensor"), None)
    weights = (P("dp"), both, both, both, turned, P("dp"), by_dp, both, both, turned, wide, wide, tall)
    return jax.shard_map(
        local,
        mesh=mesh,
        in_specs=(by_dp, by_dp) + weights + (by_dp, P()),
        out_specs=(by_dp, by_dp) + weights,
        check_vma=False,
    )
```

```python
import functools

import jax
import jax.numpy as jnp
import numpy as np
from jax import lax
from jax.experimental import pallas as pl
from jax.experimental.pallas import tpu as pltpu
from jax.sharding import PartitionSpec as P

HEAD = 64
WINDOW = 1024
LANES = 128
PLANE = 4

MESH = pl.DeviceIdType.MESH
f32 = jnp.float32
bf16 = jnp.bfloat16

eps = 1e-06
masked = -1e30


def matmul(left, right):
    return jnp.dot(left, right, preferred_element_type=f32)


def weight_grad(left, right):
    return lax.dot_general(
        left, right, (((0,), (0,)), ((), ())), preferred_element_type=f32
    )


def input_grad(left, right):
    return lax.dot_general(
        left, right, (((1,), (1,)), ((), ())), preferred_element_type=f32
    )


def rms_parts(values):
    factor = lax.rsqrt(jnp.mean(values * values, axis=-1, keepdims=True) + eps)
    return (values * factor, factor)


def silu_grad(values):
    sigma = jax.nn.sigmoid(values)
    return sigma * (1.0 + values * (1.0 - sigma))


def digits(me):
    return lax.div(me, PLANE), lax.rem(lax.div(me, 2), 2), lax.rem(me, 2)


def index_of(z, y, x):
    return z * PLANE + y * 2 + x


def push(src, dst, send, recv, device):
    copy = pltpu.make_async_remote_copy(
        src_ref=src,
        dst_ref=dst,
        send_sem=send,
        recv_sem=recv,
        device_id=device,
        device_id_type=MESH,
    )
    copy.start()
    return copy


def greet(devices):
    barrier = pltpu.get_barrier_semaphore()
    for device in devices:
        pl.semaphore_signal(barrier, inc=1, device_id=device, device_id_type=MESH)
    pl.semaphore_wait(barrier, len(devices))


def comm_params(collective_id, limit=48 << 20):
    return pltpu.CompilerParams(
        collective_id=collective_id, has_side_effects=True, vmem_limit_bytes=limit
    )


def dma(*shape):
    return pltpu.SemaphoreType.DMA(shape)


IN_HBM = pl.BlockSpec(memory_space=pl.ANY)
IN_VMEM = pl.BlockSpec(memory_space=pltpu.VMEM)


def grid_peers(depth, z, y, x):
    peers = [{"dp": index_of(lax.rem(z + k, depth), y, x)} for k in range(1, depth)]
    return peers, {"dp": index_of(z, 1 - y, x)}, {"dp": index_of(z, y, 1 - x)}


def swap_kernel(count, *refs):
    sources, targets, (send, recv) = refs[:count], refs[count : 2 * count], refs[2 * count :]
    sibling = {"tensor": 1 - lax.axis_index("tensor")}
    greet([sibling])
    copies = [
        push(a, b, send.at[i], recv.at[i], sibling)
        for i, (a, b) in enumerate(zip(sources, targets))
    ]
    for copy in copies:
        copy.wait()


def swap(arrays, collective_id):
    count = len(arrays)
    return pl.pallas_call(
        functools.partial(swap_kernel, count),
        out_shape=tuple(jax.ShapeDtypeStruct(a.shape, a.dtype) for a in arrays),
        in_specs=[IN_VMEM] * count,
        out_specs=(IN_VMEM,) * count,
        scratch_shapes=[dma(count), dma(count)],
        compiler_params=comm_params(collective_id),
        name="swap_cores",
    )(*arrays)


def dispatch_kernel(n, owners, first, second, got_first, got_second, send, recv, f_send, f_recv, own):
    me, core = lax.axis_index("dp"), lax.axis_index("tensor")
    sibling = {"tensor": 1 - core}
    greet([{"dp": lax.rem(me + k, n)} for k in range(1, n)] + [sibling])
    half = first.shape[-1] // 2
    cols = pl.ds(pl.multiple_of(core * half, half), half)
    pairs = ((first, got_first), (second, got_second))
    mine = lax.div(me, owners)
    copies = []
    for k in range(1, n):
        to = lax.rem(me + k, n)
        for i, (source, target) in enumerate(pairs):
            copies.append(
                push(
                    source.at[lax.div(to, owners), :, cols],
                    target.at[me, :, cols],
                    send.at[i, k],
                    recv.at[i, k],
                    {"dp": to},
                )
            )
    local = [
        pltpu.make_async_copy(source.at[mine], target.at[me], own.at[i])
        for i, (source, target) in enumerate(pairs)
    ]
    for copy in local:
        copy.start()
    forwards = []
    for k in range(1, n):
        source_of = lax.rem(me + n - k, n)
        for i, (source, target) in enumerate(pairs):
            copies[2 * (k - 1) + i].wait_recv()
            block = target.at[source_of, :, cols]
            forwards.append(push(block, block, f_send.at[i, k], f_recv.at[i, k], sibling))
    for copy in forwards:
        copy.wait_recv()
    for copy in local:
        copy.wait()
    for copy in copies + forwards:
        copy.wait_send()


def dispatch(first, second, n, owners):
    shape = jax.ShapeDtypeStruct((n,) + first.shape[1:], first.dtype)
    return pl.pallas_call(
        functools.partial(dispatch_kernel, n, owners),
        out_shape=(shape, shape),
        in_specs=[IN_HBM] * 2,
        out_specs=(IN_HBM, IN_HBM),
        scratch_shapes=[dma(2, n), dma(2, n), dma(2, n), dma(2, n), dma(2)],
        compiler_params=comm_params(2),
        name="dispatch_rows",
    )(first, second)


def return_kernel(n, groups, first, second, got_first, got_second, part, total, send, recv, f_send, f_recv, own):
    me, core = lax.axis_index("dp"), lax.axis_index("tensor")
    sibling = {"tensor": 1 - core}
    greet([{"dp": lax.rem(me + k, n)} for k in range(1, n)] + [sibling])
    half = first.shape[-1] // 2
    mine = pl.ds(pl.multiple_of(core * half, half), half)
    theirs = pl.ds(pl.multiple_of((1 - core) * half, half), half)
    pairs = ((first, got_first), (second, got_second))
    each = n // groups
    swaps = []
    for g in range(groups):
        block = pl.ds(g * each, each)
        for i, (source, target) in enumerate(pairs):
            swaps.append(
                push(
                    source.at[block, :, theirs],
                    part.at[i, block],
                    f_send.at[i, g],
                    f_recv.at[i, g],
                    sibling,
                )
            )
    for g in range(groups):
        block = pl.ds(g * each, each)
        for i, (source, target) in enumerate(pairs):
            swaps[2 * g + i].wait_recv()
            total[i, block] = (
                source[block, :, mine].astype(f32) + part[i, block].astype(f32)
            ).astype(bf16)
        for slot in range(g * each, (g + 1) * each):
            for i, (source, target) in enumerate(pairs):
                @pl.when(slot != me)
                def _():
                    push(
                        total.at[i, slot],
                        target.at[me],
                        send.at[i, slot],
                        recv.at[i, me],
                        {"dp": slot},
                    )
    local = [
        pltpu.make_async_copy(total.at[i, me], pairs[i][1].at[me], own.at[i]) for i in range(2)
    ]
    for copy in local:
        copy.start()
    for k in range(1, n):
        to, source_of = lax.rem(me + k, n), lax.rem(me + n - k, n)
        for i, (source, target) in enumerate(pairs):
            pltpu.make_async_remote_copy(
                total.at[i, to], target.at[source_of], send.at[i, to], recv.at[i, source_of],
                device_id={"dp": to}, device_id_type=MESH,
            ).wait()
    for copy in local:
        copy.wait()
    for copy in swaps:
        copy.wait_send()


def give_back(first, second, groups=4):
    n, capacity, width = first.shape
    half = jax.ShapeDtypeStruct((n, capacity, width // 2), first.dtype)
    buffer = pltpu.VMEM((2, n, capacity, width // 2), first.dtype)
    return pl.pallas_call(
        functools.partial(return_kernel, n, groups),
        out_shape=(half, half),
        in_specs=[IN_VMEM] * 2,
        out_specs=(IN_HBM, IN_HBM),
        scratch_shapes=[buffer, buffer, dma(2, n), dma(2, n), dma(2, groups), dma(2, groups), dma(2)],
        compiler_params=comm_params(3),
        name="return_rows",
    )(first, second)


def experts_kernel(
    n, groups, e_gate, e_up, e_down, full, got, got_gate, branch_in, cotangent, middle, probs, pick,
    routes, gains, small,
    d_middle, shared_total, g_small, shared_part, rows_back, ge_gate, ge_up, ge_down,
    rows_total, d_rows_all, gate_w, up_w, down_w, staged, shared_w, hid, d_gate, d_up, part, swapped, d_total, returned,
    inner, inner_back, shared_in, tiles, wide, ends, ends_other, d_gates, d_gates_other,
    first_l, first_r, second_l, second_r, scatter_last, p_send, p_recv, z_send, z_recv,
    s_send, s_recv, r_send, r_recv, o_send, o_recv, i_send, i_recv, e_send, e_recv, own, load, store,
):
    me, core = lax.axis_index("dp"), lax.axis_index("tensor")
    sibling = {"tensor": 1 - core}
    greet([{"dp": lax.rem(me + i, n)} for i in range(1, n)] + [sibling])
    capacity, width = got.shape[2:]
    count = branch_in.shape[0]
    half = width // 2
    mine = pl.ds(pl.multiple_of(core * half, half), half)
    theirs = pl.ds(pl.multiple_of((1 - core) * half, half), half)
    hidden = shared_w.shape[4] // 3
    loads = [
        pltpu.make_async_copy(
            full.at[:, :, :, :, pl.ds(full.shape[4] - 3 * hidden, 3 * hidden)], shared_w, load.at[2]
        )
    ]
    for copy in loads:
        copy.start()
    inner[...] = jnp.zeros_like(inner)

    step = 2 * LANES
    scatter = Scatter(
        n // PLANE,
        [(shared_w, at, step, shared_w, at + step, step, at) for at in range(0, 3 * hidden, 2 * step)],
        shared_total, (first_l, first_r, second_l, second_r, scatter_last),
        (p_send, p_recv, z_send, z_recv),
    )
    steps = scatter.plan()
    done = [0]

    def advance(count=1):
        for action, c in steps[done[0] : done[0] + count]:
            done[0] += 1
            action(c)
            if action == scatter.second and c + 4 < len(scatter.chunks):
                scatter.start(c + 4)

    pieces = []
    for source, target in ((e_gate, gate_w), (e_up, up_w), (e_down, down_w)):
        step = source.shape[0] // 4
        pieces += [(source, target, pl.ds(j * step, step)) for j in range(4)]

    def fetch(j):
        source, target, rows = pieces[j]
        return pltpu.make_async_copy(
            source.at[rows],
            staged.at[j % 2, pl.ds(0, rows.size), pl.ds(0, source.shape[1])],
            load.at[j % 2],
        )

    fetch(0).start()
    fetch(1).start()

    def take(j):
        source, target, rows = pieces[j]
        fetch(j).wait()
        target[rows, :] = staged[j % 2, : rows.size, : source.shape[1]].astype(bf16)
        if j + 2 < len(pieces):
            fetch(j + 2).start()

    swaps = {}

    def work(group):
        first, each = group * n // groups, n // groups
        slots = pl.ds(first, each)
        rows = pl.ds(first * capacity, each * capacity)
        rows_in = got[0, slots].reshape(each * capacity, width)
        gate_of = jnp.concatenate([got_gate[i].T[:capacity, 0:1] for i in range(first, first + each)], axis=0)
        d_rows = (gate_of * got[1, slots].reshape(each * capacity, width).astype(f32)).astype(bf16)
        d_rows_all[rows, :] = d_rows
        gate, up = matmul(rows_in, gate_w[...]), matmul(rows_in, up_w[...])
        sigma = 1.0 / (1.0 + jnp.exp(-gate))
        act = gate * sigma
        hid_low = (act * up).astype(bf16)
        hid[rows, :] = hid_low
        part[0, slots] = matmul(hid_low, down_w[...]).astype(bf16).reshape(each, capacity, width)
        d_hid = input_grad(d_rows, down_w[...])
        d_gate_low = (d_hid * up * (sigma * (1.0 + gate * (1.0 - sigma)))).astype(bf16)
        d_up_low = (d_hid * act).astype(bf16)
        d_gate[rows, :] = d_gate_low
        d_up[rows, :] = d_up_low
        part[1, slots] = (
            (input_grad(d_gate_low, gate_w[...]) + input_grad(d_up_low, up_w[...]))
            .astype(bf16)
            .reshape(each, capacity, width)
        )
        for a in (1, 0):
            swaps[a, group] = push(
                part.at[a, slots, :, theirs], swapped.at[a, slots],
                s_send.at[a, group], s_recv.at[a, group], sibling,
            )

    back = {}

    def give(group):
        first, each = group * n // groups, n // groups
        slots = pl.ds(first, each)
        swaps[1, group].wait_recv()
        d_total[slots] = (
            part[1, slots, :, mine].astype(f32) + swapped[1, slots].astype(f32)
        ).astype(bf16)
        homes = [{"dp": lax.rem(me + n - i, n)} for i in range(n)]
        for i in range(max(first, 1), first + each):
            back[1, i] = push(
                d_total.at[i], returned.at[me], r_send.at[i], r_recv.at[i], homes[i]
            )
        swaps[0, group].wait_recv()
        value = part[0, slots, :, mine].astype(f32) + swapped[0, slots].astype(f32)
        rows_total[slots] = value.astype(bf16)
        products = jnp.sum(value * got[1, slots, :, mine].astype(f32), axis=-1, keepdims=True)
        for i in range(first, first + each):
            row = jnp.broadcast_to(products[i - first], (capacity, LANES)).T[0:8, :]
            inner[i, :, :capacity] = row
            if i:
                back[2, i] = push(
                    rows_total.at[i], rows_back.at[me], o_send.at[i], o_recv.at[i], homes[i]
                )
                back[0, i] = push(
                    inner.at[i], inner_back.at[me], i_send.at[i], i_recv.at[i], homes[i]
                )

    loads[0].wait()
    branch, cot = branch_in[...], cotangent[...]
    sgate_w, sup_w, sdown_w = (stacked(shared_w, pl.ds(i * hidden, hidden)) for i in range(3))
    gate, up = matmul(branch, sgate_w), matmul(branch, sup_w)
    sigma = 1.0 / (1.0 + jnp.exp(-gate))
    act = gate * sigma
    shared_hid = (act * up).astype(bf16)
    shared_part[...] = input_grad(shared_hid, sdown_w)
    d_shared = matmul(cot, sdown_w)
    d_sgate = (d_shared * up * (sigma * (1.0 + gate * (1.0 - sigma)))).astype(bf16)
    d_sup = (d_shared * act).astype(bf16)
    shared_in[...] = input_grad(d_sgate, sgate_w) + input_grad(d_sup, sup_w)
    for i, (left, right) in enumerate(((branch, d_sgate), (branch, d_sup), (cot, shared_hid))):
        put_rows(shared_w, weight_grad(left, right).astype(bf16), pl.ds(i * hidden, hidden))
        for c in range(2 * i, 2 * i + 2):
            if c < 4:
                scatter.start(c)
    for j in range(12):
        take(j)
    work(0)
    advance()
    work(1)
    advance()
    give(0)
    work(2)
    advance(2)
    give(1)
    work(3)
    advance(2)
    give(2)
    advance()
    give(3)
    keep = [
        pltpu.make_async_copy(d_total.at[0], returned.at[me], own.at[0]),
        pltpu.make_async_copy(inner.at[0], inner_back.at[me], own.at[1]),
        pltpu.make_async_copy(rows_total.at[0], rows_back.at[me], own.at[2]),
    ]
    for copy in keep:
        copy.start()

    stores = []

    def emit(value, tile, target):
        slot = len(stores) % 2
        if len(stores) >= 2:
            stores[-2].wait()
        tile[slot] = value
        stores.append(pltpu.make_async_copy(tile.at[slot], target, store.at[slot]))
        stores[-1].start()
        advance()

    rows_all = got[0].reshape(n * capacity, width)
    units = hid.shape[1]
    span = min(units, 256)
    for source, target in ((d_gate, ge_gate), (d_up, ge_up)):
        for at in range(0, units, span):
            columns = pl.ds(at, span)
            emit(weight_grad(rows_all, source[:, columns]), tiles, target.at[:, columns])
    for at in range(0, units, span):
        columns = pl.ds(at, span)
        emit(weight_grad(hid[:, columns], d_rows_all[...]), wide, ge_down.at[columns, :])

    for copy in keep:
        copy.wait()
    for a in range(2):
        for i in range(1, n):
            back[a, i].wait_recv()
    lane = lax.broadcasted_iota(jnp.int32, (1, LANES), 1)
    d_pairs = matmul(pick[0] + pick[1], returned[...].reshape(n * capacity, half))
    inner_row = jnp.concatenate([inner_back[e, 0:1, :capacity] for e in range(n)], axis=1)
    d_gate_lanes = jnp.zeros((count, LANES), f32)
    for i in range(2):
        value = jnp.sum(pick[i].astype(f32) * inner_row, axis=-1, keepdims=True)
        d_gate_lanes = d_gate_lanes + jnp.where(lane == i, value, 0.0)
    d_gates[...] = d_gate_lanes
    shared_in[:, mine] = shared_in[:, mine] + d_pairs
    ends[...] = shared_in[...].astype(bf16)
    last = [
        push(ends, ends_other, e_send.at[0], e_recv.at[0], sibling),
        push(d_gates, d_gates_other, e_send.at[1], e_recv.at[1], sibling),
    ]
    for copy in last:
        copy.wait()

    middle_all = middle[...]
    d_gates_all = d_gates[...] + d_gates_other[...]
    d_probs = jnp.zeros((count, LANES), f32)
    for i in range(2):
        d_probs = d_probs + jnp.where(routes[:, i : i + 1] == lane, d_gates_all[:, i : i + 1], 0.0)
    chance = probs[...]
    d_logits = (
        chance * (d_probs - jnp.sum(chance * d_probs, axis=-1, keepdims=True))
    ).astype(bf16)
    small_all = stacked(small, pl.ds(0, LANES))
    d_branch = (
        ends[...].astype(f32) + ends_other[...].astype(f32) + input_grad(d_logits, small_all)
    )
    factor = lax.rsqrt(jnp.mean(middle_all * middle_all, axis=-1, keepdims=True) + eps)
    normed = middle_all * factor
    gain_row = jnp.sum(d_branch * normed, axis=0, keepdims=True)
    d_norm = d_branch * gains[1:2, :]
    d_middle[...] = cotangent[...].astype(f32) + factor * (
        d_norm - normed * jnp.mean(d_norm * normed, axis=-1, keepdims=True)
    )
    put_rows(
        g_small,
        jnp.where(
            lane == n, jnp.broadcast_to(gain_row, (LANES, width)).T, weight_grad(branch, d_logits)
        ).astype(bf16),
        pl.ds(0, LANES),
    )
    for copy in stores[-2:]:
        copy.wait()
    advance(len(steps))
    scatter.drain()
    for i in range(1, n):
        back[2, i].wait_recv()
    for copies in (swaps, back):
        for copy in copies.values():
            copy.wait_send()


def experts_fused(
    got, got_gate, weights, full, branch_in, cotangent, middle, probs, pick, routes, gains, near,
    depth, hidden, groups=4,
):
    n, capacity, width = got.shape[1:]
    count = branch_in.shape[0]
    units = weights[0].shape[1]
    rows = near.shape[3]
    span = min(units, 256)
    half = width // 2

    def shape(*dims, dtype=bf16):
        return jax.ShapeDtypeStruct(dims, dtype)

    slots = pltpu.VMEM((n, capacity, half), bf16)
    both = pltpu.VMEM((2, n, capacity, half), bf16)
    wide = pltpu.VMEM((n * capacity, units), bf16)
    lanes = pltpu.VMEM((n, 8, LANES), f32)
    parts = 3 * hidden // (4 * LANES)
    results = pl.pallas_call(
        functools.partial(experts_kernel, n, groups),
        out_shape=(
            shape(count, width, dtype=f32), shape(rows, 3 * hidden, dtype=f32),
            shape(depth, 2, 2, rows, LANES), shape(count, width, dtype=f32), shape(n, capacity, half),
            shape(width, units, dtype=f32), shape(width, units, dtype=f32), shape(units, width, dtype=f32),
        ),
        in_specs=[IN_HBM] * 4 + [IN_VMEM] * 10,
        out_specs=(IN_VMEM,) * 5 + (IN_HBM,) * 3,
        scratch_shapes=[
            slots,
            pltpu.VMEM((n * capacity, width), bf16),
            pltpu.VMEM((width, units), bf16), pltpu.VMEM((width, units), bf16), pltpu.VMEM((units, width), bf16),
            pltpu.VMEM((2, max(width, units) // 4, max(width, units)), f32),
            pltpu.VMEM((depth, 2, 2, rows, 3 * hidden), bf16),
            wide, wide, wide,
            pltpu.VMEM((2, n, capacity, width), bf16),
            both, slots, slots,
            lanes, lanes,
            pltpu.VMEM((count, width), f32),
            pltpu.VMEM((2, width, span), f32), pltpu.VMEM((2, span, width), f32),
            pltpu.VMEM((count, width), bf16), pltpu.VMEM((count, width), bf16),
            pltpu.VMEM((count, LANES), f32), pltpu.VMEM((count, LANES), f32),
        ] + scatter_scratch(depth, rows, 3 * hidden // 2, parts) + [
            dma(2, groups), dma(2, groups),
            dma(n), dma(n), dma(n), dma(n), dma(n), dma(n), dma(2), dma(2), dma(3), dma(3), dma(2),
        ],
        compiler_params=comm_params(7, 62 << 20),
        name="experts_and_shared",
    )(
        *weights, full, got, got_gate, branch_in, cotangent, middle, probs, pick, routes, gains,
        near[:, :, :, :, :LANES],
    )
    return results[:5] + (results[5:],)


class Scatter:
    def __init__(self, depth, chunks, total, buffers, semaphores):
        self.depth, self.chunks, self.total = depth, chunks, total
        self.first_l, self.first_r, self.second_l, self.second_r, self.last = buffers
        self.p_send, self.p_recv, self.z_send, self.z_recv = semaphores
        self.z, self.y, self.x = digits(lax.axis_index("dp"))
        self.z_peers, self.y_peer, self.x_peer = grid_peers(depth, self.z, self.y, self.x)
        self.at_l, self.at_r, l, r = [], [], 0, 0
        for left, lc, lw, right, rc, rw, out in chunks:
            self.at_l.append(pl.ds(l, lw))
            self.at_r.append(pl.ds(r, rw))
            l, r = l + lw, r + rw
        self.ones, self.twos, self.threes = {}, {}, {}

    def start(self, c):
        left, lc, lw, right, rc, rw, out = self.chunks[c]
        self.ones[c] = [
            push(
                left.at[:, :, 1 - self.x, :, pl.ds(lc, lw)],
                self.first_l.at[:, :, :, self.at_l[c]],
                self.p_send.at[c, 0], self.p_recv.at[c, 0], self.x_peer,
            ),
            push(
                right.at[:, 1 - self.y, :, :, pl.ds(rc, rw)],
                self.first_r.at[:, :, :, self.at_r[c]],
                self.p_send.at[c, 1], self.p_recv.at[c, 1], self.y_peer,
            ),
        ]

    def second(self, c):
        left, lc, lw, right, rc, rw, out = self.chunks[c]
        in_l, in_r, first_l, first_r = self.at_l[c], self.at_r[c], self.first_l, self.first_r
        for copy in self.ones[c]:
            copy.wait_recv()

        def add(i, carry):
            for j in range(2):
                first_l[i, j, :, in_l] = (
                    first_l[i, j, :, in_l].astype(f32) + left[i, j, self.x, :, pl.ds(lc, lw)].astype(f32)
                ).astype(bf16)
                first_r[i, j, :, in_r] = (
                    first_r[i, j, :, in_r].astype(f32) + right[i, self.y, j, :, pl.ds(rc, rw)].astype(f32)
                ).astype(bf16)
            return carry

        lax.fori_loop(0, self.depth, add, 0)
        self.twos[c] = [
            push(
                first_l.at[:, 1 - self.y, :, in_l], self.second_l.at[:, :, in_l],
                self.p_send.at[c, 2], self.p_recv.at[c, 2], self.y_peer,
            ),
            push(
                first_r.at[:, 1 - self.x, :, in_r], self.second_r.at[:, :, in_r],
                self.p_send.at[c, 3], self.p_recv.at[c, 3], self.x_peer,
            ),
        ]

    def third(self, c):
        for copy in self.twos[c]:
            copy.wait_recv()
        sides = (
            (self.second_l, self.first_l, self.y, self.at_l[c]),
            (self.second_r, self.first_r, self.x, self.at_r[c]),
        )

        def add(i, carry):
            for source, before, place, here in sides:
                source[i, :, here] = (
                    source[i, :, here].astype(f32) + before[i, place, :, here].astype(f32)
                ).astype(bf16)
            return carry

        lax.fori_loop(0, self.depth, add, 0)
        self.threes[c] = [
            push(
                source.at[lax.rem(self.z + k + 1, self.depth), :, here],
                self.last.at[k, side, :, here],
                self.z_send.at[c, side, k], self.z_recv.at[c, side, k], self.z_peers[k],
            )
            for side, (source, before, place, here) in enumerate(sides)
            for k in range(self.depth - 1)
        ]

    def finish(self, c):
        left, lc, lw, right, rc, rw, out = self.chunks[c]
        for copy in self.threes[c]:
            copy.wait_recv()
        for side, source, here, at, span in (
            (0, self.second_l, self.at_l[c], out, lw),
            (1, self.second_r, self.at_r[c], out + lw, rw),
        ):
            value = source[self.z, :, here].astype(f32)
            for k in range(self.depth - 1):
                value = value + self.last[k, side, :, here].astype(f32)
            self.total[:, pl.ds(at, span)] = value

    def plan(self):
        steps = []
        for c in range(len(self.chunks) + 2):
            if c < len(self.chunks):
                steps.append((self.second, c))
            if 1 <= c <= len(self.chunks):
                steps.append((self.third, c - 1))
            if c >= 2:
                steps.append((self.finish, c - 2))
        return steps

    def drain(self):
        for copies in list(self.ones.values()) + list(self.twos.values()) + list(self.threes.values()):
            for copy in copies:
                copy.wait_send()


def lanes_of(part):
    lane = lax.broadcasted_iota(jnp.int32, (1, LANES), 1)
    return (lax.div(lane, HEAD) == part).astype(f32).astype(bf16)


def swap_halves(values):
    lane = lax.broadcasted_iota(jnp.int32, (1, LANES), 1)
    low = lax.rem(lane, HEAD) < HEAD // 2
    return jnp.where(
        low, pltpu.roll(values, LANES - HEAD // 2, 1), pltpu.roll(values, HEAD // 2, 1)
    )


def put_rows(target, values, columns):
    rows = target.shape[3]
    for b in range(values.shape[0] // rows):
        target[b // PLANE, (b // 2) % 2, b % 2, :, columns] = values[b * rows : (b + 1) * rows]


def backward_kernel(
    depth, reach, per_core, shared, g_small, window, q, k, v, lse, heads_out, d_attn,
    near, gains, cosines, sines, bias, *rest,
):
    given = shared or 5
    rest, combine = rest[given:], rest[:given]
    total, d_full = rest[:2]
    rest = rest[2:]
    if not shared:
        rows_back, pick, gates, middle, shared_part = combine
        output, end, end_other, e_send, e_recv = rest[:1] + rest[-4:]
        rest = rest[1:-4]
    (
    grads, attn_t, d_heads, dq_all, dk_all, dv_all, d_part, d_swap, d_sum, d_got, gain_got,
    first_l, first_r, second_l, second_r, last, p_send, p_recv, z_send, z_recv,
    t_send, t_recv, s_send, s_recv, f_send, f_recv,
    ) = rest
    n = depth * PLANE
    me, core = lax.axis_index("dp"), lax.axis_index("tensor")
    sibling = {"tensor": 1 - core}
    plane, z_next, z_before = Plane(me), *z_neighbours(me, n)
    heads_width = q.shape[1]
    count = q.shape[0]
    pairs = heads_width // LANES
    chunks = []
    out = 0
    step = 2 * LANES
    for source in combine if shared else ():
        for at in range(0, source.shape[4], 2 * step):
            chunks.append((source, at, step, source, at + step, step, out))
            out += 2 * step
    early = len(chunks)
    widths = [(step, step)] + [(step, LANES), (LANES, step)] * pairs
    widths = widths[:pairs] + [(step, step)]
    at = 0
    for left, right in widths:
        chunks.append((grads, at, left, grads, at + left, right, out + at))
        at += left + right
    scatter = Scatter(
        depth, chunks, total, (first_l, first_r, second_l, second_r, last),
        (p_send, p_recv, z_send, z_recv),
    )
    greet(scatter.z_peers + plane.peers + [sibling, z_next, z_before])
    lead = 4
    for c in range(min(lead, early)):
        scatter.start(c)
    steps = scatter.plan()
    done = [0]

    def advance(count=1):
        for action, c in steps[done[0] : done[0] + count]:
            if action == scatter.second and c not in scatter.ones:
                break
            done[0] += 1
            action(c)
            if action == scatter.second and c + lead < early:
                scatter.start(c + lead)

    out_w = pl.ds(LANES + 3 * heads_width, heads_width)
    gain = gains[0:1, :]
    d_heads[...] = matmul(d_attn[...], stacked(near, out_w)).astype(bf16)
    put_rows(grads, weight_grad(d_attn[...], heads_out[...]).astype(bf16), pl.ds(0, heads_width))
    grads[:, :, :, :, pl.ds(heads_width, LANES)] = g_small[...]

    def normed(block):
        values = window[block].astype(f32)
        return values * lax.rsqrt(jnp.mean(values * values, axis=-1, keepdims=True) + eps)

    def turned(block, carry):
        rows = pl.ds(pl.multiple_of(block * count, count), count)
        attn_t[:, rows] = (normed(block) * gain).T.astype(bf16)
        return carry

    for block in range(reach + 1):
        turned(block, 0)
    scatter.start(early)
    own = pl.ds(reach * count, count)
    for pair in range(pairs):
        columns = pl.ds(pair * LANES, LANES)
        k_pair, v_pair, q_pair, d_pair = k[:, columns], v[:, columns], q[:, columns], d_heads[:, columns]
        k_turned = k_pair.T
        dq, dk, dv = [], None, None
        for part in range(2):
            head = 2 * pair + part
            lanes = lanes_of(part)
            q_head, d_head = q_pair * lanes, d_pair * lanes
            probs = jnp.exp(input_grad(k_pair, q_head) + bias[...] - lse[head : head + 1, :])
            d_probs = input_grad(v_pair, d_head)
            inner = jnp.sum(probs * d_probs, axis=0, keepdims=True)
            d_scores = (probs * (d_probs - inner)).astype(bf16)
            advance()
            dq.append(matmul(k_turned, d_scores)[part * HEAD : (part + 1) * HEAD, :])
            parts = matmul(d_scores, q_head), matmul(probs.astype(bf16), d_head)
            dk, dv = parts if part == 0 else (dk + parts[0], dv + parts[1])
            advance()
        dq = jnp.concatenate(dq, axis=0).T * (HEAD ** (-0.5))
        cos_own, sin_own = cosines[own, :], sines[own, :]
        dq_low = turn(dq, cos_own, -sin_own).astype(bf16)
        dk_low = turn(dk, cosines[...], -sines[...]).astype(bf16)
        dv_low = dv.astype(bf16)
        dq_all[:, columns] = dq_low
        dk_all[:, columns] = dk_low
        dv_all[:, columns] = dv_low
        at = heads_width + LANES + pair * 3 * LANES
        put_rows(grads, matmul(attn_t[:, own], dq_low).astype(bf16), pl.ds(at, LANES))
        put_rows(grads, matmul(attn_t[...], dk_low).astype(bf16), pl.ds(at + LANES, LANES))
        put_rows(grads, matmul(attn_t[...], dv_low).astype(bf16), pl.ds(at + 2 * LANES, LANES))
        if pair < pairs - 1:
            scatter.start(early + 1 + pair)
        advance(2)

    width = d_part.shape[-1] // 2
    mine = pl.ds(pl.multiple_of(core * width, width), width)
    theirs = pl.ds(pl.multiple_of((1 - core) * width, width), width)
    swaps = []
    query_v, key_v, value_v = (
        jnp.concatenate(
            [stacked(near, pl.ds(LANES * (1 + 3 * pair + i), LANES)) for pair in range(pairs)], axis=1
        )
        for i in range(3)
    )
    gain_row = jnp.zeros((1, 2 * width), f32)
    for block in range(reach + 1):
        rows = pl.ds(block * count, count)
        value = input_grad(dk_all[rows, :], key_v) + input_grad(dv_all[rows, :], value_v)
        if block == reach:
            value = value + input_grad(dq_all[...], query_v)
        gain_row = gain_row + jnp.sum(value * normed(block), axis=0, keepdims=True)
        d_part[block] = value.astype(bf16)
        swaps.append(
            push(
                d_part.at[block, :, theirs], d_swap.at[block],
                s_send.at[block], s_recv.at[block], sibling,
            )
        )
        advance()
    put_rows(
        grads,
        jnp.broadcast_to(gain_row, (LANES, 2 * width)).T.astype(bf16),
        pl.ds(heads_width + LANES + pairs * 3 * LANES, LANES),
    )
    final = len(chunks) - 1
    scatter.start(final)
    for block in range(reach + 1):
        swaps[block].wait_recv()
        d_sum[block] = (
            d_part[block, :, mine].astype(f32) + d_swap[block].astype(f32)
        ).astype(bf16)
    back = [
        push(
            d_sum.at[lax.rem(plane.places[j] - plane.place + PLANE, PLANE)],
            d_got.at[j], t_send.at[j], t_recv.at[j], plane.peers[j - 1],
        )
        for j in range(1, PLANE)
    ]
    advance(5)
    d_mine, d_before = d_sum[reach].astype(f32), d_sum[0].astype(f32)
    for j in range(1, PLANE):
        back[j - 1].wait_recv()
        ours = lax.select(plane.places[j] > plane.place, 1.0, 0.0)
        value = d_got[j].astype(f32)
        d_mine, d_before = d_mine + value * ours, d_before + value * (1.0 - ours)
    d_sum[reach] = d_before.astype(bf16)
    back.append(push(d_sum.at[reach], d_got.at[0], t_send.at[0], t_recv.at[0], z_before))
    last_swap = []
    if not shared:
        rows_all = rows_back[...].reshape(-1, width)
        moe = gates[:, 0:1] * matmul(pick[0], rows_all) + gates[:, 1:2] * matmul(pick[1], rows_all)
        end[...] = shared_part[...].astype(bf16)
        end[:, mine] = (shared_part[:, mine] + moe).astype(bf16)
        last_swap.append(push(end, end_other, e_send.at[0], e_recv.at[0], sibling))
    advance(len(steps))
    if not shared:
        last_swap[0].wait_recv()
        output[...] = (
            middle[...] + (end[...].astype(f32) + end_other[...].astype(f32))
        ).astype(bf16)
    back[-1].wait_recv()
    d_mine = d_mine + d_got[0].astype(f32)
    d_full[:, mine] = d_mine.astype(bf16)
    both = push(d_full.at[:, mine], d_full.at[:, mine], f_send.at[0], f_recv.at[0], sibling)
    split = pl.ds(per_core, LANES)
    gain_copy = push(total.at[:, split], gain_got, f_send.at[1], f_recv.at[1], sibling)
    both.wait()
    gain_copy.wait()
    total[:, split] = total[:, split] + gain_got[...]
    scatter.drain()
    for copy in back + swaps + last_swap:
        copy.wait_send()


def backward(arrays, shared, combine, rows, columns, count, heads_width, width, depth, reach):
    span = (reach + 1) * count
    half = columns // 2
    width_shared = sum(value.shape[4] for value in shared)
    parts = width_shared // (4 * LANES) + 2 + heads_width // LANES
    own = columns - width_shared
    outs = (
        jax.ShapeDtypeStruct((rows, columns), f32),
        jax.ShapeDtypeStruct((count, width), bf16),
    )
    extra = []
    if not shared:
        outs += (jax.ShapeDtypeStruct((count, width), bf16),)
        low = pltpu.VMEM((count, width), bf16)
        extra = [low, low, dma(1), dma(1)]
    arrays = list(arrays) + list(shared) + list(combine)
    return pl.pallas_call(
        functools.partial(backward_kernel, depth, reach, columns - LANES, len(shared)),
        out_shape=outs,
        in_specs=[IN_VMEM] * len(arrays),
        out_specs=(IN_VMEM,) * len(outs),
        scratch_shapes=[
            pltpu.VMEM((depth, 2, 2, rows, own), bf16),
            pltpu.VMEM((width, span), bf16),
            pltpu.VMEM((count, heads_width), bf16),
            pltpu.VMEM((count, heads_width), bf16),
            pltpu.VMEM((span, heads_width), bf16),
            pltpu.VMEM((span, heads_width), bf16),
            pltpu.VMEM((reach + 1, count, width), bf16),
            pltpu.VMEM((reach + 1, count, width // 2), bf16),
            pltpu.VMEM((reach + 1, count, width // 2), bf16),
            pltpu.VMEM((reach, count, width // 2), bf16),
            pltpu.VMEM((rows, LANES), f32),
        ] + scatter_scratch(depth, rows, half, parts) + [
            dma(reach), dma(reach), dma(reach + 1), dma(reach + 1), dma(2), dma(2),
        ] + extra,
        compiler_params=comm_params(4, 58 << 20),
        name="attention_backward",
    )(*arrays)


def scatter_scratch(depth, rows, half, parts):
    first = pltpu.VMEM((depth, 2, rows, half), bf16)
    second = pltpu.VMEM((depth, rows, half), bf16)
    return [
        first, first, second, second, pltpu.VMEM((depth - 1, 2, rows, half), bf16),
        dma(parts, 4), dma(parts, 4), dma(parts, 2, depth - 1), dma(parts, 2, depth - 1),
    ]


class Plane:
    def __init__(self, me):
        z, y, x = digits(me)
        self.place = y * 2 + x
        self.places, self.peers = [self.place], []
        for j in range(1, PLANE):
            y_j, x_j = (1 - y if j & 2 else y), (1 - x if j & 1 else x)
            self.places.append(y_j * 2 + x_j)
            self.peers.append({"dp": index_of(z, y_j, x_j)})


def z_neighbours(me, n):
    return {"dp": lax.rem(me + PLANE, n)}, {"dp": lax.rem(me + n - PLANE, n)}


class Gather:
    def __init__(self, depth, chunks, shard, full, semaphores):
        self.depth, self.chunks, self.shard, self.full = depth, chunks, shard, full
        self.z_send, self.z_recv, self.p_send, self.p_recv = semaphores
        self.z, self.y, self.x = digits(lax.axis_index("dp"))
        self.z_peers, self.y_peer, self.x_peer = grid_peers(depth, self.z, self.y, self.x)
        self.ones, self.twos, self.threes = {}, {}, {}

    def _sides(self, c):
        at, left, right = self.chunks[c]
        return pl.ds(at, left), pl.ds(at + left, right)

    def first(self, c):
        at, left, right = self.chunks[c]
        columns = pl.ds(at, left + right)
        self.ones[c] = [
            push(
                self.shard.at[:, columns],
                self.full.at[self.z, self.y, self.x, :, columns],
                self.z_send.at[c, k], self.z_recv.at[c, k], self.z_peers[k],
            )
            for k in range(self.depth - 1)
        ]

    def second(self, c):
        left, right = self._sides(c)
        for copy in self.ones[c]:
            copy.wait_recv()
        a = self.full.at[:, self.y, self.x, :, left]
        b = self.full.at[:, self.y, self.x, :, right]
        self.twos[c] = [
            push(a, a, self.p_send.at[c, 0], self.p_recv.at[c, 0], self.y_peer),
            push(b, b, self.p_send.at[c, 1], self.p_recv.at[c, 1], self.x_peer),
        ]

    def third(self, c):
        left, right = self._sides(c)
        for copy in self.twos[c]:
            copy.wait_recv()
        a = self.full.at[:, :, self.x, :, left]
        b = self.full.at[:, self.y, :, :, right]
        self.threes[c] = [
            push(a, a, self.p_send.at[c, 2], self.p_recv.at[c, 2], self.x_peer),
            push(b, b, self.p_send.at[c, 3], self.p_recv.at[c, 3], self.y_peer),
        ]

    def finish(self, c):
        for copy in self.threes[c]:
            copy.wait_recv()

    def plan(self, lead):
        count = len(self.chunks)
        steps = []
        for s in range(count + 2):
            if s < count:
                steps.append((self.second, s))
                if s + lead < count:
                    steps.append((self.first, s + lead))
            if 1 <= s <= count:
                steps.append((self.third, s - 1))
            if s >= 2:
                steps.append((self.finish, s - 2))
        return steps

    def drain(self):
        for copies in list(self.ones.values()) + list(self.twos.values()) + list(self.threes.values()):
            for copy in copies:
                copy.wait_send()


def stacked(ref, columns):
    rows = ref.shape[3]
    if rows % 16 == 0:
        return ref[:, :, :, :, columns].reshape(-1, columns.size)
    blocks = [
        ref[b // PLANE, (b // 2) % 2, b % 2, :, columns].astype(f32)
        for b in range(ref.shape[0] * PLANE)
    ]
    return jnp.concatenate(blocks, axis=0).astype(bf16)


def turn(values, cos, sin):
    return values * cos + swap_halves(values) * sin


def forward_kernel(
    depth, reach, experts, chunks, near_edges, small, w_query, w_key, w_value, out_shard, w_sgate, w_sup, down_shard,
    tokens, cotangent, routes, segments, row_cos, row_sin, block_cos, block_sin,
    full, near, window, q, k, v, lse, heads_out, cosines, sines, bias, gains, middle, branch_in, probs, gates, pick,
    *rest,
):
    n = depth * PLANE
    fused = n == experts
    if fused:
        got, got_gate, rows_send, gate_send, d_send, d_recv, e_send, e_recv, g_send, g_recv = (
            rest[:2] + rest[-8:]
        )
        rest = rest[2:-8]
        rows_out, d_rows_out = rows_send.at[0], rows_send.at[1]
    else:
        rows_out, d_rows_out = rest[:2]
        rest = rest[2:]
    (
        shard, attn_in, part, other,
        z_send, z_recv, p_send, p_recv, t_send, t_recv, f_send, f_recv, s_send, s_recv, own,
    ) = rest
    me, core = lax.axis_index("dp"), lax.axis_index("tensor")
    sibling = {"tensor": 1 - core}
    gather = Gather(depth, chunks, shard, full, (z_send, z_recv, p_send, p_recv))
    heads_width = q.shape[1]
    pairs = heads_width // LANES
    at = 0
    order = [(small, 0, LANES)]
    for pair in range(pairs):
        order += [(piece, pair * LANES, LANES) for piece in (w_query, w_key, w_value)]
    order += [(piece, 0, piece.shape[1]) for piece in (out_shard, w_sgate, w_sup, down_shard)]
    for piece, start, size in order:
        shard[:, pl.ds(at, size)] = piece[:, pl.ds(start, size)].astype(bf16)
        at += size
    plane, z_next, z_before = Plane(me), *z_neighbours(me, n)
    if fused:
        greet([{"dp": lax.rem(me + i, n)} for i in range(1, n)] + [sibling])
    else:
        greet(gather.z_peers + plane.peers + [sibling, z_next, z_before])
    count, width = tokens.shape
    half = count // 2
    rows = pl.ds(pl.multiple_of(core * half, half), half)
    from_before = push(tokens.at[rows], window.at[0, rows], t_send.at[0], t_recv.at[0], z_next)
    lead = 3
    for c in range(lead):
        gather.first(c)
    own_shard = pltpu.make_async_copy(shard, full.at[gather.z, gather.y, gather.x], own.at[0])
    own_shard.start()
    window[reach] = tokens[...]

    lane = lax.broadcasted_iota(jnp.int32, (1, LANES), 1)
    sign = jnp.where(lax.rem(lane, HEAD) < HEAD // 2, -1.0, 1.0)
    seg_query = segments[pl.ds(me, 1), :].astype(f32)
    key_place = lax.broadcasted_iota(jnp.int32, (count, count), 0)
    query_place = lax.broadcasted_iota(jnp.int32, (count, count), 1)
    for b in range(reach + 1):
        at = pl.ds(b * count, count)
        c_b, s_b = block_cos[pl.ds(me + b, 1), :], block_sin[pl.ds(me + b, 1), :]
        cosines[at, :] = c_b * row_cos[...] - s_b * row_sin[...]
        sines[at, :] = (s_b * row_cos[...] + c_b * row_sin[...]) * sign
        block = me - reach + b
        seg_key = segments[pl.ds(lax.max(block, 0), 1), :].astype(f32)
        seg_key = jnp.broadcast_to(seg_key, (LANES, count)).T[:, :1]
        distance = (reach - b) * count + query_place - key_place
        limit = lax.select(block >= 0, WINDOW, 0)
        seen = (distance >= 0) & (distance < limit) & (seg_key == seg_query)
        bias[at, :] = jnp.where(seen, 0.0, masked)

    capacity = rows_out.shape[1]
    named = [(routes[:, i : i + 1] == lane).astype(f32) for i in range(routes.shape[1])]
    below = (key_place > query_place).astype(f32).astype(bf16)
    before = matmul(below, sum(named).astype(bf16))
    slot_of = lax.broadcasted_iota(jnp.int32, (count, experts * capacity), 1)
    for i, name in enumerate(named):
        place = jnp.sum(name * before, axis=-1, keepdims=True).astype(jnp.int32)
        place = place + routes[:, i : i + 1] * capacity
        pick[i] = (slot_of == place).astype(f32).astype(bf16)
    features = pl.ds(pl.multiple_of(core * (width // 2), width // 2), width // 2)
    sent, passed = {}, {}

    def dispatch_rows(a):
        for i in range(1, n):
            to = lax.rem(me + i, n)
            sent[a, i] = push(
                rows_send.at[a, to, :, features], got.at[a, i, :, features],
                d_send.at[a, i], d_recv.at[a, i], {"dp": to},
            )
        got[a, 0] = rows_send[a, me]

    def forward_rows(a):
        for i in range(1, n):
            sent[a, i].wait_recv()
            block = got.at[a, i, :, features]
            passed[a, i] = push(block, block, e_send.at[a, i], e_recv.at[a, i], sibling)

    if fused:
        rows_send[1] = (
            weight_grad(pick[0] + pick[1], cotangent[...]).astype(bf16).reshape(rows_out.shape)
        )

    def normed(b):
        values = window[b].astype(f32)
        return values * lax.rsqrt(jnp.mean(values * values, axis=-1, keepdims=True) + eps)

    own_shard.wait()
    steps = gather.plan(lead)
    done = [0]

    def advance(until=None, waits=None):
        while done[0] < len(steps) and waits != 0:
            action, c = steps[done[0]]
            done[0] += 1
            action(c)
            if waits is not None and action != gather.first:
                waits -= 1
            if (action, c) == until:
                break

    from_before.wait_recv()
    t_copies = [from_before]
    for j in range(1, PLANE):
        source = window.at[lax.select(plane.places[j] < plane.place, 0, reach), rows]
        target = window.at[lax.rem(plane.place - plane.places[j] + PLANE, PLANE), rows]
        t_copies.append(push(source, target, t_send.at[j], t_recv.at[j], plane.peers[j - 1]))
    advance((gather.second, 1))
    forwards = []
    for j, copy in enumerate(t_copies):
        if j:
            copy.wait_recv()
        block = window.at[lax.rem(plane.places[j] - plane.place + PLANE, PLANE), rows]
        forwards.append(push(block, block, f_send.at[j], f_recv.at[j], sibling))
    landed = 0
    copies = []
    for i, (edge, c) in enumerate(near_edges):
        copies.append((c, pl.ds(landed, edge - landed), own.at[1 + i]))
        landed = edge

    def land(i):
        c, columns, semaphore = copies[i]
        advance((gather.finish, c))
        copy = pltpu.make_async_copy(
            full.at[:, :, :, :, columns], near.at[:, :, :, :, columns], semaphore
        )
        copy.start()
        copy.wait()

    land(0)
    if fused:
        dispatch_rows(1)
    for copy in forwards:
        copy.wait_recv()
    small_all = stacked(near, pl.ds(0, LANES))
    small_turned = small_all.astype(f32).T
    gain_first, gain_second = small_turned[experts : experts + 1, :], small_turned[experts + 1 : experts + 2, :]
    gains[...] = small_turned[experts : experts + 8, :]
    own_rows = pl.ds(reach * count, count)
    for b in range(reach + 1):
        attn_in[pl.ds(b * count, count), :] = (normed(b) * gain_first).astype(bf16)
    lse[...] = jnp.zeros_like(lse)
    for pair in range(pairs):
        if pair:
            land(pair)
        at = LANES * (1 + 3 * pair)
        columns = pl.ds(pair * LANES, LANES)
        products = matmul(attn_in[...], stacked(near, pl.ds(at + LANES, 2 * LANES)))
        k_pair = turn(products[:, :LANES], cosines[...], sines[...]).astype(bf16)
        v_pair = products[:, LANES:].astype(bf16)
        queries = matmul(attn_in[own_rows, :], stacked(near, pl.ds(at, LANES)))
        q_pair = (
            turn(queries, cosines[own_rows, :], sines[own_rows, :]) * (HEAD ** (-0.5))
        ).astype(bf16)
        k[:, columns], v[:, columns], q[:, columns] = k_pair, v_pair, q_pair
        v_turned = v_pair.T
        outs = []
        for part_of in range(2):
            head = 2 * pair + part_of
            scores = input_grad(k_pair, q_pair * lanes_of(part_of)) + bias[...]
            peak = jnp.max(scores, axis=0, keepdims=True)
            expo = jnp.exp(scores - peak)
            total = jnp.sum(expo, axis=0, keepdims=True)
            lse[head : head + 1, :] = peak + jnp.log(total)
            weights = (expo * (1.0 / total)).astype(bf16)
            outs.append(matmul(v_turned, weights)[part_of * HEAD : (part_of + 1) * HEAD, :])
            advance(waits=1)
        heads_out[:, columns] = jnp.concatenate(outs, axis=0).T.astype(bf16)
    land(pairs)
    out_w = stacked(near, pl.ds(LANES + 3 * heads_width, heads_width))
    part[...] = input_grad(heads_out[...], out_w).astype(bf16)
    swapped = push(part, other, s_send.at[0], s_recv.at[0], sibling)
    swapped.wait()
    middle_all = tokens[...].astype(f32) + (part[...].astype(f32) + other[...].astype(f32))
    middle[...] = middle_all
    factor = lax.rsqrt(jnp.mean(middle_all * middle_all, axis=-1, keepdims=True) + eps)
    branch = (middle_all * factor * gain_second).astype(bf16)
    branch_in[...] = branch

    logits = jnp.where(lane < experts, matmul(branch, small_all), masked)
    expo = jnp.exp(logits - jnp.max(logits, axis=-1, keepdims=True))
    chance = expo / jnp.sum(expo, axis=-1, keepdims=True)
    probs[...] = chance
    gate_lanes = jnp.zeros((count, LANES), f32)
    gate_row = jnp.zeros((1, experts * capacity), f32)
    d_gathered = None if fused else jnp.zeros((experts * capacity, width), f32)
    for i, name in enumerate(named):
        gate = jnp.sum(chance * name, axis=-1, keepdims=True)
        gate_lanes = gate_lanes + jnp.where(lane == i, gate, 0.0)
        if fused:
            gate_row = gate_row + jnp.sum(gate * pick[i].astype(f32), axis=0, keepdims=True)
        else:
            d_rows = (gate * cotangent[...].astype(f32)).astype(bf16)
            d_gathered = d_gathered + weight_grad(pick[i], d_rows)
    gates[...] = gate_lanes
    if fused:
        gate_send[...] = jnp.zeros_like(gate_send)
        for e in range(experts):
            gate_send[e, 0:1, :capacity] = gate_row[:, e * capacity : (e + 1) * capacity]
    else:
        d_rows_out[...] = d_gathered.astype(bf16).reshape(d_rows_out.shape)
    rows_out[...] = weight_grad(pick[0] + pick[1], branch).astype(bf16).reshape(rows_out.shape)
    gate_sent = []
    if fused:
        dispatch_rows(0)
        for i in range(1, n):
            to = lax.rem(me + i, n)
            gate_sent.append(
                push(gate_send.at[to], got_gate.at[i], g_send.at[i], g_recv.at[i], {"dp": to})
            )
        got_gate[0] = gate_send[me]
        advance(waits=4)
        forward_rows(1)
        advance(waits=5)
        forward_rows(0)
    advance()
    if fused:
        for copy in gate_sent:
            copy.wait_recv()
        for copy in passed.values():
            copy.wait_recv()
        for copy in list(sent.values()) + list(passed.values()) + gate_sent:
            copy.wait_send()
    gather.drain()
    for copy in t_copies + forwards:
        copy.wait_send()


def angle_tables(tok_count, blocks, reach):
    freqs = (10000.0 ** (-np.arange(HEAD // 2, dtype=np.float32) * np.float32(2.0 / HEAD))).astype(np.float64)
    freqs = np.tile(freqs, LANES // (HEAD // 2))[None, :]
    inner = np.arange(tok_count)[:, None] * freqs
    starts = np.maximum(np.arange(-reach, blocks), 0) * tok_count
    starts = np.pad(starts, (0, -len(starts) % 8))[:, None] * freqs
    return [jnp.asarray(f(a), f32) for a in (inner, starts) for f in (np.cos, np.sin)]


def forward(arrays, tokens, cotangent, routes, segments, depth, reach, experts, heads_width, hidden):
    count, width = tokens.shape
    n = depth * PLANE
    rows = arrays[0].shape[0]
    span = (reach + 1) * count
    near_width = LANES + 4 * heads_width
    columns = near_width + 3 * hidden
    capacity = count // 4
    step = 4 * LANES
    pairs = heads_width // LANES
    widths = [step] + [3 * LANES] * (pairs - 1) + [heads_width] + [step] * ((columns - near_width) // step)
    chunks, at = [], 0
    for w in widths:
        left = (w // LANES + (len(chunks) + 1) % 2) // 2 * LANES
        chunks.append((at, left, w - left))
        at += w
    near_edges = tuple((sum(widths[: c + 1]), c) for c in range(pairs + 1))
    parts = len(chunks)
    tables = angle_tables(count, n, reach)
    segment_rows = segments.reshape(-1, count)

    def shape(*dims, dtype=bf16):
        return jax.ShapeDtypeStruct(dims, dtype)

    outs = (
        shape(depth, 2, 2, rows, columns),
        shape(depth, 2, 2, rows, near_width),
        shape(reach + 1, count, width),
        shape(count, heads_width), shape(span, heads_width), shape(span, heads_width),
        shape(-(-heads_width // HEAD // 8) * 8, count, dtype=f32),
        shape(count, heads_width),
        shape(span, LANES, dtype=f32), shape(span, LANES, dtype=f32), shape(span, count, dtype=f32),
        shape(8, width, dtype=f32),
        shape(count, width, dtype=f32), shape(count, width),
        shape(count, LANES, dtype=f32), shape(count, LANES, dtype=f32),
        shape(routes.shape[1], count, experts * capacity),
    )
    if n == experts:
        outs += (shape(2, n, capacity, width), shape(n, 8, LANES, dtype=f32))
        extra = [
            pltpu.VMEM((2, n, capacity, width), bf16), pltpu.VMEM((n, 8, LANES), f32),
            dma(2, n), dma(2, n), dma(2, n), dma(2, n), dma(n), dma(n),
        ]
    else:
        outs += (shape(experts, capacity, width), shape(experts, capacity, width))
        extra = []
    inputs = list(arrays) + [tokens, cotangent, routes, segment_rows, tables[0], tables[1], tables[2], tables[3]]
    return pl.pallas_call(
        functools.partial(forward_kernel, depth, reach, experts, tuple(chunks), near_edges),
        out_shape=outs,
        in_specs=[IN_VMEM] * len(inputs),
        out_specs=(IN_HBM,) + (IN_VMEM,) * (len(outs) - 1),
        scratch_shapes=[
            pltpu.VMEM((rows, columns), bf16),
            pltpu.VMEM((span, width), bf16),
            pltpu.VMEM((count, width), bf16),
            pltpu.VMEM((count, width), bf16),
            dma(parts, depth - 1), dma(parts, depth - 1), dma(parts, 4), dma(parts, 4),
            dma(reach), dma(reach), dma(reach), dma(reach), dma(1), dma(1), dma(2 + pairs),
        ] + extra,
        compiler_params=comm_params(1, 58 << 20),
        name="gather_and_attend",
    )(*inputs)


def local(
    tokens, cotangent, attn_gain, w_query, w_key, w_value, w_out, ffn_gain, w_router,
    w_sgate, w_sup, w_sdown, e_gate, e_up, e_down, routes, segments,
):
    tok_count, width = tokens.shape
    n = lax.axis_size("dp")
    depth = n // PLANE
    me = lax.axis_index("dp")
    core = lax.axis_index("tensor")
    experts = w_router.shape[1]
    owners = n // experts
    capacity = tok_count // 4
    reach = (WINDOW + tok_count - 1) // tok_count
    shard_rows = w_query.shape[0]
    heads_width = w_query.shape[1]
    hidden = w_sgate.shape[1]
    half = width // 2

    small = jnp.pad(
        jnp.concatenate([w_router, attn_gain[:, None], ffn_gain[:, None]], axis=1),
        ((0, 0), (0, LANES - experts - 2)),
    )
    near_width = LANES + 4 * heads_width
    own_columns = near_width + LANES
    (
        full, near, window, queries, all_keys, all_values, lse, heads_out, cosines, sines, bias, gains,
        middle, branch_in, probs, gates, pick, *sent_rows,
    ) = forward(
        (small, w_query, w_key, w_value, w_out.T, w_sgate, w_sup, w_sdown.T),
        tokens, cotangent, routes, segments, depth, reach, experts, heads_width, hidden,
    )
    x_float = tokens.astype(f32)
    normed_one, scale_one = rms_parts(x_float)
    gain_first, gain_second = gains[0], gains[1]
    blocks = (depth, 2, 2, shard_rows)
    if owners == 1:
        d_middle, shared_total, small_grads, shared_part, rows_back, expert_grads = experts_fused(
            *sent_rows, (e_gate, e_up, e_down), full, branch_in, cotangent, middle, probs,
            pick, routes, gains, near, depth, hidden,
        )
        shared_grads, combine = (), (rows_back, pick, gates, middle, shared_part)
    else:
        sgate_w, sup_w, sdown_t = (
            full[:, :, :, :, near_width + i * hidden : near_width + (i + 1) * hidden].reshape(width, hidden)
            for i in range(3)
        )
        router_w = near[:, :, :, :, :experts].reshape(width, experts)
        expert_gate = e_gate.astype(bf16)
        expert_up = e_up.astype(bf16)
        expert_down = e_down.astype(bf16)
        normed_two, scale_two = rms_parts(middle)
        probs = probs[:, :experts]
        picked = (routes[:, :, None] == jnp.arange(experts, dtype=jnp.int32)[None, None, :]).astype(f32)
        d_after = cotangent.astype(f32)
        combine = ()
        rows_in, d_rows_in = dispatch(*sent_rows, n, owners)

        rows_in = rows_in.reshape(n * capacity, width)
        d_rows_in = d_rows_in.reshape(n * capacity, width)
        gate_hidden = matmul(rows_in, expert_gate)
        up_hidden = matmul(rows_in, expert_up)
        gate_act = jax.nn.silu(gate_hidden)
        expert_hidden = (gate_act * up_hidden).astype(bf16)
        part_rows = matmul(expert_hidden, expert_down).astype(bf16)
        d_hidden = input_grad(d_rows_in, expert_down)
        d_gate_hidden = (d_hidden * up_hidden * silu_grad(gate_hidden)).astype(bf16)
        d_up_hidden = (d_hidden * gate_act).astype(bf16)
        d_part_rows = (
            input_grad(d_gate_hidden, expert_gate) + input_grad(d_up_hidden, expert_up)
        ).astype(bf16)
        returned, d_returned = give_back(
            part_rows.reshape(n, capacity, width), d_part_rows.reshape(n, capacity, width)
        )
        grad_e_down = weight_grad(expert_hidden, d_rows_in)
        grad_e_gate = weight_grad(rows_in, d_gate_hidden)
        grad_e_up = weight_grad(rows_in, d_up_hidden)

        shared_gate = matmul(branch_in, sgate_w)
        shared_up = matmul(branch_in, sup_w)
        shared_act = jax.nn.silu(shared_gate)
        shared_hidden = (shared_act * shared_up).astype(bf16)
        shared_part = input_grad(shared_hidden, sdown_t)
        d_shared = matmul(cotangent, sdown_t)
        grad_sdown_t = weight_grad(cotangent, shared_hidden)
        d_sgate = (d_shared * shared_up * silu_grad(shared_gate)).astype(bf16)
        d_sup = (d_shared * shared_act).astype(bf16)
        grad_sgate = weight_grad(branch_in, d_sgate)
        grad_sup = weight_grad(branch_in, d_sup)
        d_shared_in = input_grad(d_sgate, sgate_w) + input_grad(d_sup, sup_w)

        def incoming(rows):
            rows = rows.reshape(experts, owners, capacity, half)
            if owners > 1:
                rows = jnp.sum(rows.astype(f32), axis=1).astype(bf16)
            return rows.reshape(experts * capacity, half)

        def placed(values):
            own = jnp.concatenate([values, jnp.zeros_like(values)], axis=1)
            other = jnp.concatenate([jnp.zeros_like(values), values], axis=1)
            return jnp.where(core == 0, own, other)

        result_rows, d_result_rows = incoming(returned), incoming(d_returned)
        pair_out = [matmul(pick[k], result_rows) for k in range(pick.shape[0])]
        d_pairs = matmul(pick[0] + pick[1], d_result_rows)
        moe_half = sum(gates[:, k : k + 1] * pair_out[k] for k in range(pick.shape[0]))
        d_half = lax.dynamic_slice_in_dim(cotangent, core * half, half, axis=1).astype(f32)
        d_gates_part = jnp.concatenate(
            [jnp.sum(d_half * p, axis=1, keepdims=True) for p in pair_out], axis=1
        )
        after_part = (placed(moe_half) + shared_part).astype(bf16)
        d_branch_part = (d_shared_in + placed(d_pairs)).astype(bf16)
        d_gates_part = jnp.pad(d_gates_part, ((0, 0), (0, LANES - pick.shape[0])))
        after_other, d_branch_other, d_gates_other = swap(
            [after_part, d_branch_part, d_gates_part], 6
        )
        output = (middle + (after_part.astype(f32) + after_other.astype(f32))).astype(bf16)
        d_branch_sum = d_branch_part.astype(f32) + d_branch_other.astype(f32)
        d_gates = (d_gates_part + d_gates_other)[:, : pick.shape[0]]
        d_probs = jnp.sum(d_gates[:, :, None] * picked, axis=1)
        d_logits = (probs * (d_probs - jnp.sum(probs * d_probs, axis=-1, keepdims=True))).astype(bf16)
        grad_router = weight_grad(branch_in, d_logits)
        d_branch_in = d_branch_sum + input_grad(d_logits, router_w)
        grad_gain_two = jnp.sum(d_branch_in * normed_two, axis=0)
        d_norm_two = d_branch_in * gain_second
        d_middle = d_after + scale_two * (
            d_norm_two - normed_two * jnp.mean(d_norm_two * normed_two, axis=-1, keepdims=True)
        )

        shared_grads = [
            value.astype(bf16).reshape(blocks + (hidden,)) for value in (grad_sgate, grad_sup, grad_sdown_t)
        ]
        small_grads = jnp.concatenate(
            [grad_router, grad_gain_two[:, None], jnp.zeros((width, LANES - experts - 1), f32)], axis=1
        ).astype(bf16).reshape(blocks + (LANES,))
        expert_grads = [grad_e_gate, grad_e_up, grad_e_down]
    total, d_attn_in, *combined = backward(
        [
            small_grads,
            window, queries, all_keys, all_values, lse, heads_out,
            d_middle.astype(bf16), near, gains, cosines, sines, bias,
        ],
        shared_grads, combine, shard_rows, own_columns + (3 * hidden if shared_grads else 0),
        tok_count, heads_width, width, depth, reach,
    )
    if shared_grads:
        shared_total, total = total[:, : 3 * hidden], total[:, 3 * hidden :]
    if combined:
        output = combined[0]

    def columns_of(at, count):
        return total[:, at : at + count]

    at_out = 0
    at_pairs = at_out + heads_width + LANES
    grad_parts = [
        jnp.concatenate(
            [
                columns_of(at_pairs + (3 * pair + i) * LANES, LANES)
                for pair in range(heads_width // LANES)
            ],
            axis=1,
        )
        for i in range(3)
    ]
    d_attn_in = d_attn_in.astype(f32)
    d_norm_one = d_attn_in * gain_first
    token_input_gradient = d_middle + scale_one * (
        d_norm_one - normed_one * jnp.mean(d_norm_one * normed_one, axis=-1, keepdims=True)
    )
    return (
        output,
        token_input_gradient,
        total[:, own_columns - LANES],
        grad_parts[0],
        grad_parts[1],
        grad_parts[2],
        columns_of(at_out, heads_width).T,
        total[:, at_out + heads_width + experts],
        columns_of(at_out + heads_width, experts),
        shared_total[:, :hidden],
        shared_total[:, hidden : 2 * hidden],
        shared_total[:, 2 * hidden :].T,
    ) + tuple(expert_grads)


def solution(mesh):
    by_dp, both, turned = P("dp", None), P("dp", "tensor"), P("tensor", "dp")
    wide, tall = P(None, ("dp", "tensor")), P(("dp", "tensor"), None)
    weights = (P("dp"), both, both, both, turned, P("dp"), by_dp, both, both, turned, wide, wide, tall)
    return jax.shard_map(
        local,
        mesh=mesh,
        in_specs=(by_dp, by_dp) + weights + (by_dp, P()),
        out_specs=(by_dp, by_dp) + weights,
        check_vma=False,
    )
```

```python
import functools

import jax
import jax.numpy as jnp
import numpy as np
from jax import lax
from jax.experimental import pallas as pl
from jax.experimental.pallas import tpu as pltpu
from jax.sharding import PartitionSpec as P

HEAD = 64
WINDOW = 1024
LANES = 128
PLANE = 4

MESH = pl.DeviceIdType.MESH
f32 = jnp.float32
bf16 = jnp.bfloat16

eps = 1e-06
masked = -1e30


def matmul(left, right):
    return jnp.dot(left, right, preferred_element_type=f32)


def weight_grad(left, right):
    return lax.dot_general(
        left, right, (((0,), (0,)), ((), ())), preferred_element_type=f32
    )


def input_grad(left, right):
    return lax.dot_general(
        left, right, (((1,), (1,)), ((), ())), preferred_element_type=f32
    )


def rms_parts(values):
    factor = lax.rsqrt(jnp.mean(values * values, axis=-1, keepdims=True) + eps)
    return (values * factor, factor)


def silu_grad(values):
    sigma = jax.nn.sigmoid(values)
    return sigma * (1.0 + values * (1.0 - sigma))


def digits(me):
    return lax.div(me, PLANE), lax.rem(lax.div(me, 2), 2), lax.rem(me, 2)


def index_of(z, y, x):
    return z * PLANE + y * 2 + x


def push(src, dst, send, recv, device):
    copy = pltpu.make_async_remote_copy(
        src_ref=src,
        dst_ref=dst,
        send_sem=send,
        recv_sem=recv,
        device_id=device,
        device_id_type=MESH,
    )
    copy.start()
    return copy


def greet(devices):
    barrier = pltpu.get_barrier_semaphore()
    for device in devices:
        pl.semaphore_signal(barrier, inc=1, device_id=device, device_id_type=MESH)
    pl.semaphore_wait(barrier, len(devices))


def comm_params(collective_id, limit=48 << 20):
    return pltpu.CompilerParams(
        collective_id=collective_id, has_side_effects=True, vmem_limit_bytes=limit
    )


def dma(*shape):
    return pltpu.SemaphoreType.DMA(shape)


IN_HBM = pl.BlockSpec(memory_space=pl.ANY)
IN_VMEM = pl.BlockSpec(memory_space=pltpu.VMEM)


def grid_peers(depth, z, y, x):
    peers = [{"dp": index_of(lax.rem(z + k, depth), y, x)} for k in range(1, depth)]
    return peers, {"dp": index_of(z, 1 - y, x)}, {"dp": index_of(z, y, 1 - x)}


def swap_kernel(count, *refs):
    sources, targets, (send, recv) = refs[:count], refs[count : 2 * count], refs[2 * count :]
    sibling = {"tensor": 1 - lax.axis_index("tensor")}
    greet([sibling])
    copies = [
        push(a, b, send.at[i], recv.at[i], sibling)
        for i, (a, b) in enumerate(zip(sources, targets))
    ]
    for copy in copies:
        copy.wait()


def swap(arrays, collective_id):
    count = len(arrays)
    return pl.pallas_call(
        functools.partial(swap_kernel, count),
        out_shape=tuple(jax.ShapeDtypeStruct(a.shape, a.dtype) for a in arrays),
        in_specs=[IN_VMEM] * count,
        out_specs=(IN_VMEM,) * count,
        scratch_shapes=[dma(count), dma(count)],
        compiler_params=comm_params(collective_id),
        name="swap_cores",
    )(*arrays)


def dispatch_kernel(n, owners, first, second, got_first, got_second, send, recv, f_send, f_recv, own):
    me, core = lax.axis_index("dp"), lax.axis_index("tensor")
    sibling = {"tensor": 1 - core}
    greet([{"dp": lax.rem(me + k, n)} for k in range(1, n)] + [sibling])
    half = first.shape[-1] // 2
    cols = pl.ds(pl.multiple_of(core * half, half), half)
    pairs = ((first, got_first), (second, got_second))
    mine = lax.div(me, owners)
    copies = []
    for k in range(1, n):
        to = lax.rem(me + k, n)
        for i, (source, target) in enumerate(pairs):
            copies.append(
                push(
                    source.at[lax.div(to, owners), :, cols],
                    target.at[me, :, cols],
                    send.at[i, k],
                    recv.at[i, k],
                    {"dp": to},
                )
            )
    local = [
        pltpu.make_async_copy(source.at[mine], target.at[me], own.at[i])
        for i, (source, target) in enumerate(pairs)
    ]
    for copy in local:
        copy.start()
    forwards = []
    for k in range(1, n):
        source_of = lax.rem(me + n - k, n)
        for i, (source, target) in enumerate(pairs):
            copies[2 * (k - 1) + i].wait_recv()
            block = target.at[source_of, :, cols]
            forwards.append(push(block, block, f_send.at[i, k], f_recv.at[i, k], sibling))
    for copy in forwards:
        copy.wait_recv()
    for copy in local:
        copy.wait()
    for copy in copies + forwards:
        copy.wait_send()


def dispatch(first, second, n, owners):
    shape = jax.ShapeDtypeStruct((n,) + first.shape[1:], first.dtype)
    return pl.pallas_call(
        functools.partial(dispatch_kernel, n, owners),
        out_shape=(shape, shape),
        in_specs=[IN_HBM] * 2,
        out_specs=(IN_HBM, IN_HBM),
        scratch_shapes=[dma(2, n), dma(2, n), dma(2, n), dma(2, n), dma(2)],
        compiler_params=comm_params(2),
        name="dispatch_rows",
    )(first, second)


def return_kernel(n, groups, first, second, got_first, got_second, part, total, send, recv, f_send, f_recv, own):
    me, core = lax.axis_index("dp"), lax.axis_index("tensor")
    sibling = {"tensor": 1 - core}
    greet([{"dp": lax.rem(me + k, n)} for k in range(1, n)] + [sibling])
    half = first.shape[-1] // 2
    mine = pl.ds(pl.multiple_of(core * half, half), half)
    theirs = pl.ds(pl.multiple_of((1 - core) * half, half), half)
    pairs = ((first, got_first), (second, got_second))
    each = n // groups
    swaps = []
    for g in range(groups):
        block = pl.ds(g * each, each)
        for i, (source, target) in enumerate(pairs):
            swaps.append(
                push(
                    source.at[block, :, theirs],
                    part.at[i, block],
                    f_send.at[i, g],
                    f_recv.at[i, g],
                    sibling,
                )
            )
    for g in range(groups):
        block = pl.ds(g * each, each)
        for i, (source, target) in enumerate(pairs):
            swaps[2 * g + i].wait_recv()
            total[i, block] = (
                source[block, :, mine].astype(f32) + part[i, block].astype(f32)
            ).astype(bf16)
        for slot in range(g * each, (g + 1) * each):
            for i, (source, target) in enumerate(pairs):
                @pl.when(slot != me)
                def _():
                    push(
                        total.at[i, slot],
                        target.at[me],
                        send.at[i, slot],
                        recv.at[i, me],
                        {"dp": slot},
                    )
    local = [
        pltpu.make_async_copy(total.at[i, me], pairs[i][1].at[me], own.at[i]) for i in range(2)
    ]
    for copy in local:
        copy.start()
    for k in range(1, n):
        to, source_of = lax.rem(me + k, n), lax.rem(me + n - k, n)
        for i, (source, target) in enumerate(pairs):
            pltpu.make_async_remote_copy(
                total.at[i, to], target.at[source_of], send.at[i, to], recv.at[i, source_of],
                device_id={"dp": to}, device_id_type=MESH,
            ).wait()
    for copy in local:
        copy.wait()
    for copy in swaps:
        copy.wait_send()


def give_back(first, second, groups=4):
    n, capacity, width = first.shape
    half = jax.ShapeDtypeStruct((n, capacity, width // 2), first.dtype)
    buffer = pltpu.VMEM((2, n, capacity, width // 2), first.dtype)
    return pl.pallas_call(
        functools.partial(return_kernel, n, groups),
        out_shape=(half, half),
        in_specs=[IN_VMEM] * 2,
        out_specs=(IN_HBM, IN_HBM),
        scratch_shapes=[buffer, buffer, dma(2, n), dma(2, n), dma(2, groups), dma(2, groups), dma(2)],
        compiler_params=comm_params(3),
        name="return_rows",
    )(first, second)


def experts_kernel(
    n, groups, e_gate, e_up, e_down, full, got, got_gate, branch_in, cotangent, middle, probs, pick,
    routes, gains, small,
    d_middle, shared_total, g_small, shared_part, rows_total, ge_gate, ge_up, ge_down,
    d_rows_all, gate_w, up_w, down_w, staged, shared_w, hid, d_gate, d_up, part, swapped, d_total, returned,
    inner, inner_back, shared_in, tiles, wide, ends, ends_other, d_gates, d_gates_other,
    first_l, first_r, second_l, second_r, scatter_last, p_send, p_recv, z_send, z_recv,
    s_send, s_recv, r_send, r_recv, i_send, i_recv, e_send, e_recv, own, load, store,
):
    me, core = lax.axis_index("dp"), lax.axis_index("tensor")
    sibling = {"tensor": 1 - core}
    greet([{"dp": lax.rem(me + i, n)} for i in range(1, n)] + [sibling])
    capacity, width = got.shape[2:]
    count = branch_in.shape[0]
    half = width // 2
    mine = pl.ds(pl.multiple_of(core * half, half), half)
    theirs = pl.ds(pl.multiple_of((1 - core) * half, half), half)
    hidden = shared_w.shape[4] // 3
    loads = [
        pltpu.make_async_copy(
            full.at[:, :, :, :, pl.ds(full.shape[4] - 3 * hidden, 3 * hidden)], shared_w, load.at[2]
        )
    ]
    for copy in loads:
        copy.start()
    inner[...] = jnp.zeros_like(inner)

    step = 2 * LANES
    scatter = Scatter(
        n // PLANE,
        [(shared_w, at, step, shared_w, at + step, step, at) for at in range(0, 3 * hidden, 2 * step)],
        shared_total, (first_l, first_r, second_l, second_r, scatter_last),
        (p_send, p_recv, z_send, z_recv),
    )
    steps = scatter.plan()
    done = [0]

    def advance(count=1):
        for action, c in steps[done[0] : done[0] + count]:
            done[0] += 1
            action(c)
            if action == scatter.second and c + 4 < len(scatter.chunks):
                scatter.start(c + 4)

    pieces = []
    for source, target in ((e_gate, gate_w), (e_up, up_w), (e_down, down_w)):
        step = source.shape[0] // 4
        pieces += [(source, target, pl.ds(j * step, step)) for j in range(4)]

    def fetch(j):
        source, target, rows = pieces[j]
        return pltpu.make_async_copy(
            source.at[rows],
            staged.at[j % 2, pl.ds(0, rows.size), pl.ds(0, source.shape[1])],
            load.at[j % 2],
        )

    fetch(0).start()
    fetch(1).start()

    def take(j):
        source, target, rows = pieces[j]
        fetch(j).wait()
        target[rows, :] = staged[j % 2, : rows.size, : source.shape[1]].astype(bf16)
        if j + 2 < len(pieces):
            fetch(j + 2).start()

    swaps = {}

    def work(group):
        first, each = group * n // groups, n // groups
        slots = pl.ds(first, each)
        rows = pl.ds(first * capacity, each * capacity)
        rows_in = got[0, slots].reshape(each * capacity, width)
        gate_of = jnp.concatenate([got_gate[i].T[:capacity, 0:1] for i in range(first, first + each)], axis=0)
        d_rows = (gate_of * got[1, slots].reshape(each * capacity, width).astype(f32)).astype(bf16)
        d_rows_all[rows, :] = d_rows
        gate, up = matmul(rows_in, gate_w[...]), matmul(rows_in, up_w[...])
        sigma = 1.0 / (1.0 + jnp.exp(-gate))
        act = gate * sigma
        hid_low = (act * up).astype(bf16)
        hid[rows, :] = hid_low
        part[0, slots] = matmul(hid_low, down_w[...]).astype(bf16).reshape(each, capacity, width)
        d_hid = input_grad(d_rows, down_w[...])
        d_gate_low = (d_hid * up * (sigma * (1.0 + gate * (1.0 - sigma)))).astype(bf16)
        d_up_low = (d_hid * act).astype(bf16)
        d_gate[rows, :] = d_gate_low
        d_up[rows, :] = d_up_low
        part[1, slots] = (
            (input_grad(d_gate_low, gate_w[...]) + input_grad(d_up_low, up_w[...]))
            .astype(bf16)
            .reshape(each, capacity, width)
        )
        for a in (1, 0):
            swaps[a, group] = push(
                part.at[a, slots, :, theirs], swapped.at[a, slots],
                s_send.at[a, group], s_recv.at[a, group], sibling,
            )

    back = {}

    def give(group):
        first, each = group * n // groups, n // groups
        slots = pl.ds(first, each)
        swaps[1, group].wait_recv()
        d_total[slots] = (
            part[1, slots, :, mine].astype(f32) + swapped[1, slots].astype(f32)
        ).astype(bf16)
        homes = [{"dp": lax.rem(me + n - i, n)} for i in range(n)]
        for i in range(max(first, 1), first + each):
            back[1, i] = push(
                d_total.at[i], returned.at[me], r_send.at[i], r_recv.at[i], homes[i]
            )
        swaps[0, group].wait_recv()
        value = part[0, slots, :, mine].astype(f32) + swapped[0, slots].astype(f32)
        rows_total[slots] = value.astype(bf16)
        products = jnp.sum(value * got[1, slots, :, mine].astype(f32), axis=-1, keepdims=True)
        for i in range(first, first + each):
            row = jnp.broadcast_to(products[i - first], (capacity, LANES)).T[0:8, :]
            inner[i, :, :capacity] = row
            if i:
                back[0, i] = push(
                    inner.at[i], inner_back.at[me], i_send.at[i], i_recv.at[i], homes[i]
                )

    loads[0].wait()
    branch, cot = branch_in[...], cotangent[...]
    sgate_w, sup_w, sdown_w = (stacked(shared_w, pl.ds(i * hidden, hidden)) for i in range(3))
    gate, up = matmul(branch, sgate_w), matmul(branch, sup_w)
    sigma = 1.0 / (1.0 + jnp.exp(-gate))
    act = gate * sigma
    shared_hid = (act * up).astype(bf16)
    shared_part[...] = input_grad(shared_hid, sdown_w)
    d_shared = matmul(cot, sdown_w)
    d_sgate = (d_shared * up * (sigma * (1.0 + gate * (1.0 - sigma)))).astype(bf16)
    d_sup = (d_shared * act).astype(bf16)
    shared_in[...] = input_grad(d_sgate, sgate_w) + input_grad(d_sup, sup_w)
    for i, (left, right) in enumerate(((branch, d_sgate), (branch, d_sup), (cot, shared_hid))):
        put_rows(shared_w, weight_grad(left, right).astype(bf16), pl.ds(i * hidden, hidden))
        for c in range(2 * i, 2 * i + 2):
            if c < 4:
                scatter.start(c)
    for j in range(12):
        take(j)
    work(0)
    work(1)
    give(0)
    advance()
    work(2)
    give(1)
    advance(2)
    work(3)
    give(2)
    give(3)
    advance()
    keep = [
        pltpu.make_async_copy(d_total.at[0], returned.at[me], own.at[0]),
        pltpu.make_async_copy(inner.at[0], inner_back.at[me], own.at[1]),
    ]
    for copy in keep:
        copy.start()

    stores = []

    def emit(value, tile, target):
        slot = len(stores) % 2
        if len(stores) >= 2:
            stores[-2].wait()
        tile[slot] = value
        stores.append(pltpu.make_async_copy(tile.at[slot], target, store.at[slot]))
        stores[-1].start()
        advance()

    rows_all = got[0].reshape(n * capacity, width)
    units = hid.shape[1]
    span = min(units, 256)
    for source, target in ((d_gate, ge_gate), (d_up, ge_up)):
        for at in range(0, units, span):
            columns = pl.ds(at, span)
            emit(weight_grad(rows_all, source[:, columns]), tiles, target.at[:, columns])
    for at in range(0, units, span):
        columns = pl.ds(at, span)
        emit(weight_grad(hid[:, columns], d_rows_all[...]), wide, ge_down.at[columns, :])

    for copy in keep:
        copy.wait()
    for a in range(2):
        for i in range(1, n):
            back[a, i].wait_recv()
    lane = lax.broadcasted_iota(jnp.int32, (1, LANES), 1)
    d_pairs = matmul(pick[0] + pick[1], returned[...].reshape(n * capacity, half))
    inner_row = jnp.concatenate([inner_back[e, 0:1, :capacity] for e in range(n)], axis=1)
    d_gate_lanes = jnp.zeros((count, LANES), f32)
    for i in range(2):
        value = jnp.sum(pick[i].astype(f32) * inner_row, axis=-1, keepdims=True)
        d_gate_lanes = d_gate_lanes + jnp.where(lane == i, value, 0.0)
    d_gates[...] = d_gate_lanes
    shared_in[:, mine] = shared_in[:, mine] + d_pairs
    ends[...] = shared_in[...].astype(bf16)
    last = [
        push(ends, ends_other, e_send.at[0], e_recv.at[0], sibling),
        push(d_gates, d_gates_other, e_send.at[1], e_recv.at[1], sibling),
    ]
    for copy in last:
        copy.wait()

    middle_all = middle[...]
    d_gates_all = d_gates[...] + d_gates_other[...]
    d_probs = jnp.zeros((count, LANES), f32)
    for i in range(2):
        d_probs = d_probs + jnp.where(routes[:, i : i + 1] == lane, d_gates_all[:, i : i + 1], 0.0)
    chance = probs[...]
    d_logits = (
        chance * (d_probs - jnp.sum(chance * d_probs, axis=-1, keepdims=True))
    ).astype(bf16)
    small_all = stacked(small, pl.ds(0, LANES))
    d_branch = (
        ends[...].astype(f32) + ends_other[...].astype(f32) + input_grad(d_logits, small_all)
    )
    factor = lax.rsqrt(jnp.mean(middle_all * middle_all, axis=-1, keepdims=True) + eps)
    normed = middle_all * factor
    gain_row = jnp.sum(d_branch * normed, axis=0, keepdims=True)
    d_norm = d_branch * gains[1:2, :]
    d_middle[...] = cotangent[...].astype(f32) + factor * (
        d_norm - normed * jnp.mean(d_norm * normed, axis=-1, keepdims=True)
    )
    put_rows(
        g_small,
        jnp.where(
            lane == n, jnp.broadcast_to(gain_row, (LANES, width)).T, weight_grad(branch, d_logits)
        ).astype(bf16),
        pl.ds(0, LANES),
    )
    for copy in stores[-2:]:
        copy.wait()
    advance(len(steps))
    scatter.drain()
    for copies in (swaps, back):
        for copy in copies.values():
            copy.wait_send()


def experts_fused(
    got, got_gate, weights, full, branch_in, cotangent, middle, probs, pick, routes, gains, near,
    depth, hidden, groups=4,
):
    n, capacity, width = got.shape[1:]
    count = branch_in.shape[0]
    units = weights[0].shape[1]
    rows = near.shape[3]
    span = min(units, 256)
    half = width // 2

    def shape(*dims, dtype=bf16):
        return jax.ShapeDtypeStruct(dims, dtype)

    slots = pltpu.VMEM((n, capacity, half), bf16)
    both = pltpu.VMEM((2, n, capacity, half), bf16)
    wide = pltpu.VMEM((n * capacity, units), bf16)
    lanes = pltpu.VMEM((n, 8, LANES), f32)
    parts = 3 * hidden // (4 * LANES)
    results = pl.pallas_call(
        functools.partial(experts_kernel, n, groups),
        out_shape=(
            shape(count, width, dtype=f32), shape(rows, 3 * hidden, dtype=f32),
            shape(depth, 2, 2, rows, LANES), shape(count, width, dtype=f32), shape(n, capacity, half),
            shape(width, units, dtype=f32), shape(width, units, dtype=f32), shape(units, width, dtype=f32),
        ),
        in_specs=[IN_HBM] * 4 + [IN_VMEM] * 10,
        out_specs=(IN_VMEM,) * 5 + (IN_HBM,) * 3,
        scratch_shapes=[
            pltpu.VMEM((n * capacity, width), bf16),
            pltpu.VMEM((width, units), bf16), pltpu.VMEM((width, units), bf16), pltpu.VMEM((units, width), bf16),
            pltpu.VMEM((2, max(width, units) // 4, max(width, units)), f32),
            pltpu.VMEM((depth, 2, 2, rows, 3 * hidden), bf16),
            wide, wide, wide,
            pltpu.VMEM((2, n, capacity, width), bf16),
            both, slots, slots,
            lanes, lanes,
            pltpu.VMEM((count, width), f32),
            pltpu.VMEM((2, width, span), f32), pltpu.VMEM((2, span, width), f32),
            pltpu.VMEM((count, width), bf16), pltpu.VMEM((count, width), bf16),
            pltpu.VMEM((count, LANES), f32), pltpu.VMEM((count, LANES), f32),
        ] + scatter_scratch(depth, rows, 3 * hidden // 2, parts) + [
            dma(2, groups), dma(2, groups),
            dma(n), dma(n), dma(n), dma(n), dma(2), dma(2), dma(2), dma(3), dma(2),
        ],
        compiler_params=comm_params(7, 62 << 20),
        name="experts_and_shared",
    )(
        *weights, full, got, got_gate, branch_in, cotangent, middle, probs, pick, routes, gains,
        near[:, :, :, :, :LANES],
    )
    return results[:5] + (results[5:],)


class Scatter:
    def __init__(self, depth, chunks, total, buffers, semaphores):
        self.depth, self.chunks, self.total = depth, chunks, total
        self.first_l, self.first_r, self.second_l, self.second_r, self.last = buffers
        self.p_send, self.p_recv, self.z_send, self.z_recv = semaphores
        self.z, self.y, self.x = digits(lax.axis_index("dp"))
        self.z_peers, self.y_peer, self.x_peer = grid_peers(depth, self.z, self.y, self.x)
        self.at_l, self.at_r, l, r = [], [], 0, 0
        for left, lc, lw, right, rc, rw, out in chunks:
            self.at_l.append(pl.ds(l, lw))
            self.at_r.append(pl.ds(r, rw))
            l, r = l + lw, r + rw
        self.ones, self.twos, self.threes = {}, {}, {}

    def start(self, c):
        left, lc, lw, right, rc, rw, out = self.chunks[c]
        self.ones[c] = [
            push(
                left.at[:, :, 1 - self.x, :, pl.ds(lc, lw)],
                self.first_l.at[:, :, :, self.at_l[c]],
                self.p_send.at[c, 0], self.p_recv.at[c, 0], self.x_peer,
            ),
            push(
                right.at[:, 1 - self.y, :, :, pl.ds(rc, rw)],
                self.first_r.at[:, :, :, self.at_r[c]],
                self.p_send.at[c, 1], self.p_recv.at[c, 1], self.y_peer,
            ),
        ]

    def second(self, c):
        left, lc, lw, right, rc, rw, out = self.chunks[c]
        in_l, in_r, first_l, first_r = self.at_l[c], self.at_r[c], self.first_l, self.first_r
        for copy in self.ones[c]:
            copy.wait_recv()

        def add(i, carry):
            for j in range(2):
                first_l[i, j, :, in_l] = (
                    first_l[i, j, :, in_l].astype(f32) + left[i, j, self.x, :, pl.ds(lc, lw)].astype(f32)
                ).astype(bf16)
                first_r[i, j, :, in_r] = (
                    first_r[i, j, :, in_r].astype(f32) + right[i, self.y, j, :, pl.ds(rc, rw)].astype(f32)
                ).astype(bf16)
            return carry

        lax.fori_loop(0, self.depth, add, 0)
        self.twos[c] = [
            push(
                first_l.at[:, 1 - self.y, :, in_l], self.second_l.at[:, :, in_l],
                self.p_send.at[c, 2], self.p_recv.at[c, 2], self.y_peer,
            ),
            push(
                first_r.at[:, 1 - self.x, :, in_r], self.second_r.at[:, :, in_r],
                self.p_send.at[c, 3], self.p_recv.at[c, 3], self.x_peer,
            ),
        ]

    def third(self, c):
        for copy in self.twos[c]:
            copy.wait_recv()
        sides = (
            (self.second_l, self.first_l, self.y, self.at_l[c]),
            (self.second_r, self.first_r, self.x, self.at_r[c]),
        )

        def add(i, carry):
            for source, before, place, here in sides:
                source[i, :, here] = (
                    source[i, :, here].astype(f32) + before[i, place, :, here].astype(f32)
                ).astype(bf16)
            return carry

        lax.fori_loop(0, self.depth, add, 0)
        self.threes[c] = [
            push(
                source.at[lax.rem(self.z + k + 1, self.depth), :, here],
                self.last.at[k, side, :, here],
                self.z_send.at[c, side, k], self.z_recv.at[c, side, k], self.z_peers[k],
            )
            for side, (source, before, place, here) in enumerate(sides)
            for k in range(self.depth - 1)
        ]

    def finish(self, c):
        left, lc, lw, right, rc, rw, out = self.chunks[c]
        for copy in self.threes[c]:
            copy.wait_recv()
        for side, source, here, at, span in (
            (0, self.second_l, self.at_l[c], out, lw),
            (1, self.second_r, self.at_r[c], out + lw, rw),
        ):
            value = source[self.z, :, here].astype(f32)
            for k in range(self.depth - 1):
                value = value + self.last[k, side, :, here].astype(f32)
            self.total[:, pl.ds(at, span)] = value

    def plan(self):
        steps = []
        for c in range(len(self.chunks) + 2):
            if c < len(self.chunks):
                steps.append((self.second, c))
            if 1 <= c <= len(self.chunks):
                steps.append((self.third, c - 1))
            if c >= 2:
                steps.append((self.finish, c - 2))
        return steps

    def drain(self):
        for copies in list(self.ones.values()) + list(self.twos.values()) + list(self.threes.values()):
            for copy in copies:
                copy.wait_send()


def lanes_of(part):
    lane = lax.broadcasted_iota(jnp.int32, (1, LANES), 1)
    return (lax.div(lane, HEAD) == part).astype(f32).astype(bf16)


def swap_halves(values):
    lane = lax.broadcasted_iota(jnp.int32, (1, LANES), 1)
    low = lax.rem(lane, HEAD) < HEAD // 2
    return jnp.where(
        low, pltpu.roll(values, LANES - HEAD // 2, 1), pltpu.roll(values, HEAD // 2, 1)
    )


def put_rows(target, values, columns):
    rows = target.shape[3]
    for b in range(values.shape[0] // rows):
        target[b // PLANE, (b // 2) % 2, b % 2, :, columns] = values[b * rows : (b + 1) * rows]


def backward_kernel(
    depth, reach, per_core, shared, w_query, w_key, w_value, g_small, window, q, k, v, lse, heads_out, d_attn,
    near, gains, cosines, sines, bias, *rest,
):
    given = shared or 5
    rest, combine = rest[given:], rest[:given]
    total, d_full = rest[:2]
    rest = rest[2:]
    if not shared:
        rows_total, pick, gates, middle, shared_part = combine
        output, rows_back, end, end_other, o_send, o_recv, e_send, e_recv, keep = rest[:1] + rest[-8:]
        rest = rest[1:-8]
    (
    grads, attn_t, d_heads, dq_all, dk_all, dv_all, d_part, d_swap, d_sum, d_got, gain_got,
    first_l, first_r, second_l, second_r, last, p_send, p_recv, z_send, z_recv,
    t_send, t_recv, s_send, s_recv, f_send, f_recv,
    ) = rest
    n = depth * PLANE
    me, core = lax.axis_index("dp"), lax.axis_index("tensor")
    sibling = {"tensor": 1 - core}
    plane, z_next, z_before = Plane(me), *z_neighbours(me, n)
    heads_width = q.shape[1]
    count = q.shape[0]
    pairs = heads_width // LANES
    chunks = []
    out = 0
    step = 2 * LANES
    for source in combine if shared else ():
        for at in range(0, source.shape[4], 2 * step):
            chunks.append((source, at, step, source, at + step, step, out))
            out += 2 * step
    early = len(chunks)
    widths = [(step, step)] + [(step, LANES), (LANES, step)] * pairs
    widths = widths[: pairs + 1]
    at = 0
    for left, right in widths:
        chunks.append((grads, at, left, grads, at + left, right, out + at))
        at += left + right
    scatter = Scatter(
        depth, chunks, total, (first_l, first_r, second_l, second_r, last),
        (p_send, p_recv, z_send, z_recv),
    )
    if shared:
        greet(scatter.z_peers + plane.peers + [sibling, z_next, z_before])
    else:
        greet([{"dp": lax.rem(me + i, n)} for i in range(1, n)] + [sibling])
    lead = 4
    for c in range(min(lead, early)):
        scatter.start(c)
    steps = scatter.plan()
    done = [0]

    def advance(count=1):
        for action, c in steps[done[0] : done[0] + count]:
            if action == scatter.second and c not in scatter.ones:
                break
            done[0] += 1
            action(c)
            if action == scatter.second and c + lead < early:
                scatter.start(c + lead)

    out_w = pl.ds(LANES + 3 * heads_width, heads_width)
    gain = gains[0:1, :]
    d_heads[...] = matmul(d_attn[...], stacked(near, out_w)).astype(bf16)
    put_rows(grads, weight_grad(d_attn[...], heads_out[...]).astype(bf16), pl.ds(0, heads_width))
    grads[:, :, :, :, pl.ds(heads_width, LANES)] = g_small[...]

    def normed(block):
        values = window[block].astype(f32)
        return values * lax.rsqrt(jnp.mean(values * values, axis=-1, keepdims=True) + eps)

    def turned(block, carry):
        rows = pl.ds(pl.multiple_of(block * count, count), count)
        attn_t[:, rows] = (normed(block) * gain).T.astype(bf16)
        return carry

    for block in range(reach + 1):
        turned(block, 0)
    scatter.start(early)
    home = []
    if not shared:
        home = [
            push(
                rows_total.at[i], rows_back.at[me], o_send.at[i], o_recv.at[i],
                {"dp": lax.rem(me + n - i, n)},
            )
            for i in range(1, n)
        ]
        kept = pltpu.make_async_copy(rows_total.at[0], rows_back.at[me], keep.at[0])
        kept.start()
    own = pl.ds(reach * count, count)
    for pair in range(pairs):
        columns = pl.ds(pair * LANES, LANES)
        k_pair, v_pair, q_pair, d_pair = k[:, columns], v[:, columns], q[:, columns], d_heads[:, columns]
        k_turned = k_pair.T
        dq, dk, dv = [], None, None
        for part in range(2):
            head = 2 * pair + part
            lanes = lanes_of(part)
            q_head, d_head = q_pair * lanes, d_pair * lanes
            probs = jnp.exp(input_grad(k_pair, q_head) + bias[...] - lse[head : head + 1, :])
            d_probs = input_grad(v_pair, d_head)
            inner = jnp.sum(probs * d_probs, axis=0, keepdims=True)
            d_scores = (probs * (d_probs - inner)).astype(bf16)
            advance(1 if shared else 0)
            dq.append(matmul(k_turned, d_scores)[part * HEAD : (part + 1) * HEAD, :])
            parts = matmul(d_scores, q_head), matmul(probs.astype(bf16), d_head)
            dk, dv = parts if part == 0 else (dk + parts[0], dv + parts[1])
            advance(1 if shared else 0)
        dq = jnp.concatenate(dq, axis=0).T * (HEAD ** (-0.5))
        cos_own, sin_own = cosines[own, :], sines[own, :]
        dq_low = turn(dq, cos_own, -sin_own).astype(bf16)
        dk_low = turn(dk, cosines[...], -sines[...]).astype(bf16)
        dv_low = dv.astype(bf16)
        dq_all[:, columns] = dq_low
        dk_all[:, columns] = dk_low
        dv_all[:, columns] = dv_low
        at = heads_width + LANES + pair * 3 * LANES
        put_rows(grads, matmul(attn_t[:, own], dq_low).astype(bf16), pl.ds(at, LANES))
        put_rows(grads, matmul(attn_t[...], dk_low).astype(bf16), pl.ds(at + LANES, LANES))
        put_rows(grads, matmul(attn_t[...], dv_low).astype(bf16), pl.ds(at + 2 * LANES, LANES))
        scatter.start(early + 1 + pair)
        advance(2 if shared else pair + 1)

    width = d_part.shape[-1] // 2
    mine = pl.ds(pl.multiple_of(core * width, width), width)
    theirs = pl.ds(pl.multiple_of((1 - core) * width, width), width)
    swaps = []
    query_v, key_v, value_v = (
        jnp.concatenate(
            [stacked(near, pl.ds(LANES * (1 + 3 * pair + i), LANES)) for pair in range(pairs)], axis=1
        )
        for i in range(3)
    )
    for block in range(reach + 1):
        rows = pl.ds(block * count, count)
        value = input_grad(dk_all[rows, :], key_v) + input_grad(dv_all[rows, :], value_v)
        if block == reach:
            value = value + input_grad(dq_all[...], query_v)
        d_part[block] = value.astype(bf16)
        swaps.append(
            push(
                d_part.at[block, :, theirs], d_swap.at[block],
                s_send.at[block], s_recv.at[block], sibling,
            )
        )
    for block in range(reach + 1):
        swaps[block].wait_recv()
        d_sum[block] = (
            d_part[block, :, mine].astype(f32) + d_swap[block].astype(f32)
        ).astype(bf16)
    back = [
        push(
            d_sum.at[lax.rem(plane.places[j] - plane.place + PLANE, PLANE)],
            d_got.at[j], t_send.at[j], t_recv.at[j], plane.peers[j - 1],
        )
        for j in range(1, PLANE)
    ]
    advance(5)
    d_mine, d_before = d_sum[reach].astype(f32), d_sum[0].astype(f32)
    for j in range(1, PLANE):
        back[j - 1].wait_recv()
        ours = lax.select(plane.places[j] > plane.place, 1.0, 0.0)
        value = d_got[j].astype(f32)
        d_mine, d_before = d_mine + value * ours, d_before + value * (1.0 - ours)
    d_sum[reach] = d_before.astype(bf16)
    back.append(push(d_sum.at[reach], d_got.at[0], t_send.at[0], t_recv.at[0], z_before))
    last_swap = []
    if not shared:
        kept.wait()
        for copy in home:
            copy.wait_recv()
        rows_all = rows_back[...].reshape(-1, width)
        moe = gates[:, 0:1] * matmul(pick[0], rows_all) + gates[:, 1:2] * matmul(pick[1], rows_all)
        end[...] = shared_part[...].astype(bf16)
        end[:, mine] = (shared_part[:, mine] + moe).astype(bf16)
        last_swap.append(push(end, end_other, e_send.at[0], e_recv.at[0], sibling))
    advance(len(steps))
    if not shared:
        last_swap[0].wait_recv()
        output[...] = (
            middle[...] + (end[...].astype(f32) + end_other[...].astype(f32))
        ).astype(bf16)
    back[-1].wait_recv()
    d_mine = d_mine + d_got[0].astype(f32)
    d_full[:, mine] = d_mine.astype(bf16)
    both = push(d_full.at[:, mine], d_full.at[:, mine], f_send.at[0], f_recv.at[0], sibling)
    gain_sum = jnp.zeros((total.shape[0], 1), f32)
    at = out + heads_width + LANES
    for pair in range(pairs):
        for i, source in enumerate((w_query, w_key, w_value)):
            rounded = source[:, pl.ds(pair * LANES, LANES)].astype(bf16).astype(f32)
            products = total[:, pl.ds(at + (3 * pair + i) * LANES, LANES)] * rounded
            gain_sum = gain_sum + jnp.sum(products, axis=-1, keepdims=True)
    split = pl.ds(per_core, LANES)
    total[:, split] = jnp.broadcast_to(gain_sum, (total.shape[0], LANES))
    gain_copy = push(total.at[:, split], gain_got, f_send.at[1], f_recv.at[1], sibling)
    both.wait()
    gain_copy.wait()
    total[:, split] = total[:, split] + gain_got[...]
    scatter.drain()
    for copy in back + swaps + last_swap + home:
        copy.wait_send()


def backward(arrays, shared, combine, rows, columns, count, heads_width, width, depth, reach):
    span = (reach + 1) * count
    summed = columns - LANES
    half = -(-summed // (2 * LANES)) * LANES
    width_shared = sum(value.shape[4] for value in shared)
    parts = width_shared // (4 * LANES) + 1 + heads_width // LANES
    own = summed - width_shared
    outs = (
        jax.ShapeDtypeStruct((rows, columns), f32),
        jax.ShapeDtypeStruct((count, width), bf16),
    )
    extra = []
    if not shared:
        outs += (jax.ShapeDtypeStruct((count, width), bf16),)
        low = pltpu.VMEM((count, width), bf16)
        n = depth * PLANE
        extra = [
            pltpu.VMEM(combine[0].shape, bf16), low, low, dma(n), dma(n), dma(1), dma(1), dma(1)
        ]
    arrays = list(arrays) + list(shared) + list(combine)
    return pl.pallas_call(
        functools.partial(backward_kernel, depth, reach, columns - LANES, len(shared)),
        out_shape=outs,
        in_specs=[IN_VMEM] * len(arrays),
        out_specs=(IN_VMEM,) * len(outs),
        scratch_shapes=[
            pltpu.VMEM((depth, 2, 2, rows, own), bf16),
            pltpu.VMEM((width, span), bf16),
            pltpu.VMEM((count, heads_width), bf16),
            pltpu.VMEM((count, heads_width), bf16),
            pltpu.VMEM((span, heads_width), bf16),
            pltpu.VMEM((span, heads_width), bf16),
            pltpu.VMEM((reach + 1, count, width), bf16),
            pltpu.VMEM((reach + 1, count, width // 2), bf16),
            pltpu.VMEM((reach + 1, count, width // 2), bf16),
            pltpu.VMEM((reach, count, width // 2), bf16),
            pltpu.VMEM((rows, LANES), f32),
        ] + scatter_scratch(depth, rows, half, parts) + [
            dma(reach), dma(reach), dma(reach + 1), dma(reach + 1), dma(2), dma(2),
        ] + extra,
        compiler_params=comm_params(4, 58 << 20),
        name="attention_backward",
    )(*arrays)


def scatter_scratch(depth, rows, half, parts):
    first = pltpu.VMEM((depth, 2, rows, half), bf16)
    second = pltpu.VMEM((depth, rows, half), bf16)
    return [
        first, first, second, second, pltpu.VMEM((depth - 1, 2, rows, half), bf16),
        dma(parts, 4), dma(parts, 4), dma(parts, 2, depth - 1), dma(parts, 2, depth - 1),
    ]


class Plane:
    def __init__(self, me):
        z, y, x = digits(me)
        self.place = y * 2 + x
        self.places, self.peers = [self.place], []
        for j in range(1, PLANE):
            y_j, x_j = (1 - y if j & 2 else y), (1 - x if j & 1 else x)
            self.places.append(y_j * 2 + x_j)
            self.peers.append({"dp": index_of(z, y_j, x_j)})


def z_neighbours(me, n):
    return {"dp": lax.rem(me + PLANE, n)}, {"dp": lax.rem(me + n - PLANE, n)}


class Gather:
    def __init__(self, depth, chunks, shard, full, semaphores):
        self.depth, self.chunks, self.shard, self.full = depth, chunks, shard, full
        self.z_send, self.z_recv, self.p_send, self.p_recv = semaphores
        self.z, self.y, self.x = digits(lax.axis_index("dp"))
        self.z_peers, self.y_peer, self.x_peer = grid_peers(depth, self.z, self.y, self.x)
        self.ones, self.twos, self.threes = {}, {}, {}

    def _sides(self, c):
        at, left, right = self.chunks[c]
        return pl.ds(at, left), pl.ds(at + left, right)

    def first(self, c):
        at, left, right = self.chunks[c]
        columns = pl.ds(at, left + right)
        self.ones[c] = [
            push(
                self.shard.at[:, columns],
                self.full.at[self.z, self.y, self.x, :, columns],
                self.z_send.at[c, k], self.z_recv.at[c, k], self.z_peers[k],
            )
            for k in range(self.depth - 1)
        ]

    def second(self, c):
        left, right = self._sides(c)
        for copy in self.ones[c]:
            copy.wait_recv()
        a = self.full.at[:, self.y, self.x, :, left]
        b = self.full.at[:, self.y, self.x, :, right]
        self.twos[c] = [
            push(a, a, self.p_send.at[c, 0], self.p_recv.at[c, 0], self.y_peer),
            push(b, b, self.p_send.at[c, 1], self.p_recv.at[c, 1], self.x_peer),
        ]

    def third(self, c):
        left, right = self._sides(c)
        for copy in self.twos[c]:
            copy.wait_recv()
        a = self.full.at[:, :, self.x, :, left]
        b = self.full.at[:, self.y, :, :, right]
        self.threes[c] = [
            push(a, a, self.p_send.at[c, 2], self.p_recv.at[c, 2], self.x_peer),
            push(b, b, self.p_send.at[c, 3], self.p_recv.at[c, 3], self.y_peer),
        ]

    def finish(self, c):
        for copy in self.threes[c]:
            copy.wait_recv()

    def plan(self, lead):
        count = len(self.chunks)
        steps = []
        for s in range(count + 2):
            if s < count:
                steps.append((self.second, s))
                if s + lead < count:
                    steps.append((self.first, s + lead))
            if 1 <= s <= count:
                steps.append((self.third, s - 1))
            if s >= 2:
                steps.append((self.finish, s - 2))
        return steps

    def drain(self):
        for copies in list(self.ones.values()) + list(self.twos.values()) + list(self.threes.values()):
            for copy in copies:
                copy.wait_send()


def stacked(ref, columns):
    rows = ref.shape[3]
    if rows % 16 == 0:
        return ref[:, :, :, :, columns].reshape(-1, columns.size)
    blocks = [
        ref[b // PLANE, (b // 2) % 2, b % 2, :, columns].astype(f32)
        for b in range(ref.shape[0] * PLANE)
    ]
    return jnp.concatenate(blocks, axis=0).astype(bf16)


def turn(values, cos, sin):
    return values * cos + swap_halves(values) * sin


def forward_kernel(
    depth, reach, experts, chunks, near_edges, small, w_query, w_key, w_value, out_shard, w_sgate, w_sup, down_shard,
    tokens, cotangent, routes, segments, row_cos, row_sin, block_cos, block_sin,
    full, near, window, q, k, v, lse, heads_out, cosines, sines, bias, gains, middle, branch_in, probs, gates, pick,
    *rest,
):
    n = depth * PLANE
    fused = n == experts
    if fused:
        got, got_gate, rows_send, gate_send, d_send, d_recv, e_send, e_recv, g_send, g_recv = (
            rest[:2] + rest[-8:]
        )
        rest = rest[2:-8]
        rows_out, d_rows_out = rows_send.at[0], rows_send.at[1]
    else:
        rows_out, d_rows_out = rest[:2]
        rest = rest[2:]
    (
        shard, attn_in, part, other,
        z_send, z_recv, p_send, p_recv, t_send, t_recv, f_send, f_recv, s_send, s_recv, own,
    ) = rest
    me, core = lax.axis_index("dp"), lax.axis_index("tensor")
    sibling = {"tensor": 1 - core}
    gather = Gather(depth, chunks, shard, full, (z_send, z_recv, p_send, p_recv))
    heads_width = q.shape[1]
    pairs = heads_width // LANES
    at = 0
    order = [(small, 0, LANES)]
    for pair in range(pairs):
        order += [(piece, pair * LANES, LANES) for piece in (w_query, w_key, w_value)]
    order += [(piece, 0, piece.shape[1]) for piece in (out_shard, w_sgate, w_sup, down_shard)]
    for piece, start, size in order:
        shard[:, pl.ds(at, size)] = piece[:, pl.ds(start, size)].astype(bf16)
        at += size
    plane, z_next, z_before = Plane(me), *z_neighbours(me, n)
    if fused:
        greet([{"dp": lax.rem(me + i, n)} for i in range(1, n)] + [sibling])
    else:
        greet(gather.z_peers + plane.peers + [sibling, z_next, z_before])
    count, width = tokens.shape
    half = count // 2
    rows = pl.ds(pl.multiple_of(core * half, half), half)
    from_before = push(tokens.at[rows], window.at[0, rows], t_send.at[0], t_recv.at[0], z_next)
    lead = 3
    for c in range(lead):
        gather.first(c)
    own_shard = pltpu.make_async_copy(shard, full.at[gather.z, gather.y, gather.x], own.at[0])
    own_shard.start()
    window[reach] = tokens[...]

    lane = lax.broadcasted_iota(jnp.int32, (1, LANES), 1)
    sign = jnp.where(lax.rem(lane, HEAD) < HEAD // 2, -1.0, 1.0)
    seg_query = segments[pl.ds(me, 1), :].astype(f32)
    key_place = lax.broadcasted_iota(jnp.int32, (count, count), 0)
    query_place = lax.broadcasted_iota(jnp.int32, (count, count), 1)
    for b in range(reach + 1):
        at = pl.ds(b * count, count)
        c_b, s_b = block_cos[pl.ds(me + b, 1), :], block_sin[pl.ds(me + b, 1), :]
        cosines[at, :] = c_b * row_cos[...] - s_b * row_sin[...]
        sines[at, :] = (s_b * row_cos[...] + c_b * row_sin[...]) * sign
        block = me - reach + b
        seg_key = segments[pl.ds(lax.max(block, 0), 1), :].astype(f32)
        seg_key = jnp.broadcast_to(seg_key, (LANES, count)).T[:, :1]
        distance = (reach - b) * count + query_place - key_place
        limit = lax.select(block >= 0, WINDOW, 0)
        seen = (distance >= 0) & (distance < limit) & (seg_key == seg_query)
        bias[at, :] = jnp.where(seen, 0.0, masked)

    capacity = rows_out.shape[1]
    named = [(routes[:, i : i + 1] == lane).astype(f32) for i in range(routes.shape[1])]
    below = (key_place > query_place).astype(f32).astype(bf16)
    before = matmul(below, sum(named).astype(bf16))
    slot_of = lax.broadcasted_iota(jnp.int32, (count, experts * capacity), 1)
    for i, name in enumerate(named):
        place = jnp.sum(name * before, axis=-1, keepdims=True).astype(jnp.int32)
        place = place + routes[:, i : i + 1] * capacity
        pick[i] = (slot_of == place).astype(f32).astype(bf16)
    features = pl.ds(pl.multiple_of(core * (width // 2), width // 2), width // 2)
    sent, passed = {}, {}

    def dispatch_rows(a):
        for i in range(1, n):
            to = lax.rem(me + i, n)
            sent[a, i] = push(
                rows_send.at[a, to, :, features], got.at[a, i, :, features],
                d_send.at[a, i], d_recv.at[a, i], {"dp": to},
            )
        got[a, 0] = rows_send[a, me]

    def forward_rows(a):
        for i in range(1, n):
            sent[a, i].wait_recv()
            block = got.at[a, i, :, features]
            passed[a, i] = push(block, block, e_send.at[a, i], e_recv.at[a, i], sibling)

    if fused:
        rows_send[1] = (
            weight_grad(pick[0] + pick[1], cotangent[...]).astype(bf16).reshape(rows_out.shape)
        )

    def normed(b):
        values = window[b].astype(f32)
        return values * lax.rsqrt(jnp.mean(values * values, axis=-1, keepdims=True) + eps)

    own_shard.wait()
    steps = gather.plan(lead)
    done = [0]

    def advance(until=None, waits=None):
        while done[0] < len(steps) and waits != 0:
            action, c = steps[done[0]]
            done[0] += 1
            action(c)
            if waits is not None and action != gather.first:
                waits -= 1
            if (action, c) == until:
                break

    from_before.wait_recv()
    t_copies = [from_before]
    for j in range(1, PLANE):
        source = window.at[lax.select(plane.places[j] < plane.place, 0, reach), rows]
        target = window.at[lax.rem(plane.place - plane.places[j] + PLANE, PLANE), rows]
        t_copies.append(push(source, target, t_send.at[j], t_recv.at[j], plane.peers[j - 1]))
    advance((gather.second, 1))
    forwards = []
    for j, copy in enumerate(t_copies):
        if j:
            copy.wait_recv()
        block = window.at[lax.rem(plane.places[j] - plane.place + PLANE, PLANE), rows]
        forwards.append(push(block, block, f_send.at[j], f_recv.at[j], sibling))
    landed = 0
    copies = []
    for i, (edge, c) in enumerate(near_edges):
        copies.append((c, pl.ds(landed, edge - landed), own.at[1 + i]))
        landed = edge

    def land(i):
        c, columns, semaphore = copies[i]
        advance((gather.finish, c))
        copy = pltpu.make_async_copy(
            full.at[:, :, :, :, columns], near.at[:, :, :, :, columns], semaphore
        )
        copy.start()
        copy.wait()

    land(0)
    if fused:
        dispatch_rows(1)
    for copy in forwards:
        copy.wait_recv()
    small_all = stacked(near, pl.ds(0, LANES))
    small_turned = small_all.astype(f32).T
    gain_first, gain_second = small_turned[experts : experts + 1, :], small_turned[experts + 1 : experts + 2, :]
    gains[...] = small_turned[experts : experts + 8, :]
    own_rows = pl.ds(reach * count, count)
    for b in range(reach + 1):
        attn_in[pl.ds(b * count, count), :] = (normed(b) * gain_first).astype(bf16)
    lse[...] = jnp.zeros_like(lse)
    for pair in range(pairs):
        if pair:
            land(pair)
        at = LANES * (1 + 3 * pair)
        columns = pl.ds(pair * LANES, LANES)
        products = matmul(attn_in[...], stacked(near, pl.ds(at + LANES, 2 * LANES)))
        k_pair = turn(products[:, :LANES], cosines[...], sines[...]).astype(bf16)
        v_pair = products[:, LANES:].astype(bf16)
        queries = matmul(attn_in[own_rows, :], stacked(near, pl.ds(at, LANES)))
        q_pair = (
            turn(queries, cosines[own_rows, :], sines[own_rows, :]) * (HEAD ** (-0.5))
        ).astype(bf16)
        k[:, columns], v[:, columns], q[:, columns] = k_pair, v_pair, q_pair
        v_turned = v_pair.T
        outs = []
        for part_of in range(2):
            head = 2 * pair + part_of
            scores = input_grad(k_pair, q_pair * lanes_of(part_of)) + bias[...]
            peak = jnp.max(scores, axis=0, keepdims=True)
            expo = jnp.exp(scores - peak)
            total = jnp.sum(expo, axis=0, keepdims=True)
            lse[head : head + 1, :] = peak + jnp.log(total)
            weights = (expo * (1.0 / total)).astype(bf16)
            outs.append(matmul(v_turned, weights)[part_of * HEAD : (part_of + 1) * HEAD, :])
            advance(waits=1)
        heads_out[:, columns] = jnp.concatenate(outs, axis=0).T.astype(bf16)
    land(pairs)
    out_w = stacked(near, pl.ds(LANES + 3 * heads_width, heads_width))
    part[...] = input_grad(heads_out[...], out_w).astype(bf16)
    swapped = push(part, other, s_send.at[0], s_recv.at[0], sibling)
    swapped.wait()
    middle_all = tokens[...].astype(f32) + (part[...].astype(f32) + other[...].astype(f32))
    middle[...] = middle_all
    factor = lax.rsqrt(jnp.mean(middle_all * middle_all, axis=-1, keepdims=True) + eps)
    branch = (middle_all * factor * gain_second).astype(bf16)
    branch_in[...] = branch

    logits = jnp.where(lane < experts, matmul(branch, small_all), masked)
    expo = jnp.exp(logits - jnp.max(logits, axis=-1, keepdims=True))
    chance = expo / jnp.sum(expo, axis=-1, keepdims=True)
    probs[...] = chance
    gate_lanes = jnp.zeros((count, LANES), f32)
    gate_row = jnp.zeros((1, experts * capacity), f32)
    d_gathered = None if fused else jnp.zeros((experts * capacity, width), f32)
    for i, name in enumerate(named):
        gate = jnp.sum(chance * name, axis=-1, keepdims=True)
        gate_lanes = gate_lanes + jnp.where(lane == i, gate, 0.0)
        if fused:
            gate_row = gate_row + jnp.sum(gate * pick[i].astype(f32), axis=0, keepdims=True)
        else:
            d_rows = (gate * cotangent[...].astype(f32)).astype(bf16)
            d_gathered = d_gathered + weight_grad(pick[i], d_rows)
    gates[...] = gate_lanes
    if fused:
        gate_send[...] = jnp.zeros_like(gate_send)
        for e in range(experts):
            gate_send[e, 0:1, :capacity] = gate_row[:, e * capacity : (e + 1) * capacity]
    else:
        d_rows_out[...] = d_gathered.astype(bf16).reshape(d_rows_out.shape)
    rows_out[...] = weight_grad(pick[0] + pick[1], branch).astype(bf16).reshape(rows_out.shape)
    gate_sent = []
    if fused:
        dispatch_rows(0)
        for i in range(1, n):
            to = lax.rem(me + i, n)
            gate_sent.append(
                push(gate_send.at[to], got_gate.at[i], g_send.at[i], g_recv.at[i], {"dp": to})
            )
        got_gate[0] = gate_send[me]
        advance(waits=4)
        forward_rows(1)
        advance(waits=5)
        forward_rows(0)
    advance()
    if fused:
        for copy in gate_sent:
            copy.wait_recv()
        for copy in passed.values():
            copy.wait_recv()
        for copy in list(sent.values()) + list(passed.values()) + gate_sent:
            copy.wait_send()
    gather.drain()
    for copy in t_copies + forwards:
        copy.wait_send()


def angle_tables(tok_count, blocks, reach):
    freqs = (10000.0 ** (-np.arange(HEAD // 2, dtype=np.float32) * np.float32(2.0 / HEAD))).astype(np.float64)
    freqs = np.tile(freqs, LANES // (HEAD // 2))[None, :]
    inner = np.arange(tok_count)[:, None] * freqs
    starts = np.maximum(np.arange(-reach, blocks), 0) * tok_count
    starts = np.pad(starts, (0, -len(starts) % 8))[:, None] * freqs
    return [jnp.asarray(f(a), f32) for a in (inner, starts) for f in (np.cos, np.sin)]


def forward(arrays, tokens, cotangent, routes, segments, depth, reach, experts, heads_width, hidden):
    count, width = tokens.shape
    n = depth * PLANE
    rows = arrays[0].shape[0]
    span = (reach + 1) * count
    near_width = LANES + 4 * heads_width
    columns = near_width + 3 * hidden
    capacity = count // 4
    step = 4 * LANES
    pairs = heads_width // LANES
    widths = [step] + [3 * LANES] * (pairs - 1) + [heads_width] + [step] * ((columns - near_width) // step)
    chunks, at = [], 0
    for w in widths:
        left = (w // LANES + (len(chunks) + 1) % 2) // 2 * LANES
        chunks.append((at, left, w - left))
        at += w
    near_edges = tuple((sum(widths[: c + 1]), c) for c in range(pairs + 1))
    parts = len(chunks)
    tables = angle_tables(count, n, reach)
    segment_rows = segments.reshape(-1, count)

    def shape(*dims, dtype=bf16):
        return jax.ShapeDtypeStruct(dims, dtype)

    outs = (
        shape(depth, 2, 2, rows, columns),
        shape(depth, 2, 2, rows, near_width),
        shape(reach + 1, count, width),
        shape(count, heads_width), shape(span, heads_width), shape(span, heads_width),
        shape(-(-heads_width // HEAD // 8) * 8, count, dtype=f32),
        shape(count, heads_width),
        shape(span, LANES, dtype=f32), shape(span, LANES, dtype=f32), shape(span, count, dtype=f32),
        shape(8, width, dtype=f32),
        shape(count, width, dtype=f32), shape(count, width),
        shape(count, LANES, dtype=f32), shape(count, LANES, dtype=f32),
        shape(routes.shape[1], count, experts * capacity),
    )
    if n == experts:
        outs += (shape(2, n, capacity, width), shape(n, 8, LANES, dtype=f32))
        extra = [
            pltpu.VMEM((2, n, capacity, width), bf16), pltpu.VMEM((n, 8, LANES), f32),
            dma(2, n), dma(2, n), dma(2, n), dma(2, n), dma(n), dma(n),
        ]
    else:
        outs += (shape(experts, capacity, width), shape(experts, capacity, width))
        extra = []
    inputs = list(arrays) + [tokens, cotangent, routes, segment_rows, tables[0], tables[1], tables[2], tables[3]]
    return pl.pallas_call(
        functools.partial(forward_kernel, depth, reach, experts, tuple(chunks), near_edges),
        out_shape=outs,
        in_specs=[IN_VMEM] * len(inputs),
        out_specs=(IN_HBM,) + (IN_VMEM,) * (len(outs) - 1),
        scratch_shapes=[
            pltpu.VMEM((rows, columns), bf16),
            pltpu.VMEM((span, width), bf16),
            pltpu.VMEM((count, width), bf16),
            pltpu.VMEM((count, width), bf16),
            dma(parts, depth - 1), dma(parts, depth - 1), dma(parts, 4), dma(parts, 4),
            dma(reach), dma(reach), dma(reach), dma(reach), dma(1), dma(1), dma(2 + pairs),
        ] + extra,
        compiler_params=comm_params(1, 58 << 20),
        name="gather_and_attend",
    )(*inputs)


def local(
    tokens, cotangent, attn_gain, w_query, w_key, w_value, w_out, ffn_gain, w_router,
    w_sgate, w_sup, w_sdown, e_gate, e_up, e_down, routes, segments,
):
    tok_count, width = tokens.shape
    n = lax.axis_size("dp")
    depth = n // PLANE
    me = lax.axis_index("dp")
    core = lax.axis_index("tensor")
    experts = w_router.shape[1]
    owners = n // experts
    capacity = tok_count // 4
    reach = (WINDOW + tok_count - 1) // tok_count
    shard_rows = w_query.shape[0]
    heads_width = w_query.shape[1]
    hidden = w_sgate.shape[1]
    half = width // 2

    small = jnp.pad(
        jnp.concatenate([w_router, attn_gain[:, None], ffn_gain[:, None]], axis=1),
        ((0, 0), (0, LANES - experts - 2)),
    )
    near_width = LANES + 4 * heads_width
    own_columns = near_width + LANES
    (
        full, near, window, queries, all_keys, all_values, lse, heads_out, cosines, sines, bias, gains,
        middle, branch_in, probs, gates, pick, *sent_rows,
    ) = forward(
        (small, w_query, w_key, w_value, w_out.T, w_sgate, w_sup, w_sdown.T),
        tokens, cotangent, routes, segments, depth, reach, experts, heads_width, hidden,
    )
    x_float = tokens.astype(f32)
    normed_one, scale_one = rms_parts(x_float)
    gain_first, gain_second = gains[0], gains[1]
    blocks = (depth, 2, 2, shard_rows)
    if owners == 1:
        d_middle, shared_total, small_grads, shared_part, rows_back, expert_grads = experts_fused(
            *sent_rows, (e_gate, e_up, e_down), full, branch_in, cotangent, middle, probs,
            pick, routes, gains, near, depth, hidden,
        )
        shared_grads, combine = (), (rows_back, pick, gates, middle, shared_part)
    else:
        sgate_w, sup_w, sdown_t = (
            full[:, :, :, :, near_width + i * hidden : near_width + (i + 1) * hidden].reshape(width, hidden)
            for i in range(3)
        )
        router_w = near[:, :, :, :, :experts].reshape(width, experts)
        expert_gate = e_gate.astype(bf16)
        expert_up = e_up.astype(bf16)
        expert_down = e_down.astype(bf16)
        normed_two, scale_two = rms_parts(middle)
        probs = probs[:, :experts]
        picked = (routes[:, :, None] == jnp.arange(experts, dtype=jnp.int32)[None, None, :]).astype(f32)
        d_after = cotangent.astype(f32)
        combine = ()
        rows_in, d_rows_in = dispatch(*sent_rows, n, owners)

        rows_in = rows_in.reshape(n * capacity, width)
        d_rows_in = d_rows_in.reshape(n * capacity, width)
        gate_hidden = matmul(rows_in, expert_gate)
        up_hidden = matmul(rows_in, expert_up)
        gate_act = jax.nn.silu(gate_hidden)
        expert_hidden = (gate_act * up_hidden).astype(bf16)
        part_rows = matmul(expert_hidden, expert_down).astype(bf16)
        d_hidden = input_grad(d_rows_in, expert_down)
        d_gate_hidden = (d_hidden * up_hidden * silu_grad(gate_hidden)).astype(bf16)
        d_up_hidden = (d_hidden * gate_act).astype(bf16)
        d_part_rows = (
            input_grad(d_gate_hidden, expert_gate) + input_grad(d_up_hidden, expert_up)
        ).astype(bf16)
        returned, d_returned = give_back(
            part_rows.reshape(n, capacity, width), d_part_rows.reshape(n, capacity, width)
        )
        grad_e_down = weight_grad(expert_hidden, d_rows_in)
        grad_e_gate = weight_grad(rows_in, d_gate_hidden)
        grad_e_up = weight_grad(rows_in, d_up_hidden)

        shared_gate = matmul(branch_in, sgate_w)
        shared_up = matmul(branch_in, sup_w)
        shared_act = jax.nn.silu(shared_gate)
        shared_hidden = (shared_act * shared_up).astype(bf16)
        shared_part = input_grad(shared_hidden, sdown_t)
        d_shared = matmul(cotangent, sdown_t)
        grad_sdown_t = weight_grad(cotangent, shared_hidden)
        d_sgate = (d_shared * shared_up * silu_grad(shared_gate)).astype(bf16)
        d_sup = (d_shared * shared_act).astype(bf16)
        grad_sgate = weight_grad(branch_in, d_sgate)
        grad_sup = weight_grad(branch_in, d_sup)
        d_shared_in = input_grad(d_sgate, sgate_w) + input_grad(d_sup, sup_w)

        def incoming(rows):
            rows = rows.reshape(experts, owners, capacity, half)
            if owners > 1:
                rows = jnp.sum(rows.astype(f32), axis=1).astype(bf16)
            return rows.reshape(experts * capacity, half)

        def placed(values):
            own = jnp.concatenate([values, jnp.zeros_like(values)], axis=1)
            other = jnp.concatenate([jnp.zeros_like(values), values], axis=1)
            return jnp.where(core == 0, own, other)

        result_rows, d_result_rows = incoming(returned), incoming(d_returned)
        pair_out = [matmul(pick[k], result_rows) for k in range(pick.shape[0])]
        d_pairs = matmul(pick[0] + pick[1], d_result_rows)
        moe_half = sum(gates[:, k : k + 1] * pair_out[k] for k in range(pick.shape[0]))
        d_half = lax.dynamic_slice_in_dim(cotangent, core * half, half, axis=1).astype(f32)
        d_gates_part = jnp.concatenate(
            [jnp.sum(d_half * p, axis=1, keepdims=True) for p in pair_out], axis=1
        )
        after_part = (placed(moe_half) + shared_part).astype(bf16)
        d_branch_part = (d_shared_in + placed(d_pairs)).astype(bf16)
        d_gates_part = jnp.pad(d_gates_part, ((0, 0), (0, LANES - pick.shape[0])))
        after_other, d_branch_other, d_gates_other = swap(
            [after_part, d_branch_part, d_gates_part], 6
        )
        output = (middle + (after_part.astype(f32) + after_other.astype(f32))).astype(bf16)
        d_branch_sum = d_branch_part.astype(f32) + d_branch_other.astype(f32)
        d_gates = (d_gates_part + d_gates_other)[:, : pick.shape[0]]
        d_probs = jnp.sum(d_gates[:, :, None] * picked, axis=1)
        d_logits = (probs * (d_probs - jnp.sum(probs * d_probs, axis=-1, keepdims=True))).astype(bf16)
        grad_router = weight_grad(branch_in, d_logits)
        d_branch_in = d_branch_sum + input_grad(d_logits, router_w)
        grad_gain_two = jnp.sum(d_branch_in * normed_two, axis=0)
        d_norm_two = d_branch_in * gain_second
        d_middle = d_after + scale_two * (
            d_norm_two - normed_two * jnp.mean(d_norm_two * normed_two, axis=-1, keepdims=True)
        )

        shared_grads = [
            value.astype(bf16).reshape(blocks + (hidden,)) for value in (grad_sgate, grad_sup, grad_sdown_t)
        ]
        small_grads = jnp.concatenate(
            [grad_router, grad_gain_two[:, None], jnp.zeros((width, LANES - experts - 1), f32)], axis=1
        ).astype(bf16).reshape(blocks + (LANES,))
        expert_grads = [grad_e_gate, grad_e_up, grad_e_down]
    total, d_attn_in, *combined = backward(
        [
            w_query, w_key, w_value, small_grads,
            window, queries, all_keys, all_values, lse, heads_out,
            d_middle.astype(bf16), near, gains, cosines, sines, bias,
        ],
        shared_grads, combine, shard_rows, own_columns + (3 * hidden if shared_grads else 0),
        tok_count, heads_width, width, depth, reach,
    )
    if shared_grads:
        shared_total, total = total[:, : 3 * hidden], total[:, 3 * hidden :]
    if combined:
        output = combined[0]

    def columns_of(at, count):
        return total[:, at : at + count]

    at_out = 0
    at_pairs = at_out + heads_width + LANES
    grad_parts = [
        jnp.concatenate(
            [
                columns_of(at_pairs + (3 * pair + i) * LANES, LANES)
                for pair in range(heads_width // LANES)
            ],
            axis=1,
        )
        for i in range(3)
    ]
    d_attn_in = d_attn_in.astype(f32)
    d_norm_one = d_attn_in * gain_first
    token_input_gradient = d_middle + scale_one * (
        d_norm_one - normed_one * jnp.mean(d_norm_one * normed_one, axis=-1, keepdims=True)
    )
    return (
        output,
        token_input_gradient,
        total[:, own_columns - LANES] / attn_gain.astype(bf16).astype(f32),
        grad_parts[0],
        grad_parts[1],
        grad_parts[2],
        columns_of(at_out, heads_width).T,
        total[:, at_out + heads_width + experts],
        columns_of(at_out + heads_width, experts),
        shared_total[:, :hidden],
        shared_total[:, hidden : 2 * hidden],
        shared_total[:, 2 * hidden :].T,
    ) + tuple(expert_grads)


def solution(mesh):
    by_dp, both, turned = P("dp", None), P("dp", "tensor"), P("tensor", "dp")
    wide, tall = P(None, ("dp", "tensor")), P(("dp", "tensor"), None)
    weights = (P("dp"), both, both, both, turned, P("dp"), by_dp, both, both, turned, wide, wide, tall)
    return jax.shard_map(
        local,
        mesh=mesh,
        in_specs=(by_dp, by_dp) + weights + (by_dp, P()),
        out_specs=(by_dp, by_dp) + weights,
        check_vma=False,
    )
```

```python
import functools

import jax
import jax.numpy as jnp
import numpy as np
from jax import lax
from jax.experimental import pallas as pl
from jax.experimental.pallas import tpu as pltpu
from jax.sharding import PartitionSpec as P

HEAD = 64
WINDOW = 1024
LANES = 128
PLANE = 4

MESH = pl.DeviceIdType.MESH
f32 = jnp.float32
bf16 = jnp.bfloat16

eps = 1e-06
masked = -1e30


def matmul(left, right):
    return jnp.dot(left, right, preferred_element_type=f32)


def weight_grad(left, right):
    return lax.dot_general(
        left, right, (((0,), (0,)), ((), ())), preferred_element_type=f32
    )


def input_grad(left, right):
    return lax.dot_general(
        left, right, (((1,), (1,)), ((), ())), preferred_element_type=f32
    )


def rms_parts(values):
    factor = lax.rsqrt(jnp.mean(values * values, axis=-1, keepdims=True) + eps)
    return (values * factor, factor)


def silu_grad(values):
    sigma = jax.nn.sigmoid(values)
    return sigma * (1.0 + values * (1.0 - sigma))


def digits(me):
    return lax.div(me, PLANE), lax.rem(lax.div(me, 2), 2), lax.rem(me, 2)


def index_of(z, y, x):
    return z * PLANE + y * 2 + x


def push(src, dst, send, recv, device):
    copy = pltpu.make_async_remote_copy(
        src_ref=src,
        dst_ref=dst,
        send_sem=send,
        recv_sem=recv,
        device_id=device,
        device_id_type=MESH,
    )
    copy.start()
    return copy


def greet(devices):
    barrier = pltpu.get_barrier_semaphore()
    for device in devices:
        pl.semaphore_signal(barrier, inc=1, device_id=device, device_id_type=MESH)
    pl.semaphore_wait(barrier, len(devices))


def comm_params(collective_id, limit=48 << 20):
    return pltpu.CompilerParams(
        collective_id=collective_id, has_side_effects=True, vmem_limit_bytes=limit
    )


def dma(*shape):
    return pltpu.SemaphoreType.DMA(shape)


IN_HBM = pl.BlockSpec(memory_space=pl.ANY)
IN_VMEM = pl.BlockSpec(memory_space=pltpu.VMEM)


def grid_peers(depth, z, y, x):
    peers = [{"dp": index_of(lax.rem(z + k, depth), y, x)} for k in range(1, depth)]
    return peers, {"dp": index_of(z, 1 - y, x)}, {"dp": index_of(z, y, 1 - x)}


def swap_kernel(count, *refs):
    sources, targets, (send, recv) = refs[:count], refs[count : 2 * count], refs[2 * count :]
    sibling = {"tensor": 1 - lax.axis_index("tensor")}
    greet([sibling])
    copies = [
        push(a, b, send.at[i], recv.at[i], sibling)
        for i, (a, b) in enumerate(zip(sources, targets))
    ]
    for copy in copies:
        copy.wait()


def swap(arrays, collective_id):
    count = len(arrays)
    return pl.pallas_call(
        functools.partial(swap_kernel, count),
        out_shape=tuple(jax.ShapeDtypeStruct(a.shape, a.dtype) for a in arrays),
        in_specs=[IN_VMEM] * count,
        out_specs=(IN_VMEM,) * count,
        scratch_shapes=[dma(count), dma(count)],
        compiler_params=comm_params(collective_id),
        name="swap_cores",
    )(*arrays)


def dispatch_kernel(n, owners, first, second, got_first, got_second, send, recv, f_send, f_recv, own):
    me, core = lax.axis_index("dp"), lax.axis_index("tensor")
    sibling = {"tensor": 1 - core}
    greet([{"dp": lax.rem(me + k, n)} for k in range(1, n)] + [sibling])
    half = first.shape[-1] // 2
    cols = pl.ds(pl.multiple_of(core * half, half), half)
    pairs = ((first, got_first), (second, got_second))
    mine = lax.div(me, owners)
    copies = []
    for k in range(1, n):
        to = lax.rem(me + k, n)
        for i, (source, target) in enumerate(pairs):
            copies.append(
                push(
                    source.at[lax.div(to, owners), :, cols],
                    target.at[me, :, cols],
                    send.at[i, k],
                    recv.at[i, k],
                    {"dp": to},
                )
            )
    local = [
        pltpu.make_async_copy(source.at[mine], target.at[me], own.at[i])
        for i, (source, target) in enumerate(pairs)
    ]
    for copy in local:
        copy.start()
    forwards = []
    for k in range(1, n):
        source_of = lax.rem(me + n - k, n)
        for i, (source, target) in enumerate(pairs):
            copies[2 * (k - 1) + i].wait_recv()
            block = target.at[source_of, :, cols]
            forwards.append(push(block, block, f_send.at[i, k], f_recv.at[i, k], sibling))
    for copy in forwards:
        copy.wait_recv()
    for copy in local:
        copy.wait()
    for copy in copies + forwards:
        copy.wait_send()


def dispatch(first, second, n, owners):
    shape = jax.ShapeDtypeStruct((n,) + first.shape[1:], first.dtype)
    return pl.pallas_call(
        functools.partial(dispatch_kernel, n, owners),
        out_shape=(shape, shape),
        in_specs=[IN_HBM] * 2,
        out_specs=(IN_HBM, IN_HBM),
        scratch_shapes=[dma(2, n), dma(2, n), dma(2, n), dma(2, n), dma(2)],
        compiler_params=comm_params(2),
        name="dispatch_rows",
    )(first, second)


def return_kernel(n, groups, first, second, got_first, got_second, part, total, send, recv, f_send, f_recv, own):
    me, core = lax.axis_index("dp"), lax.axis_index("tensor")
    sibling = {"tensor": 1 - core}
    greet([{"dp": lax.rem(me + k, n)} for k in range(1, n)] + [sibling])
    half = first.shape[-1] // 2
    mine = pl.ds(pl.multiple_of(core * half, half), half)
    theirs = pl.ds(pl.multiple_of((1 - core) * half, half), half)
    pairs = ((first, got_first), (second, got_second))
    each = n // groups
    swaps = []
    for g in range(groups):
        block = pl.ds(g * each, each)
        for i, (source, target) in enumerate(pairs):
            swaps.append(
                push(
                    source.at[block, :, theirs],
                    part.at[i, block],
                    f_send.at[i, g],
                    f_recv.at[i, g],
                    sibling,
                )
            )
    for g in range(groups):
        block = pl.ds(g * each, each)
        for i, (source, target) in enumerate(pairs):
            swaps[2 * g + i].wait_recv()
            total[i, block] = (
                source[block, :, mine].astype(f32) + part[i, block].astype(f32)
            ).astype(bf16)
        for slot in range(g * each, (g + 1) * each):
            for i, (source, target) in enumerate(pairs):
                @pl.when(slot != me)
                def _():
                    push(
                        total.at[i, slot],
                        target.at[me],
                        send.at[i, slot],
                        recv.at[i, me],
                        {"dp": slot},
                    )
    local = [
        pltpu.make_async_copy(total.at[i, me], pairs[i][1].at[me], own.at[i]) for i in range(2)
    ]
    for copy in local:
        copy.start()
    for k in range(1, n):
        to, source_of = lax.rem(me + k, n), lax.rem(me + n - k, n)
        for i, (source, target) in enumerate(pairs):
            pltpu.make_async_remote_copy(
                total.at[i, to], target.at[source_of], send.at[i, to], recv.at[i, source_of],
                device_id={"dp": to}, device_id_type=MESH,
            ).wait()
    for copy in local:
        copy.wait()
    for copy in swaps:
        copy.wait_send()


def give_back(first, second, groups=4):
    n, capacity, width = first.shape
    half = jax.ShapeDtypeStruct((n, capacity, width // 2), first.dtype)
    buffer = pltpu.VMEM((2, n, capacity, width // 2), first.dtype)
    return pl.pallas_call(
        functools.partial(return_kernel, n, groups),
        out_shape=(half, half),
        in_specs=[IN_VMEM] * 2,
        out_specs=(IN_HBM, IN_HBM),
        scratch_shapes=[buffer, buffer, dma(2, n), dma(2, n), dma(2, groups), dma(2, groups), dma(2)],
        compiler_params=comm_params(3),
        name="return_rows",
    )(first, second)


def experts_kernel(
    n, groups, e_gate, e_up, e_down, full, got, got_gate, branch_in, cotangent, middle, probs, pick,
    routes, gains, small,
    d_middle, shared_total, g_small, shared_part, rows_total, ge_gate, ge_up, ge_down,
    d_rows_all, gate_w, up_w, down_w, staged, shared_w, hid, d_gate, d_up, part, swapped, d_total, returned,
    inner, inner_back, shared_in, tiles, wide, ends, ends_other, d_gates, d_gates_other,
    first_l, first_r, second_l, second_r, scatter_last, p_send, p_recv, z_send, z_recv,
    s_send, s_recv, r_send, r_recv, i_send, i_recv, e_send, e_recv, own, load, store,
):
    me, core = lax.axis_index("dp"), lax.axis_index("tensor")
    sibling = {"tensor": 1 - core}
    greet([{"dp": lax.rem(me + i, n)} for i in range(1, n)] + [sibling])
    capacity, width = got.shape[2:]
    count = branch_in.shape[0]
    half = width // 2
    mine = pl.ds(pl.multiple_of(core * half, half), half)
    theirs = pl.ds(pl.multiple_of((1 - core) * half, half), half)
    hidden = shared_w.shape[4] // 3
    loads = [
        pltpu.make_async_copy(
            full.at[:, :, :, :, pl.ds(full.shape[4] - 3 * hidden, 3 * hidden)], shared_w, load.at[2]
        )
    ]
    for copy in loads:
        copy.start()
    inner[...] = jnp.zeros_like(inner)

    step = 2 * LANES
    scatter = Scatter(
        n // PLANE,
        [(shared_w, at, step, shared_w, at + step, step, at) for at in range(0, 3 * hidden, 2 * step)],
        shared_total, (first_l, first_r, second_l, second_r, scatter_last),
        (p_send, p_recv, z_send, z_recv),
    )
    steps = scatter.plan()
    done = [0]

    def advance(count=1):
        for action, c in steps[done[0] : done[0] + count]:
            done[0] += 1
            action(c)
            if action == scatter.second and c + 4 < len(scatter.chunks):
                scatter.start(c + 4)

    pieces = []
    for source, target in ((e_gate, gate_w), (e_up, up_w), (e_down, down_w)):
        step = source.shape[0] // 4
        pieces += [(source, target, pl.ds(j * step, step)) for j in range(4)]

    def fetch(j):
        source, target, rows = pieces[j]
        return pltpu.make_async_copy(
            source.at[rows],
            staged.at[j % 2, pl.ds(0, rows.size), pl.ds(0, source.shape[1])],
            load.at[j % 2],
        )

    fetch(0).start()
    fetch(1).start()

    def take(j):
        source, target, rows = pieces[j]
        fetch(j).wait()
        target[rows, :] = staged[j % 2, : rows.size, : source.shape[1]].astype(bf16)
        if j + 2 < len(pieces):
            fetch(j + 2).start()

    swaps = {}

    def work(group):
        first, each = group * n // groups, n // groups
        slots = pl.ds(first, each)
        rows = pl.ds(first * capacity, each * capacity)
        rows_in = got[0, slots].reshape(each * capacity, width)
        gate_of = jnp.concatenate([got_gate[i].T[:capacity, 0:1] for i in range(first, first + each)], axis=0)
        d_rows = (gate_of * got[1, slots].reshape(each * capacity, width).astype(f32)).astype(bf16)
        d_rows_all[rows, :] = d_rows
        gate, up = matmul(rows_in, gate_w[...]), matmul(rows_in, up_w[...])
        sigma = 1.0 / (1.0 + jnp.exp(-gate))
        act = gate * sigma
        hid_low = (act * up).astype(bf16)
        hid[rows, :] = hid_low
        part[0, slots] = matmul(hid_low, down_w[...]).astype(bf16).reshape(each, capacity, width)
        d_hid = input_grad(d_rows, down_w[...])
        d_gate_low = (d_hid * up * (sigma * (1.0 + gate * (1.0 - sigma)))).astype(bf16)
        d_up_low = (d_hid * act).astype(bf16)
        d_gate[rows, :] = d_gate_low
        d_up[rows, :] = d_up_low
        part[1, slots] = (
            (input_grad(d_gate_low, gate_w[...]) + input_grad(d_up_low, up_w[...]))
            .astype(bf16)
            .reshape(each, capacity, width)
        )
        for a in (1, 0):
            swaps[a, group] = push(
                part.at[a, slots, :, theirs], swapped.at[a, slots],
                s_send.at[a, group], s_recv.at[a, group], sibling,
            )

    back = {}

    def give(group):
        first, each = group * n // groups, n // groups
        slots = pl.ds(first, each)
        swaps[1, group].wait_recv()
        d_total[slots] = (
            part[1, slots, :, mine].astype(f32) + swapped[1, slots].astype(f32)
        ).astype(bf16)
        homes = [{"dp": lax.rem(me + n - i, n)} for i in range(n)]
        for i in range(max(first, 1), first + each):
            back[1, i] = push(
                d_total.at[i], returned.at[me], r_send.at[i], r_recv.at[i], homes[i]
            )
        swaps[0, group].wait_recv()
        value = part[0, slots, :, mine].astype(f32) + swapped[0, slots].astype(f32)
        rows_total[slots] = value.astype(bf16)
        products = jnp.sum(value * got[1, slots, :, mine].astype(f32), axis=-1, keepdims=True)
        for i in range(first, first + each):
            row = jnp.broadcast_to(products[i - first], (capacity, LANES)).T[0:8, :]
            inner[i, :, :capacity] = row
            if i:
                back[0, i] = push(
                    inner.at[i], inner_back.at[me], i_send.at[i], i_recv.at[i], homes[i]
                )

    loads[0].wait()
    branch, cot = branch_in[...], cotangent[...]
    sgate_w, sup_w, sdown_w = (stacked(shared_w, pl.ds(i * hidden, hidden)) for i in range(3))
    gate, up = matmul(branch, sgate_w), matmul(branch, sup_w)
    sigma = 1.0 / (1.0 + jnp.exp(-gate))
    act = gate * sigma
    shared_hid = (act * up).astype(bf16)
    shared_part[...] = input_grad(shared_hid, sdown_w)
    d_shared = matmul(cot, sdown_w)
    d_sgate = (d_shared * up * (sigma * (1.0 + gate * (1.0 - sigma)))).astype(bf16)
    d_sup = (d_shared * act).astype(bf16)
    shared_in[...] = input_grad(d_sgate, sgate_w) + input_grad(d_sup, sup_w)
    for i, (left, right) in enumerate(((branch, d_sgate), (branch, d_sup), (cot, shared_hid))):
        put_rows(shared_w, weight_grad(left, right).astype(bf16), pl.ds(i * hidden, hidden))
        for c in range(2 * i, 2 * i + 2):
            if c < 4:
                scatter.start(c)
    for j in range(12):
        take(j)
    work(0)
    work(1)
    give(0)
    advance()
    work(2)
    give(1)
    advance(2)
    work(3)
    give(2)
    give(3)
    advance()
    keep = [
        pltpu.make_async_copy(d_total.at[0], returned.at[me], own.at[0]),
        pltpu.make_async_copy(inner.at[0], inner_back.at[me], own.at[1]),
    ]
    for copy in keep:
        copy.start()

    stores = []

    def emit(value, tile, target):
        slot = len(stores) % 2
        if len(stores) >= 2:
            stores[-2].wait()
        tile[slot] = value.astype(bf16)
        stores.append(pltpu.make_async_copy(tile.at[slot], target, store.at[slot]))
        stores[-1].start()
        advance()

    rows_all = got[0].reshape(n * capacity, width)
    units = hid.shape[1]
    span = min(units, 256)
    for source, target in ((d_gate, ge_gate), (d_up, ge_up)):
        for at in range(0, units, span):
            columns = pl.ds(at, span)
            emit(weight_grad(rows_all, source[:, columns]), tiles, target.at[:, columns])
    for at in range(0, units, span):
        columns = pl.ds(at, span)
        emit(weight_grad(hid[:, columns], d_rows_all[...]), wide, ge_down.at[columns, :])

    for copy in keep:
        copy.wait()
    for a in range(2):
        for i in range(1, n):
            back[a, i].wait_recv()
    lane = lax.broadcasted_iota(jnp.int32, (1, LANES), 1)
    d_pairs = matmul(pick[0] + pick[1], returned[...].reshape(n * capacity, half))
    inner_row = jnp.concatenate([inner_back[e, 0:1, :capacity] for e in range(n)], axis=1)
    d_gate_lanes = jnp.zeros((count, LANES), f32)
    for i in range(2):
        value = jnp.sum(pick[i].astype(f32) * inner_row, axis=-1, keepdims=True)
        d_gate_lanes = d_gate_lanes + jnp.where(lane == i, value, 0.0)
    d_gates[...] = d_gate_lanes
    shared_in[:, mine] = shared_in[:, mine] + d_pairs
    ends[...] = shared_in[...].astype(bf16)
    last = [
        push(ends, ends_other, e_send.at[0], e_recv.at[0], sibling),
        push(d_gates, d_gates_other, e_send.at[1], e_recv.at[1], sibling),
    ]
    for copy in last:
        copy.wait()

    middle_all = middle[...]
    d_gates_all = d_gates[...] + d_gates_other[...]
    routes_turned = jnp.concatenate(
        [routes[...].astype(f32), jnp.zeros((LANES - routes.shape[0], count), f32)], axis=0
    ).T.astype(jnp.int32)
    d_probs = jnp.zeros((count, LANES), f32)
    for i in range(2):
        d_probs = d_probs + jnp.where(routes_turned[:, i : i + 1] == lane, d_gates_all[:, i : i + 1], 0.0)
    chance = probs[...]
    d_logits = (
        chance * (d_probs - jnp.sum(chance * d_probs, axis=-1, keepdims=True))
    ).astype(bf16)
    small_all = small[...]
    d_branch = (
        ends[...].astype(f32) + ends_other[...].astype(f32) + input_grad(d_logits, small_all)
    )
    factor = lax.rsqrt(jnp.mean(middle_all * middle_all, axis=-1, keepdims=True) + eps)
    normed = middle_all * factor
    gain_row = jnp.sum(d_branch * normed, axis=0, keepdims=True)
    d_norm = d_branch * gains[1:2, :]
    d_middle[...] = cotangent[...].astype(f32) + factor * (
        d_norm - normed * jnp.mean(d_norm * normed, axis=-1, keepdims=True)
    )
    put_rows(
        g_small,
        jnp.where(
            lane == n, jnp.broadcast_to(gain_row, (LANES, width)).T, weight_grad(branch, d_logits)
        ).astype(bf16),
        pl.ds(0, LANES),
    )
    for copy in stores[-2:]:
        copy.wait()
    advance(len(steps))
    scatter.drain()
    for copies in (swaps, back):
        for copy in copies.values():
            copy.wait_send()


def experts_fused(
    got, got_gate, weights, full, branch_in, cotangent, middle, probs, pick, routes, gains, small,
    depth, rows, hidden, groups=4,
):
    n, capacity, width = got.shape[1:]
    count = branch_in.shape[0]
    units = weights[0].shape[1]
    span = min(units, 256)
    half = width // 2

    def shape(*dims, dtype=bf16):
        return jax.ShapeDtypeStruct(dims, dtype)

    slots = pltpu.VMEM((n, capacity, half), bf16)
    both = pltpu.VMEM((2, n, capacity, half), bf16)
    wide = pltpu.VMEM((n * capacity, units), bf16)
    lanes = pltpu.VMEM((n, 8, LANES), f32)
    parts = 3 * hidden // (4 * LANES)
    results = pl.pallas_call(
        functools.partial(experts_kernel, n, groups),
        out_shape=(
            shape(count, width, dtype=f32), shape(rows, 3 * hidden, dtype=f32),
            shape(depth, 2, 2, rows, LANES), shape(count, width, dtype=f32), shape(n, capacity, half),
            shape(width, units), shape(width, units), shape(units, width),
        ),
        in_specs=[IN_HBM] * 4 + [IN_VMEM] * 10,
        out_specs=(IN_VMEM,) * 5 + (IN_HBM,) * 3,
        scratch_shapes=[
            pltpu.VMEM((n * capacity, width), bf16),
            pltpu.VMEM((width, units), bf16), pltpu.VMEM((width, units), bf16), pltpu.VMEM((units, width), bf16),
            pltpu.VMEM((2, max(width, units) // 4, max(width, units)), f32),
            pltpu.VMEM((depth, 2, 2, rows, 3 * hidden), bf16),
            wide, wide, wide,
            pltpu.VMEM((2, n, capacity, width), bf16),
            both, slots, slots,
            lanes, lanes,
            pltpu.VMEM((count, width), f32),
            pltpu.VMEM((2, width, span), bf16), pltpu.VMEM((2, span, width), bf16),
            pltpu.VMEM((count, width), bf16), pltpu.VMEM((count, width), bf16),
            pltpu.VMEM((count, LANES), f32), pltpu.VMEM((count, LANES), f32),
        ] + scatter_scratch(depth, rows, 3 * hidden // 2, parts) + [
            dma(2, groups), dma(2, groups),
            dma(n), dma(n), dma(n), dma(n), dma(2), dma(2), dma(2), dma(3), dma(2),
        ],
        compiler_params=comm_params(7, 62 << 20),
        name="experts_and_shared",
    )(
        *weights, full, got, got_gate, branch_in, cotangent, middle, probs, pick, routes.T, gains,
        small,
    )
    return results[:5] + ([value.astype(f32) for value in results[5:]],)


class Scatter:
    def __init__(self, depth, chunks, total, buffers, semaphores):
        self.depth, self.chunks, self.total = depth, chunks, total
        self.first_l, self.first_r, self.second_l, self.second_r, self.last = buffers
        self.p_send, self.p_recv, self.z_send, self.z_recv = semaphores
        self.z, self.y, self.x = digits(lax.axis_index("dp"))
        self.z_peers, self.y_peer, self.x_peer = grid_peers(depth, self.z, self.y, self.x)
        self.at_l, self.at_r, l, r = [], [], 0, 0
        for left, lc, lw, right, rc, rw, out in chunks:
            self.at_l.append(pl.ds(l, lw))
            self.at_r.append(pl.ds(r, rw))
            l, r = l + lw, r + rw
        self.ones, self.twos, self.threes = {}, {}, {}

    def start(self, c):
        left, lc, lw, right, rc, rw, out = self.chunks[c]
        self.ones[c] = [
            push(
                left.at[:, :, 1 - self.x, :, pl.ds(lc, lw)],
                self.first_l.at[:, :, :, self.at_l[c]],
                self.p_send.at[c, 0], self.p_recv.at[c, 0], self.x_peer,
            ),
            push(
                right.at[:, 1 - self.y, :, :, pl.ds(rc, rw)],
                self.first_r.at[:, :, :, self.at_r[c]],
                self.p_send.at[c, 1], self.p_recv.at[c, 1], self.y_peer,
            ),
        ]

    def second(self, c):
        left, lc, lw, right, rc, rw, out = self.chunks[c]
        in_l, in_r, first_l, first_r = self.at_l[c], self.at_r[c], self.first_l, self.first_r
        for copy in self.ones[c]:
            copy.wait_recv()

        def add(i, carry):
            for j in range(2):
                first_l[i, j, :, in_l] = (
                    first_l[i, j, :, in_l].astype(f32) + left[i, j, self.x, :, pl.ds(lc, lw)].astype(f32)
                ).astype(bf16)
                first_r[i, j, :, in_r] = (
                    first_r[i, j, :, in_r].astype(f32) + right[i, self.y, j, :, pl.ds(rc, rw)].astype(f32)
                ).astype(bf16)
            return carry

        lax.fori_loop(0, self.depth, add, 0)
        self.twos[c] = [
            push(
                first_l.at[:, 1 - self.y, :, in_l], self.second_l.at[:, :, in_l],
                self.p_send.at[c, 2], self.p_recv.at[c, 2], self.y_peer,
            ),
            push(
                first_r.at[:, 1 - self.x, :, in_r], self.second_r.at[:, :, in_r],
                self.p_send.at[c, 3], self.p_recv.at[c, 3], self.x_peer,
            ),
        ]

    def third(self, c):
        for copy in self.twos[c]:
            copy.wait_recv()
        sides = (
            (self.second_l, self.first_l, self.y, self.at_l[c]),
            (self.second_r, self.first_r, self.x, self.at_r[c]),
        )

        def add(i, carry):
            for source, before, place, here in sides:
                source[i, :, here] = (
                    source[i, :, here].astype(f32) + before[i, place, :, here].astype(f32)
                ).astype(bf16)
            return carry

        lax.fori_loop(0, self.depth, add, 0)
        self.threes[c] = [
            push(
                source.at[lax.rem(self.z + k + 1, self.depth), :, here],
                self.last.at[k, side, :, here],
                self.z_send.at[c, side, k], self.z_recv.at[c, side, k], self.z_peers[k],
            )
            for side, (source, before, place, here) in enumerate(sides)
            for k in range(self.depth - 1)
        ]

    def finish(self, c):
        left, lc, lw, right, rc, rw, out = self.chunks[c]
        for copy in self.threes[c]:
            copy.wait_recv()
        for side, source, here, at, span in (
            (0, self.second_l, self.at_l[c], out, lw),
            (1, self.second_r, self.at_r[c], out + lw, rw),
        ):
            value = source[self.z, :, here].astype(f32)
            for k in range(self.depth - 1):
                value = value + self.last[k, side, :, here].astype(f32)
            self.total[:, pl.ds(at, span)] = value

    def plan(self):
        count = len(self.chunks)
        steps = []
        for c in range(count + 1):
            if c < count:
                steps.append((self.second, c))
            if c >= 1:
                steps.append((self.third, c - 1))
        return steps + [(self.finish, c) for c in range(count)]

    def drain(self):
        for copies in list(self.ones.values()) + list(self.twos.values()) + list(self.threes.values()):
            for copy in copies:
                copy.wait_send()


def lanes_of(part):
    lane = lax.broadcasted_iota(jnp.int32, (1, LANES), 1)
    return (lax.div(lane, HEAD) == part).astype(f32).astype(bf16)


def swap_halves(values):
    lane = lax.broadcasted_iota(jnp.int32, (1, LANES), 1)
    low = lax.rem(lane, HEAD) < HEAD // 2
    return jnp.where(
        low, pltpu.roll(values, LANES - HEAD // 2, 1), pltpu.roll(values, HEAD // 2, 1)
    )


def put_rows(target, values, columns):
    rows = target.shape[3]
    for b in range(values.shape[0] // rows):
        target[b // PLANE, (b // 2) % 2, b % 2, :, columns] = values[b * rows : (b + 1) * rows]


def backward_kernel(
    depth, reach, per_core, shared, w_query, w_key, w_value, g_small, window, q, k, v, lse, heads_out, d_middle,
    near, gains, cosines, sines, bias, *rest,
):
    given = shared or 5
    rest, combine = rest[given:], rest[:given]
    total, d_tokens, d_full = rest[:2] + rest[-1:]
    rest = rest[2:-1]
    if not shared:
        rows_total, pick, gates, middle, shared_part = combine
        output, rows_back, end, end_other, o_send, o_recv, e_send, e_recv, keep = rest[:1] + rest[-8:]
        rest = rest[1:-8]
    (
    grads, attn_t, d_heads, dq_all, dk_all, dv_all, d_part, d_swap, d_sum, d_got, gain_got,
    first_l, first_r, second_l, second_r, last, p_send, p_recv, z_send, z_recv,
    t_send, t_recv, s_send, s_recv, f_send, f_recv,
    ) = rest
    n = depth * PLANE
    me, core = lax.axis_index("dp"), lax.axis_index("tensor")
    sibling = {"tensor": 1 - core}
    plane, z_next, z_before = Plane(me), *z_neighbours(me, n)
    heads_width = q.shape[1]
    count = q.shape[0]
    pairs = heads_width // LANES
    chunks = []
    out = 0
    step = 2 * LANES
    for source in combine if shared else ():
        for at in range(0, source.shape[4], 2 * step):
            chunks.append((source, at, step, source, at + step, step, out))
            out += 2 * step
    early = len(chunks)
    widths = [(step, step)] + [(step, LANES), (LANES, step)] * pairs
    widths = widths[: pairs + 1]
    at = 0
    for left, right in widths:
        chunks.append((grads, at, left, grads, at + left, right, out + at))
        at += left + right
    scatter = Scatter(
        depth, chunks, total, (first_l, first_r, second_l, second_r, last),
        (p_send, p_recv, z_send, z_recv),
    )
    if shared:
        greet(scatter.z_peers + plane.peers + [sibling, z_next, z_before])
    else:
        greet([{"dp": lax.rem(me + i, n)} for i in range(1, n)] + [sibling])
    lead = 4
    for c in range(min(lead, early)):
        scatter.start(c)
    steps = scatter.plan()
    done = [0]

    def advance(count=1):
        for action, c in steps[done[0] : done[0] + count]:
            if action == scatter.second and c not in scatter.ones:
                break
            done[0] += 1
            action(c)
            if action == scatter.second and c + lead < early:
                scatter.start(c + lead)

    out_w = pl.ds(LANES + 3 * heads_width, heads_width)
    gain = gains[0:1, :]
    d_attn = d_middle[...].astype(bf16)
    d_heads[...] = matmul(d_attn, stacked(near, out_w)).astype(bf16)
    put_rows(grads, weight_grad(d_attn, heads_out[...]).astype(bf16), pl.ds(0, heads_width))
    grads[:, :, :, :, pl.ds(heads_width, LANES)] = g_small[...]

    def normed(block):
        values = window[block].astype(f32)
        return values * lax.rsqrt(jnp.mean(values * values, axis=-1, keepdims=True) + eps)

    def turned(block, carry):
        rows = pl.ds(pl.multiple_of(block * count, count), count)
        attn_t[:, rows] = (normed(block) * gain).T.astype(bf16)
        return carry

    for block in range(reach + 1):
        turned(block, 0)
    scatter.start(early)
    home = []
    if not shared:
        home = [
            push(
                rows_total.at[i], rows_back.at[me], o_send.at[i], o_recv.at[i],
                {"dp": lax.rem(me + n - i, n)},
            )
            for i in range(1, n)
        ]
        kept = pltpu.make_async_copy(rows_total.at[0], rows_back.at[me], keep.at[0])
        kept.start()
    own = pl.ds(reach * count, count)
    for pair in range(pairs):
        columns = pl.ds(pair * LANES, LANES)
        k_pair, v_pair, q_pair, d_pair = k[:, columns], v[:, columns], q[:, columns], d_heads[:, columns]
        k_turned = k_pair.T
        dq, dk, dv = [], None, None
        for part in range(2):
            head = 2 * pair + part
            lanes = lanes_of(part)
            q_head, d_head = q_pair * lanes, d_pair * lanes
            probs = jnp.exp(input_grad(k_pair, q_head) + bias[...] - lse[head : head + 1, :])
            d_probs = input_grad(v_pair, d_head)
            inner = jnp.sum(probs * d_probs, axis=0, keepdims=True)
            d_scores = (probs * (d_probs - inner)).astype(bf16)
            advance(1 if shared else 0)
            dq.append(matmul(k_turned, d_scores)[part * HEAD : (part + 1) * HEAD, :])
            parts = matmul(d_scores, q_head), matmul(probs.astype(bf16), d_head)
            dk, dv = parts if part == 0 else (dk + parts[0], dv + parts[1])
            advance(1 if shared else 0)
        dq = jnp.concatenate(dq, axis=0).T * (HEAD ** (-0.5))
        cos_own, sin_own = cosines[own, :], sines[own, :]
        dq_low = turn(dq, cos_own, -sin_own).astype(bf16)
        dk_low = turn(dk, cosines[...], -sines[...]).astype(bf16)
        dv_low = dv.astype(bf16)
        dq_all[:, columns] = dq_low
        dk_all[:, columns] = dk_low
        dv_all[:, columns] = dv_low
        at = heads_width + LANES + pair * 3 * LANES
        put_rows(grads, matmul(attn_t[:, own], dq_low).astype(bf16), pl.ds(at, LANES))
        put_rows(grads, matmul(attn_t[...], dk_low).astype(bf16), pl.ds(at + LANES, LANES))
        put_rows(grads, matmul(attn_t[...], dv_low).astype(bf16), pl.ds(at + 2 * LANES, LANES))
        scatter.start(early + 1 + pair)
        advance(2 if shared else min(pair + 1, 2))

    width = d_part.shape[-1] // 2
    mine = pl.ds(pl.multiple_of(core * width, width), width)
    theirs = pl.ds(pl.multiple_of((1 - core) * width, width), width)
    swaps = {}
    query_v, key_v, value_v = (
        jnp.concatenate(
            [stacked(near, pl.ds(LANES * (1 + 3 * pair + i), LANES)) for pair in range(pairs)], axis=1
        )
        for i in range(3)
    )
    back = [None] * (PLANE - 1)

    def meet(block):
        swaps[block].wait_recv()
        d_sum[block] = (
            d_part[block, :, mine].astype(f32) + d_swap[block].astype(f32)
        ).astype(bf16)

    blocks = list(range(1, reach)) + [0, reach]
    for i, block in enumerate(blocks):
        rows = pl.ds(block * count, count)
        value = input_grad(dk_all[rows, :], key_v) + input_grad(dv_all[rows, :], value_v)
        if block == reach:
            value = value + input_grad(dq_all[...], query_v)
        d_part[block] = value.astype(bf16)
        swaps[block] = push(
            d_part.at[block, :, theirs], d_swap.at[block],
            s_send.at[block], s_recv.at[block], sibling,
        )
        if i:
            meet(blocks[i - 1])
        if i == reach - 1:
            for j in range(1, PLANE):
                back[j - 1] = push(
                    d_sum.at[lax.rem(plane.places[j] - plane.place + PLANE, PLANE)],
                    d_got.at[j], t_send.at[j], t_recv.at[j], plane.peers[j - 1],
                )
    meet(reach)
    swaps = list(swaps.values())
    advance(1)
    last_swap = []
    if not shared:
        kept.wait()
        for copy in home:
            copy.wait_recv()
        rows_all = rows_back[...].reshape(-1, width)
        moe = gates[:, 0:1] * matmul(pick[0], rows_all) + gates[:, 1:2] * matmul(pick[1], rows_all)
        end[...] = shared_part[...].astype(bf16)
        end[:, mine] = (shared_part[:, mine] + moe).astype(bf16)
        last_swap.append(push(end, end_other, e_send.at[0], e_recv.at[0], sibling))
    d_mine, d_before = d_sum[reach].astype(f32), d_sum[0].astype(f32)
    for j in range(1, PLANE):
        back[j - 1].wait_recv()
        ours = lax.select(plane.places[j] > plane.place, 1.0, 0.0)
        value = d_got[j].astype(f32)
        d_mine, d_before = d_mine + value * ours, d_before + value * (1.0 - ours)
    d_sum[reach] = d_before.astype(bf16)
    back.append(push(d_sum.at[reach], d_got.at[0], t_send.at[0], t_recv.at[0], z_before))
    advance(len(steps))
    if not shared:
        last_swap[0].wait_recv()
        output[...] = (
            middle[...] + (end[...].astype(f32) + end_other[...].astype(f32))
        ).astype(bf16)
    back[-1].wait_recv()
    d_mine = d_mine + d_got[0].astype(f32)
    d_full[:, mine] = d_mine.astype(bf16)
    both = push(d_full.at[:, mine], d_full.at[:, mine], f_send.at[0], f_recv.at[0], sibling)
    gain_sum = jnp.zeros((total.shape[0], 1), f32)
    at = out + heads_width + LANES
    for pair in range(pairs):
        for i, source in enumerate((w_query, w_key, w_value)):
            rounded = source[:, pl.ds(pair * LANES, LANES)].astype(bf16).astype(f32)
            products = total[:, pl.ds(at + (3 * pair + i) * LANES, LANES)] * rounded
            gain_sum = gain_sum + jnp.sum(products, axis=-1, keepdims=True)
    split = pl.ds(per_core, LANES)
    total[:, split] = jnp.broadcast_to(gain_sum, (total.shape[0], LANES))
    gain_copy = push(total.at[:, split], gain_got, f_send.at[1], f_recv.at[1], sibling)
    both.wait()
    gain_copy.wait()
    total[:, split] = total[:, split] + gain_got[...]
    values = window[reach].astype(f32)
    factor = lax.rsqrt(jnp.mean(values * values, axis=-1, keepdims=True) + eps)
    values = values * factor
    d_norm = d_full[...].astype(f32) * gain
    d_tokens[...] = d_middle[...] + factor * (
        d_norm - values * jnp.mean(d_norm * values, axis=-1, keepdims=True)
    )
    scatter.drain()
    for copy in back + swaps + last_swap + home:
        copy.wait_send()


def backward(arrays, shared, combine, rows, columns, count, heads_width, width, depth, reach):
    span = (reach + 1) * count
    summed = columns - LANES
    half = -(-summed // (2 * LANES)) * LANES
    width_shared = sum(value.shape[4] for value in shared)
    parts = width_shared // (4 * LANES) + 1 + heads_width // LANES
    own = summed - width_shared
    outs = (
        jax.ShapeDtypeStruct((rows, columns), f32),
        jax.ShapeDtypeStruct((count, width), f32),
    )
    extra = []
    if not shared:
        outs += (jax.ShapeDtypeStruct((count, width), bf16),)
        low = pltpu.VMEM((count, width), bf16)
        n = depth * PLANE
        extra = [
            pltpu.VMEM(combine[0].shape, bf16), low, low, dma(n), dma(n), dma(1), dma(1), dma(1)
        ]
    arrays = list(arrays) + list(shared) + list(combine)
    return pl.pallas_call(
        functools.partial(backward_kernel, depth, reach, columns - LANES, len(shared)),
        out_shape=outs,
        in_specs=[IN_VMEM] * len(arrays),
        out_specs=(IN_VMEM,) * len(outs),
        scratch_shapes=[
            pltpu.VMEM((depth, 2, 2, rows, own), bf16),
            pltpu.VMEM((width, span), bf16),
            pltpu.VMEM((count, heads_width), bf16),
            pltpu.VMEM((count, heads_width), bf16),
            pltpu.VMEM((span, heads_width), bf16),
            pltpu.VMEM((span, heads_width), bf16),
            pltpu.VMEM((reach + 1, count, width), bf16),
            pltpu.VMEM((reach + 1, count, width // 2), bf16),
            pltpu.VMEM((reach + 1, count, width // 2), bf16),
            pltpu.VMEM((reach, count, width // 2), bf16),
            pltpu.VMEM((rows, LANES), f32),
        ] + scatter_scratch(depth, rows, half, parts) + [
            dma(reach), dma(reach), dma(reach + 1), dma(reach + 1), dma(2), dma(2),
        ] + extra + [pltpu.VMEM((count, width), bf16)],
        compiler_params=comm_params(4, 58 << 20),
        name="attention_backward",
    )(*arrays)


def scatter_scratch(depth, rows, half, parts):
    first = pltpu.VMEM((depth, 2, rows, half), bf16)
    second = pltpu.VMEM((depth, rows, half), bf16)
    return [
        first, first, second, second, pltpu.VMEM((depth - 1, 2, rows, half), bf16),
        dma(parts, 4), dma(parts, 4), dma(parts, 2, depth - 1), dma(parts, 2, depth - 1),
    ]


class Plane:
    def __init__(self, me):
        z, y, x = digits(me)
        self.place = y * 2 + x
        self.places, self.peers = [self.place], []
        for j in range(1, PLANE):
            y_j, x_j = (1 - y if j & 2 else y), (1 - x if j & 1 else x)
            self.places.append(y_j * 2 + x_j)
            self.peers.append({"dp": index_of(z, y_j, x_j)})


def z_neighbours(me, n):
    return {"dp": lax.rem(me + PLANE, n)}, {"dp": lax.rem(me + n - PLANE, n)}


class Gather:
    def __init__(self, depth, chunks, shard, full, semaphores):
        self.depth, self.chunks, self.shard, self.full = depth, chunks, shard, full
        self.z_send, self.z_recv, self.p_send, self.p_recv = semaphores
        self.z, self.y, self.x = digits(lax.axis_index("dp"))
        self.z_peers, self.y_peer, self.x_peer = grid_peers(depth, self.z, self.y, self.x)
        self.ones, self.twos, self.threes = {}, {}, {}

    def _sides(self, c):
        at, left, right = self.chunks[c]
        return pl.ds(at, left), pl.ds(at + left, right)

    def first(self, c):
        at, left, right = self.chunks[c]
        columns = pl.ds(at, left + right)
        self.ones[c] = [
            push(
                self.shard.at[:, columns],
                self.full.at[self.z, self.y, self.x, :, columns],
                self.z_send.at[c, k], self.z_recv.at[c, k], self.z_peers[k],
            )
            for k in range(self.depth - 1)
        ]

    def second(self, c):
        left, right = self._sides(c)
        for copy in self.ones[c]:
            copy.wait_recv()
        a = self.full.at[:, self.y, self.x, :, left]
        b = self.full.at[:, self.y, self.x, :, right]
        self.twos[c] = [
            push(a, a, self.p_send.at[c, 0], self.p_recv.at[c, 0], self.y_peer),
            push(b, b, self.p_send.at[c, 1], self.p_recv.at[c, 1], self.x_peer),
        ]

    def third(self, c):
        left, right = self._sides(c)
        for copy in self.twos[c]:
            copy.wait_recv()
        a = self.full.at[:, :, self.x, :, left]
        b = self.full.at[:, self.y, :, :, right]
        self.threes[c] = [
            push(a, a, self.p_send.at[c, 2], self.p_recv.at[c, 2], self.x_peer),
            push(b, b, self.p_send.at[c, 3], self.p_recv.at[c, 3], self.y_peer),
        ]

    def finish(self, c):
        for copy in self.threes[c]:
            copy.wait_recv()

    def plan(self, lead, near):
        count = len(self.chunks)
        steps = []
        for s in range(count + 2):
            if s < count:
                steps.append((self.second, s))
                if s + lead < count:
                    steps.append((self.first, s + lead))
            if 1 <= s <= count:
                steps.append((self.third, s - 1))
            if 2 <= s < near + 2:
                steps.append((self.finish, s - 2))
        return steps + [(self.finish, c) for c in range(near, count)]

    def drain(self):
        for copies in list(self.ones.values()) + list(self.twos.values()) + list(self.threes.values()):
            for copy in copies:
                copy.wait_send()


def stacked(ref, columns):
    rows = ref.shape[3]
    if rows % 16 == 0:
        return ref[:, :, :, :, columns].reshape(-1, columns.size)
    blocks = [
        ref[b // PLANE, (b // 2) % 2, b % 2, :, columns].astype(f32)
        for b in range(ref.shape[0] * PLANE)
    ]
    return jnp.concatenate(blocks, axis=0).astype(bf16)


def turn(values, cos, sin):
    return values * cos + swap_halves(values) * sin


def forward_kernel(
    depth, reach, experts, chunks, near_edges, w_router, attn_gain, ffn_gain, w_query, w_key, w_value, out_shard, w_sgate, w_sup, down_shard,
    tokens, cotangent, routes, segments, row_cos, row_sin, block_cos, block_sin,
    full, near, small, window, q, k, v, lse, heads_out, cosines, sines, bias, gains, middle, branch_in, probs, gates, pick,
    *rest,
):
    n = depth * PLANE
    fused = n == experts
    if fused:
        got, got_gate, rows_send, gate_send, d_send, d_recv, e_send, e_recv, g_send, g_recv = (
            rest[:2] + rest[-8:]
        )
        rest = rest[2:-8]
        rows_out, d_rows_out = rows_send.at[0], rows_send.at[1]
    else:
        rows_out, d_rows_out = rest[:2]
        rest = rest[2:]
    (
        shard, attn_in, part, other,
        z_send, z_recv, p_send, p_recv, t_send, t_recv, f_send, f_recv, s_send, s_recv, own,
    ) = rest
    me, core = lax.axis_index("dp"), lax.axis_index("tensor")
    sibling = {"tensor": 1 - core}
    gather = Gather(depth, chunks, shard, full, (z_send, z_recv, p_send, p_recv))
    heads_width = q.shape[1]
    pairs = heads_width // LANES
    order = [None]
    for pair in range(pairs):
        order += [(piece, pair * LANES, LANES) for piece in (w_query, w_key, w_value)]
    order += [(piece, 0, piece.shape[1]) for piece in (out_shard, w_sgate, w_sup, down_shard)]
    def pack(pieces, at):
        for piece, start, size in pieces:
            shard[:, pl.ds(at, size)] = piece[:, pl.ds(start, size)].astype(bf16)
            at += size
        return at

    turned_small = jnp.concatenate(
        [w_router[...], attn_gain[...], ffn_gain[...], jnp.zeros((LANES - experts - 2, w_router.shape[1]), f32)],
        axis=0,
    )
    shard[:, pl.ds(0, LANES)] = turned_small.T.astype(bf16)
    at = pack(order[1:4], LANES)
    plane, z_next, z_before = Plane(me), *z_neighbours(me, n)
    if fused:
        greet([{"dp": lax.rem(me + i, n)} for i in range(1, n)] + [sibling])
    else:
        greet(gather.z_peers + plane.peers + [sibling, z_next, z_before])
    count, width = tokens.shape
    half = count // 2
    rows = pl.ds(pl.multiple_of(core * half, half), half)
    lead = 3
    gather.first(0)
    from_before = push(tokens.at[rows], window.at[0, rows], t_send.at[0], t_recv.at[0], z_next)
    pack(order[4:], at)
    for c in range(1, lead):
        gather.first(c)
    own_shard = pltpu.make_async_copy(shard, full.at[gather.z, gather.y, gather.x], own.at[0])
    own_shard.start()
    window[reach] = tokens[...]

    lane = lax.broadcasted_iota(jnp.int32, (1, LANES), 1)
    sign = jnp.where(lax.rem(lane, HEAD) < HEAD // 2, -1.0, 1.0)
    lines = count // LANES

    def segment_row(block):
        part = segments[pl.ds(block * lines, lines), :].astype(f32)
        return jnp.concatenate([part[i : i + 1, :] for i in range(lines)], axis=1)

    seg_query = segment_row(me)
    routes_turned = jnp.concatenate(
        [routes[...].astype(f32), jnp.zeros((LANES - routes.shape[0], count), f32)], axis=0
    ).T.astype(jnp.int32)
    tops = routes.shape[0]
    key_place = lax.broadcasted_iota(jnp.int32, (count, count), 0)
    query_place = lax.broadcasted_iota(jnp.int32, (count, count), 1)
    for b in range(reach + 1):
        at = pl.ds(b * count, count)
        c_b, s_b = block_cos[pl.ds(me + b, 1), :], block_sin[pl.ds(me + b, 1), :]
        cosines[at, :] = c_b * row_cos[...] - s_b * row_sin[...]
        sines[at, :] = (s_b * row_cos[...] + c_b * row_sin[...]) * sign
        block = me - reach + b
        seg_key = segment_row(lax.max(block, 0))
        seg_key = jnp.broadcast_to(seg_key, (LANES, count)).T[:, :1]
        distance = (reach - b) * count + query_place - key_place
        limit = lax.select(block >= 0, WINDOW, 0)
        seen = (distance >= 0) & (distance < limit) & (seg_key == seg_query)
        bias[at, :] = jnp.where(seen, 0.0, masked)

    capacity = rows_out.shape[1]
    named = [(routes_turned[:, i : i + 1] == lane).astype(f32) for i in range(tops)]
    below = (key_place > query_place).astype(f32).astype(bf16)
    before = matmul(below, sum(named).astype(bf16))
    slot_of = lax.broadcasted_iota(jnp.int32, (count, experts * capacity), 1)
    for i, name in enumerate(named):
        place = jnp.sum(name * before, axis=-1, keepdims=True).astype(jnp.int32)
        place = place + routes_turned[:, i : i + 1] * capacity
        pick[i] = (slot_of == place).astype(f32).astype(bf16)
    features = pl.ds(pl.multiple_of(core * (width // 2), width // 2), width // 2)
    sent, passed = {}, {}

    def dispatch_rows(a):
        for i in range(1, n):
            to = lax.rem(me + i, n)
            sent[a, i] = push(
                rows_send.at[a, to, :, features], got.at[a, i, :, features],
                d_send.at[a, i], d_recv.at[a, i], {"dp": to},
            )
        got[a, 0] = rows_send[a, me]

    def forward_rows(a):
        for i in range(1, n):
            sent[a, i].wait_recv()
            block = got.at[a, i, :, features]
            passed[a, i] = push(block, block, e_send.at[a, i], e_recv.at[a, i], sibling)

    if fused:
        rows_send[1] = (
            weight_grad(pick[0] + pick[1], cotangent[...]).astype(bf16).reshape(rows_out.shape)
        )

    def normed(b):
        values = window[b].astype(f32)
        return values * lax.rsqrt(jnp.mean(values * values, axis=-1, keepdims=True) + eps)

    own_shard.wait()
    steps = gather.plan(lead, len(near_edges))
    done = [0]

    def advance(until=None, waits=None):
        while done[0] < len(steps) and waits != 0:
            action, c = steps[done[0]]
            done[0] += 1
            action(c)
            if waits is not None and action != gather.first:
                waits -= 1
            if (action, c) == until:
                break

    from_before.wait_recv()
    t_copies = [from_before]
    for j in range(1, PLANE):
        source = window.at[lax.select(plane.places[j] < plane.place, 0, reach), rows]
        target = window.at[lax.rem(plane.place - plane.places[j] + PLANE, PLANE), rows]
        t_copies.append(push(source, target, t_send.at[j], t_recv.at[j], plane.peers[j - 1]))
    advance((gather.second, 1))
    forwards = []
    for j, copy in enumerate(t_copies):
        if j:
            copy.wait_recv()
        block = window.at[lax.rem(plane.places[j] - plane.place + PLANE, PLANE), rows]
        forwards.append(push(block, block, f_send.at[j], f_recv.at[j], sibling))
    landed = 0
    copies = []
    for i, (edge, c) in enumerate(near_edges):
        copies.append((c, pl.ds(landed, edge - landed), own.at[1 + i]))
        landed = edge

    def land(i):
        c, columns, semaphore = copies[i]
        advance((gather.finish, c))
        copy = pltpu.make_async_copy(
            full.at[:, :, :, :, columns], near.at[:, :, :, :, columns], semaphore
        )
        copy.start()
        copy.wait()

    land(0)
    if fused:
        dispatch_rows(1)
    for copy in forwards:
        copy.wait_recv()
    small_all = stacked(near, pl.ds(0, LANES))
    small[...] = small_all
    small_turned = small_all.astype(f32).T
    gain_first, gain_second = small_turned[experts : experts + 1, :], small_turned[experts + 1 : experts + 2, :]
    gains[...] = small_turned[experts : experts + 8, :]
    own_rows = pl.ds(reach * count, count)
    for b in range(reach + 1):
        attn_in[pl.ds(b * count, count), :] = (normed(b) * gain_first).astype(bf16)
    lse[...] = jnp.zeros_like(lse)
    for pair in range(pairs):
        if pair:
            land(pair)
        at = LANES * (1 + 3 * pair)
        columns = pl.ds(pair * LANES, LANES)
        products = matmul(attn_in[...], stacked(near, pl.ds(at + LANES, 2 * LANES)))
        k_pair = turn(products[:, :LANES], cosines[...], sines[...]).astype(bf16)
        v_pair = products[:, LANES:].astype(bf16)
        queries = matmul(attn_in[own_rows, :], stacked(near, pl.ds(at, LANES)))
        q_pair = (
            turn(queries, cosines[own_rows, :], sines[own_rows, :]) * (HEAD ** (-0.5))
        ).astype(bf16)
        k[:, columns], v[:, columns], q[:, columns] = k_pair, v_pair, q_pair
        v_turned = v_pair.T
        outs = []
        for part_of in range(2):
            head = 2 * pair + part_of
            scores = input_grad(k_pair, q_pair * lanes_of(part_of)) + bias[...]
            peak = jnp.max(scores, axis=0, keepdims=True)
            expo = jnp.exp(scores - peak)
            total = jnp.sum(expo, axis=0, keepdims=True)
            lse[head : head + 1, :] = peak + jnp.log(total)
            weights = (expo * (1.0 / total)).astype(bf16)
            outs.append(matmul(v_turned, weights)[part_of * HEAD : (part_of + 1) * HEAD, :])
            advance(waits=1)
        heads_out[:, columns] = jnp.concatenate(outs, axis=0).T.astype(bf16)
    land(pairs)
    out_w = stacked(near, pl.ds(LANES + 3 * heads_width, heads_width))
    part[...] = input_grad(heads_out[...], out_w).astype(bf16)
    swapped = push(part, other, s_send.at[0], s_recv.at[0], sibling)
    swapped.wait()
    middle_all = tokens[...].astype(f32) + (part[...].astype(f32) + other[...].astype(f32))
    middle[...] = middle_all
    factor = lax.rsqrt(jnp.mean(middle_all * middle_all, axis=-1, keepdims=True) + eps)
    branch = (middle_all * factor * gain_second).astype(bf16)
    branch_in[...] = branch

    logits = jnp.where(lane < experts, matmul(branch, small_all), masked)
    expo = jnp.exp(logits - jnp.max(logits, axis=-1, keepdims=True))
    chance = expo / jnp.sum(expo, axis=-1, keepdims=True)
    probs[...] = chance
    gate_lanes = jnp.zeros((count, LANES), f32)
    gate_row = jnp.zeros((1, experts * capacity), f32)
    d_gathered = None if fused else jnp.zeros((experts * capacity, width), f32)
    for i, name in enumerate(named):
        gate = jnp.sum(chance * name, axis=-1, keepdims=True)
        gate_lanes = gate_lanes + jnp.where(lane == i, gate, 0.0)
        if fused:
            gate_row = gate_row + jnp.sum(gate * pick[i].astype(f32), axis=0, keepdims=True)
        else:
            d_rows = (gate * cotangent[...].astype(f32)).astype(bf16)
            d_gathered = d_gathered + weight_grad(pick[i], d_rows)
    gates[...] = gate_lanes
    if fused:
        gate_send[...] = jnp.zeros_like(gate_send)
        for e in range(experts):
            gate_send[e, 0:1, :capacity] = gate_row[:, e * capacity : (e + 1) * capacity]
    else:
        d_rows_out[...] = d_gathered.astype(bf16).reshape(d_rows_out.shape)
    rows_out[...] = weight_grad(pick[0] + pick[1], branch).astype(bf16).reshape(rows_out.shape)
    gate_sent = []
    if fused:
        dispatch_rows(0)
        for i in range(1, n):
            to = lax.rem(me + i, n)
            gate_sent.append(
                push(gate_send.at[to], got_gate.at[i], g_send.at[i], g_recv.at[i], {"dp": to})
            )
        got_gate[0] = gate_send[me]
        advance(waits=4)
        forward_rows(1)
        advance(waits=5)
        forward_rows(0)
    advance()
    if fused:
        for copy in gate_sent:
            copy.wait_recv()
        for copy in passed.values():
            copy.wait_recv()
        for copy in list(sent.values()) + list(passed.values()) + gate_sent:
            copy.wait_send()
    gather.drain()
    for copy in t_copies + forwards:
        copy.wait_send()


def angle_tables(tok_count, blocks, reach):
    freqs = (10000.0 ** (-np.arange(HEAD // 2, dtype=np.float32) * np.float32(2.0 / HEAD))).astype(np.float64)
    freqs = np.tile(freqs, LANES // (HEAD // 2))[None, :]
    inner = np.arange(tok_count)[:, None] * freqs
    starts = np.maximum(np.arange(-reach, blocks), 0) * tok_count
    starts = np.pad(starts, (0, -len(starts) % 8))[:, None] * freqs
    return [jnp.asarray(f(a), f32) for a in (inner, starts) for f in (np.cos, np.sin)]


def forward(arrays, tokens, cotangent, routes, segments, depth, reach, experts, heads_width, hidden):
    count, width = tokens.shape
    n = depth * PLANE
    rows = arrays[3].shape[0]
    span = (reach + 1) * count
    near_width = LANES + 4 * heads_width
    columns = near_width + 3 * hidden
    capacity = count // 4
    step = 4 * LANES
    pairs = heads_width // LANES
    widths = [step] + [3 * LANES] * (pairs - 1) + [heads_width] + [step] * ((columns - near_width) // step)
    chunks, at = [], 0
    for w in widths:
        left = (w // LANES + (len(chunks) + 1) % 2) // 2 * LANES
        chunks.append((at, left, w - left))
        at += w
    near_edges = tuple((sum(widths[: c + 1]), c) for c in range(pairs + 1))
    parts = len(chunks)
    tables = angle_tables(count, n, reach)
    segment_rows = segments.reshape(-1, LANES)

    def shape(*dims, dtype=bf16):
        return jax.ShapeDtypeStruct(dims, dtype)

    outs = (
        shape(depth, 2, 2, rows, columns),
        shape(depth, 2, 2, rows, near_width),
        shape(width, LANES),
        shape(reach + 1, count, width),
        shape(count, heads_width), shape(span, heads_width), shape(span, heads_width),
        shape(-(-heads_width // HEAD // 8) * 8, count, dtype=f32),
        shape(count, heads_width),
        shape(span, LANES, dtype=f32), shape(span, LANES, dtype=f32), shape(span, count, dtype=f32),
        shape(8, width, dtype=f32),
        shape(count, width, dtype=f32), shape(count, width),
        shape(count, LANES, dtype=f32), shape(count, LANES, dtype=f32),
        shape(routes.shape[1], count, experts * capacity),
    )
    if n == experts:
        outs += (shape(2, n, capacity, width), shape(n, 8, LANES, dtype=f32))
        extra = [
            pltpu.VMEM((2, n, capacity, width), bf16), pltpu.VMEM((n, 8, LANES), f32),
            dma(2, n), dma(2, n), dma(2, n), dma(2, n), dma(n), dma(n),
        ]
    else:
        outs += (shape(experts, capacity, width), shape(experts, capacity, width))
        extra = []
    inputs = list(arrays) + [tokens, cotangent, routes.T, segment_rows, tables[0], tables[1], tables[2], tables[3]]
    return pl.pallas_call(
        functools.partial(forward_kernel, depth, reach, experts, tuple(chunks), near_edges),
        out_shape=outs,
        in_specs=[IN_VMEM] * len(inputs),
        out_specs=(IN_HBM,) + (IN_VMEM,) * (len(outs) - 1),
        scratch_shapes=[
            pltpu.VMEM((rows, columns), bf16),
            pltpu.VMEM((span, width), bf16),
            pltpu.VMEM((count, width), bf16),
            pltpu.VMEM((count, width), bf16),
            dma(parts, depth - 1), dma(parts, depth - 1), dma(parts, 4), dma(parts, 4),
            dma(reach), dma(reach), dma(reach), dma(reach), dma(1), dma(1), dma(2 + pairs),
        ] + extra,
        compiler_params=comm_params(1, 58 << 20),
        name="gather_and_attend",
    )(*inputs)


def local(
    tokens, cotangent, attn_gain, w_query, w_key, w_value, w_out, ffn_gain, w_router,
    w_sgate, w_sup, w_sdown, e_gate, e_up, e_down, routes, segments,
):
    tok_count, width = tokens.shape
    n = lax.axis_size("dp")
    depth = n // PLANE
    me = lax.axis_index("dp")
    core = lax.axis_index("tensor")
    experts = w_router.shape[1]
    owners = n // experts
    capacity = tok_count // 4
    reach = (WINDOW + tok_count - 1) // tok_count
    shard_rows = w_query.shape[0]
    heads_width = w_query.shape[1]
    hidden = w_sgate.shape[1]
    half = width // 2

    near_width = LANES + 4 * heads_width
    own_columns = near_width + LANES
    (
        full, near, small, window, queries, all_keys, all_values, lse, heads_out, cosines, sines, bias, gains,
        middle, branch_in, probs, gates, pick, *sent_rows,
    ) = forward(
        (w_router.T, attn_gain[None, :], ffn_gain[None, :], w_query, w_key, w_value, w_out.T, w_sgate, w_sup, w_sdown.T),
        tokens, cotangent, routes, segments, depth, reach, experts, heads_width, hidden,
    )
    gain_second = gains[1]
    blocks = (depth, 2, 2, shard_rows)
    if owners == 1:
        d_middle, shared_total, small_grads, shared_part, rows_back, expert_grads = experts_fused(
            *sent_rows, (e_gate, e_up, e_down), full, branch_in, cotangent, middle, probs,
            pick, routes, gains, small, depth, shard_rows, hidden,
        )
        shared_grads, combine = (), (rows_back, pick, gates, middle, shared_part)
    else:
        sgate_w, sup_w, sdown_t = (
            full[:, :, :, :, near_width + i * hidden : near_width + (i + 1) * hidden].reshape(width, hidden)
            for i in range(3)
        )
        router_w = small[:, :experts]
        expert_gate = e_gate.astype(bf16)
        expert_up = e_up.astype(bf16)
        expert_down = e_down.astype(bf16)
        normed_two, scale_two = rms_parts(middle)
        probs = probs[:, :experts]
        picked = (routes[:, :, None] == jnp.arange(experts, dtype=jnp.int32)[None, None, :]).astype(f32)
        d_after = cotangent.astype(f32)
        combine = ()
        rows_in, d_rows_in = dispatch(*sent_rows, n, owners)

        rows_in = rows_in.reshape(n * capacity, width)
        d_rows_in = d_rows_in.reshape(n * capacity, width)
        gate_hidden = matmul(rows_in, expert_gate)
        up_hidden = matmul(rows_in, expert_up)
        gate_act = jax.nn.silu(gate_hidden)
        expert_hidden = (gate_act * up_hidden).astype(bf16)
        part_rows = matmul(expert_hidden, expert_down).astype(bf16)
        d_hidden = input_grad(d_rows_in, expert_down)
        d_gate_hidden = (d_hidden * up_hidden * silu_grad(gate_hidden)).astype(bf16)
        d_up_hidden = (d_hidden * gate_act).astype(bf16)
        d_part_rows = (
            input_grad(d_gate_hidden, expert_gate) + input_grad(d_up_hidden, expert_up)
        ).astype(bf16)
        returned, d_returned = give_back(
            part_rows.reshape(n, capacity, width), d_part_rows.reshape(n, capacity, width)
        )
        grad_e_down = weight_grad(expert_hidden, d_rows_in)
        grad_e_gate = weight_grad(rows_in, d_gate_hidden)
        grad_e_up = weight_grad(rows_in, d_up_hidden)

        shared_gate = matmul(branch_in, sgate_w)
        shared_up = matmul(branch_in, sup_w)
        shared_act = jax.nn.silu(shared_gate)
        shared_hidden = (shared_act * shared_up).astype(bf16)
        shared_part = input_grad(shared_hidden, sdown_t)
        d_shared = matmul(cotangent, sdown_t)
        grad_sdown_t = weight_grad(cotangent, shared_hidden)
        d_sgate = (d_shared * shared_up * silu_grad(shared_gate)).astype(bf16)
        d_sup = (d_shared * shared_act).astype(bf16)
        grad_sgate = weight_grad(branch_in, d_sgate)
        grad_sup = weight_grad(branch_in, d_sup)
        d_shared_in = input_grad(d_sgate, sgate_w) + input_grad(d_sup, sup_w)

        def incoming(rows):
            rows = rows.reshape(experts, owners, capacity, half)
            if owners > 1:
                rows = jnp.sum(rows.astype(f32), axis=1).astype(bf16)
            return rows.reshape(experts * capacity, half)

        def placed(values):
            own = jnp.concatenate([values, jnp.zeros_like(values)], axis=1)
            other = jnp.concatenate([jnp.zeros_like(values), values], axis=1)
            return jnp.where(core == 0, own, other)

        result_rows, d_result_rows = incoming(returned), incoming(d_returned)
        pair_out = [matmul(pick[k], result_rows) for k in range(pick.shape[0])]
        d_pairs = matmul(pick[0] + pick[1], d_result_rows)
        moe_half = sum(gates[:, k : k + 1] * pair_out[k] for k in range(pick.shape[0]))
        d_half = lax.dynamic_slice_in_dim(cotangent, core * half, half, axis=1).astype(f32)
        d_gates_part = jnp.concatenate(
            [jnp.sum(d_half * p, axis=1, keepdims=True) for p in pair_out], axis=1
        )
        after_part = (placed(moe_half) + shared_part).astype(bf16)
        d_branch_part = (d_shared_in + placed(d_pairs)).astype(bf16)
        d_gates_part = jnp.pad(d_gates_part, ((0, 0), (0, LANES - pick.shape[0])))
        after_other, d_branch_other, d_gates_other = swap(
            [after_part, d_branch_part, d_gates_part], 6
        )
        output = (middle + (after_part.astype(f32) + after_other.astype(f32))).astype(bf16)
        d_branch_sum = d_branch_part.astype(f32) + d_branch_other.astype(f32)
        d_gates = (d_gates_part + d_gates_other)[:, : pick.shape[0]]
        d_probs = jnp.sum(d_gates[:, :, None] * picked, axis=1)
        d_logits = (probs * (d_probs - jnp.sum(probs * d_probs, axis=-1, keepdims=True))).astype(bf16)
        grad_router = weight_grad(branch_in, d_logits)
        d_branch_in = d_branch_sum + input_grad(d_logits, router_w)
        grad_gain_two = jnp.sum(d_branch_in * normed_two, axis=0)
        d_norm_two = d_branch_in * gain_second
        d_middle = d_after + scale_two * (
            d_norm_two - normed_two * jnp.mean(d_norm_two * normed_two, axis=-1, keepdims=True)
        )

        shared_grads = [
            value.astype(bf16).reshape(blocks + (hidden,)) for value in (grad_sgate, grad_sup, grad_sdown_t)
        ]
        small_grads = jnp.concatenate(
            [grad_router, grad_gain_two[:, None], jnp.zeros((width, LANES - experts - 1), f32)], axis=1
        ).astype(bf16).reshape(blocks + (LANES,))
        expert_grads = [grad_e_gate, grad_e_up, grad_e_down]
    total, token_input_gradient, *combined = backward(
        [
            w_query, w_key, w_value, small_grads,
            window, queries, all_keys, all_values, lse, heads_out,
            d_middle, near, gains, cosines, sines, bias,
        ],
        shared_grads, combine, shard_rows, own_columns + (3 * hidden if shared_grads else 0),
        tok_count, heads_width, width, depth, reach,
    )
    if shared_grads:
        shared_total, total = total[:, : 3 * hidden], total[:, 3 * hidden :]
    if combined:
        output = combined[0]

    def columns_of(at, count):
        return total[:, at : at + count]

    at_out = 0
    at_pairs = at_out + heads_width + LANES
    grad_parts = [
        jnp.concatenate(
            [
                columns_of(at_pairs + (3 * pair + i) * LANES, LANES)
                for pair in range(heads_width // LANES)
            ],
            axis=1,
        )
        for i in range(3)
    ]
    return (
        output,
        token_input_gradient,
        total[:, own_columns - LANES] / attn_gain.astype(bf16).astype(f32),
        grad_parts[0],
        grad_parts[1],
        grad_parts[2],
        columns_of(at_out, heads_width).T,
        total[:, at_out + heads_width + experts],
        columns_of(at_out + heads_width, experts),
        shared_total[:, :hidden],
        shared_total[:, hidden : 2 * hidden],
        shared_total[:, 2 * hidden :].T,
    ) + tuple(expert_grads)


def solution(mesh):
    by_dp, both, turned = P("dp", None), P("dp", "tensor"), P("tensor", "dp")
    wide, tall = P(None, ("dp", "tensor")), P(("dp", "tensor"), None)
    weights = (P("dp"), both, both, both, turned, P("dp"), by_dp, both, both, turned, wide, wide, tall)
    return jax.shard_map(
        local,
        mesh=mesh,
        in_specs=(by_dp, by_dp) + weights + (by_dp, P()),
        out_specs=(by_dp, by_dp) + weights,
        check_vma=False,
    )
```

```python
import functools

import jax
import jax.numpy as jnp
import numpy as np
from jax import lax
from jax.experimental import pallas as pl
from jax.experimental.pallas import tpu as pltpu
from jax.sharding import PartitionSpec as P

HEAD = 64
WINDOW = 1024
LANES = 128
PLANE = 4

MESH = pl.DeviceIdType.MESH
f32 = jnp.float32
bf16 = jnp.bfloat16

eps = 1e-06
masked = -1e30


def matmul(left, right):
    return jnp.dot(left, right, preferred_element_type=f32)


def weight_grad(left, right):
    return lax.dot_general(
        left, right, (((0,), (0,)), ((), ())), preferred_element_type=f32
    )


def input_grad(left, right):
    return lax.dot_general(
        left, right, (((1,), (1,)), ((), ())), preferred_element_type=f32
    )


def rms_parts(values):
    factor = lax.rsqrt(jnp.mean(values * values, axis=-1, keepdims=True) + eps)
    return (values * factor, factor)


def silu_grad(values):
    sigma = jax.nn.sigmoid(values)
    return sigma * (1.0 + values * (1.0 - sigma))


def digits(me):
    return lax.div(me, PLANE), lax.rem(lax.div(me, 2), 2), lax.rem(me, 2)


def index_of(z, y, x):
    return z * PLANE + y * 2 + x


def push(src, dst, send, recv, device):
    copy = pltpu.make_async_remote_copy(
        src_ref=src,
        dst_ref=dst,
        send_sem=send,
        recv_sem=recv,
        device_id=device,
        device_id_type=MESH,
    )
    copy.start()
    return copy


def greet(devices):
    barrier = pltpu.get_barrier_semaphore()
    for device in devices:
        pl.semaphore_signal(barrier, inc=1, device_id=device, device_id_type=MESH)
    pl.semaphore_wait(barrier, len(devices))


def comm_params(collective_id, limit=48 << 20):
    return pltpu.CompilerParams(
        collective_id=collective_id, has_side_effects=True, vmem_limit_bytes=limit
    )


def dma(*shape):
    return pltpu.SemaphoreType.DMA(shape)


IN_HBM = pl.BlockSpec(memory_space=pl.ANY)
IN_VMEM = pl.BlockSpec(memory_space=pltpu.VMEM)


def grid_peers(depth, z, y, x):
    peers = [{"dp": index_of(lax.rem(z + k, depth), y, x)} for k in range(1, depth)]
    return peers, {"dp": index_of(z, 1 - y, x)}, {"dp": index_of(z, y, 1 - x)}


def swap_kernel(count, *refs):
    sources, targets, (send, recv) = refs[:count], refs[count : 2 * count], refs[2 * count :]
    sibling = {"tensor": 1 - lax.axis_index("tensor")}
    greet([sibling])
    copies = [
        push(a, b, send.at[i], recv.at[i], sibling)
        for i, (a, b) in enumerate(zip(sources, targets))
    ]
    for copy in copies:
        copy.wait()


def swap(arrays, collective_id):
    count = len(arrays)
    return pl.pallas_call(
        functools.partial(swap_kernel, count),
        out_shape=tuple(jax.ShapeDtypeStruct(a.shape, a.dtype) for a in arrays),
        in_specs=[IN_VMEM] * count,
        out_specs=(IN_VMEM,) * count,
        scratch_shapes=[dma(count), dma(count)],
        compiler_params=comm_params(collective_id),
        name="swap_cores",
    )(*arrays)


def dispatch_kernel(n, owners, first, second, got_first, got_second, send, recv, f_send, f_recv, own):
    me, core = lax.axis_index("dp"), lax.axis_index("tensor")
    sibling = {"tensor": 1 - core}
    greet([{"dp": lax.rem(me + k, n)} for k in range(1, n)] + [sibling])
    half = first.shape[-1] // 2
    cols = pl.ds(pl.multiple_of(core * half, half), half)
    pairs = ((first, got_first), (second, got_second))
    mine = lax.div(me, owners)
    copies = []
    for k in range(1, n):
        to = lax.rem(me + k, n)
        for i, (source, target) in enumerate(pairs):
            copies.append(
                push(
                    source.at[lax.div(to, owners), :, cols],
                    target.at[me, :, cols],
                    send.at[i, k],
                    recv.at[i, k],
                    {"dp": to},
                )
            )
    local = [
        pltpu.make_async_copy(source.at[mine], target.at[me], own.at[i])
        for i, (source, target) in enumerate(pairs)
    ]
    for copy in local:
        copy.start()
    forwards = []
    for k in range(1, n):
        source_of = lax.rem(me + n - k, n)
        for i, (source, target) in enumerate(pairs):
            copies[2 * (k - 1) + i].wait_recv()
            block = target.at[source_of, :, cols]
            forwards.append(push(block, block, f_send.at[i, k], f_recv.at[i, k], sibling))
    for copy in forwards:
        copy.wait_recv()
    for copy in local:
        copy.wait()
    for copy in copies + forwards:
        copy.wait_send()


def dispatch(first, second, n, owners):
    shape = jax.ShapeDtypeStruct((n,) + first.shape[1:], first.dtype)
    return pl.pallas_call(
        functools.partial(dispatch_kernel, n, owners),
        out_shape=(shape, shape),
        in_specs=[IN_HBM] * 2,
        out_specs=(IN_HBM, IN_HBM),
        scratch_shapes=[dma(2, n), dma(2, n), dma(2, n), dma(2, n), dma(2)],
        compiler_params=comm_params(2),
        name="dispatch_rows",
    )(first, second)


def return_kernel(n, groups, first, second, got_first, got_second, part, total, send, recv, f_send, f_recv, own):
    me, core = lax.axis_index("dp"), lax.axis_index("tensor")
    sibling = {"tensor": 1 - core}
    greet([{"dp": lax.rem(me + k, n)} for k in range(1, n)] + [sibling])
    half = first.shape[-1] // 2
    mine = pl.ds(pl.multiple_of(core * half, half), half)
    theirs = pl.ds(pl.multiple_of((1 - core) * half, half), half)
    pairs = ((first, got_first), (second, got_second))
    each = n // groups
    swaps = []
    for g in range(groups):
        block = pl.ds(g * each, each)
        for i, (source, target) in enumerate(pairs):
            swaps.append(
                push(
                    source.at[block, :, theirs],
                    part.at[i, block],
                    f_send.at[i, g],
                    f_recv.at[i, g],
                    sibling,
                )
            )
    for g in range(groups):
        block = pl.ds(g * each, each)
        for i, (source, target) in enumerate(pairs):
            swaps[2 * g + i].wait_recv()
            total[i, block] = (
                source[block, :, mine].astype(f32) + part[i, block].astype(f32)
            ).astype(bf16)
        for slot in range(g * each, (g + 1) * each):
            for i, (source, target) in enumerate(pairs):
                @pl.when(slot != me)
                def _():
                    push(
                        total.at[i, slot],
                        target.at[me],
                        send.at[i, slot],
                        recv.at[i, me],
                        {"dp": slot},
                    )
    local = [
        pltpu.make_async_copy(total.at[i, me], pairs[i][1].at[me], own.at[i]) for i in range(2)
    ]
    for copy in local:
        copy.start()
    for k in range(1, n):
        to, source_of = lax.rem(me + k, n), lax.rem(me + n - k, n)
        for i, (source, target) in enumerate(pairs):
            pltpu.make_async_remote_copy(
                total.at[i, to], target.at[source_of], send.at[i, to], recv.at[i, source_of],
                device_id={"dp": to}, device_id_type=MESH,
            ).wait()
    for copy in local:
        copy.wait()
    for copy in swaps:
        copy.wait_send()


def give_back(first, second, groups=4):
    n, capacity, width = first.shape
    half = jax.ShapeDtypeStruct((n, capacity, width // 2), first.dtype)
    buffer = pltpu.VMEM((2, n, capacity, width // 2), first.dtype)
    return pl.pallas_call(
        functools.partial(return_kernel, n, groups),
        out_shape=(half, half),
        in_specs=[IN_VMEM] * 2,
        out_specs=(IN_HBM, IN_HBM),
        scratch_shapes=[buffer, buffer, dma(2, n), dma(2, n), dma(2, groups), dma(2, groups), dma(2)],
        compiler_params=comm_params(3),
        name="return_rows",
    )(first, second)


def experts_kernel(
    n, groups, e_gate, e_up, e_down, full, got, got_gate, branch_in, cotangent, middle, probs, pick,
    routes, gains, small,
    d_middle, shared_total, g_small, shared_part, rows_total, ge_gate, ge_up, ge_down,
    d_rows_all, gate_w, up_w, down_w, staged, shared_w, hid, d_gate, d_up, part, swapped, d_total, returned,
    inner, inner_back, shared_in, tiles, wide, ends, ends_other, d_gates, d_gates_other,
    first_l, first_r, second_l, second_r, scatter_last, p_send, p_recv, z_send, z_recv,
    s_send, s_recv, r_send, r_recv, i_send, i_recv, e_send, e_recv, own, load, store,
):
    me, core = lax.axis_index("dp"), lax.axis_index("tensor")
    sibling = {"tensor": 1 - core}
    greet([{"dp": lax.rem(me + i, n)} for i in range(1, n)] + [sibling])
    capacity, width = got.shape[2:]
    count = branch_in.shape[0]
    half = width // 2
    mine = pl.ds(pl.multiple_of(core * half, half), half)
    theirs = pl.ds(pl.multiple_of((1 - core) * half, half), half)
    hidden = shared_w.shape[4] // 3
    loads = [
        pltpu.make_async_copy(
            full.at[:, :, :, :, pl.ds(full.shape[4] - 3 * hidden, 3 * hidden)], shared_w, load.at[2]
        )
    ]
    for copy in loads:
        copy.start()
    inner[...] = jnp.zeros_like(inner)

    step = 2 * LANES
    scatter = Scatter(
        n // PLANE,
        [(shared_w, at, step, shared_w, at + step, step, at) for at in range(0, 3 * hidden, 2 * step)],
        shared_total, (first_l, first_r, second_l, second_r, scatter_last),
        (p_send, p_recv, z_send, z_recv),
    )
    steps = scatter.plan()
    done = [0]

    def advance(count=1):
        for action, c in steps[done[0] : done[0] + count]:
            done[0] += 1
            action(c)
            if action == scatter.second and c + 4 < len(scatter.chunks):
                scatter.start(c + 4)

    pieces = []
    for source, target in ((e_gate, gate_w), (e_up, up_w), (e_down, down_w)):
        step = source.shape[0] // 4
        pieces += [(source, target, pl.ds(j * step, step)) for j in range(4)]

    def fetch(j):
        source, target, rows = pieces[j]
        return pltpu.make_async_copy(
            source.at[rows],
            staged.at[j % 2, pl.ds(0, rows.size), pl.ds(0, source.shape[1])],
            load.at[j % 2],
        )

    fetch(0).start()
    fetch(1).start()

    def take(j):
        source, target, rows = pieces[j]
        fetch(j).wait()
        target[rows, :] = staged[j % 2, : rows.size, : source.shape[1]].astype(bf16)
        if j + 2 < len(pieces):
            fetch(j + 2).start()

    swaps = {}

    def work(group):
        first, each = group * n // groups, n // groups
        slots = pl.ds(first, each)
        rows = pl.ds(first * capacity, each * capacity)
        rows_in = got[0, slots].reshape(each * capacity, width)
        gate_of = jnp.concatenate([got_gate[i].T[:capacity, 0:1] for i in range(first, first + each)], axis=0)
        d_rows = (gate_of * got[1, slots].reshape(each * capacity, width).astype(f32)).astype(bf16)
        d_rows_all[rows, :] = d_rows
        gate, up = matmul(rows_in, gate_w[...]), matmul(rows_in, up_w[...])
        sigma = 1.0 / (1.0 + jnp.exp(-gate))
        act = gate * sigma
        hid_low = (act * up).astype(bf16)
        hid[rows, :] = hid_low
        part[0, slots] = matmul(hid_low, down_w[...]).astype(bf16).reshape(each, capacity, width)
        d_hid = input_grad(d_rows, down_w[...])
        d_gate_low = (d_hid * up * (sigma * (1.0 + gate * (1.0 - sigma)))).astype(bf16)
        d_up_low = (d_hid * act).astype(bf16)
        d_gate[rows, :] = d_gate_low
        d_up[rows, :] = d_up_low
        part[1, slots] = (
            (input_grad(d_gate_low, gate_w[...]) + input_grad(d_up_low, up_w[...]))
            .astype(bf16)
            .reshape(each, capacity, width)
        )
        for a in (1, 0):
            swaps[a, group] = push(
                part.at[a, slots, :, theirs], swapped.at[a, slots],
                s_send.at[a, group], s_recv.at[a, group], sibling,
            )

    back = {}

    def give(group):
        first, each = group * n // groups, n // groups
        slots = pl.ds(first, each)
        swaps[1, group].wait_recv()
        d_total[slots] = (
            part[1, slots, :, mine].astype(f32) + swapped[1, slots].astype(f32)
        ).astype(bf16)
        homes = [{"dp": lax.rem(me + n - i, n)} for i in range(n)]
        for i in range(max(first, 1), first + each):
            back[1, i] = push(
                d_total.at[i], returned.at[me], r_send.at[i], r_recv.at[i], homes[i]
            )
        swaps[0, group].wait_recv()
        value = part[0, slots, :, mine].astype(f32) + swapped[0, slots].astype(f32)
        rows_total[slots] = value.astype(bf16)
        products = jnp.sum(value * got[1, slots, :, mine].astype(f32), axis=-1, keepdims=True)
        for i in range(first, first + each):
            row = jnp.broadcast_to(products[i - first], (capacity, LANES)).T[0:8, :]
            inner[i, :, :capacity] = row
            if i:
                back[0, i] = push(
                    inner.at[i], inner_back.at[me], i_send.at[i], i_recv.at[i], homes[i]
                )

    loads[0].wait()
    branch, cot = branch_in[...], cotangent[...]
    sgate_w, sup_w, sdown_w = (stacked(shared_w, pl.ds(i * hidden, hidden)) for i in range(3))
    gate, up = matmul(branch, sgate_w), matmul(branch, sup_w)
    sigma = 1.0 / (1.0 + jnp.exp(-gate))
    act = gate * sigma
    shared_hid = (act * up).astype(bf16)
    shared_part[...] = input_grad(shared_hid, sdown_w)
    d_shared = matmul(cot, sdown_w)
    d_sgate = (d_shared * up * (sigma * (1.0 + gate * (1.0 - sigma)))).astype(bf16)
    d_sup = (d_shared * act).astype(bf16)
    shared_in[...] = input_grad(d_sgate, sgate_w) + input_grad(d_sup, sup_w)
    for i, (left, right) in enumerate(((branch, d_sgate), (branch, d_sup), (cot, shared_hid))):
        put_rows(shared_w, weight_grad(left, right).astype(bf16), pl.ds(i * hidden, hidden))
        for c in range(2 * i, 2 * i + 2):
            if c < 4:
                scatter.start(c)
    for j in range(12):
        take(j)
    work(0)
    work(1)
    give(0)
    advance()
    work(2)
    give(1)
    advance()
    work(3)
    give(2)
    advance()
    give(3)
    advance()
    keep = [
        pltpu.make_async_copy(d_total.at[0], returned.at[me], own.at[0]),
        pltpu.make_async_copy(inner.at[0], inner_back.at[me], own.at[1]),
    ]
    for copy in keep:
        copy.start()

    stores = []

    def emit(value, tile, target):
        slot = len(stores) % 2
        if len(stores) >= 2:
            stores[-2].wait()
        tile[slot] = value.astype(bf16)
        stores.append(pltpu.make_async_copy(tile.at[slot], target, store.at[slot]))
        stores[-1].start()
        advance()

    rows_all = got[0].reshape(n * capacity, width)
    units = hid.shape[1]
    span = min(units, 256)
    for source, target in ((d_gate, ge_gate), (d_up, ge_up)):
        for at in range(0, units, span):
            columns = pl.ds(at, span)
            emit(weight_grad(rows_all, source[:, columns]), tiles, target.at[:, columns])
    for at in range(0, units, span):
        columns = pl.ds(at, span)
        emit(weight_grad(hid[:, columns], d_rows_all[...]), wide, ge_down.at[columns, :])

    for copy in keep:
        copy.wait()
    for a in range(2):
        for i in range(1, n):
            back[a, i].wait_recv()
    lane = lax.broadcasted_iota(jnp.int32, (1, LANES), 1)
    d_pairs = matmul(pick[0] + pick[1], returned[...].reshape(n * capacity, half))
    inner_row = jnp.concatenate([inner_back[e, 0:1, :capacity] for e in range(n)], axis=1)
    d_gate_lanes = jnp.zeros((count, LANES), f32)
    for i in range(2):
        value = jnp.sum(pick[i].astype(f32) * inner_row, axis=-1, keepdims=True)
        d_gate_lanes = d_gate_lanes + jnp.where(lane == i, value, 0.0)
    d_gates[...] = d_gate_lanes
    shared_in[:, mine] = shared_in[:, mine] + d_pairs
    ends[...] = shared_in[...].astype(bf16)
    last = [
        push(ends, ends_other, e_send.at[0], e_recv.at[0], sibling),
        push(d_gates, d_gates_other, e_send.at[1], e_recv.at[1], sibling),
    ]
    for copy in last:
        copy.wait()

    middle_all = middle[...]
    d_gates_all = d_gates[...] + d_gates_other[...]
    routes_turned = jnp.concatenate(
        [routes[...].astype(f32), jnp.zeros((LANES - routes.shape[0], count), f32)], axis=0
    ).T.astype(jnp.int32)
    d_probs = jnp.zeros((count, LANES), f32)
    for i in range(2):
        d_probs = d_probs + jnp.where(routes_turned[:, i : i + 1] == lane, d_gates_all[:, i : i + 1], 0.0)
    chance = probs[...]
    d_logits = (
        chance * (d_probs - jnp.sum(chance * d_probs, axis=-1, keepdims=True))
    ).astype(bf16)
    small_all = small[...]
    d_branch = (
        ends[...].astype(f32) + ends_other[...].astype(f32) + input_grad(d_logits, small_all)
    )
    factor = lax.rsqrt(jnp.mean(middle_all * middle_all, axis=-1, keepdims=True) + eps)
    normed = middle_all * factor
    gain_row = jnp.sum(d_branch * normed, axis=0, keepdims=True)
    d_norm = d_branch * gains[1:2, :]
    d_middle[...] = cotangent[...].astype(f32) + factor * (
        d_norm - normed * jnp.mean(d_norm * normed, axis=-1, keepdims=True)
    )
    put_rows(
        g_small,
        jnp.where(
            lane == n, jnp.broadcast_to(gain_row, (LANES, width)).T, weight_grad(branch, d_logits)
        ).astype(bf16),
        pl.ds(0, LANES),
    )
    for copy in stores[-2:]:
        copy.wait()
    advance(len(steps))
    scatter.drain()
    for copies in (swaps, back):
        for copy in copies.values():
            copy.wait_send()


def experts_fused(
    got, got_gate, weights, full, branch_in, cotangent, middle, probs, pick, routes, gains, small,
    depth, rows, hidden, groups=4,
):
    n, capacity, width = got.shape[1:]
    count = branch_in.shape[0]
    units = weights[0].shape[1]
    span = min(units, 256)
    half = width // 2

    def shape(*dims, dtype=bf16):
        return jax.ShapeDtypeStruct(dims, dtype)

    slots = pltpu.VMEM((n, capacity, half), bf16)
    both = pltpu.VMEM((2, n, capacity, half), bf16)
    wide = pltpu.VMEM((n * capacity, units), bf16)
    lanes = pltpu.VMEM((n, 8, LANES), f32)
    parts = 3 * hidden // (4 * LANES)
    results = pl.pallas_call(
        functools.partial(experts_kernel, n, groups),
        out_shape=(
            shape(count, width, dtype=f32), shape(rows, 3 * hidden, dtype=f32),
            shape(depth, 2, 2, rows, LANES), shape(count, width, dtype=f32), shape(n, capacity, half),
            shape(width, units), shape(width, units), shape(units, width),
        ),
        in_specs=[IN_HBM] * 4 + [IN_VMEM] * 10,
        out_specs=(IN_VMEM,) * 5 + (IN_HBM,) * 3,
        scratch_shapes=[
            pltpu.VMEM((n * capacity, width), bf16),
            pltpu.VMEM((width, units), bf16), pltpu.VMEM((width, units), bf16), pltpu.VMEM((units, width), bf16),
            pltpu.VMEM((2, max(width, units) // 4, max(width, units)), f32),
            pltpu.VMEM((depth, 2, 2, rows, 3 * hidden), bf16),
            wide, wide, wide,
            pltpu.VMEM((2, n, capacity, width), bf16),
            both, slots, slots,
            lanes, lanes,
            pltpu.VMEM((count, width), f32),
            pltpu.VMEM((2, width, span), bf16), pltpu.VMEM((2, span, width), bf16),
            pltpu.VMEM((count, width), bf16), pltpu.VMEM((count, width), bf16),
            pltpu.VMEM((count, LANES), f32), pltpu.VMEM((count, LANES), f32),
        ] + scatter_scratch(depth, rows, 3 * hidden // 2, parts) + [
            dma(2, groups), dma(2, groups),
            dma(n), dma(n), dma(n), dma(n), dma(2), dma(2), dma(2), dma(3), dma(2),
        ],
        compiler_params=comm_params(7, 62 << 20),
        name="experts_and_shared",
    )(
        *weights, full, got, got_gate, branch_in, cotangent, middle, probs, pick, routes.T, gains,
        small,
    )
    return results[:5] + ([value.astype(f32) for value in results[5:]],)


class Scatter:
    def __init__(self, depth, chunks, total, buffers, semaphores):
        self.depth, self.chunks, self.total = depth, chunks, total
        self.first_l, self.first_r, self.second_l, self.second_r, self.last = buffers
        self.p_send, self.p_recv, self.z_send, self.z_recv = semaphores
        self.z, self.y, self.x = digits(lax.axis_index("dp"))
        self.z_peers, self.y_peer, self.x_peer = grid_peers(depth, self.z, self.y, self.x)
        self.at_l, self.at_r, l, r = [], [], 0, 0
        for left, lc, lw, right, rc, rw, out in chunks:
            self.at_l.append(pl.ds(l, lw))
            self.at_r.append(pl.ds(r, rw))
            l, r = l + lw, r + rw
        self.ones, self.twos, self.threes = {}, {}, {}

    def start(self, c):
        left, lc, lw, right, rc, rw, out = self.chunks[c]
        self.ones[c] = [
            push(
                left.at[:, :, 1 - self.x, :, pl.ds(lc, lw)],
                self.first_l.at[:, :, :, self.at_l[c]],
                self.p_send.at[c, 0], self.p_recv.at[c, 0], self.x_peer,
            ),
            push(
                right.at[:, 1 - self.y, :, :, pl.ds(rc, rw)],
                self.first_r.at[:, :, :, self.at_r[c]],
                self.p_send.at[c, 1], self.p_recv.at[c, 1], self.y_peer,
            ),
        ]

    def second(self, c):
        left, lc, lw, right, rc, rw, out = self.chunks[c]
        in_l, in_r, first_l, first_r = self.at_l[c], self.at_r[c], self.first_l, self.first_r
        for copy in self.ones[c]:
            copy.wait_recv()

        def add(i, carry):
            for j in range(2):
                first_l[i, j, :, in_l] = (
                    first_l[i, j, :, in_l].astype(f32) + left[i, j, self.x, :, pl.ds(lc, lw)].astype(f32)
                ).astype(bf16)
                first_r[i, j, :, in_r] = (
                    first_r[i, j, :, in_r].astype(f32) + right[i, self.y, j, :, pl.ds(rc, rw)].astype(f32)
                ).astype(bf16)
            return carry

        lax.fori_loop(0, self.depth, add, 0)
        self.twos[c] = [
            push(
                first_l.at[:, 1 - self.y, :, in_l], self.second_l.at[:, :, in_l],
                self.p_send.at[c, 2], self.p_recv.at[c, 2], self.y_peer,
            ),
            push(
                first_r.at[:, 1 - self.x, :, in_r], self.second_r.at[:, :, in_r],
                self.p_send.at[c, 3], self.p_recv.at[c, 3], self.x_peer,
            ),
        ]

    def third(self, c):
        for copy in self.twos[c]:
            copy.wait_recv()
        sides = (
            (self.second_l, self.first_l, self.y, self.at_l[c]),
            (self.second_r, self.first_r, self.x, self.at_r[c]),
        )

        def add(i, carry):
            for source, before, place, here in sides:
                source[i, :, here] = (
                    source[i, :, here].astype(f32) + before[i, place, :, here].astype(f32)
                ).astype(bf16)
            return carry

        lax.fori_loop(0, self.depth, add, 0)
        self.threes[c] = [
            push(
                source.at[lax.rem(self.z + k + 1, self.depth), :, here],
                self.last.at[k, side, :, here],
                self.z_send.at[c, side, k], self.z_recv.at[c, side, k], self.z_peers[k],
            )
            for side, (source, before, place, here) in enumerate(sides)
            for k in range(self.depth - 1)
        ]

    def finish(self, c):
        left, lc, lw, right, rc, rw, out = self.chunks[c]
        for copy in self.threes[c]:
            copy.wait_recv()
        for side, source, here, at, span in (
            (0, self.second_l, self.at_l[c], out, lw),
            (1, self.second_r, self.at_r[c], out + lw, rw),
        ):
            value = source[self.z, :, here].astype(f32)
            for k in range(self.depth - 1):
                value = value + self.last[k, side, :, here].astype(f32)
            self.total[:, pl.ds(at, span)] = value

    def plan(self):
        count = len(self.chunks)
        steps = []
        for c in range(count + 1):
            if c < count:
                steps.append((self.second, c))
            if c >= 1:
                steps.append((self.third, c - 1))
        return steps + [(self.finish, c) for c in range(count)]

    def drain(self):
        for copies in list(self.ones.values()) + list(self.twos.values()) + list(self.threes.values()):
            for copy in copies:
                copy.wait_send()


def lanes_of(part):
    lane = lax.broadcasted_iota(jnp.int32, (1, LANES), 1)
    return (lax.div(lane, HEAD) == part).astype(f32).astype(bf16)


def swap_halves(values):
    lane = lax.broadcasted_iota(jnp.int32, (1, LANES), 1)
    low = lax.rem(lane, HEAD) < HEAD // 2
    return jnp.where(
        low, pltpu.roll(values, LANES - HEAD // 2, 1), pltpu.roll(values, HEAD // 2, 1)
    )


def put_rows(target, values, columns):
    rows = target.shape[3]
    for b in range(values.shape[0] // rows):
        target[b // PLANE, (b // 2) % 2, b % 2, :, columns] = values[b * rows : (b + 1) * rows]


def backward_kernel(
    depth, reach, per_core, shared, w_query, w_key, w_value, g_small, window, q, k, v, lse, heads_out, d_middle,
    near, gains, cosines, sines, bias, *rest,
):
    given = shared or 5
    rest, combine = rest[given:], rest[:given]
    total, d_tokens, d_full = rest[:2] + rest[-1:]
    rest = rest[2:-1]
    if not shared:
        rows_total, pick, gates, middle, shared_part = combine
        output, rows_back, end, end_other, o_send, o_recv, e_send, e_recv, keep = rest[:1] + rest[-8:]
        rest = rest[1:-8]
    (
    grads, attn_t, d_heads, dq_all, dk_all, dv_all, d_part, d_swap, d_sum, d_got, gain_got,
    first_l, first_r, second_l, second_r, last, p_send, p_recv, z_send, z_recv,
    t_send, t_recv, s_send, s_recv, f_send, f_recv,
    ) = rest
    n = depth * PLANE
    me, core = lax.axis_index("dp"), lax.axis_index("tensor")
    sibling = {"tensor": 1 - core}
    plane, z_next, z_before = Plane(me), *z_neighbours(me, n)
    heads_width = q.shape[1]
    count = q.shape[0]
    pairs = heads_width // LANES
    chunks = []
    out = 0
    step = 2 * LANES
    for source in combine if shared else ():
        for at in range(0, source.shape[4], 2 * step):
            chunks.append((source, at, step, source, at + step, step, out))
            out += 2 * step
    early = len(chunks)
    widths = [(step, step)] + [(step, LANES), (LANES, step)] * pairs
    widths = widths[: pairs + 1]
    at = 0
    for left, right in widths:
        chunks.append((grads, at, left, grads, at + left, right, out + at))
        at += left + right
    scatter = Scatter(
        depth, chunks, total, (first_l, first_r, second_l, second_r, last),
        (p_send, p_recv, z_send, z_recv),
    )
    if shared:
        greet(scatter.z_peers + plane.peers + [sibling, z_next, z_before])
    else:
        greet([{"dp": lax.rem(me + i, n)} for i in range(1, n)] + [sibling])
    lead = 4
    for c in range(min(lead, early)):
        scatter.start(c)
    steps = scatter.plan()
    done = [0]

    def advance(count=1):
        for action, c in steps[done[0] : done[0] + count]:
            if action == scatter.second and c not in scatter.ones:
                break
            done[0] += 1
            action(c)
            if action == scatter.second and c + lead < early:
                scatter.start(c + lead)

    out_w = pl.ds(LANES + 3 * heads_width, heads_width)
    gain = gains[0:1, :]
    d_attn = d_middle[...].astype(bf16)
    d_heads[...] = matmul(d_attn, stacked(near, out_w)).astype(bf16)
    put_rows(grads, weight_grad(d_attn, heads_out[...]).astype(bf16), pl.ds(0, heads_width))
    grads[:, :, :, :, pl.ds(heads_width, LANES)] = g_small[...]

    def normed(block):
        values = window[block].astype(f32)
        return values * lax.rsqrt(jnp.mean(values * values, axis=-1, keepdims=True) + eps)

    def turned(block, carry):
        rows = pl.ds(pl.multiple_of(block * count, count), count)
        attn_t[:, rows] = (normed(block) * gain).T.astype(bf16)
        return carry

    for block in range(reach + 1):
        turned(block, 0)
    scatter.start(early)
    home = []
    if not shared:
        home = [
            push(
                rows_total.at[i], rows_back.at[me], o_send.at[i], o_recv.at[i],
                {"dp": lax.rem(me + n - i, n)},
            )
            for i in range(1, n)
        ]
        kept = pltpu.make_async_copy(rows_total.at[0], rows_back.at[me], keep.at[0])
        kept.start()
    own = pl.ds(reach * count, count)
    for pair in range(pairs):
        columns = pl.ds(pair * LANES, LANES)
        k_pair, v_pair, q_pair, d_pair = k[:, columns], v[:, columns], q[:, columns], d_heads[:, columns]
        k_turned = k_pair.T
        dq, dk, dv = [], None, None
        for part in range(2):
            head = 2 * pair + part
            lanes = lanes_of(part)
            q_head, d_head = q_pair * lanes, d_pair * lanes
            probs = jnp.exp(input_grad(k_pair, q_head) + bias[...] - lse[head : head + 1, :])
            d_probs = input_grad(v_pair, d_head)
            inner = jnp.sum(probs * d_probs, axis=0, keepdims=True)
            d_scores = (probs * (d_probs - inner)).astype(bf16)
            advance(1 if shared else 0)
            dq.append(matmul(k_turned, d_scores)[part * HEAD : (part + 1) * HEAD, :])
            parts = matmul(d_scores, q_head), matmul(probs.astype(bf16), d_head)
            dk, dv = parts if part == 0 else (dk + parts[0], dv + parts[1])
            advance(1 if shared else 0)
        dq = jnp.concatenate(dq, axis=0).T * (HEAD ** (-0.5))
        cos_own, sin_own = cosines[own, :], sines[own, :]
        dq_low = turn(dq, cos_own, -sin_own).astype(bf16)
        dk_low = turn(dk, cosines[...], -sines[...]).astype(bf16)
        dv_low = dv.astype(bf16)
        dq_all[:, columns] = dq_low
        dk_all[:, columns] = dk_low
        dv_all[:, columns] = dv_low
        at = heads_width + LANES + pair * 3 * LANES
        put_rows(grads, matmul(attn_t[:, own], dq_low).astype(bf16), pl.ds(at, LANES))
        put_rows(grads, matmul(attn_t[...], dk_low).astype(bf16), pl.ds(at + LANES, LANES))
        put_rows(grads, matmul(attn_t[...], dv_low).astype(bf16), pl.ds(at + 2 * LANES, LANES))
        scatter.start(early + 1 + pair)
        advance(2 if shared else min(pair + 1, 2))

    width = d_part.shape[-1] // 2
    mine = pl.ds(pl.multiple_of(core * width, width), width)
    theirs = pl.ds(pl.multiple_of((1 - core) * width, width), width)
    swaps = {}
    query_v, key_v, value_v = (
        jnp.concatenate(
            [stacked(near, pl.ds(LANES * (1 + 3 * pair + i), LANES)) for pair in range(pairs)], axis=1
        )
        for i in range(3)
    )
    back = [None] * (PLANE - 1)

    def meet(block):
        swaps[block].wait_recv()
        d_sum[block] = (
            d_part[block, :, mine].astype(f32) + d_swap[block].astype(f32)
        ).astype(bf16)

    blocks = list(range(1, reach)) + [0, reach]
    for i, block in enumerate(blocks):
        rows = pl.ds(block * count, count)
        value = input_grad(dk_all[rows, :], key_v) + input_grad(dv_all[rows, :], value_v)
        if block == reach:
            value = value + input_grad(dq_all[...], query_v)
        d_part[block] = value.astype(bf16)
        swaps[block] = push(
            d_part.at[block, :, theirs], d_swap.at[block],
            s_send.at[block], s_recv.at[block], sibling,
        )
        if i:
            meet(blocks[i - 1])
        if i == reach - 1:
            for j in range(1, PLANE):
                back[j - 1] = push(
                    d_sum.at[lax.rem(plane.places[j] - plane.place + PLANE, PLANE)],
                    d_got.at[j], t_send.at[j], t_recv.at[j], plane.peers[j - 1],
                )
    meet(reach)
    swaps = list(swaps.values())
    advance(1)
    last_swap = []
    if not shared:
        kept.wait()
        for copy in home:
            copy.wait_recv()
        rows_all = rows_back[...].reshape(-1, width)
        moe = gates[:, 0:1] * matmul(pick[0], rows_all) + gates[:, 1:2] * matmul(pick[1], rows_all)
        end[...] = shared_part[...].astype(bf16)
        end[:, mine] = (shared_part[:, mine] + moe).astype(bf16)
        last_swap.append(push(end, end_other, e_send.at[0], e_recv.at[0], sibling))
    d_mine, d_before = d_sum[reach].astype(f32), d_sum[0].astype(f32)
    for j in range(1, PLANE):
        back[j - 1].wait_recv()
        ours = lax.select(plane.places[j] > plane.place, 1.0, 0.0)
        value = d_got[j].astype(f32)
        d_mine, d_before = d_mine + value * ours, d_before + value * (1.0 - ours)
    d_sum[reach] = d_before.astype(bf16)
    back.append(push(d_sum.at[reach], d_got.at[0], t_send.at[0], t_recv.at[0], z_before))
    advance(len(steps))
    if not shared:
        last_swap[0].wait_recv()
        output[...] = (
            middle[...] + (end[...].astype(f32) + end_other[...].astype(f32))
        ).astype(bf16)
    back[-1].wait_recv()
    d_mine = d_mine + d_got[0].astype(f32)
    d_full[:, mine] = d_mine.astype(bf16)
    both = push(d_full.at[:, mine], d_full.at[:, mine], f_send.at[0], f_recv.at[0], sibling)
    gain_sum = jnp.zeros((total.shape[0], 1), f32)
    at = out + heads_width + LANES
    for pair in range(pairs):
        for i, source in enumerate((w_query, w_key, w_value)):
            rounded = source[:, pl.ds(pair * LANES, LANES)].astype(bf16).astype(f32)
            products = total[:, pl.ds(at + (3 * pair + i) * LANES, LANES)] * rounded
            gain_sum = gain_sum + jnp.sum(products, axis=-1, keepdims=True)
    split = pl.ds(per_core, LANES)
    total[:, split] = jnp.broadcast_to(gain_sum, (total.shape[0], LANES))
    gain_copy = push(total.at[:, split], gain_got, f_send.at[1], f_recv.at[1], sibling)
    both.wait()
    gain_copy.wait()
    total[:, split] = total[:, split] + gain_got[...]
    values = window[reach].astype(f32)
    factor = lax.rsqrt(jnp.mean(values * values, axis=-1, keepdims=True) + eps)
    values = values * factor
    d_norm = d_full[...].astype(f32) * gain
    d_tokens[...] = d_middle[...] + factor * (
        d_norm - values * jnp.mean(d_norm * values, axis=-1, keepdims=True)
    )
    scatter.drain()
    for copy in back + swaps + last_swap + home:
        copy.wait_send()


def backward(arrays, shared, combine, rows, columns, count, heads_width, width, depth, reach):
    span = (reach + 1) * count
    summed = columns - LANES
    half = -(-summed // (2 * LANES)) * LANES
    width_shared = sum(value.shape[4] for value in shared)
    parts = width_shared // (4 * LANES) + 1 + heads_width // LANES
    own = summed - width_shared
    outs = (
        jax.ShapeDtypeStruct((rows, columns), f32),
        jax.ShapeDtypeStruct((count, width), f32),
    )
    extra = []
    if not shared:
        outs += (jax.ShapeDtypeStruct((count, width), bf16),)
        low = pltpu.VMEM((count, width), bf16)
        n = depth * PLANE
        extra = [
            pltpu.VMEM(combine[0].shape, bf16), low, low, dma(n), dma(n), dma(1), dma(1), dma(1)
        ]
    arrays = list(arrays) + list(shared) + list(combine)
    return pl.pallas_call(
        functools.partial(backward_kernel, depth, reach, columns - LANES, len(shared)),
        out_shape=outs,
        in_specs=[IN_VMEM] * len(arrays),
        out_specs=(IN_VMEM,) * len(outs),
        scratch_shapes=[
            pltpu.VMEM((depth, 2, 2, rows, own), bf16),
            pltpu.VMEM((width, span), bf16),
            pltpu.VMEM((count, heads_width), bf16),
            pltpu.VMEM((count, heads_width), bf16),
            pltpu.VMEM((span, heads_width), bf16),
            pltpu.VMEM((span, heads_width), bf16),
            pltpu.VMEM((reach + 1, count, width), bf16),
            pltpu.VMEM((reach + 1, count, width // 2), bf16),
            pltpu.VMEM((reach + 1, count, width // 2), bf16),
            pltpu.VMEM((reach, count, width // 2), bf16),
            pltpu.VMEM((rows, LANES), f32),
        ] + scatter_scratch(depth, rows, half, parts) + [
            dma(reach), dma(reach), dma(reach + 1), dma(reach + 1), dma(2), dma(2),
        ] + extra + [pltpu.VMEM((count, width), bf16)],
        compiler_params=comm_params(4, 58 << 20),
        name="attention_backward",
    )(*arrays)


def scatter_scratch(depth, rows, half, parts):
    first = pltpu.VMEM((depth, 2, rows, half), bf16)
    second = pltpu.VMEM((depth, rows, half), bf16)
    return [
        first, first, second, second, pltpu.VMEM((depth - 1, 2, rows, half), bf16),
        dma(parts, 4), dma(parts, 4), dma(parts, 2, depth - 1), dma(parts, 2, depth - 1),
    ]


class Plane:
    def __init__(self, me):
        z, y, x = digits(me)
        self.place = y * 2 + x
        self.places, self.peers = [self.place], []
        for j in range(1, PLANE):
            y_j, x_j = (1 - y if j & 2 else y), (1 - x if j & 1 else x)
            self.places.append(y_j * 2 + x_j)
            self.peers.append({"dp": index_of(z, y_j, x_j)})


def z_neighbours(me, n):
    return {"dp": lax.rem(me + PLANE, n)}, {"dp": lax.rem(me + n - PLANE, n)}


class Gather:
    def __init__(self, depth, chunks, shard, full, semaphores):
        self.depth, self.chunks, self.shard, self.full = depth, chunks, shard, full
        self.z_send, self.z_recv, self.p_send, self.p_recv = semaphores
        self.z, self.y, self.x = digits(lax.axis_index("dp"))
        self.z_peers, self.y_peer, self.x_peer = grid_peers(depth, self.z, self.y, self.x)
        self.ones, self.twos, self.threes = {}, {}, {}

    def _sides(self, c):
        at, left, right = self.chunks[c]
        return pl.ds(at, left), pl.ds(at + left, right)

    def first(self, c):
        at, left, right = self.chunks[c]
        columns = pl.ds(at, left + right)
        self.ones[c] = [
            push(
                self.shard.at[:, columns],
                self.full.at[self.z, self.y, self.x, :, columns],
                self.z_send.at[c, k], self.z_recv.at[c, k], self.z_peers[k],
            )
            for k in range(self.depth - 1)
        ]

    def second(self, c):
        left, right = self._sides(c)
        for copy in self.ones[c]:
            copy.wait_recv()
        a = self.full.at[:, self.y, self.x, :, left]
        b = self.full.at[:, self.y, self.x, :, right]
        self.twos[c] = [
            push(a, a, self.p_send.at[c, 0], self.p_recv.at[c, 0], self.y_peer),
            push(b, b, self.p_send.at[c, 1], self.p_recv.at[c, 1], self.x_peer),
        ]

    def third(self, c):
        left, right = self._sides(c)
        for copy in self.twos[c]:
            copy.wait_recv()
        a = self.full.at[:, :, self.x, :, left]
        b = self.full.at[:, self.y, :, :, right]
        self.threes[c] = [
            push(a, a, self.p_send.at[c, 2], self.p_recv.at[c, 2], self.x_peer),
            push(b, b, self.p_send.at[c, 3], self.p_recv.at[c, 3], self.y_peer),
        ]

    def finish(self, c):
        for copy in self.threes[c]:
            copy.wait_recv()

    def plan(self, lead, near):
        count = len(self.chunks)
        steps = []
        for s in range(count + 2):
            if s < count:
                steps.append((self.second, s))
                if s + lead < count:
                    steps.append((self.first, s + lead))
            if 1 <= s <= count:
                steps.append((self.third, s - 1))
            if 2 <= s < near + 2:
                steps.append((self.finish, s - 2))
        return steps + [(self.finish, c) for c in range(near, count)]

    def drain(self):
        for copies in list(self.ones.values()) + list(self.twos.values()) + list(self.threes.values()):
            for copy in copies:
                copy.wait_send()


def stacked(ref, columns):
    rows = ref.shape[3]
    if rows % 16 == 0:
        return ref[:, :, :, :, columns].reshape(-1, columns.size)
    blocks = [
        ref[b // PLANE, (b // 2) % 2, b % 2, :, columns].astype(f32)
        for b in range(ref.shape[0] * PLANE)
    ]
    return jnp.concatenate(blocks, axis=0).astype(bf16)


def turn(values, cos, sin):
    return values * cos + swap_halves(values) * sin


def forward_kernel(
    depth, reach, experts, chunks, near_edges, w_router, attn_gain, ffn_gain, w_query, w_key, w_value, out_shard, w_sgate, w_sup, down_shard,
    tokens, cotangent, routes, segments, row_cos, row_sin, block_cos, block_sin,
    full, near, small, window, q, k, v, lse, heads_out, cosines, sines, bias, gains, middle, branch_in, probs, gates, pick,
    *rest,
):
    n = depth * PLANE
    fused = n == experts
    if fused:
        got, got_gate, rows_send, gate_send, d_send, d_recv, e_send, e_recv, g_send, g_recv = (
            rest[:2] + rest[-8:]
        )
        rest = rest[2:-8]
        rows_out, d_rows_out = rows_send.at[0], rows_send.at[1]
    else:
        rows_out, d_rows_out = rest[:2]
        rest = rest[2:]
    (
        shard, attn_in, part, other,
        z_send, z_recv, p_send, p_recv, t_send, t_recv, f_send, f_recv, s_send, s_recv, own,
    ) = rest
    me, core = lax.axis_index("dp"), lax.axis_index("tensor")
    sibling = {"tensor": 1 - core}
    gather = Gather(depth, chunks, shard, full, (z_send, z_recv, p_send, p_recv))
    heads_width = q.shape[1]
    pairs = heads_width // LANES
    order = [None]
    for pair in range(pairs):
        order += [(piece, pair * LANES, LANES) for piece in (w_query, w_key, w_value)]
    order += [(piece, 0, piece.shape[1]) for piece in (out_shard, w_sgate, w_sup, down_shard)]
    def pack(pieces, at):
        for piece, start, size in pieces:
            shard[:, pl.ds(at, size)] = piece[:, pl.ds(start, size)].astype(bf16)
            at += size
        return at

    turned_small = jnp.concatenate(
        [w_router[...], attn_gain[...], ffn_gain[...], jnp.zeros((LANES - experts - 2, w_router.shape[1]), f32)],
        axis=0,
    )
    shard[:, pl.ds(0, LANES)] = turned_small.T.astype(bf16)
    at = pack(order[1:4], LANES)
    plane, z_next, z_before = Plane(me), *z_neighbours(me, n)
    if fused:
        greet([{"dp": lax.rem(me + i, n)} for i in range(1, n)] + [sibling])
    else:
        greet(gather.z_peers + plane.peers + [sibling, z_next, z_before])
    count, width = tokens.shape
    half = count // 2
    rows = pl.ds(pl.multiple_of(core * half, half), half)
    lead = 3
    gather.first(0)
    from_before = push(tokens.at[rows], window.at[0, rows], t_send.at[0], t_recv.at[0], z_next)
    pack(order[4:], at)
    for c in range(1, lead):
        gather.first(c)
    own_shard = pltpu.make_async_copy(shard, full.at[gather.z, gather.y, gather.x], own.at[0])
    own_shard.start()
    window[reach] = tokens[...]

    lane = lax.broadcasted_iota(jnp.int32, (1, LANES), 1)
    sign = jnp.where(lax.rem(lane, HEAD) < HEAD // 2, -1.0, 1.0)
    lines = count // LANES

    def segment_row(block):
        part = segments[pl.ds(block * lines, lines), :].astype(f32)
        return jnp.concatenate([part[i : i + 1, :] for i in range(lines)], axis=1)

    seg_query = segment_row(me)
    routes_turned = jnp.concatenate(
        [routes[...].astype(f32), jnp.zeros((LANES - routes.shape[0], count), f32)], axis=0
    ).T.astype(jnp.int32)
    tops = routes.shape[0]
    key_place = lax.broadcasted_iota(jnp.int32, (count, count), 0)
    query_place = lax.broadcasted_iota(jnp.int32, (count, count), 1)
    for b in range(reach + 1):
        at = pl.ds(b * count, count)
        c_b, s_b = block_cos[pl.ds(me + b, 1), :], block_sin[pl.ds(me + b, 1), :]
        cosines[at, :] = c_b * row_cos[...] - s_b * row_sin[...]
        sines[at, :] = (s_b * row_cos[...] + c_b * row_sin[...]) * sign
        block = me - reach + b
        seg_key = segment_row(lax.max(block, 0))
        seg_key = jnp.broadcast_to(seg_key, (LANES, count)).T[:, :1]
        distance = (reach - b) * count + query_place - key_place
        limit = lax.select(block >= 0, WINDOW, 0)
        seen = (distance >= 0) & (distance < limit) & (seg_key == seg_query)
        bias[at, :] = jnp.where(seen, 0.0, masked)

    capacity = rows_out.shape[1]
    named = [(routes_turned[:, i : i + 1] == lane).astype(f32) for i in range(tops)]
    below = (key_place > query_place).astype(f32).astype(bf16)
    before = matmul(below, sum(named).astype(bf16))
    slot_of = lax.broadcasted_iota(jnp.int32, (count, experts * capacity), 1)
    for i, name in enumerate(named):
        place = jnp.sum(name * before, axis=-1, keepdims=True).astype(jnp.int32)
        place = place + routes_turned[:, i : i + 1] * capacity
        pick[i] = (slot_of == place).astype(f32).astype(bf16)
    features = pl.ds(pl.multiple_of(core * (width // 2), width // 2), width // 2)
    sent, passed = {}, {}

    def dispatch_rows(a):
        for i in range(1, n):
            to = lax.rem(me + i, n)
            sent[a, i] = push(
                rows_send.at[a, to, :, features], got.at[a, i, :, features],
                d_send.at[a, i], d_recv.at[a, i], {"dp": to},
            )
        got[a, 0] = rows_send[a, me]

    def forward_rows(a):
        for i in range(1, n):
            sent[a, i].wait_recv()
            block = got.at[a, i, :, features]
            passed[a, i] = push(block, block, e_send.at[a, i], e_recv.at[a, i], sibling)

    if fused:
        rows_send[1] = (
            weight_grad(pick[0] + pick[1], cotangent[...]).astype(bf16).reshape(rows_out.shape)
        )

    def normed(b):
        values = window[b].astype(f32)
        return values * lax.rsqrt(jnp.mean(values * values, axis=-1, keepdims=True) + eps)

    own_shard.wait()
    steps = gather.plan(lead, len(near_edges))
    done = [0]

    def advance(until=None, waits=None):
        while done[0] < len(steps) and waits != 0:
            action, c = steps[done[0]]
            done[0] += 1
            action(c)
            if waits is not None and action != gather.first:
                waits -= 1
            if (action, c) == until:
                break

    from_before.wait_recv()
    t_copies = [from_before]
    for j in range(1, PLANE):
        source = window.at[lax.select(plane.places[j] < plane.place, 0, reach), rows]
        target = window.at[lax.rem(plane.place - plane.places[j] + PLANE, PLANE), rows]
        t_copies.append(push(source, target, t_send.at[j], t_recv.at[j], plane.peers[j - 1]))
    advance((gather.second, 1))
    forwards = []
    for j, copy in enumerate(t_copies):
        if j:
            copy.wait_recv()
        block = window.at[lax.rem(plane.places[j] - plane.place + PLANE, PLANE), rows]
        forwards.append(push(block, block, f_send.at[j], f_recv.at[j], sibling))
    landed = 0
    copies = []
    for i, (edge, c) in enumerate(near_edges):
        copies.append((c, pl.ds(landed, edge - landed), own.at[1 + i]))
        landed = edge

    def land(i):
        c, columns, semaphore = copies[i]
        advance((gather.finish, c))
        copy = pltpu.make_async_copy(
            full.at[:, :, :, :, columns], near.at[:, :, :, :, columns], semaphore
        )
        copy.start()
        copy.wait()

    land(0)
    for copy in forwards:
        copy.wait_recv()
    small_all = stacked(near, pl.ds(0, LANES))
    small[...] = small_all
    small_turned = small_all.astype(f32).T
    gain_first, gain_second = small_turned[experts : experts + 1, :], small_turned[experts + 1 : experts + 2, :]
    gains[...] = small_turned[experts : experts + 8, :]
    own_rows = pl.ds(reach * count, count)
    for b in range(reach + 1):
        attn_in[pl.ds(b * count, count), :] = (normed(b) * gain_first).astype(bf16)
    lse[...] = jnp.zeros_like(lse)
    for pair in range(pairs):
        if pair:
            land(pair)
        if fused and pair == pairs // 2:
            dispatch_rows(1)
        at = LANES * (1 + 3 * pair)
        columns = pl.ds(pair * LANES, LANES)
        products = matmul(attn_in[...], stacked(near, pl.ds(at + LANES, 2 * LANES)))
        k_pair = turn(products[:, :LANES], cosines[...], sines[...]).astype(bf16)
        v_pair = products[:, LANES:].astype(bf16)
        queries = matmul(attn_in[own_rows, :], stacked(near, pl.ds(at, LANES)))
        q_pair = (
            turn(queries, cosines[own_rows, :], sines[own_rows, :]) * (HEAD ** (-0.5))
        ).astype(bf16)
        k[:, columns], v[:, columns], q[:, columns] = k_pair, v_pair, q_pair
        v_turned = v_pair.T
        outs = []
        for part_of in range(2):
            head = 2 * pair + part_of
            scores = input_grad(k_pair, q_pair * lanes_of(part_of)) + bias[...]
            peak = jnp.max(scores, axis=0, keepdims=True)
            expo = jnp.exp(scores - peak)
            total = jnp.sum(expo, axis=0, keepdims=True)
            lse[head : head + 1, :] = peak + jnp.log(total)
            weights = (expo * (1.0 / total)).astype(bf16)
            outs.append(matmul(v_turned, weights)[part_of * HEAD : (part_of + 1) * HEAD, :])
            advance(waits=1)
        heads_out[:, columns] = jnp.concatenate(outs, axis=0).T.astype(bf16)
    land(pairs)
    out_w = stacked(near, pl.ds(LANES + 3 * heads_width, heads_width))
    part[...] = input_grad(heads_out[...], out_w).astype(bf16)
    swapped = push(part, other, s_send.at[0], s_recv.at[0], sibling)
    swapped.wait()
    middle_all = tokens[...].astype(f32) + (part[...].astype(f32) + other[...].astype(f32))
    middle[...] = middle_all
    factor = lax.rsqrt(jnp.mean(middle_all * middle_all, axis=-1, keepdims=True) + eps)
    branch = (middle_all * factor * gain_second).astype(bf16)
    branch_in[...] = branch

    logits = jnp.where(lane < experts, matmul(branch, small_all), masked)
    expo = jnp.exp(logits - jnp.max(logits, axis=-1, keepdims=True))
    chance = expo / jnp.sum(expo, axis=-1, keepdims=True)
    probs[...] = chance
    gate_lanes = jnp.zeros((count, LANES), f32)
    gate_row = jnp.zeros((1, experts * capacity), f32)
    d_gathered = None if fused else jnp.zeros((experts * capacity, width), f32)
    for i, name in enumerate(named):
        gate = jnp.sum(chance * name, axis=-1, keepdims=True)
        gate_lanes = gate_lanes + jnp.where(lane == i, gate, 0.0)
        if fused:
            gate_row = gate_row + jnp.sum(gate * pick[i].astype(f32), axis=0, keepdims=True)
        else:
            d_rows = (gate * cotangent[...].astype(f32)).astype(bf16)
            d_gathered = d_gathered + weight_grad(pick[i], d_rows)
    gates[...] = gate_lanes
    if fused:
        gate_send[...] = jnp.zeros_like(gate_send)
        for e in range(experts):
            gate_send[e, 0:1, :capacity] = gate_row[:, e * capacity : (e + 1) * capacity]
    else:
        d_rows_out[...] = d_gathered.astype(bf16).reshape(d_rows_out.shape)
    rows_out[...] = weight_grad(pick[0] + pick[1], branch).astype(bf16).reshape(rows_out.shape)
    gate_sent = []
    if fused:
        dispatch_rows(0)
        for i in range(1, n):
            to = lax.rem(me + i, n)
            gate_sent.append(
                push(gate_send.at[to], got_gate.at[i], g_send.at[i], g_recv.at[i], {"dp": to})
            )
        got_gate[0] = gate_send[me]
        advance(waits=4)
        forward_rows(1)
        advance(waits=5)
        forward_rows(0)
    advance()
    if fused:
        for copy in gate_sent:
            copy.wait_recv()
        for copy in passed.values():
            copy.wait_recv()
        for copy in list(sent.values()) + list(passed.values()) + gate_sent:
            copy.wait_send()
    gather.drain()
    for copy in t_copies + forwards:
        copy.wait_send()


def angle_tables(tok_count, blocks, reach):
    freqs = (10000.0 ** (-np.arange(HEAD // 2, dtype=np.float32) * np.float32(2.0 / HEAD))).astype(np.float64)
    freqs = np.tile(freqs, LANES // (HEAD // 2))[None, :]
    inner = np.arange(tok_count)[:, None] * freqs
    starts = np.maximum(np.arange(-reach, blocks), 0) * tok_count
    starts = np.pad(starts, (0, -len(starts) % 8))[:, None] * freqs
    return [jnp.asarray(f(a), f32) for a in (inner, starts) for f in (np.cos, np.sin)]


def forward(arrays, tokens, cotangent, routes, segments, depth, reach, experts, heads_width, hidden):
    count, width = tokens.shape
    n = depth * PLANE
    rows = arrays[3].shape[0]
    span = (reach + 1) * count
    near_width = LANES + 4 * heads_width
    columns = near_width + 3 * hidden
    capacity = count // 4
    step = 4 * LANES
    pairs = heads_width // LANES
    widths = [step] + [3 * LANES] * (pairs - 1) + [heads_width] + [2 * step] * ((columns - near_width) // (2 * step))
    chunks, at = [], 0
    for w in widths:
        left = (w // LANES + (len(chunks) + 1) % 2) // 2 * LANES
        chunks.append((at, left, w - left))
        at += w
    near_edges = tuple((sum(widths[: c + 1]), c) for c in range(pairs + 1))
    parts = len(chunks)
    tables = angle_tables(count, n, reach)
    segment_rows = segments.reshape(-1, LANES)

    def shape(*dims, dtype=bf16):
        return jax.ShapeDtypeStruct(dims, dtype)

    outs = (
        shape(depth, 2, 2, rows, columns),
        shape(depth, 2, 2, rows, near_width),
        shape(width, LANES),
        shape(reach + 1, count, width),
        shape(count, heads_width), shape(span, heads_width), shape(span, heads_width),
        shape(-(-heads_width // HEAD // 8) * 8, count, dtype=f32),
        shape(count, heads_width),
        shape(span, LANES, dtype=f32), shape(span, LANES, dtype=f32), shape(span, count, dtype=f32),
        shape(8, width, dtype=f32),
        shape(count, width, dtype=f32), shape(count, width),
        shape(count, LANES, dtype=f32), shape(count, LANES, dtype=f32),
        shape(routes.shape[1], count, experts * capacity),
    )
    if n == experts:
        outs += (shape(2, n, capacity, width), shape(n, 8, LANES, dtype=f32))
        extra = [
            pltpu.VMEM((2, n, capacity, width), bf16), pltpu.VMEM((n, 8, LANES), f32),
            dma(2, n), dma(2, n), dma(2, n), dma(2, n), dma(n), dma(n),
        ]
    else:
        outs += (shape(experts, capacity, width), shape(experts, capacity, width))
        extra = []
    inputs = list(arrays) + [tokens, cotangent, routes.T, segment_rows, tables[0], tables[1], tables[2], tables[3]]
    return pl.pallas_call(
        functools.partial(forward_kernel, depth, reach, experts, tuple(chunks), near_edges),
        out_shape=outs,
        in_specs=[IN_VMEM] * len(inputs),
        out_specs=(IN_HBM,) + (IN_VMEM,) * (len(outs) - 1),
        scratch_shapes=[
            pltpu.VMEM((rows, columns), bf16),
            pltpu.VMEM((span, width), bf16),
            pltpu.VMEM((count, width), bf16),
            pltpu.VMEM((count, width), bf16),
            dma(parts, depth - 1), dma(parts, depth - 1), dma(parts, 4), dma(parts, 4),
            dma(reach), dma(reach), dma(reach), dma(reach), dma(1), dma(1), dma(2 + pairs),
        ] + extra,
        compiler_params=comm_params(1, 58 << 20),
        name="gather_and_attend",
    )(*inputs)


def local(
    tokens, cotangent, attn_gain, w_query, w_key, w_value, w_out, ffn_gain, w_router,
    w_sgate, w_sup, w_sdown, e_gate, e_up, e_down, routes, segments,
):
    tok_count, width = tokens.shape
    n = lax.axis_size("dp")
    depth = n // PLANE
    me = lax.axis_index("dp")
    core = lax.axis_index("tensor")
    experts = w_router.shape[1]
    owners = n // experts
    capacity = tok_count // 4
    reach = (WINDOW + tok_count - 1) // tok_count
    shard_rows = w_query.shape[0]
    heads_width = w_query.shape[1]
    hidden = w_sgate.shape[1]
    half = width // 2

    near_width = LANES + 4 * heads_width
    own_columns = near_width + LANES
    (
        full, near, small, window, queries, all_keys, all_values, lse, heads_out, cosines, sines, bias, gains,
        middle, branch_in, probs, gates, pick, *sent_rows,
    ) = forward(
        (w_router.T, attn_gain[None, :], ffn_gain[None, :], w_query, w_key, w_value, w_out.T, w_sgate, w_sup, w_sdown.T),
        tokens, cotangent, routes, segments, depth, reach, experts, heads_width, hidden,
    )
    gain_second = gains[1]
    blocks = (depth, 2, 2, shard_rows)
    if owners == 1:
        d_middle, shared_total, small_grads, shared_part, rows_back, expert_grads = experts_fused(
            *sent_rows, (e_gate, e_up, e_down), full, branch_in, cotangent, middle, probs,
            pick, routes, gains, small, depth, shard_rows, hidden,
        )
        shared_grads, combine = (), (rows_back, pick, gates, middle, shared_part)
    else:
        sgate_w, sup_w, sdown_t = (
            full[:, :, :, :, near_width + i * hidden : near_width + (i + 1) * hidden].reshape(width, hidden)
            for i in range(3)
        )
        router_w = small[:, :experts]
        expert_gate = e_gate.astype(bf16)
        expert_up = e_up.astype(bf16)
        expert_down = e_down.astype(bf16)
        normed_two, scale_two = rms_parts(middle)
        probs = probs[:, :experts]
        picked = (routes[:, :, None] == jnp.arange(experts, dtype=jnp.int32)[None, None, :]).astype(f32)
        d_after = cotangent.astype(f32)
        combine = ()
        rows_in, d_rows_in = dispatch(*sent_rows, n, owners)

        rows_in = rows_in.reshape(n * capacity, width)
        d_rows_in = d_rows_in.reshape(n * capacity, width)
        gate_hidden = matmul(rows_in, expert_gate)
        up_hidden = matmul(rows_in, expert_up)
        gate_act = jax.nn.silu(gate_hidden)
        expert_hidden = (gate_act * up_hidden).astype(bf16)
        part_rows = matmul(expert_hidden, expert_down).astype(bf16)
        d_hidden = input_grad(d_rows_in, expert_down)
        d_gate_hidden = (d_hidden * up_hidden * silu_grad(gate_hidden)).astype(bf16)
        d_up_hidden = (d_hidden * gate_act).astype(bf16)
        d_part_rows = (
            input_grad(d_gate_hidden, expert_gate) + input_grad(d_up_hidden, expert_up)
        ).astype(bf16)
        returned, d_returned = give_back(
            part_rows.reshape(n, capacity, width), d_part_rows.reshape(n, capacity, width)
        )
        grad_e_down = weight_grad(expert_hidden, d_rows_in)
        grad_e_gate = weight_grad(rows_in, d_gate_hidden)
        grad_e_up = weight_grad(rows_in, d_up_hidden)

        shared_gate = matmul(branch_in, sgate_w)
        shared_up = matmul(branch_in, sup_w)
        shared_act = jax.nn.silu(shared_gate)
        shared_hidden = (shared_act * shared_up).astype(bf16)
        shared_part = input_grad(shared_hidden, sdown_t)
        d_shared = matmul(cotangent, sdown_t)
        grad_sdown_t = weight_grad(cotangent, shared_hidden)
        d_sgate = (d_shared * shared_up * silu_grad(shared_gate)).astype(bf16)
        d_sup = (d_shared * shared_act).astype(bf16)
        grad_sgate = weight_grad(branch_in, d_sgate)
        grad_sup = weight_grad(branch_in, d_sup)
        d_shared_in = input_grad(d_sgate, sgate_w) + input_grad(d_sup, sup_w)

        def incoming(rows):
            rows = rows.reshape(experts, owners, capacity, half)
            if owners > 1:
                rows = jnp.sum(rows.astype(f32), axis=1).astype(bf16)
            return rows.reshape(experts * capacity, half)

        def placed(values):
            own = jnp.concatenate([values, jnp.zeros_like(values)], axis=1)
            other = jnp.concatenate([jnp.zeros_like(values), values], axis=1)
            return jnp.where(core == 0, own, other)

        result_rows, d_result_rows = incoming(returned), incoming(d_returned)
        pair_out = [matmul(pick[k], result_rows) for k in range(pick.shape[0])]
        d_pairs = matmul(pick[0] + pick[1], d_result_rows)
        moe_half = sum(gates[:, k : k + 1] * pair_out[k] for k in range(pick.shape[0]))
        d_half = lax.dynamic_slice_in_dim(cotangent, core * half, half, axis=1).astype(f32)
        d_gates_part = jnp.concatenate(
            [jnp.sum(d_half * p, axis=1, keepdims=True) for p in pair_out], axis=1
        )
        after_part = (placed(moe_half) + shared_part).astype(bf16)
        d_branch_part = (d_shared_in + placed(d_pairs)).astype(bf16)
        d_gates_part = jnp.pad(d_gates_part, ((0, 0), (0, LANES - pick.shape[0])))
        after_other, d_branch_other, d_gates_other = swap(
            [after_part, d_branch_part, d_gates_part], 6
        )
        output = (middle + (after_part.astype(f32) + after_other.astype(f32))).astype(bf16)
        d_branch_sum = d_branch_part.astype(f32) + d_branch_other.astype(f32)
        d_gates = (d_gates_part + d_gates_other)[:, : pick.shape[0]]
        d_probs = jnp.sum(d_gates[:, :, None] * picked, axis=1)
        d_logits = (probs * (d_probs - jnp.sum(probs * d_probs, axis=-1, keepdims=True))).astype(bf16)
        grad_router = weight_grad(branch_in, d_logits)
        d_branch_in = d_branch_sum + input_grad(d_logits, router_w)
        grad_gain_two = jnp.sum(d_branch_in * normed_two, axis=0)
        d_norm_two = d_branch_in * gain_second
        d_middle = d_after + scale_two * (
            d_norm_two - normed_two * jnp.mean(d_norm_two * normed_two, axis=-1, keepdims=True)
        )

        shared_grads = [
            value.astype(bf16).reshape(blocks + (hidden,)) for value in (grad_sgate, grad_sup, grad_sdown_t)
        ]
        small_grads = jnp.concatenate(
            [grad_router, grad_gain_two[:, None], jnp.zeros((width, LANES - experts - 1), f32)], axis=1
        ).astype(bf16).reshape(blocks + (LANES,))
        expert_grads = [grad_e_gate, grad_e_up, grad_e_down]
    total, token_input_gradient, *combined = backward(
        [
            w_query, w_key, w_value, small_grads,
            window, queries, all_keys, all_values, lse, heads_out,
            d_middle, near, gains, cosines, sines, bias,
        ],
        shared_grads, combine, shard_rows, own_columns + (3 * hidden if shared_grads else 0),
        tok_count, heads_width, width, depth, reach,
    )
    if shared_grads:
        shared_total, total = total[:, : 3 * hidden], total[:, 3 * hidden :]
    if combined:
        output = combined[0]

    def columns_of(at, count):
        return total[:, at : at + count]

    at_out = 0
    at_pairs = at_out + heads_width + LANES
    grad_parts = [
        jnp.concatenate(
            [
                columns_of(at_pairs + (3 * pair + i) * LANES, LANES)
                for pair in range(heads_width // LANES)
            ],
            axis=1,
        )
        for i in range(3)
    ]
    return (
        output,
        token_input_gradient,
        total[:, own_columns - LANES] / attn_gain.astype(bf16).astype(f32),
        grad_parts[0],
        grad_parts[1],
        grad_parts[2],
        columns_of(at_out, heads_width).T,
        total[:, at_out + heads_width + experts],
        columns_of(at_out + heads_width, experts),
        shared_total[:, :hidden],
        shared_total[:, hidden : 2 * hidden],
        shared_total[:, 2 * hidden :].T,
    ) + tuple(expert_grads)


def solution(mesh):
    by_dp, both, turned = P("dp", None), P("dp", "tensor"), P("tensor", "dp")
    wide, tall = P(None, ("dp", "tensor")), P(("dp", "tensor"), None)
    weights = (P("dp"), both, both, both, turned, P("dp"), by_dp, both, both, turned, wide, wide, tall)
    return jax.shard_map(
        local,
        mesh=mesh,
        in_specs=(by_dp, by_dp) + weights + (by_dp, P()),
        out_specs=(by_dp, by_dp) + weights,
        check_vma=False,
    )
```
